32 devices in a mesh: expert: 8 (over z, x), shard: 4 (over y, core).
Axes of the slice: x: 2, y: 2, z: 4, core: 2. Of those that a mesh axis runs over, the one named last changes fastest.
Arguments:
- tokens: bfloat16 [32, 1024, 768], P(('expert', 'shard')), may hold values from -6 to 6
- segments: int32 [32, 1024], P(('expert', 'shard')), may hold values from 0 to 15, never falling along the last dimension, each value on 1 to 512 neighbouring positions
- routes: int32 [32, 1024, 1], P(('expert', 'shard')), may hold values from 0 to 7
- order: int32 [32, 1024], P(('expert', 'shard')), may hold values from 0 to 1023, each once within a row
- gain_attn: bfloat16 [768], P('shard'), may hold values from 0.099609375 to 1.8984375
- w_query: bfloat16 [768, 768], P('shard'), may hold values from -0.21875 to 0.21875
- w_key: bfloat16 [768, 768], P('shard'), may hold values from -0.21875 to 0.21875
- w_value: bfloat16 [768, 768], P('shard'), may hold values from -0.21875 to 0.21875
- w_output: bfloat16 [768, 768], P('shard'), may hold values from -1.75 to 1.75
- rel_bias: bfloat16 [32, 12], P('shard'), may hold values from -6 to 6
- gain_ffn: bfloat16 [768], P('shard'), may hold values from 0.099609375 to 1.8984375
- w_router: bfloat16 [768, 8], P('shard'), may hold values from -0.109375 to 0.109375
- w_in: bfloat16 [8, 768, 3072], P('expert', None, 'shard'), may hold values from -0.21875 to 0.21875
- w_out: bfloat16 [8, 3072, 768], P('expert', 'shard'), may hold values from -1.75 to 1.75
- cotangent: bfloat16 [32, 1024, 768], P(('expert', 'shard')), may hold values from -6 to 6
Outputs:
- mixed: bfloat16 [32, 1024, 768], P(('expert', 'shard'))
- d_tokens: bfloat16 [32, 1024, 768], P(('expert', 'shard'))
- grad_gain_attn: float32 [768], P('shard')
- grad_w_query: float32 [768, 768], P('shard')
- grad_w_key: float32 [768, 768], P('shard')
- grad_w_value: float32 [768, 768], P('shard')
- grad_w_output: float32 [768, 768], P('shard')
- grad_rel_bias: float32 [32, 12], P('shard')
- grad_gain_ffn: float32 [768], P('shard')
- grad_w_router: float32 [768, 8], P('shard')
- grad_w_in: float32 [8, 768, 3072], P('expert', None, 'shard')
- grad_w_out: float32 [8, 3072, 768], P('expert', 'shard')
The draws below stay inside these ranges and needn't reach their ends.
Inputs may be any that keep to these rules, and one draw needn't show every extreme that they name: `segments`: document numbers never fall along a sequence. `order`: each sequence's row holds every position number once.
All inputs are finite; a program needn't handle non-finite values.
Results may differ from the reference program's by a relative error of at most 0.019.
Values may be sent and summed in bfloat16 or wider, within the bound.
A program may use at most 320 MiB of HBM per device.

```python
import math
import jax
import jax.numpy as jnp
import numpy as np
from jax import lax

D = 768
HEADS = 12
HEAD_DIM = 64
FF = 3072
BUCKETS = 32
LEN = 1024
SEQ_DEV = 1
SEQS = 32
EXPERTS = 8
CAP = 160


def level_of(stream_key, dims, pieces, smallest, high):
    level, own = 1.0, jax.random.fold_in(stream_key, 6)
    for dim, parts in pieces:
        steps = jnp.exp(jax.random.uniform(jax.random.fold_in(own, dim), (parts,), jnp.float32, smallest / len(pieces), high / len(pieces)))
        level = level * jnp.repeat(steps, dims[dim] // parts).reshape([-1 if axis == dim else 1 for axis in range(len(dims))])
    return level


def different_ones(key, rows, count, top, lift):
    ranking = jax.random.permutation(jax.random.fold_in(key, 1), count)
    favour = ranking
    for power in range(3):
        favour = favour * favour // count
    favour = favour * lift // count
    tickets = jax.random.randint(jax.random.fold_in(key, 2), (rows, count), 0, 4096) + favour
    fixed_rows = jax.random.permutation(jax.random.fold_in(key, 3), rows)[jnp.arange(count) % rows]
    tickets = jnp.where(jnp.arange(rows)[:, None] == fixed_rows[None, :], 1 << 14, tickets)
    score = tickets * count + jnp.arange(count)
    return lax.top_k(score.astype(jnp.int32), top)[1].astype(jnp.int32)


def profile(number_of, total, reach, slope):
    portions = [(1 << 20) // math.isqrt(grade ** slope) + 1 for grade in range(2, number_of + 1)]
    surplus, given = total - reach - (number_of - 1), [1] * (number_of - 1)
    while surplus > 0:
        candidates = [i for i in range(number_of - 1) if given[i] < reach]
        whole, budget = sum([portions[i] for i in candidates]), surplus
        for i in candidates:
            extra = min(reach - given[i], max(1, budget * portions[i] // whole), surplus)
            given[i] = given[i] + extra
            surplus = surplus - extra
    return np.array([reach] + given)


def uneven_parts(own_key, amount, total, limit, lean):
    if amount == 2:
        one = jax.random.randint(own_key, (), max(1, total - limit), min(limit, total - 1) + 1)
        return jnp.stack([one, total - one])
    sizes = jnp.asarray(profile(amount, total, limit, lean), jnp.int32)
    couples = (amount - 1) // 2
    giver, taker = sizes[1:1 + 2 * couples:2], sizes[2:2 + 2 * couples:2]
    room = jnp.minimum(giver - 1, limit - taker)
    shifted = jax.random.randint(jax.random.fold_in(own_key, 1), (couples,), 0, 1 << 20) % (room + 1)
    sizes = sizes.at[1:1 + 2 * couples:2].set(giver - shifted).at[2:2 + 2 * couples:2].set(taker + shifted)
    return sizes[jax.random.permutation(jax.random.fold_in(own_key, 2), amount)]


def centred(rng, shape, scale, most, shards=(), held_as=jnp.bfloat16):
    array = jax.random.normal(rng, shape, jnp.float32) * scale
    if len(shards) > 0:
        array = level_of(rng, shape, shards, -0.22, 0.18) * array
    return jnp.clip(array, min=-most, max=most).astype(held_as)


def setup_inputs(seed: int = 0) -> dict:
    splits = jax.random.split(jax.random.key(seed), 16)
    tokens = centred(splits[0], (SEQS, LEN, D), 1.0, 6.0, ((0, 32),))
    segments = jax.vmap(lambda own: jnp.searchsorted(jnp.cumsum(uneven_parts(own, max(LEN // 64, 4), LEN, LEN // 2, 2)), jnp.arange(LEN), side="right"))(jax.random.split(splits[1], SEQS)).reshape((SEQS, LEN)).astype(jnp.int32)
    routes = different_ones(splits[2], SEQS * LEN, EXPERTS, 1, 1024).reshape((SEQS, LEN, 1))
    order = jax.vmap(lambda own: jax.random.permutation(own, LEN))(jax.random.split(splits[3], SEQS)).reshape((SEQS, LEN)).astype(jnp.int32)
    gain_attn = jnp.clip(1.0 + 0.18 * jax.random.normal(splits[4], (D,), jnp.float32), 0.099609375, 1.8984375).astype(jnp.bfloat16)
    w_query = centred(splits[5], (D, D), D ** -0.5, 0.21875, ((0, 4),))
    w_key = centred(splits[6], (D, D), D ** -0.5, 0.21875, ((0, 4),))
    w_value = centred(splits[7], (D, D), D ** -0.5, 0.21875, ((0, 4),))
    w_output = centred(splits[8], (D, D), (D // 64) ** -0.5, 1.75, ((0, 4),))
    rel_bias = centred(splits[9], (BUCKETS, HEADS), 1.0, 6.0, ((0, 4),))
    gain_ffn = jnp.clip(1.0 + 0.18 * jax.random.normal(splits[10], (D,), jnp.float32), 0.099609375, 1.8984375).astype(jnp.bfloat16)
    w_router = centred(splits[11], (D, EXPERTS), (D * 4) ** -0.5, 0.109375, ((0, 4),))
    w_in = centred(splits[12], (EXPERTS, D, FF), D ** -0.5, 0.21875, ((0, 8), (2, 4)))
    w_out = centred(splits[13], (EXPERTS, FF, D), (2.0 * EXPERTS * FF ** -0.5), 1.75, ((0, 8), (1, 4)))
    cotangent = centred(splits[14], (SEQS, LEN, D), 1.0, 6.0, ((0, 32),))
    return dict(tokens=tokens, segments=segments, routes=routes, order=order, gain_attn=gain_attn, w_query=w_query, w_key=w_key, w_value=w_value, w_output=w_output, rel_bias=rel_bias, gain_ffn=gain_ffn, w_router=w_router, w_in=w_in, w_out=w_out, cotangent=cotangent)


EPS = 1e-06
NEG = -1000000000.0
EDGES = (12, 16, 23, 32, 46, 64, 91)
HIGH = lax.Precision.HIGHEST

@jax.custom_vjp
def low(v):
    return lax.optimization_barrier(v.astype(jnp.bfloat16)).astype(jnp.float32)

@jax.custom_vjp
def low_back(v):
    return v

def low_keep(v):
    return (low(v), None)

def low_pass(kept, grad):
    return (grad,)

def back_keep(v):
    return (v, None)

def back_low(kept, grad):
    return (low(grad),)
low.defvjp(low_keep, low_pass)
low_back.defvjp(back_keep, back_low)

def bucket_index(offset):
    magnitude = jnp.abs(offset)
    far = 8 + sum(((magnitude >= edge).astype(jnp.int32) for edge in EDGES))
    near = jnp.where(magnitude < 8, magnitude, far)
    return near + 16 * (offset > 0).astype(jnp.int32)

def rms_norm(values, gain):
    return values * lax.rsqrt(lax.optimization_barrier(jnp.mean(values * values, axis=-1, keepdims=True)) + EPS) * gain

def slot_numbers(route_rows, order):
    blocks = SEQS // SEQ_DEV
    per_block = SEQ_DEV * LEN
    route_blocks = route_rows.reshape(blocks, per_block)
    ranks = jnp.arange(SEQ_DEV, dtype=jnp.int32)[None, :, None] * LEN + order.reshape(blocks, SEQ_DEV, LEN)
    ranks = ranks.reshape(blocks, per_block)

    def count_block(pair):
        chosen_route, rank = pair
        same_route = chosen_route[:, None] == chosen_route[None, :]
        earlier = rank[None, :] < rank[:, None]
        return lax.optimization_barrier(jnp.sum((same_route & earlier).astype(jnp.int32), axis=1))
    return (lax.map(count_block, (route_blocks, ranks)).reshape(-1), blocks)

def reference(tokens, segments, routes, order, gain_attn, w_query, w_key, w_value, w_output, rel_bias, gain_ffn, w_router, w_in, w_out, cotangent):
    route = routes[..., 0].reshape(-1)
    slot, blocks = slot_numbers(routes[..., 0], order)
    total = route.shape[0]
    token_ids = jnp.arange(total, dtype=jnp.int32)
    block_of = token_ids // (SEQ_DEV * LEN)
    kept = slot < CAP
    flat_place = (route * blocks + block_of) * CAP + slot
    places = EXPERTS * blocks * CAP
    target = jnp.where(kept, flat_place, places)
    slot_token = jnp.zeros((places,), jnp.int32).at[target].set(token_ids, mode='drop')
    slot_valid = jnp.zeros((places,), jnp.float32).at[target].set(1.0, mode='drop')
    fetch = jnp.where(kept, flat_place, 0)
    keep_weight = kept.astype(jnp.float32)
    chosen = (route[:, None] == jnp.arange(EXPERTS, dtype=jnp.int32)[None, :]).astype(jnp.float32)
    positions = jnp.arange(LEN, dtype=jnp.int32)
    bucket = bucket_index(positions[None, :] - positions[:, None])
    group = math.gcd(SEQS, max(1, 4096 // LEN))
    seg_groups = segments.reshape(SEQS // group, group, LEN)
    scale = HEAD_DIM ** (-0.5)

    def forward(inputs, gain_one, query_w, key_w, value_w, output_w, table, gain_two, router_w, inner_w, outer_w):
        flat_in = inputs.reshape(total, D)
        normed = low(rms_norm(flat_in, gain_one))
        query = low(low_back(jnp.dot(normed, query_w, precision=HIGH)))
        key = low(low_back(jnp.dot(normed, key_w, precision=HIGH)))
        value = low(low_back(jnp.dot(normed, value_w, precision=HIGH)))
        bias = jnp.transpose(table[bucket], (2, 0, 1))

        def attend(block):
            query_g, key_g, value_g, seg_g = block
            scores = jnp.einsum('glhd,gmhd->ghlm', query_g, key_g, precision=HIGH) * scale + bias[None]
            scores = low_back(scores)
            mask = seg_g[:, :, None] == seg_g[:, None, :]
            scores = jnp.where(mask[:, None], scores, NEG)
            probs = low(jax.nn.softmax(scores, axis=-1))
            return jnp.einsum('ghlm,gmhd->glhd', probs, value_g, precision=HIGH)
        five_dims = (SEQS // group, group, LEN, HEADS, HEAD_DIM)
        context = lax.map(jax.checkpoint(attend), (query.reshape(five_dims), key.reshape(five_dims), value.reshape(five_dims), seg_groups))
        context = low(low_back(context.reshape(total, D)))
        branch = low_back(jnp.dot(context, output_w, precision=HIGH))
        resid = flat_in + branch
        normed_two = low(rms_norm(resid, gain_two))
        logits = low_back(jnp.dot(normed_two, router_w, precision=HIGH))
        gate = lax.optimization_barrier(jnp.sum(jax.nn.softmax(logits, axis=-1) * chosen, axis=-1))
        expert_in = low_back(normed_two)
        rows = (expert_in[slot_token] * slot_valid[:, None]).reshape(EXPERTS, blocks * CAP, D)

        def expert(piece):
            rows_e, inner_e, outer_e = piece
            before = low_back(jnp.dot(rows_e, inner_e, precision=HIGH))
            active = low(jax.nn.gelu(before))
            return low(low_back(jnp.dot(active, outer_e, precision=HIGH)))
        results = lax.map(jax.checkpoint(expert), (rows, inner_w, outer_w)).reshape(places, D)
        mixed = resid + results[fetch] * (gate * keep_weight)[:, None]
        return mixed.reshape(SEQS, LEN, D)
    arrays = (tokens.astype(jnp.float32), gain_attn.astype(jnp.float32), w_query.astype(jnp.float32), w_key.astype(jnp.float32), w_value.astype(jnp.float32), w_output.astype(jnp.float32), rel_bias.astype(jnp.float32), gain_ffn.astype(jnp.float32), w_router.astype(jnp.float32), w_in.astype(jnp.float32), w_out.astype(jnp.float32))
    mixed, pullback = jax.vjp(forward, *arrays)
    grads = pullback(cotangent.astype(jnp.float32))
    return (mixed.astype(jnp.bfloat16), grads[0].astype(jnp.bfloat16), grads[1], grads[2], grads[3], grads[4], grads[5], grads[6], grads[7], grads[8], grads[9], grads[10])
```

```python
import functools

import jax
import jax.numpy as jnp
from jax import lax
from jax.experimental import pallas as pl
from jax.experimental.pallas import tpu as pltpu
from jax.sharding import PartitionSpec as P
HEAD_DIM=64
BLK=128
EDGES = (12, 16, 23, 32, 46, 64, 91)
BIG=1e9
def bucket_index(offset):
    magnitude = jnp.abs(offset)
    far = 8 + sum(((magnitude >= edge).astype(jnp.int32) for edge in EDGES))
    near = jnp.where(magnitude < 8, magnitude, far)
    return near + 16 * (offset > 0).astype(jnp.int32)

def dot_nt(a,b): return lax.dot_general(a,b,(((1,),(1,)),((),())),preferred_element_type=jnp.float32)
def dot_nn(a,b): return lax.dot_general(a,b,(((1,),(0,)),((),())),preferred_element_type=jnp.float32)

def head_mask():
    lane=lax.broadcasted_iota(jnp.int32,(BLK,2*HEAD_DIM),1)
    return (lane<HEAD_DIM).astype(jnp.float32).astype(jnp.bfloat16)

def build_bias(w_ref, bias_ref, nblk):
    rows=(2*nblk-1)*BLK
    near=(nblk-2)*BLK
    for h in range(2):
        c=slice(h*BLK,(h+1)*BLK)
        w=w_ref[0,h:h+1,:]
        low=w[:,511:512]
        high=w[:,0:1]
        bias_ref[0:near,c]=jnp.broadcast_to(low,(near,BLK))
        bias_ref[near+3*BLK:rows,c]=jnp.broadcast_to(high,(near,BLK))
        r=pltpu.roll(jnp.broadcast_to(w,(BLK,512)),0,1,stride=1,stride_axis=0)
        bias_ref[near:near+BLK,c]=r[:,384:512]
        bias_ref[near+BLK:near+2*BLK,c]=r[:,256:384]
        bias_ref[near+2*BLK:near+3*BLK,c]=r[:,128:256]

def by_width(nblk, count, run):
    for n in range(1,nblk+1):
        @pl.when(count==n)
        def _(): run(n*BLK)

def pair_of(block, mask):
    return jnp.concatenate([block*mask, block*(1-mask)],axis=0)

def fwd_kernel(nblk, lo_ref, nb_ref, q_ref,k_ref,v_ref,segq_ref,segk_ref,w_ref,ctx_ref,lse_ref,vt_ref,bias_ref):
    build_bias(w_ref,bias_ref,nblk)
    for b in range(nblk):
        s=slice(b*BLK,(b+1)*BLK)
        vt_ref[:,s]=v_ref[s,:].astype(jnp.float32).T.astype(jnp.bfloat16)
    mask=head_mask()
    def body(qb,_):
        rows=pl.ds(pl.multiple_of(qb*BLK,BLK),BLK)
        lob=lo_ref[qb]
        sq=segq_ref[rows,:]
        q_cat=jnp.concatenate([pair_of(q_ref[rows,:],mask),jnp.concatenate([sq,sq],axis=0)],axis=1)
        def run(W):
            lo=pl.multiple_of(lob*BLK,BLK)
            ks=pl.ds(lo,W)
            st=dot_nt(jnp.concatenate([k_ref[ks,:],segk_ref[ks,:]],axis=1),q_cat)
            st=st+bias_ref[pl.ds(pl.multiple_of((lob-qb+nblk-1)*BLK,BLK),W),:]
            m=jnp.max(st,axis=0,keepdims=True)
            e=jnp.exp(st-m)
            l=jnp.sum(e,axis=0,keepdims=True)
            ot=dot_nn(vt_ref[:,ks],e.astype(jnp.bfloat16))/l
            o=jnp.concatenate([ot[:HEAD_DIM,:BLK],ot[HEAD_DIM:,BLK:]],axis=0)
            ctx_ref[rows,:]=o.T.astype(jnp.bfloat16)
            lse_ref[0,pl.ds(qb,1),:]=m+jnp.log(l)
        by_width(nblk,nb_ref[qb],run)
        return 0
    lax.fori_loop(0,nblk,body,0)

def bwd_kernel(nblk, lo_ref, nb_ref, q_ref,k_ref,v_ref,do_ref,ctx_ref,lse_ref,segq_ref,segk_ref,w_ref,dq_ref,dk_ref,dv_ref,near_ref,far_ref,kt_ref,bias_ref,acc_ref,dka_ref,dva_ref):
    build_bias(w_ref,bias_ref,nblk)
    for b in range(nblk):
        s=slice(b*BLK,(b+1)*BLK)
        kt_ref[:,s]=k_ref[s,:].astype(jnp.float32).T.astype(jnp.bfloat16)
    acc_ref[...]=jnp.zeros_like(acc_ref)
    dka_ref[...]=jnp.zeros_like(dka_ref)
    dva_ref[...]=jnp.zeros_like(dva_ref)
    mask=head_mask()
    row=lax.broadcasted_iota(jnp.int32,(16,2*HEAD_DIM),0)
    lane=lax.broadcasted_iota(jnp.int32,(16,2*HEAD_DIM),1)
    pick=((lane//HEAD_DIM)==row).astype(jnp.float32).astype(jnp.bfloat16)
    def body(qb,_):
        rows=pl.ds(pl.multiple_of(qb*BLK,BLK),BLK)
        lob=lo_ref[qb]
        sq=segq_ref[rows,:]
        q2=pair_of(q_ref[rows,:],mask)
        q_cat=jnp.concatenate([q2,jnp.concatenate([sq,sq],axis=0)],axis=1)
        do=do_ref[rows,:]
        do2=pair_of(do,mask)
        prod=do.astype(jnp.float32)*ctx_ref[rows,:].astype(jnp.float32)
        hi=prod.astype(jnp.bfloat16)
        lo_part=(prod-hi.astype(jnp.float32)).astype(jnp.bfloat16)
        dl=dot_nt(pick,hi)+dot_nt(pick,lo_part)
        delta=jnp.concatenate([dl[0:1],dl[1:2]],axis=1)
        lse=lse_ref[0,pl.ds(qb,1),:]
        def run(W):
            lo=pl.multiple_of(lob*BLK,BLK)
            ks=pl.ds(lo,W)
            bs=pl.ds(pl.multiple_of((lob-qb+nblk-1)*BLK,BLK),W)
            st=dot_nt(jnp.concatenate([k_ref[ks,:],segk_ref[ks,:]],axis=1),q_cat)
            p=jnp.exp(st+bias_ref[bs,:]-lse)
            dp=dot_nt(v_ref[ks,:],do2)
            ds=p*(dp-delta)
            acc_ref[bs,:]+=ds
            dsb=ds.astype(jnp.bfloat16)
            dva_ref[ks,:]+=dot_nn(p.astype(jnp.bfloat16),do2)
            dka_ref[ks,:]+=dot_nn(dsb,q2)
            dqt=dot_nn(kt_ref[:,ks],dsb)
            d=jnp.concatenate([dqt[:HEAD_DIM,:BLK],dqt[HEAD_DIM:,BLK:]],axis=0)*(HEAD_DIM**-0.5)
            dq_ref[rows,:]=d.T.astype(jnp.bfloat16)
        by_width(nblk,nb_ref[qb],run)
        return 0
    lax.fori_loop(0,nblk,body,0)
    dk_ref[...]=dka_ref[...].astype(jnp.bfloat16)
    dv_ref[...]=dva_ref[...].astype(jnp.bfloat16)
    near=(nblk-2)*BLK
    total=(2*nblk-1)*BLK
    for h in range(2):
        c=slice(h*BLK,(h+1)*BLK)
        wide=jnp.concatenate([jnp.zeros((BLK,BLK),jnp.float32),acc_ref[near+2*BLK:near+3*BLK,c],acc_ref[near+BLK:near+2*BLK,c],acc_ref[near:near+BLK,c]],axis=1)
        back=pltpu.roll(wide[::1],0,1,stride=1,stride_axis=0) if False else unroll_rows(wide)
        near_ref[0,h:h+1,:]=jnp.sum(back,axis=0,keepdims=True)
        low=jnp.sum(acc_ref[0:near,c],axis=0,keepdims=True)
        high=jnp.sum(acc_ref[near+3*BLK:total,c],axis=0,keepdims=True)
        far_ref[0,h:h+1,:]=jnp.concatenate([low,high],axis=1)

def unroll_rows(wide):
    n=wide.shape[1]
    out=wide
    row=lax.broadcasted_iota(jnp.int32,wide.shape,0)
    bit=1
    while bit<wide.shape[0]:
        out=jnp.where((row & bit)!=0,pltpu.roll(out,n-bit,1),out)
        bit*=2
    return out

def pair_spec(nrow): return pl.BlockSpec((nrow,2*HEAD_DIM),lambda p,*_:(0,p))
def full_spec(shape): return pl.BlockSpec(shape,lambda p,*_:(0,)*len(shape))
def lead_spec(shape): return pl.BlockSpec((1,)+shape,lambda p,*_:(p,0,0))

def attn_fwd(lo,nb,q,k,v,segq,segk,w):
    L,D=q.shape; nblk=L//BLK; pairs=D//(2*HEAD_DIM)
    return pl.pallas_call(functools.partial(fwd_kernel,nblk),
        grid_spec=pltpu.PrefetchScalarGridSpec(num_scalar_prefetch=2,grid=(pairs,),
          in_specs=[pair_spec(L)]*3+[full_spec((L,128))]*2+[lead_spec((2,512))],
          out_specs=[pair_spec(L),lead_spec((nblk,2*BLK))],
          scratch_shapes=[pltpu.VMEM((2*HEAD_DIM,L),jnp.bfloat16),pltpu.VMEM(((2*nblk-1)*BLK,2*BLK),jnp.float32)]),
        out_shape=[jax.ShapeDtypeStruct((L,D),jnp.bfloat16),jax.ShapeDtypeStruct((pairs,nblk,2*BLK),jnp.float32)],
        compiler_params=pltpu.CompilerParams(vmem_limit_bytes=40*2**20),
        cost_estimate=pl.CostEstimate(flops=2*10**9,bytes_accessed=8*2**20,transcendentals=6*10**6))(lo,nb,q,k,v,segq,segk,w)

def attn_bwd(lo,nb,q,k,v,do,ctx,lse,segq,segk,w):
    L,D=q.shape; nblk=L//BLK; pairs=D//(2*HEAD_DIM)
    return pl.pallas_call(functools.partial(bwd_kernel,nblk),
        grid_spec=pltpu.PrefetchScalarGridSpec(num_scalar_prefetch=2,grid=(pairs,),
          in_specs=[pair_spec(L)]*5+[lead_spec((nblk,2*BLK))]+[full_spec((L,128))]*2+[lead_spec((2,512))],
          out_specs=[pair_spec(L)]*3+[lead_spec((2,512)),lead_spec((2,256))],
          scratch_shapes=[pltpu.VMEM((2*HEAD_DIM,L),jnp.bfloat16),pltpu.VMEM(((2*nblk-1)*BLK,2*BLK),jnp.float32),pltpu.VMEM(((2*nblk-1)*BLK,2*BLK),jnp.float32),
             pltpu.VMEM((L,2*HEAD_DIM),jnp.float32),pltpu.VMEM((L,2*HEAD_DIM),jnp.float32)]),
        out_shape=[jax.ShapeDtypeStruct((L,D),jnp.bfloat16)]*3+[jax.ShapeDtypeStruct((pairs,2,512),jnp.float32),jax.ShapeDtypeStruct((pairs,2,256),jnp.float32)],
        compiler_params=pltpu.CompilerParams(vmem_limit_bytes=40*2**20),
        cost_estimate=pl.CostEstimate(flops=4*10**9,bytes_accessed=16*2**20,transcendentals=6*10**6))(lo,nb,q,k,v,do,ctx,lse,segq,segk,w)

def seg_arrays(seg):
    L=seg.shape[0]; nblk=L//BLK
    ids=jnp.arange(128,dtype=jnp.int32)
    segq=(seg[:,None]==ids[None,:]).astype(jnp.bfloat16)
    segk=jnp.where((seg[:,None]!=ids[None,:])&(ids[None,:]<16),-BIG,0.0).astype(jnp.bfloat16)
    sb=seg.reshape(nblk,BLK)
    first=jnp.sum((seg[None,:]<sb[:,:1]).astype(jnp.int32),axis=1)
    last=jnp.sum((seg[None,:]<=sb[:,-1:]).astype(jnp.int32),axis=1)
    lo=first//BLK
    nb=(last+BLK-1)//BLK-lo
    return segq,segk,lo.astype(jnp.int32),nb.astype(jnp.int32)

def bias_lanes(table):
    off=-(jnp.arange(512,dtype=jnp.int32)-256)
    oh=(bucket_index(off)[None,:]==jnp.arange(table.shape[0],dtype=jnp.int32)[:,None]).astype(jnp.bfloat16)
    w=lax.dot_general(table,oh,(((0,),(0,)),((),())),preferred_element_type=jnp.float32)
    return w.reshape(-1,2,512)

def table_grad(near,far,buckets):
    off=-(jnp.arange(512,dtype=jnp.int32)-256)
    oh=(bucket_index(off)[:,None]==jnp.arange(buckets,dtype=jnp.int32)[None,:]).astype(jnp.float32)
    n=jnp.einsum("hx,xb->bh",near.reshape(-1,512),oh,precision=lax.Precision.HIGHEST)
    f=far.reshape(-1,2,128).sum(-1)
    ids=jnp.arange(buckets,dtype=jnp.int32)[:,None]
    return n+jnp.where(ids==15,f[None,:,0],0)+jnp.where(ids==31,f[None,:,1],0)

TILE=256
def gelu_parts(x):
    c=0.7978845608028654
    x2=x*x
    t=jnp.tanh(x*(c+(c*0.044715)*x2))
    half=0.5*(1.0+t)
    slope=half+0.5*x*(1.0-t*t)*(c+(3*c*0.044715)*x2)
    return x*half,slope

def expert_kernel(count, parts, *refs):
    rows=refs[:count]; cots=refs[count:2*count]
    wi_refs=refs[2*count:2*count+parts]; wo_refs=refs[2*count+parts:2*count+2*parts]
    refs=refs[2*count+2*parts:]
    outs=refs[:count]; act_ref,db_ref,dg_ref=refs[count:count+3]
    x_ref,c_ref,wi_buf,wo_buf,acc_ref,dga_ref,act_buf,db_buf,w_sem,o_sem=refs[count+3:]
    block=wi_refs[0].shape[1]
    per=block//TILE
    total=parts*per
    for k in range(parts):
        pltpu.make_async_copy(wi_refs[k],wi_buf.at[k],w_sem.at[0,k]).start()
        pltpu.make_async_copy(wo_refs[k],wo_buf.at[k],w_sem.at[1,k]).start()
    first=0
    for i in range(count):
        n=rows[i].shape[0]
        x_ref[first:first+n,:]=rows[i][...]
        c_ref[first:first+n,:]=cots[i][...]
        first+=n
    acc_ref[...]=jnp.zeros_like(acc_ref)
    dga_ref[...]=jnp.zeros_like(dga_ref)
    def out_copies(step,slot):
        cols=pl.ds(pl.multiple_of(step*TILE,TILE),TILE)
        return (pltpu.make_async_copy(act_buf.at[slot],act_ref.at[:,cols],o_sem.at[0,slot]),
                pltpu.make_async_copy(db_buf.at[slot],db_ref.at[:,cols],o_sem.at[1,slot]))
    for k in range(parts):
        pltpu.make_async_copy(wi_refs[k],wi_buf.at[k],w_sem.at[0,k]).wait()
        pltpu.make_async_copy(wo_refs[k],wo_buf.at[k],w_sem.at[1,k]).wait()
        def body(c,_):
            step=k*per+c
            slot=lax.rem(step,2)
            @pl.when(step>=2)
            def _():
                for cp in out_copies(step-2,slot): cp.wait()
            cols=pl.ds(pl.multiple_of(c*TILE,TILE),TILE)
            wi=wi_buf[k,:,cols]
            wo=wo_buf[k,cols,:]
            before=dot_nn(x_ref[...],wi)
            up=dot_nt(c_ref[...],wo)
            active,slope=gelu_parts(before)
            prod=active*up
            dga_ref[...]+=prod[:,:128]+prod[:,128:]
            act_buf[slot]=active.astype(jnp.bfloat16)
            db=(up*slope).astype(jnp.bfloat16)
            db_buf[slot]=db
            acc_ref[...]+=dot_nt(db,wi)
            for cp in out_copies(step,slot): cp.start()
            return 0
        lax.fori_loop(0,per,body,0)
    first=0
    for i in range(count):
        n=rows[i].shape[0]
        outs[i][...]=acc_ref[first:first+n,:].astype(jnp.bfloat16)
        first+=n
    ones=jnp.ones((8,128),jnp.bfloat16)
    sums=dga_ref[...]
    hi=sums.astype(jnp.bfloat16)
    rest=sums-hi.astype(jnp.float32)
    mid=rest.astype(jnp.bfloat16)
    low=(rest-mid.astype(jnp.float32)).astype(jnp.bfloat16)
    dg_ref[...]=dot_nt(ones,hi)+dot_nt(ones,mid)+dot_nt(ones,low)
    for step in (total-2,total-1):
        for cp in out_copies(step,step%2): cp.wait()

def expert_half(rows,cots,w_ins,w_outs):
    count=len(rows); parts=len(w_ins)
    width,block=w_ins[0].shape
    R=sum(r.shape[0] for r in rows)
    vm=pl.BlockSpec(memory_space=pltpu.VMEM); hb=pl.BlockSpec(memory_space=pl.ANY)
    outs=pl.pallas_call(functools.partial(expert_kernel,count,parts),
        in_specs=[vm]*(2*count)+[hb]*(2*parts),
        out_specs=[vm]*count+[hb,hb,vm],
        out_shape=[jax.ShapeDtypeStruct(r.shape,jnp.bfloat16) for r in rows]+[jax.ShapeDtypeStruct((R,parts*block),jnp.bfloat16)]*2+[jax.ShapeDtypeStruct((8,R),jnp.float32)],
        scratch_shapes=[pltpu.VMEM((R,width),jnp.bfloat16)]*2+[pltpu.VMEM((parts,width,block),jnp.bfloat16),pltpu.VMEM((parts,block,width),jnp.bfloat16),
            pltpu.VMEM((R,width),jnp.float32),pltpu.VMEM((R,128),jnp.float32),pltpu.VMEM((2,R,TILE),jnp.bfloat16),pltpu.VMEM((2,R,TILE),jnp.bfloat16),
            pltpu.SemaphoreType.DMA((2,parts)),pltpu.SemaphoreType.DMA((2,2))],
        compiler_params=pltpu.CompilerParams(vmem_limit_bytes=48*2**20),
        cost_estimate=pl.CostEstimate(flops=6*R*width*parts*block,bytes_accessed=20*2**20,transcendentals=R*parts*block))(*rows,*cots,*w_ins,*w_outs)
    return outs[:count],outs[count],outs[count+1],outs[count+2][0]

EPS = 1e-06
BF = jnp.bfloat16
F32 = jnp.float32


def dot_tn(a, b):
    return lax.dot_general(a, b, (((0,), (0,)), ((), ())), preferred_element_type=F32)


def swap(value, axis, size, bit):
    return lax.ppermute(value, axis, [(i, i ^ bit) for i in range(size)])


def direct(size):
    return size <= 8 and size & (size - 1) == 0


def exchange(blocks, size):
    if direct(size):
        return [blocks[0]] + [swap(blocks[k], "expert", size, k) for k in range(1, size)]
    out = lax.all_to_all(jnp.stack(blocks), "expert", split_axis=0, concat_axis=0, tiled=True)
    return [out[k] for k in range(size)]


def gather_shards(value, size):
    if size == 4:
        far = swap(value, "shard", size, 2)
        near = swap(value, "shard", size, 1)
        return [value, near, far, swap(far, "shard", size, 1)]
    return [value] + [swap(value, "shard", size, k) for k in range(1, size)]


def reduce_shards(blocks, size):
    if size == 4:
        near1 = swap(blocks[3].astype(BF), "shard", size, 1)
        near0 = swap(blocks[1].astype(BF), "shard", size, 1)
        other = swap((blocks[2].astype(F32) + near1.astype(F32)).astype(BF), "shard", size, 2)
        return blocks[0].astype(F32) + near0.astype(F32) + other.astype(F32)
    total = blocks[0].astype(F32)
    for k in range(1, size):
        total = total + swap(blocks[k].astype(BF), "shard", size, k).astype(F32)
    return total


def reduce_experts(value, size, index):
    if not direct(size):
        return lax.psum(value, "expert")
    rows = value.shape[0] // size
    pieces = [
        lax.dynamic_slice_in_dim(value, (index ^ k) * rows, rows, 0).astype(BF) for k in range(size)
    ]
    total = sum(piece.astype(F32) for piece in exchange(pieces, size)).astype(BF)
    out = jnp.zeros(value.shape, BF)
    out = lax.dynamic_update_slice_in_dim(out, total, index * rows, 0)
    for k in range(1, size):
        out = lax.dynamic_update_slice_in_dim(
            out, swap(total, "expert", size, k), (index ^ k) * rows, 0
        )
    return out.astype(F32)


def in_order(blocks, index):
    rows = blocks[0].shape[0]
    out = jnp.zeros((rows * len(blocks),) + blocks[0].shape[1:], blocks[0].dtype)
    for k, block in enumerate(blocks):
        out = lax.dynamic_update_slice_in_dim(out, block, (index ^ k) * rows, 0)
    return out


def per_device(
    tokens,
    segments,
    routes,
    order,
    gain_attn,
    w_query,
    w_key,
    w_value,
    w_output,
    rel_bias,
    gain_ffn,
    w_router,
    w_in,
    w_out,
    cotangent,
):
    seq_count, length, width = tokens.shape
    total = seq_count * length
    experts = lax.axis_size("expert")
    shards = lax.axis_size("shard")
    me = lax.axis_index("expert")
    my_shard = lax.axis_index("shard")
    capacity = (5 * total + 4 * experts - 1) // (4 * experts)
    cells = experts * capacity
    heads = rel_bias.shape[1]
    own = w_query.shape[0]
    own_buckets = rel_bias.shape[0]
    buckets = own_buckets * shards
    small = jnp.concatenate([gain_attn[:, None], gain_ffn[:, None], w_router], axis=1)
    small = jnp.pad(small, ((0, 0), (0, 128 - small.shape[1])))
    small = lax.dynamic_update_slice(small, rel_bias, (0, 128 - heads))
    first_pack = jnp.concatenate([w_query, w_key, w_value, small], axis=1)
    first_all = in_order(gather_shards(first_pack, shards), my_shard)
    output_all = in_order(gather_shards(w_output, shards), my_shard)
    inners = gather_shards(w_in[0], shards)
    outers = gather_shards(w_out[0], shards)
    route = routes.reshape(total)
    ranks = (jnp.arange(seq_count, dtype=jnp.int32)[:, None] * length + order).reshape(total)
    same_route = route[:, None] == route[None, :]
    earlier = ranks[None, :] < ranks[:, None]
    slot = jnp.sum((same_route & earlier).astype(jnp.int32), axis=1)
    kept = slot < capacity
    partner = route ^ me if direct(experts) else route
    place = jnp.where(kept, partner * capacity + slot, -1)
    spread = (jnp.arange(cells, dtype=jnp.int32)[:, None] == place[None, :]).astype(BF)
    chosen = (route[:, None] == jnp.arange(experts, dtype=jnp.int32)[None, :]).astype(F32)

    def to_blocks(values):
        slots = dot_nn(spread, values).astype(values.dtype)
        return [slots[k * capacity : (k + 1) * capacity] for k in range(experts)]

    cot = cotangent.reshape(total, width)
    cot_blocks = exchange(to_blocks(cot), experts)
    inputs = tokens.reshape(total, width).astype(F32)
    scale_one = lax.rsqrt(jnp.mean(inputs * inputs, axis=-1, keepdims=True) + EPS)
    unit_one = inputs * scale_one
    base = 3 * width
    query_all, key_all, value_all = (first_all[:, i * width : (i + 1) * width] for i in range(3))
    gain_one = first_all[:, base].astype(F32)
    gain_two = first_all[:, base + 1].astype(F32)
    router_all = first_all[:, base + 2 : base + 2 + experts]
    table = first_all[:, base + 128 - heads :].reshape(shards, own, heads)[:, :own_buckets]
    table = table.reshape(buckets, heads)
    normed_low = (unit_one * gain_one).astype(BF)
    query = (dot_nn(normed_low, query_all).astype(BF) * (HEAD_DIM**-0.5)).astype(BF)
    key = dot_nn(normed_low, key_all).astype(BF)
    value = dot_nn(normed_low, value_all).astype(BF)
    bias = bias_lanes(table)
    seg = [seg_arrays(segments[i]) for i in range(seq_count)]
    rows_of = [slice(i * length, (i + 1) * length) for i in range(seq_count)]
    forward = [
        attn_fwd(s[2], s[3], query[r], key[r], value[r], s[0], s[1], bias)
        for s, r in zip(seg, rows_of)
    ]
    context = jnp.concatenate([f[0] for f in forward], axis=0) if seq_count > 1 else forward[0][0]
    resid = inputs + dot_nn(context, output_all)
    scale_two = lax.rsqrt(jnp.mean(resid * resid, axis=-1, keepdims=True) + EPS)
    unit_two = resid * scale_two
    normed_two_low = (unit_two * gain_two).astype(BF)
    logits = dot_nn(normed_two_low, router_all)
    probs = jax.nn.softmax(logits, axis=-1)
    gate = jnp.sum(probs * chosen, axis=-1)
    keep_weight = kept.astype(F32)
    keep_gate = gate * keep_weight
    row_blocks = exchange(to_blocks(normed_two_low), experts)
    gate_slots = jnp.sum(jnp.where(place[None, :] == jnp.arange(cells)[:, None], gate[None, :], 0), axis=1)
    gate_blocks = exchange(
        [gate_slots[None, k * capacity : (k + 1) * capacity] for k in range(experts)], experts
    )
    half = experts // 2
    if direct(experts):
        near = expert_half(row_blocks[:half], cot_blocks[:half], inners, outers)
        far = expert_half(row_blocks[half:], cot_blocks[half:], inners, outers)
        back = list(near[0]) + list(far[0])
    else:
        joined = [jnp.concatenate(b, axis=0) for b in (row_blocks[:half], row_blocks[half:], cot_blocks[:half], cot_blocks[half:])]
        near = expert_half([joined[0]], [joined[2]], inners, outers)
        far = expert_half([joined[1]], [joined[3]], inners, outers)
        back = [b for part in (near, far) for b in jnp.split(part[0][0], half, axis=0)]
    gate_back = jnp.concatenate([near[3], far[3]])
    back = exchange(back, experts)
    gate_back = exchange(
        [gate_back[None, k * capacity : (k + 1) * capacity] for k in range(experts)], experts
    )
    active = jnp.concatenate([near[1], far[1]], axis=0)
    d_before = jnp.concatenate([near[2], far[2]], axis=0)
    rows_all = jnp.concatenate(row_blocks, axis=0)
    cot_all = jnp.concatenate(cot_blocks, axis=0)
    gate_all = jnp.concatenate(gate_blocks, axis=1)[0][:, None]
    d_out_rows = (cot_all.astype(F32) * gate_all).astype(BF)
    gated_rows = (rows_all.astype(F32) * gate_all).astype(BF)
    block = w_in.shape[2]
    parts = [slice(k * block, (k + 1) * block) for k in range(shards)]
    grad_outer = reduce_shards([dot_tn(active[:, p], d_out_rows) for p in parts], shards)
    grad_inner = reduce_shards([dot_tn(gated_rows, d_before[:, p]) for p in parts], shards)
    outer_all = jnp.concatenate(outers, axis=0)
    expert_out = dot_nn(active, outer_all).astype(BF)
    out_back = exchange(
        [expert_out[k * capacity : (k + 1) * capacity] for k in range(experts)], experts
    )
    upstream = cot.astype(F32)
    d_rows = dot_tn(spread, jnp.concatenate(back, axis=0))
    gate_cells = jnp.concatenate(gate_back, axis=1)[0]
    d_gate = jnp.sum(
        jnp.where(place[:, None] == jnp.arange(cells)[None, :], gate_cells[None, :], 0), axis=1
    )
    d_logits = (probs * (d_gate[:, None] * chosen - (d_gate * gate)[:, None])).astype(BF)
    d_router = dot_tn(normed_two_low, d_logits)
    d_normed_two = dot_nt(d_logits, router_all) + keep_gate[:, None] * d_rows
    d_gain_two = jnp.sum(d_normed_two * unit_two, axis=0)
    pulled = gain_two * d_normed_two
    d_resid = upstream + scale_two * (
        pulled - unit_two * jnp.mean(unit_two * pulled, axis=-1, keepdims=True)
    )
    d_branch = d_resid.astype(BF)
    d_context = dot_nt(d_branch, output_all).astype(BF)
    d_output_w = dot_tn(context, d_branch)

    def shard_blocks(values):
        return [
            lax.dynamic_slice_in_dim(values, (my_shard ^ k) * own, own, 0) for k in range(shards)
        ]

    sum_output = reduce_experts(
        reduce_shards(shard_blocks(d_output_w.astype(BF)), shards), experts, me
    )
    backward = [
        attn_bwd(s[2], s[3], query[r], key[r], value[r], d_context[r], f[0], f[1], s[0], s[1], bias)
        for s, r, f in zip(seg, rows_of, forward)
    ]
    d_query, d_key, d_value = (
        jnp.concatenate([b[i] for b in backward], axis=0) if seq_count > 1 else backward[0][i]
        for i in range(3)
    )
    d_table = sum(table_grad(b[3], b[4], buckets) for b in backward)
    d_weights = [dot_tn(normed_low, d).astype(BF) for d in (d_query, d_key, d_value)]
    d_normed = (
        dot_nt(d_query, query_all) + dot_nt(d_key, key_all) + dot_nt(d_value, value_all)
    )
    d_gain_one = jnp.sum(d_normed * unit_one, axis=0)
    pulled_one = gain_one * d_normed
    d_tokens = d_resid + scale_one * (
        pulled_one - unit_one * jnp.mean(unit_one * pulled_one, axis=-1, keepdims=True)
    )
    tail = jnp.concatenate([d_gain_one[:, None], d_gain_two[:, None], d_router], axis=1)
    tail = jnp.pad(tail, ((0, 0), (0, 128 - tail.shape[1]))).reshape(shards, own, 128)
    tail = lax.dynamic_update_slice(
        tail, d_table.reshape(shards, own_buckets, heads), (0, 0, 128 - heads)
    ).reshape(width, 128)
    last = jnp.concatenate(d_weights + [tail.astype(BF)], axis=1)
    last = reduce_experts(reduce_shards(shard_blocks(last), shards), experts, me)
    arrived = dot_tn(spread, jnp.concatenate(out_back, axis=0))
    mixed = resid + keep_gate[:, None] * arrived
    return (
        mixed.astype(BF).reshape(tokens.shape),
        d_tokens.astype(BF).reshape(tokens.shape),
        last[:, base],
        last[:, :width],
        last[:, width : 2 * width],
        last[:, 2 * width : base],
        sum_output,
        last[:own_buckets, base + 128 - heads :],
        last[:, base + 1],
        last[:, base + 2 : base + 2 + experts],
        grad_inner[None],
        grad_outer[None],
    )


def solution(mesh):
    in_specs = (
        P(("expert", "shard"), None, None),
        P(("expert", "shard"), None),
        P(("expert", "shard"), None, None),
        P(("expert", "shard"), None),
        P("shard"),
        P("shard", None),
        P("shard", None),
        P("shard", None),
        P("shard", None),
        P("shard", None),
        P("shard"),
        P("shard", None),
        P("expert", None, "shard"),
        P("expert", "shard", None),
        P(("expert", "shard"), None, None),
    )
    out_specs = (
        P(("expert", "shard"), None, None),
        P(("expert", "shard"), None, None),
        P("shard"),
        P("shard", None),
        P("shard", None),
        P("shard", None),
        P("shard", None),
        P("shard", None),
        P("shard"),
        P("shard", None),
        P("expert", None, "shard"),
        P("expert", "shard", None),
    )
    return jax.shard_map(
        per_device, mesh=mesh, in_specs=in_specs, out_specs=out_specs, check_vma=False
    )
```

```python
import functools

import jax
import jax.numpy as jnp
from jax import lax
from jax.experimental import pallas as pl
from jax.experimental.pallas import tpu as pltpu
from jax.sharding import PartitionSpec as P
HEAD_DIM=64
BLK=128
EDGES = (12, 16, 23, 32, 46, 64, 91)
BIG=1e9
def bucket_index(offset):
    magnitude = jnp.abs(offset)
    far = 8 + sum(((magnitude >= edge).astype(jnp.int32) for edge in EDGES))
    near = jnp.where(magnitude < 8, magnitude, far)
    return near + 16 * (offset > 0).astype(jnp.int32)

def dot_nt(a,b): return lax.dot_general(a,b,(((1,),(1,)),((),())),preferred_element_type=jnp.float32)
def dot_nn(a,b): return lax.dot_general(a,b,(((1,),(0,)),((),())),preferred_element_type=jnp.float32)

def head_mask():
    lane=lax.broadcasted_iota(jnp.int32,(BLK,2*HEAD_DIM),1)
    return (lane<HEAD_DIM).astype(jnp.float32).astype(jnp.bfloat16)

def build_bias(w_ref, bias_ref, nblk):
    rows=(2*nblk-1)*BLK
    near=(nblk-2)*BLK
    for h in range(2):
        c=slice(h*BLK,(h+1)*BLK)
        w=w_ref[0,h:h+1,:]
        low=w[:,511:512]
        high=w[:,0:1]
        bias_ref[0:near,c]=jnp.broadcast_to(low,(near,BLK))
        bias_ref[near+3*BLK:rows,c]=jnp.broadcast_to(high,(near,BLK))
        r=pltpu.roll(jnp.broadcast_to(w,(BLK,512)),0,1,stride=1,stride_axis=0)
        bias_ref[near:near+BLK,c]=r[:,384:512]
        bias_ref[near+BLK:near+2*BLK,c]=r[:,256:384]
        bias_ref[near+2*BLK:near+3*BLK,c]=r[:,128:256]

def by_width(nblk, count, run):
    for n in range(1,nblk+1):
        @pl.when(count==n)
        def _(): run(n*BLK)

def pair_of(block, mask):
    return jnp.concatenate([block*mask, block*(1-mask)],axis=0)

def fwd_kernel(nblk, lo_ref, nb_ref, q_ref,k_ref,v_ref,segq_ref,segk_ref,w_ref,ctx_ref,lse_ref,vt_ref,bias_ref):
    build_bias(w_ref,bias_ref,nblk)
    for b in range(nblk):
        s=slice(b*BLK,(b+1)*BLK)
        vt_ref[:,s]=v_ref[s,:].astype(jnp.float32).T.astype(jnp.bfloat16)
    mask=head_mask()
    def body(qb,_):
        rows=pl.ds(pl.multiple_of(qb*BLK,BLK),BLK)
        lob=lo_ref[qb]
        sq=segq_ref[rows,:]
        q_cat=jnp.concatenate([pair_of(q_ref[rows,:],mask),jnp.concatenate([sq,sq],axis=0)],axis=1)
        def run(W):
            lo=pl.multiple_of(lob*BLK,BLK)
            ks=pl.ds(lo,W)
            st=dot_nt(jnp.concatenate([k_ref[ks,:],segk_ref[ks,:]],axis=1),q_cat)
            st=st+bias_ref[pl.ds(pl.multiple_of((lob-qb+nblk-1)*BLK,BLK),W),:]
            m=jnp.max(st,axis=0,keepdims=True)
            e=jnp.exp(st-m)
            l=jnp.sum(e,axis=0,keepdims=True)
            ot=dot_nn(vt_ref[:,ks],e.astype(jnp.bfloat16))/l
            o=jnp.concatenate([ot[:HEAD_DIM,:BLK],ot[HEAD_DIM:,BLK:]],axis=0)
            ctx_ref[rows,:]=o.T.astype(jnp.bfloat16)
            lse_ref[0,pl.ds(qb,1),:]=m+jnp.log(l)
        by_width(nblk,nb_ref[qb],run)
        return 0
    lax.fori_loop(0,nblk,body,0)

def bwd_kernel(nblk, lo_ref, nb_ref, q_ref,k_ref,v_ref,do_ref,ctx_ref,lse_ref,segq_ref,segk_ref,w_ref,dq_ref,dk_ref,dv_ref,near_ref,far_ref,kt_ref,bias_ref,acc_ref,dka_ref,dva_ref):
    build_bias(w_ref,bias_ref,nblk)
    for b in range(nblk):
        s=slice(b*BLK,(b+1)*BLK)
        kt_ref[:,s]=k_ref[s,:].astype(jnp.float32).T.astype(jnp.bfloat16)
    acc_ref[...]=jnp.zeros_like(acc_ref)
    dka_ref[...]=jnp.zeros_like(dka_ref)
    dva_ref[...]=jnp.zeros_like(dva_ref)
    mask=head_mask()
    row=lax.broadcasted_iota(jnp.int32,(16,2*HEAD_DIM),0)
    lane=lax.broadcasted_iota(jnp.int32,(16,2*HEAD_DIM),1)
    pick=((lane//HEAD_DIM)==row).astype(jnp.float32).astype(jnp.bfloat16)
    def body(qb,_):
        rows=pl.ds(pl.multiple_of(qb*BLK,BLK),BLK)
        lob=lo_ref[qb]
        sq=segq_ref[rows,:]
        q2=pair_of(q_ref[rows,:],mask)
        q_cat=jnp.concatenate([q2,jnp.concatenate([sq,sq],axis=0)],axis=1)
        do=do_ref[rows,:]
        do2=pair_of(do,mask)
        prod=do.astype(jnp.float32)*ctx_ref[rows,:].astype(jnp.float32)
        hi=prod.astype(jnp.bfloat16)
        lo_part=(prod-hi.astype(jnp.float32)).astype(jnp.bfloat16)
        dl=dot_nt(pick,hi)+dot_nt(pick,lo_part)
        delta=jnp.concatenate([dl[0:1],dl[1:2]],axis=1)
        lse=lse_ref[0,pl.ds(qb,1),:]
        def run(W):
            lo=pl.multiple_of(lob*BLK,BLK)
            ks=pl.ds(lo,W)
            bs=pl.ds(pl.multiple_of((lob-qb+nblk-1)*BLK,BLK),W)
            st=dot_nt(jnp.concatenate([k_ref[ks,:],segk_ref[ks,:]],axis=1),q_cat)
            p=jnp.exp(st+bias_ref[bs,:]-lse)
            dp=dot_nt(v_ref[ks,:],do2)
            ds=p*(dp-delta)
            acc_ref[bs,:]+=ds
            dsb=ds.astype(jnp.bfloat16)
            dva_ref[ks,:]+=dot_nn(p.astype(jnp.bfloat16),do2)
            dka_ref[ks,:]+=dot_nn(dsb,q2)
            dqt=dot_nn(kt_ref[:,ks],dsb)
            d=jnp.concatenate([dqt[:HEAD_DIM,:BLK],dqt[HEAD_DIM:,BLK:]],axis=0)*(HEAD_DIM**-0.5)
            dq_ref[rows,:]=d.T.astype(jnp.bfloat16)
        by_width(nblk,nb_ref[qb],run)
        return 0
    lax.fori_loop(0,nblk,body,0)
    dk_ref[...]=dka_ref[...].astype(jnp.bfloat16)
    dv_ref[...]=dva_ref[...].astype(jnp.bfloat16)
    near=(nblk-2)*BLK
    total=(2*nblk-1)*BLK
    for h in range(2):
        c=slice(h*BLK,(h+1)*BLK)
        wide=jnp.concatenate([jnp.zeros((BLK,BLK),jnp.float32),acc_ref[near+2*BLK:near+3*BLK,c],acc_ref[near+BLK:near+2*BLK,c],acc_ref[near:near+BLK,c]],axis=1)
        back=pltpu.roll(wide[::1],0,1,stride=1,stride_axis=0) if False else unroll_rows(wide)
        near_ref[0,h:h+1,:]=jnp.sum(back,axis=0,keepdims=True)
        low=jnp.sum(acc_ref[0:near,c],axis=0,keepdims=True)
        high=jnp.sum(acc_ref[near+3*BLK:total,c],axis=0,keepdims=True)
        far_ref[0,h:h+1,:]=jnp.concatenate([low,high],axis=1)

def unroll_rows(wide):
    n=wide.shape[1]
    out=wide
    row=lax.broadcasted_iota(jnp.int32,wide.shape,0)
    bit=1
    while bit<wide.shape[0]:
        out=jnp.where((row & bit)!=0,pltpu.roll(out,n-bit,1),out)
        bit*=2
    return out

def pair_spec(nrow): return pl.BlockSpec((nrow,2*HEAD_DIM),lambda p,*_:(0,p))
def full_spec(shape): return pl.BlockSpec(shape,lambda p,*_:(0,)*len(shape))
def lead_spec(shape): return pl.BlockSpec((1,)+shape,lambda p,*_:(p,0,0))

def attn_fwd(lo,nb,q,k,v,segq,segk,w):
    L,D=q.shape; nblk=L//BLK; pairs=D//(2*HEAD_DIM)
    return pl.pallas_call(functools.partial(fwd_kernel,nblk),
        grid_spec=pltpu.PrefetchScalarGridSpec(num_scalar_prefetch=2,grid=(pairs,),
          in_specs=[pair_spec(L)]*3+[full_spec((L,128))]*2+[lead_spec((2,512))],
          out_specs=[pair_spec(L),lead_spec((nblk,2*BLK))],
          scratch_shapes=[pltpu.VMEM((2*HEAD_DIM,L),jnp.bfloat16),pltpu.VMEM(((2*nblk-1)*BLK,2*BLK),jnp.float32)]),
        out_shape=[jax.ShapeDtypeStruct((L,D),jnp.bfloat16),jax.ShapeDtypeStruct((pairs,nblk,2*BLK),jnp.float32)],
        compiler_params=pltpu.CompilerParams(vmem_limit_bytes=40*2**20),
        cost_estimate=pl.CostEstimate(flops=2*10**9,bytes_accessed=8*2**20,transcendentals=6*10**6))(lo,nb,q,k,v,segq,segk,w)

def attn_bwd(lo,nb,q,k,v,do,ctx,lse,segq,segk,w):
    L,D=q.shape; nblk=L//BLK; pairs=D//(2*HEAD_DIM)
    return pl.pallas_call(functools.partial(bwd_kernel,nblk),
        grid_spec=pltpu.PrefetchScalarGridSpec(num_scalar_prefetch=2,grid=(pairs,),
          in_specs=[pair_spec(L)]*5+[lead_spec((nblk,2*BLK))]+[full_spec((L,128))]*2+[lead_spec((2,512))],
          out_specs=[pair_spec(L)]*3+[lead_spec((2,512)),lead_spec((2,256))],
          scratch_shapes=[pltpu.VMEM((2*HEAD_DIM,L),jnp.bfloat16),pltpu.VMEM(((2*nblk-1)*BLK,2*BLK),jnp.float32),pltpu.VMEM(((2*nblk-1)*BLK,2*BLK),jnp.float32),
             pltpu.VMEM((L,2*HEAD_DIM),jnp.float32),pltpu.VMEM((L,2*HEAD_DIM),jnp.float32)]),
        out_shape=[jax.ShapeDtypeStruct((L,D),jnp.bfloat16)]*3+[jax.ShapeDtypeStruct((pairs,2,512),jnp.float32),jax.ShapeDtypeStruct((pairs,2,256),jnp.float32)],
        compiler_params=pltpu.CompilerParams(vmem_limit_bytes=40*2**20),
        cost_estimate=pl.CostEstimate(flops=4*10**9,bytes_accessed=16*2**20,transcendentals=6*10**6))(lo,nb,q,k,v,do,ctx,lse,segq,segk,w)

def seg_arrays(seg):
    L=seg.shape[0]; nblk=L//BLK
    ids=jnp.arange(128,dtype=jnp.int32)
    segq=(seg[:,None]==ids[None,:]).astype(jnp.bfloat16)
    segk=jnp.where((seg[:,None]!=ids[None,:])&(ids[None,:]<16),-BIG,0.0).astype(jnp.bfloat16)
    sb=seg.reshape(nblk,BLK)
    first=jnp.sum((seg[None,:]<sb[:,:1]).astype(jnp.int32),axis=1)
    last=jnp.sum((seg[None,:]<=sb[:,-1:]).astype(jnp.int32),axis=1)
    lo=first//BLK
    nb=(last+BLK-1)//BLK-lo
    return segq,segk,lo.astype(jnp.int32),nb.astype(jnp.int32)

def bias_lanes(table):
    off=-(jnp.arange(512,dtype=jnp.int32)-256)
    oh=(bucket_index(off)[None,:]==jnp.arange(table.shape[0],dtype=jnp.int32)[:,None]).astype(jnp.bfloat16)
    w=lax.dot_general(table,oh,(((0,),(0,)),((),())),preferred_element_type=jnp.float32)
    return w.reshape(-1,2,512)

def table_grad(near,far,buckets):
    off=-(jnp.arange(512,dtype=jnp.int32)-256)
    oh=(bucket_index(off)[:,None]==jnp.arange(buckets,dtype=jnp.int32)[None,:]).astype(jnp.float32)
    n=jnp.einsum("hx,xb->bh",near.reshape(-1,512),oh,precision=lax.Precision.HIGHEST)
    f=far.reshape(-1,2,128).sum(-1)
    ids=jnp.arange(buckets,dtype=jnp.int32)[:,None]
    return n+jnp.where(ids==15,f[None,:,0],0)+jnp.where(ids==31,f[None,:,1],0)

TILE=256
def gelu_parts(x):
    c=0.7978845608028654
    x2=x*x
    t=jnp.tanh(x*(c+(c*0.044715)*x2))
    half=0.5*(1.0+t)
    slope=half+0.5*x*(1.0-t*t)*(c+(3*c*0.044715)*x2)
    return x*half,slope

def expert_kernel(count, parts, *refs):
    rows=refs[:count]; cots=refs[count:2*count]
    wi_refs=refs[2*count:2*count+parts]; wo_refs=refs[2*count+parts:2*count+2*parts]
    refs=refs[2*count+2*parts:]
    outs=refs[:count]; act_ref,db_ref,dg_ref=refs[count:count+3]
    x_ref,c_ref,wi_buf,wo_buf,acc_ref,dga_ref,act_buf,db_buf,w_sem,o_sem=refs[count+3:]
    block=wi_refs[0].shape[1]
    per=block//TILE
    total=parts*per
    for k in range(parts):
        pltpu.make_async_copy(wi_refs[k],wi_buf.at[k],w_sem.at[0,k]).start()
        pltpu.make_async_copy(wo_refs[k],wo_buf.at[k],w_sem.at[1,k]).start()
    first=0
    for i in range(count):
        n=rows[i].shape[0]
        x_ref[first:first+n,:]=rows[i][...]
        c_ref[first:first+n,:]=cots[i][...]
        first+=n
    acc_ref[...]=jnp.zeros_like(acc_ref)
    dga_ref[...]=jnp.zeros_like(dga_ref)
    def out_copies(step,slot):
        cols=pl.ds(pl.multiple_of(step*TILE,TILE),TILE)
        return (pltpu.make_async_copy(act_buf.at[slot],act_ref.at[:,cols],o_sem.at[0,slot]),
                pltpu.make_async_copy(db_buf.at[slot],db_ref.at[:,cols],o_sem.at[1,slot]))
    for k in range(parts):
        pltpu.make_async_copy(wi_refs[k],wi_buf.at[k],w_sem.at[0,k]).wait()
        pltpu.make_async_copy(wo_refs[k],wo_buf.at[k],w_sem.at[1,k]).wait()
        def body(c,_):
            step=k*per+c
            slot=lax.rem(step,2)
            @pl.when(step>=2)
            def _():
                for cp in out_copies(step-2,slot): cp.wait()
            cols=pl.ds(pl.multiple_of(c*TILE,TILE),TILE)
            wi=wi_buf[k,:,cols]
            wo=wo_buf[k,cols,:]
            before=dot_nn(x_ref[...],wi)
            up=dot_nt(c_ref[...],wo)
            active,slope=gelu_parts(before)
            prod=active*up
            dga_ref[...]+=prod[:,:128]+prod[:,128:]
            act_buf[slot]=active.astype(jnp.bfloat16)
            db=(up*slope).astype(jnp.bfloat16)
            db_buf[slot]=db
            acc_ref[...]+=dot_nt(db,wi)
            for cp in out_copies(step,slot): cp.start()
            return 0
        lax.fori_loop(0,per,body,0)
    first=0
    for i in range(count):
        n=rows[i].shape[0]
        outs[i][...]=acc_ref[first:first+n,:].astype(jnp.bfloat16)
        first+=n
    ones=jnp.ones((8,128),jnp.bfloat16)
    sums=dga_ref[...]
    hi=sums.astype(jnp.bfloat16)
    rest=sums-hi.astype(jnp.float32)
    mid=rest.astype(jnp.bfloat16)
    low=(rest-mid.astype(jnp.float32)).astype(jnp.bfloat16)
    dg_ref[...]=dot_nt(ones,hi)+dot_nt(ones,mid)+dot_nt(ones,low)
    for step in (total-2,total-1):
        for cp in out_copies(step,step%2): cp.wait()

def expert_half(rows,cots,w_ins,w_outs):
    count=len(rows); parts=len(w_ins)
    width,block=w_ins[0].shape
    R=sum(r.shape[0] for r in rows)
    vm=pl.BlockSpec(memory_space=pltpu.VMEM); hb=pl.BlockSpec(memory_space=pl.ANY)
    outs=pl.pallas_call(functools.partial(expert_kernel,count,parts),
        in_specs=[vm]*(2*count)+[hb]*(2*parts),
        out_specs=[vm]*count+[hb,hb,vm],
        out_shape=[jax.ShapeDtypeStruct(r.shape,jnp.bfloat16) for r in rows]+[jax.ShapeDtypeStruct((R,parts*block),jnp.bfloat16)]*2+[jax.ShapeDtypeStruct((8,R),jnp.float32)],
        scratch_shapes=[pltpu.VMEM((R,width),jnp.bfloat16)]*2+[pltpu.VMEM((parts,width,block),jnp.bfloat16),pltpu.VMEM((parts,block,width),jnp.bfloat16),
            pltpu.VMEM((R,width),jnp.float32),pltpu.VMEM((R,128),jnp.float32),pltpu.VMEM((2,R,TILE),jnp.bfloat16),pltpu.VMEM((2,R,TILE),jnp.bfloat16),
            pltpu.SemaphoreType.DMA((2,parts)),pltpu.SemaphoreType.DMA((2,2))],
        compiler_params=pltpu.CompilerParams(vmem_limit_bytes=48*2**20),
        cost_estimate=pl.CostEstimate(flops=6*R*width*parts*block,bytes_accessed=20*2**20,transcendentals=R*parts*block))(*rows,*cots,*w_ins,*w_outs)
    return outs[:count],outs[count],outs[count+1],outs[count+2][0]

MESH = pl.DeviceIdType.MESH


def shard_peer(bit):
    return (lax.axis_index("expert"), lax.axis_index("shard") ^ bit)


def expert_peer(bit):
    return (lax.axis_index("expert") ^ bit, lax.axis_index("shard"))


def greet(peers):
    barrier = pltpu.get_barrier_semaphore()
    for peer in peers:
        pl.semaphore_signal(barrier, inc=1, device_id=peer, device_id_type=MESH)
    pl.semaphore_wait(barrier, len(peers))


def send(src, dst, send_sem, recv_sem, peer):
    copy = pltpu.make_async_remote_copy(
        src_ref=src, dst_ref=dst, send_sem=send_sem, recv_sem=recv_sem, device_id=peer, device_id_type=MESH
    )
    copy.start()
    return copy


def project_kernel(x_ref, small_in, q_in, k_in, v_in, o_in, q_ref, k_ref, v_ref, normed_ref, small_ref, all_ref,
                   small_buf, w_buf, unit_ref, sem_send, sem_recv, sem_own, sem_out):
    shard = lax.axis_index("shard")
    own = q_in.shape[0]

    def rows(bit):
        return pl.ds(pl.multiple_of((shard ^ bit) * own, 64), own)

    ins = [small_in, q_in, k_in, v_in, o_in]
    bufs = [small_buf] + [w_buf.at[i] for i in range(4)]
    count = len(ins)
    locals_ = []
    for i in range(count):
        copy = pltpu.make_async_copy(ins[i], bufs[i].at[rows(0)], sem_own.at[i])
        copy.start()
        locals_.append(copy)
    greet([shard_peer(1), shard_peer(2)])
    far, near, passed = [], [], []
    for i in range(count):
        far.append(send(ins[i], bufs[i].at[rows(0)], sem_send.at[0, i], sem_recv.at[0, i], shard_peer(2)))
    for i in range(count):
        near.append(send(ins[i], bufs[i].at[rows(0)], sem_send.at[1, i], sem_recv.at[1, i], shard_peer(1)))
    length, width = x_ref.shape
    tile = 256

    def unit(t, _):
        r = pl.ds(pl.multiple_of(t * tile, tile), tile)
        x = x_ref[r, :].astype(jnp.float32)
        unit_ref[r, :] = x * lax.rsqrt(jnp.mean(x * x, axis=-1, keepdims=True) + 1e-6)
        return 0

    lax.fori_loop(0, length // tile, unit, 0)

    def finish(i):
        far[i].wait_recv()
        passed.append(
            send(bufs[i].at[rows(2)], bufs[i].at[rows(2)], sem_send.at[2, i], sem_recv.at[2, i], shard_peer(1))
        )
        locals_[i].wait()
        near[i].wait_recv()
        passed[i].wait_recv()

    finish(0)
    small = small_buf[...]
    small_ref[...] = small
    gain = jnp.concatenate(
        [small[c * 128 : (c + 1) * 128, :].astype(jnp.float32).T[0:1] for c in range(width // 128)], axis=1
    )

    def norm(t, _):
        r = pl.ds(pl.multiple_of(t * tile, tile), tile)
        normed_ref[r, :] = (unit_ref[r, :] * gain).astype(jnp.bfloat16)
        return 0

    lax.fori_loop(0, length // tile, norm, 0)
    outs = []
    for i, out in ((1, q_ref), (2, k_ref), (3, v_ref)):
        finish(i)
        copy = pltpu.make_async_copy(w_buf.at[i - 1], all_ref.at[i - 1], sem_out.at[i - 1])
        copy.start()
        outs.append(copy)

        def project(t, _):
            r = pl.ds(pl.multiple_of(t * tile, tile), tile)
            y = dot_nn(normed_ref[r, :], w_buf[i - 1]).astype(jnp.bfloat16)
            if i == 1:
                y = (y.astype(jnp.float32) * HEAD_DIM**-0.5).astype(jnp.bfloat16)
            out[r, :] = y
            return 0

        lax.fori_loop(0, length // tile, project, 0)
    finish(4)
    copy = pltpu.make_async_copy(w_buf.at[3], all_ref.at[3], sem_out.at[3])
    copy.start()
    outs.append(copy)
    for c in outs:
        c.wait()
    for c in far + near + passed:
        c.wait_send()


def project(x, small, weights):
    length, width = x.shape
    own = small.shape[0]
    vm = pl.BlockSpec(memory_space=pltpu.VMEM)
    hb = pl.BlockSpec(memory_space=pl.ANY)
    bf = jnp.bfloat16
    return pl.pallas_call(
        project_kernel,
        in_specs=[vm] + [hb] * 5,
        out_specs=[vm] * 5 + [hb],
        out_shape=[jax.ShapeDtypeStruct((length, width), bf)] * 4
        + [jax.ShapeDtypeStruct((width, 128), bf), jax.ShapeDtypeStruct((4, width, width), bf)],
        scratch_shapes=[
            pltpu.VMEM((width, 128), bf),
            pltpu.VMEM((4, width, width), bf),
            pltpu.VMEM((length, width), jnp.float32),
            pltpu.SemaphoreType.DMA((3, 5)),
            pltpu.SemaphoreType.DMA((3, 5)),
            pltpu.SemaphoreType.DMA((5,)),
            pltpu.SemaphoreType.DMA((4,)),
        ],
        compiler_params=pltpu.CompilerParams(collective_id=0, has_side_effects=True, vmem_limit_bytes=40 * 2**20),
        cost_estimate=pl.CostEstimate(flops=4 * 10**9, bytes_accessed=20 * 2**20, transcendentals=0),
    )(x, small, *weights)


def gate_columns(line, count, width):
    column = jnp.broadcast_to(line, (128, 256)).T[:count]
    return jnp.concatenate([column] * (width // 128), axis=1)


def experts_kernel(
    size, cap, tile,
    rows_in, gate_in, cot_in, own_in, far_in,
    back_out, dgate_out, mine_out, other_out, result_out,
    rows, gates, cots, weights, active, d_before, total, d_gate, back, d_gates, back_in, d_gates_in,
    gated, gated_t, g_send, g_recv, stage, result,
    w_sem, wr_sem, row_send, row_recv, gate_send, gate_recv, back_send, back_recv, dg_send, dg_recv,
    g_sem_send, g_sem_recv, own_sem, out_sem,
):
    width = weights.shape[2]
    block = weights.shape[3]
    per = block // tile
    group = 2
    count = group * cap

    def part(k):
        return pl.ds(k * cap, cap)

    local = [
        pltpu.make_async_copy(own_in, weights.at[0], w_sem.at[0]),
        pltpu.make_async_copy(far_in, weights.at[2], w_sem.at[1]),
        pltpu.make_async_copy(cot_in, cots, w_sem.at[2]),
        pltpu.make_async_copy(rows_in.at[0], rows.at[part(0)], w_sem.at[3]),
        pltpu.make_async_copy(gate_in.at[0], gates.at[0], w_sem.at[4]),
    ]
    for c in local:
        c.start()
    greet([expert_peer(k) for k in range(1, size)] + [shard_peer(1)])
    sent = []
    arrive = {}
    order = sorted(range(1, size), key=lambda k: (-(k >> 1) if k > 1 else 0))
    for k in order:
        arrive[k] = [
            send(gate_in.at[k], gates.at[k], gate_send.at[k], gate_recv.at[k], expert_peer(k)),
            send(rows_in.at[k], rows.at[part(k)], row_send.at[k], row_recv.at[k], expert_peer(k)),
        ]
        sent += arrive[k]
    moved = [
        send(own_in, weights.at[1], wr_sem.at[0, 0], wr_sem.at[1, 0], shard_peer(1)),
        send(far_in, weights.at[3], wr_sem.at[0, 1], wr_sem.at[1, 1], shard_peer(1)),
    ]
    sent += moved
    d_gates[...] = jnp.zeros_like(d_gates)
    for c in local:
        c.wait()
    for c in moved:
        c.wait_recv()
    ones = jnp.ones((8, 128), jnp.bfloat16)
    returned = {}
    groups = size // group
    for i in range(groups):
        g = i ^ (i >> 1)
        mine = slice(g * count, (g + 1) * count)
        for k in range(group * g, group * (g + 1)):
            if k:
                for c in arrive[k]:
                    c.wait_recv()
        total[...] = jnp.zeros_like(total)
        d_gate[...] = jnp.zeros_like(d_gate)

        def step(t, _):
            kk = t // per
            cols = pl.ds(pl.multiple_of(lax.rem(t, per) * tile, tile), tile)
            where = pl.ds(pl.multiple_of(t * tile, tile), tile)
            wi = weights[kk, 0, :, cols]
            wo = weights[kk, 1, cols, :]
            before = dot_nn(rows[mine, :], wi)
            up = dot_nt(cots[mine, :], wo)
            value, slope = gelu_parts(before)
            prod = value * up
            d_gate[...] += sum(prod[:, c * 128 : (c + 1) * 128] for c in range(tile // 128))
            active[mine, where] = value.astype(jnp.bfloat16)
            db = (up * slope).astype(jnp.bfloat16)
            d_before[mine, where] = db
            total[...] += dot_nt(db, wi)
            return 0

        lax.fori_loop(0, weights.shape[0] * per, step, 0)
        back[mine, :] = total[...].astype(jnp.bfloat16)
        for k in range(group * g, group * (g + 1)):
            sums = d_gate[(k - group * g) * cap : (k - group * g + 1) * cap, :]
            hi = sums.astype(jnp.bfloat16)
            rest = sums - hi.astype(jnp.float32)
            mid = rest.astype(jnp.bfloat16)
            low = (rest - mid.astype(jnp.float32)).astype(jnp.bfloat16)
            d_gates[k, :, 0:cap] = dot_nt(ones, hi) + dot_nt(ones, mid) + dot_nt(ones, low)
            if k:
                returned[k] = [
                    send(d_gates.at[k], d_gates_in.at[k], dg_send.at[k], dg_recv.at[k], expert_peer(k)),
                    send(back.at[part(k)], back_in.at[part(k)], back_send.at[k], back_recv.at[k], expert_peer(k)),
                ]
                sent += returned[k]
    for k in range(size):
        column = gate_columns(gates[k, 0:1, :], cap, width)
        gated[k * cap : (k + 1) * cap, :] = (cots[k * cap : (k + 1) * cap, :].astype(jnp.float32) * column).astype(jnp.bfloat16)
        scaled = rows[k * cap : (k + 1) * cap, :].astype(jnp.float32) * column
        result[k * cap : (k + 1) * cap, :] = scaled.astype(jnp.bfloat16)
    every = size * cap
    for c in range(width // 128):
        for r in range(every // 128):
            gated_t[c * 128 : (c + 1) * 128, r * 128 : (r + 1) * 128] = (
                result[r * 128 : (r + 1) * 128, c * 128 : (c + 1) * 128].astype(jnp.float32).T.astype(jnp.bfloat16)
            )
    strip = 256
    exchanged = []
    finals = []
    for n, kk in enumerate((1, 3, 2, 0)):
        def outer(t, _):
            where = pl.ds(pl.multiple_of(kk * block + t * strip, strip), strip)
            out = pl.ds(pl.multiple_of(t * strip, strip), strip)
            y = dot_tn(active[:, where], gated[...])
            if n < 2:
                g_send[n, 1, out, :] = y.astype(jnp.bfloat16)
            else:
                stage[1, out, :] = y
            return 0

        def inner(t, _):
            out = pl.ds(pl.multiple_of(t * strip, strip), strip)
            y = dot_nn(gated_t[out, :], d_before[:, kk * block : (kk + 1) * block])
            if n < 2:
                g_send[n, 0, out, :] = y.astype(jnp.bfloat16)
            else:
                stage[0, out, :] = y
            return 0

        lax.fori_loop(0, block // strip, outer, 0)
        lax.fori_loop(0, width // strip, inner, 0)
        if n < 2:
            c = send(g_send.at[n], g_recv.at[n], g_sem_send.at[n], g_sem_recv.at[n], shard_peer(1))
            exchanged.append(c)
            sent.append(c)
        else:
            m = 1 if kk == 2 else 0
            exchanged[m].wait_recv()
            if kk == 2:
                exchanged[1].wait_send()
                def add(t, _):
                    out = pl.ds(pl.multiple_of(t * strip, strip), strip)
                    for h in range(2):
                        g_send[1, h, out, :] = (stage[h, out, :] + g_recv[m, h, out, :].astype(jnp.float32)).astype(jnp.bfloat16)
                    return 0
                lax.fori_loop(0, block // strip, add, 0)
                c = pltpu.make_async_copy(g_send.at[1], other_out, out_sem.at[0])
            else:
                def add(t, _):
                    out = pl.ds(pl.multiple_of(t * strip, strip), strip)
                    for h in range(2):
                        stage[h, out, :] = stage[h, out, :] + g_recv[m, h, out, :].astype(jnp.float32)
                    return 0
                lax.fori_loop(0, block // strip, add, 0)
                c = pltpu.make_async_copy(stage, mine_out, out_sem.at[1])
            c.start()
            finals.append(c)

    def produce(r, _):
        span = pl.ds(pl.multiple_of(r * cap, 16), cap)
        y = sum(dot_nn(active[span, kk * block : (kk + 1) * block], weights[kk, 1]) for kk in range(4))
        result[span, :] = y.astype(jnp.bfloat16)
        return 0

    lax.fori_loop(0, size, produce, 0)
    c = pltpu.make_async_copy(result, result_out, out_sem.at[2])
    c.start()
    finals.append(c)
    back_in[part(0), :] = back[part(0), :]
    d_gates_in[0] = d_gates[0]
    for k in range(1, size):
        for c in returned[k]:
            c.wait_recv()
    for c in (
        pltpu.make_async_copy(back_in, back_out, out_sem.at[3]),
        pltpu.make_async_copy(d_gates_in, dgate_out, out_sem.at[4]),
    ):
        c.start()
        finals.append(c)
    for c in finals:
        c.wait()
    for c in sent:
        if c is not exchanged[1]:
            c.wait_send()


def run_experts(rows, gates, cots, own, far):
    size, cap, width = rows.shape
    block = own.shape[2]
    bf = jnp.bfloat16
    f32 = jnp.float32
    every = size * cap
    hb = pl.BlockSpec(memory_space=pl.ANY)
    vm = pltpu.VMEM
    dma = pltpu.SemaphoreType.DMA
    return pl.pallas_call(
        functools.partial(experts_kernel, size, cap, 256),
        in_specs=[hb] * 5,
        out_specs=[hb] * 5,
        out_shape=[
            jax.ShapeDtypeStruct((every, width), bf),
            jax.ShapeDtypeStruct((size, 8, 256), f32),
            jax.ShapeDtypeStruct((2, width, block), f32),
            jax.ShapeDtypeStruct((2, width, block), bf),
            jax.ShapeDtypeStruct((every, width), bf),
        ],
        scratch_shapes=[
            vm((every, width), bf),
            vm((size, 8, 256), f32),
            vm((every, width), bf),
            vm((4, 2, width, block), bf),
            vm((every, 4 * block), bf),
            vm((every, 4 * block), bf),
            vm((2 * cap, width), f32),
            vm((2 * cap, 128), f32),
            vm((every, width), bf),
            vm((size, 8, 256), f32),
            vm((every, width), bf),
            vm((size, 8, 256), f32),
            vm((every, width), bf),
            vm((width, every), bf),
            vm((2, 2, width, block), bf),
            vm((2, 2, width, block), bf),
            vm((2, width, block), f32),
            vm((every, width), bf),
            dma((5,)),
            dma((2, 2)),
        ]
        + [dma((size,))] * 8
        + [dma((2,)), dma((2,)), dma((1,)), dma((5,))],
        compiler_params=pltpu.CompilerParams(collective_id=1, has_side_effects=True, vmem_limit_bytes=60 * 2**20),
        cost_estimate=pl.CostEstimate(flops=36 * 10**9, bytes_accessed=30 * 2**20, transcendentals=4 * 10**6),
    )(rows, gates, cots, own, far)

EPS = 1e-06
BF = jnp.bfloat16
F32 = jnp.float32


def dot_tn(a, b):
    return lax.dot_general(a, b, (((0,), (0,)), ((), ())), preferred_element_type=F32)


def swap(value, axis, size, bit):
    return lax.ppermute(value, axis, [(i, i ^ bit) for i in range(size)])


def direct(size):
    return size <= 8 and size & (size - 1) == 0


def exchange(blocks, size):
    if direct(size):
        return [blocks[0]] + [swap(blocks[k], "expert", size, k) for k in range(1, size)]
    out = lax.all_to_all(jnp.stack(blocks), "expert", split_axis=0, concat_axis=0, tiled=True)
    return [out[k] for k in range(size)]


def gather_shards(value, size):
    if size == 4:
        far = swap(value, "shard", size, 2)
        near = swap(value, "shard", size, 1)
        return [value, near, far, swap(far, "shard", size, 1)]
    return [value] + [swap(value, "shard", size, k) for k in range(1, size)]


def reduce_shards(blocks, size):
    if size == 4:
        near1 = swap(blocks[3].astype(BF), "shard", size, 1)
        near0 = swap(blocks[1].astype(BF), "shard", size, 1)
        other = swap((blocks[2].astype(F32) + near1.astype(F32)).astype(BF), "shard", size, 2)
        return blocks[0].astype(F32) + near0.astype(F32) + other.astype(F32)
    total = blocks[0].astype(F32)
    for k in range(1, size):
        total = total + swap(blocks[k].astype(BF), "shard", size, k).astype(F32)
    return total


def reduce_experts(value, size, index):
    if not direct(size):
        return lax.psum(value, "expert")
    rows = value.shape[0] // size
    pieces = [
        lax.dynamic_slice_in_dim(value, (index ^ k) * rows, rows, 0).astype(BF) for k in range(size)
    ]
    total = sum(piece.astype(F32) for piece in exchange(pieces, size)).astype(BF)
    out = jnp.zeros(value.shape, BF)
    out = lax.dynamic_update_slice_in_dim(out, total, index * rows, 0)
    for k in range(1, size):
        out = lax.dynamic_update_slice_in_dim(
            out, swap(total, "expert", size, k), (index ^ k) * rows, 0
        )
    return out.astype(F32)


def in_order(blocks, index):
    rows = blocks[0].shape[0]
    out = jnp.zeros((rows * len(blocks),) + blocks[0].shape[1:], blocks[0].dtype)
    for k, block in enumerate(blocks):
        out = lax.dynamic_update_slice_in_dim(out, block, (index ^ k) * rows, 0)
    return out


def experts_by_collectives(row_blocks, gate_slots, cot_blocks, inner, outer, size, shards, cap):
    inners = gather_shards(inner, shards)
    outers = gather_shards(outer, shards)
    cells, width = size * cap, row_blocks.shape[2]
    rows = jnp.concatenate(exchange(list(row_blocks), size), axis=0)
    cots = jnp.concatenate(cot_blocks, axis=0)
    gates = jnp.concatenate(exchange(list(gate_slots.reshape(size, cap)), size))[:, None]
    half = cells // 2
    parts = [expert_half([rows[i : i + half]], [cots[i : i + half]], inners, outers) for i in (0, half)]
    back, active, d_before, d_gate = (
        jnp.concatenate([p[0][0] if i == 0 else p[i] for p in parts], axis=0) for i in range(4)
    )
    back = jnp.concatenate(exchange(list(back.reshape(size, cap, width)), size), axis=0)
    d_gate = jnp.concatenate(exchange(list(d_gate.reshape(size, cap)), size))
    d_out = (cots.astype(F32) * gates).astype(BF)
    gated = (rows.astype(F32) * gates).astype(BF)
    block = inner.shape[1]
    spans = [slice(k * block, (k + 1) * block) for k in range(shards)]
    grad_outer = reduce_shards([dot_tn(active[:, p], d_out) for p in spans], shards)
    grad_inner = reduce_shards([dot_tn(gated, d_before[:, p]) for p in spans], shards)
    result = dot_nn(active, jnp.concatenate(outers, axis=0)).astype(BF).reshape(size, cap, width)
    result = jnp.concatenate(exchange(list(result), size), axis=0)
    return back, d_gate, grad_inner, grad_outer, result


def per_device(
    tokens,
    segments,
    routes,
    order,
    gain_attn,
    w_query,
    w_key,
    w_value,
    w_output,
    rel_bias,
    gain_ffn,
    w_router,
    w_in,
    w_out,
    cotangent,
):
    seq_count, length, width = tokens.shape
    total = seq_count * length
    experts = lax.axis_size("expert")
    shards = lax.axis_size("shard")
    me = lax.axis_index("expert")
    my_shard = lax.axis_index("shard")
    capacity = (5 * total + 4 * experts - 1) // (4 * experts)
    cells = experts * capacity
    heads = rel_bias.shape[1]
    own = w_query.shape[0]
    own_buckets = rel_bias.shape[0]
    buckets = own_buckets * shards
    small = jnp.concatenate([gain_attn[:, None], gain_ffn[:, None], w_router], axis=1)
    small = jnp.pad(small, ((0, 0), (0, 128 - small.shape[1])))
    small = lax.dynamic_update_slice(small, rel_bias, (0, 128 - heads))
    route = routes.reshape(total)
    ranks = (jnp.arange(seq_count, dtype=jnp.int32)[:, None] * length + order).reshape(total)
    same_route = route[:, None] == route[None, :]
    earlier = ranks[None, :] < ranks[:, None]
    slot = jnp.sum((same_route & earlier).astype(jnp.int32), axis=1)
    kept = slot < capacity
    partner = route ^ me if direct(experts) else route
    place = jnp.where(kept, partner * capacity + slot, -1)
    spread = (jnp.arange(cells, dtype=jnp.int32)[:, None] == place[None, :]).astype(BF)
    chosen = (route[:, None] == jnp.arange(experts, dtype=jnp.int32)[None, :]).astype(F32)

    def to_blocks(values):
        slots = dot_nn(spread, values).astype(values.dtype)
        return [slots[k * capacity : (k + 1) * capacity] for k in range(experts)]

    cot = cotangent.reshape(total, width)
    cot_blocks = exchange(to_blocks(cot), experts)
    query, key, value, normed_low, small_all, weights_all = project(
        tokens.reshape(total, width), small, (w_query, w_key, w_value, w_output)
    )
    query_all, key_all, value_all, output_all = (weights_all[i] for i in range(4))
    own_pair = jnp.concatenate([w_in, w_out], axis=0)
    own_pair, query = lax.optimization_barrier((own_pair, query))
    far_pair = swap(own_pair, "shard", shards, 2)
    inputs = tokens.reshape(total, width).astype(F32)
    scale_one = lax.rsqrt(jnp.mean(inputs * inputs, axis=-1, keepdims=True) + EPS)
    unit_one = inputs * scale_one
    base = 3 * width
    gain_one = small_all[:, 0].astype(F32)
    gain_two = small_all[:, 1].astype(F32)
    router_all = small_all[:, 2 : 2 + experts]
    table = small_all[:, 128 - heads :].reshape(shards, own, heads)[:, :own_buckets]
    table = table.reshape(buckets, heads)
    bias = bias_lanes(table)
    seg = [seg_arrays(segments[i]) for i in range(seq_count)]
    rows_of = [slice(i * length, (i + 1) * length) for i in range(seq_count)]
    forward = [
        attn_fwd(s[2], s[3], query[r], key[r], value[r], s[0], s[1], bias)
        for s, r in zip(seg, rows_of)
    ]
    context = jnp.concatenate([f[0] for f in forward], axis=0) if seq_count > 1 else forward[0][0]
    resid = inputs + dot_nn(context, output_all)
    scale_two = lax.rsqrt(jnp.mean(resid * resid, axis=-1, keepdims=True) + EPS)
    unit_two = resid * scale_two
    normed_two_low = (unit_two * gain_two).astype(BF)
    logits = dot_nn(normed_two_low, router_all)
    probs = jax.nn.softmax(logits, axis=-1)
    gate = jnp.sum(probs * chosen, axis=-1)
    keep_weight = kept.astype(F32)
    keep_gate = gate * keep_weight
    gate_slots = jnp.sum(jnp.where(place[None, :] == jnp.arange(cells)[:, None], gate[None, :], 0), axis=1)
    row_blocks = dot_nn(spread, normed_two_low).astype(BF).reshape(experts, capacity, width)
    if direct(experts):
        gate_lines = jnp.pad(gate_slots.reshape(experts, 1, capacity), ((0, 0), (0, 7), (0, 256 - capacity)))
        back, gate_back, mine, other, expert_out = run_experts(
            row_blocks, gate_lines, jnp.concatenate(cot_blocks, axis=0), own_pair, far_pair
        )
        gate_cells = gate_back[:, 0, :capacity].reshape(cells)
        grads = mine + swap(other, "shard", shards, 2).astype(F32)
        grad_inner, grad_outer = grads[0], grads[1]
        out_cells = jnp.concatenate(
            exchange([expert_out[k * capacity : (k + 1) * capacity] for k in range(experts)], experts), axis=0
        )
    else:
        back, gate_cells, grad_inner, grad_outer, out_cells = experts_by_collectives(
            row_blocks, gate_slots, cot_blocks, w_in[0], w_out[0], experts, shards, capacity
        )
    upstream = cot.astype(F32)
    d_rows = dot_tn(spread, back)
    d_gate = jnp.sum(
        jnp.where(place[:, None] == jnp.arange(cells)[None, :], gate_cells[None, :], 0), axis=1
    )
    d_logits = (probs * (d_gate[:, None] * chosen - (d_gate * gate)[:, None])).astype(BF)
    d_router = dot_tn(normed_two_low, d_logits)
    d_normed_two = dot_nt(d_logits, router_all) + keep_gate[:, None] * d_rows
    d_gain_two = jnp.sum(d_normed_two * unit_two, axis=0)
    pulled = gain_two * d_normed_two
    d_resid = upstream + scale_two * (
        pulled - unit_two * jnp.mean(unit_two * pulled, axis=-1, keepdims=True)
    )
    d_branch = d_resid.astype(BF)
    d_context = dot_nt(d_branch, output_all).astype(BF)
    d_output_w = dot_tn(context, d_branch)

    def shard_blocks(values):
        return [
            lax.dynamic_slice_in_dim(values, (my_shard ^ k) * own, own, 0) for k in range(shards)
        ]

    sum_output = reduce_experts(
        reduce_shards(shard_blocks(d_output_w.astype(BF)), shards), experts, me
    )
    backward = [
        attn_bwd(s[2], s[3], query[r], key[r], value[r], d_context[r], f[0], f[1], s[0], s[1], bias)
        for s, r, f in zip(seg, rows_of, forward)
    ]
    d_query, d_key, d_value = (
        jnp.concatenate([b[i] for b in backward], axis=0) if seq_count > 1 else backward[0][i]
        for i in range(3)
    )
    d_table = sum(table_grad(b[3], b[4], buckets) for b in backward)
    d_weights = [dot_tn(normed_low, d).astype(BF) for d in (d_query, d_key, d_value)]
    d_normed = (
        dot_nt(d_query, query_all) + dot_nt(d_key, key_all) + dot_nt(d_value, value_all)
    )
    d_gain_one = jnp.sum(d_normed * unit_one, axis=0)
    pulled_one = gain_one * d_normed
    d_tokens = d_resid + scale_one * (
        pulled_one - unit_one * jnp.mean(unit_one * pulled_one, axis=-1, keepdims=True)
    )
    tail = jnp.concatenate([d_gain_one[:, None], d_gain_two[:, None], d_router], axis=1)
    tail = jnp.pad(tail, ((0, 0), (0, 128 - tail.shape[1]))).reshape(shards, own, 128)
    tail = lax.dynamic_update_slice(
        tail, d_table.reshape(shards, own_buckets, heads), (0, 0, 128 - heads)
    ).reshape(width, 128)
    last = jnp.concatenate(d_weights + [tail.astype(BF)], axis=1)
    last = reduce_experts(reduce_shards(shard_blocks(last), shards), experts, me)
    arrived = dot_tn(spread, out_cells)
    mixed = resid + keep_gate[:, None] * arrived
    return (
        mixed.astype(BF).reshape(tokens.shape),
        d_tokens.astype(BF).reshape(tokens.shape),
        last[:, base],
        last[:, :width],
        last[:, width : 2 * width],
        last[:, 2 * width : base],
        sum_output,
        last[:own_buckets, base + 128 - heads :],
        last[:, base + 1],
        last[:, base + 2 : base + 2 + experts],
        grad_inner[None],
        grad_outer[None],
    )


def solution(mesh):
    in_specs = (
        P(("expert", "shard"), None, None),
        P(("expert", "shard"), None),
        P(("expert", "shard"), None, None),
        P(("expert", "shard"), None),
        P("shard"),
        P("shard", None),
        P("shard", None),
        P("shard", None),
        P("shard", None),
        P("shard", None),
        P("shard"),
        P("shard", None),
        P("expert", None, "shard"),
        P("expert", "shard", None),
        P(("expert", "shard"), None, None),
    )
    out_specs = (
        P(("expert", "shard"), None, None),
        P(("expert", "shard"), None, None),
        P("shard"),
        P("shard", None),
        P("shard", None),
        P("shard", None),
        P("shard", None),
        P("shard", None),
        P("shard"),
        P("shard", None),
        P("expert", None, "shard"),
        P("expert", "shard", None),
    )
    return jax.shard_map(
        per_device, mesh=mesh, in_specs=in_specs, out_specs=out_specs, check_vma=False
    )
```

```python
import functools

import jax
import jax.numpy as jnp
from jax import lax
from jax.experimental import pallas as pl
from jax.experimental.pallas import tpu as pltpu
from jax.sharding import PartitionSpec as P
HEAD_DIM=64
BLK=128
EDGES = (12, 16, 23, 32, 46, 64, 91)
BIG=1e9
def bucket_index(offset):
    magnitude = jnp.abs(offset)
    far = 8 + sum(((magnitude >= edge).astype(jnp.int32) for edge in EDGES))
    near = jnp.where(magnitude < 8, magnitude, far)
    return near + 16 * (offset > 0).astype(jnp.int32)

def dot_nt(a,b): return lax.dot_general(a,b,(((1,),(1,)),((),())),preferred_element_type=jnp.float32)
def dot_nn(a,b): return lax.dot_general(a,b,(((1,),(0,)),((),())),preferred_element_type=jnp.float32)

def head_mask():
    lane=lax.broadcasted_iota(jnp.int32,(BLK,2*HEAD_DIM),1)
    return (lane<HEAD_DIM).astype(jnp.float32).astype(jnp.bfloat16)

def build_bias(w_ref, bias_ref, nblk, pairs):
    rows = (2 * nblk - 1) * BLK
    near = (nblk - 2) * BLK
    for j in range(pairs):
        for h in range(2):
            c = slice((2 * j + h) * BLK, (2 * j + h + 1) * BLK)
            w = w_ref[j, h : h + 1, :]
            bias_ref[0:near, c] = jnp.broadcast_to(w[:, 511:512], (near, BLK))
            bias_ref[near + 3 * BLK : rows, c] = jnp.broadcast_to(w[:, 0:1], (near, BLK))
            r = pltpu.roll(jnp.broadcast_to(w, (BLK, 512)), 0, 1, stride=1, stride_axis=0)
            bias_ref[near : near + BLK, c] = r[:, 384:512]
            bias_ref[near + BLK : near + 2 * BLK, c] = r[:, 256:384]
            bias_ref[near + 2 * BLK : near + 3 * BLK, c] = r[:, 128:256]


def by_width(nblk, count, run):
    for n in range(1, nblk + 1):

        @pl.when(count == n)
        def _():
            run(n * BLK)


def pair_of(block, mask):
    return jnp.concatenate([block * mask, block * (1 - mask)], axis=0)


def flip(src_ref, dst_ref, nblk, pairs):
    for j in range(pairs):
        c = slice(j * BLK, (j + 1) * BLK)
        for b in range(nblk):
            s = slice(b * BLK, (b + 1) * BLK)
            dst_ref[c, s] = src_ref[s, c].astype(jnp.float32).T.astype(jnp.bfloat16)


def join_heads(wide):
    return jnp.concatenate([wide[:HEAD_DIM, :BLK], wide[HEAD_DIM:, BLK:]], axis=0)


def fwd_kernel(nblk, pairs, lo_ref, nb_ref, q_ref, k_ref, v_ref, segq_ref, segk_ref, w_ref, ctx_ref, lse_ref, vt_ref, bias_ref):
    build_bias(w_ref, bias_ref, nblk, pairs)
    flip(v_ref, vt_ref, nblk, pairs)
    mask = head_mask()
    lanes = [slice(j * BLK, (j + 1) * BLK) for j in range(pairs)]
    both = [slice(2 * j * BLK, 2 * (j + 1) * BLK) for j in range(pairs)]

    def body(qb, _):
        rows = pl.ds(pl.multiple_of(qb * BLK, BLK), BLK)
        lob = lo_ref[qb]
        sq = segq_ref[rows, :]
        sq = jnp.concatenate([sq, sq], axis=0)
        q_cat = [jnp.concatenate([pair_of(q_ref[rows, c], mask), sq], axis=1) for c in lanes]

        def run(W):
            ks = pl.ds(pl.multiple_of(lob * BLK, BLK), W)
            bs = pl.ds(pl.multiple_of((lob - qb + nblk - 1) * BLK, BLK), W)
            sk = segk_ref[ks, :]
            st = [
                dot_nt(jnp.concatenate([k_ref[ks, c], sk], axis=1), q) + bias_ref[bs, d]
                for c, d, q in zip(lanes, both, q_cat)
            ]
            m = [jnp.max(x, axis=0, keepdims=True) for x in st]
            e = [jnp.exp(x - y) for x, y in zip(st, m)]
            l = [jnp.sum(x, axis=0, keepdims=True) for x in e]
            ot = [dot_nn(vt_ref[c, ks], x.astype(jnp.bfloat16)) / y for c, x, y in zip(lanes, e, l)]
            for j, c in enumerate(lanes):
                ctx_ref[rows, c] = join_heads(ot[j]).T.astype(jnp.bfloat16)
                lse_ref[j, pl.ds(qb, 1), :] = m[j] + jnp.log(l[j])

        by_width(nblk, nb_ref[qb], run)
        return 0

    lax.fori_loop(0, nblk, body, 0)


def bwd_kernel(
    nblk, pairs, lo_ref, nb_ref, q_ref, k_ref, v_ref, do_ref, ctx_ref, lse_ref, segq_ref, segk_ref, w_ref,
    dq_ref, dk_ref, dv_ref, near_ref, far_ref, kt_ref, bias_ref, acc_ref, dka_ref, dva_ref,
):
    build_bias(w_ref, bias_ref, nblk, pairs)
    flip(k_ref, kt_ref, nblk, pairs)
    acc_ref[...] = jnp.zeros_like(acc_ref)
    dka_ref[...] = jnp.zeros_like(dka_ref)
    dva_ref[...] = jnp.zeros_like(dva_ref)
    mask = head_mask()
    lanes = [slice(j * BLK, (j + 1) * BLK) for j in range(pairs)]
    both = [slice(2 * j * BLK, 2 * (j + 1) * BLK) for j in range(pairs)]
    row = lax.broadcasted_iota(jnp.int32, (16, 2 * HEAD_DIM), 0)
    lane = lax.broadcasted_iota(jnp.int32, (16, 2 * HEAD_DIM), 1)
    pick = ((lane // HEAD_DIM) == row).astype(jnp.float32).astype(jnp.bfloat16)

    def body(qb, _):
        rows = pl.ds(pl.multiple_of(qb * BLK, BLK), BLK)
        lob = lo_ref[qb]
        sq = segq_ref[rows, :]
        sq = jnp.concatenate([sq, sq], axis=0)
        q2 = [pair_of(q_ref[rows, c], mask) for c in lanes]
        q_cat = [jnp.concatenate([q, sq], axis=1) for q in q2]
        do2 = [pair_of(do_ref[rows, c], mask) for c in lanes]
        delta = []
        for c in lanes:
            prod = do_ref[rows, c].astype(jnp.float32) * ctx_ref[rows, c].astype(jnp.float32)
            hi = prod.astype(jnp.bfloat16)
            low = (prod - hi.astype(jnp.float32)).astype(jnp.bfloat16)
            dl = dot_nt(pick, hi) + dot_nt(pick, low)
            delta.append(jnp.concatenate([dl[0:1], dl[1:2]], axis=1))
        lse = [lse_ref[j, pl.ds(qb, 1), :] for j in range(pairs)]

        def run(W):
            ks = pl.ds(pl.multiple_of(lob * BLK, BLK), W)
            bs = pl.ds(pl.multiple_of((lob - qb + nblk - 1) * BLK, BLK), W)
            sk = segk_ref[ks, :]
            st = [dot_nt(jnp.concatenate([k_ref[ks, c], sk], axis=1), q) for c, q in zip(lanes, q_cat)]
            dp = [dot_nt(v_ref[ks, c], d) for c, d in zip(lanes, do2)]
            p = [jnp.exp(x + bias_ref[bs, d] - y) for x, d, y in zip(st, both, lse)]
            ds = [x * (y - z) for x, y, z in zip(p, dp, delta)]
            dsb = [x.astype(jnp.bfloat16) for x in ds]
            for j, (c, d) in enumerate(zip(lanes, both)):
                acc_ref[bs, d] += ds[j]
                dva_ref[ks, c] += dot_nn(p[j].astype(jnp.bfloat16), do2[j])
                dka_ref[ks, c] += dot_nn(dsb[j], q2[j])
                dqt = join_heads(dot_nn(kt_ref[c, ks], dsb[j])) * (HEAD_DIM**-0.5)
                dq_ref[rows, c] = dqt.T.astype(jnp.bfloat16)

        by_width(nblk, nb_ref[qb], run)
        return 0

    lax.fori_loop(0, nblk, body, 0)
    dk_ref[...] = dka_ref[...].astype(jnp.bfloat16)
    dv_ref[...] = dva_ref[...].astype(jnp.bfloat16)
    near = (nblk - 2) * BLK
    total = (2 * nblk - 1) * BLK
    for j in range(pairs):
        for h in range(2):
            c = slice((2 * j + h) * BLK, (2 * j + h + 1) * BLK)
            wide = jnp.concatenate(
                [
                    jnp.zeros((BLK, BLK), jnp.float32),
                    acc_ref[near + 2 * BLK : near + 3 * BLK, c],
                    acc_ref[near + BLK : near + 2 * BLK, c],
                    acc_ref[near : near + BLK, c],
                ],
                axis=1,
            )
            near_ref[j, h : h + 1, :] = jnp.sum(unroll_rows(wide), axis=0, keepdims=True)
            low = jnp.sum(acc_ref[0:near, c], axis=0, keepdims=True)
            high = jnp.sum(acc_ref[near + 3 * BLK : total, c], axis=0, keepdims=True)
            far_ref[j, h : h + 1, :] = jnp.concatenate([low, high], axis=1)


def unroll_rows(wide):
    n=wide.shape[1]
    out=wide
    row=lax.broadcasted_iota(jnp.int32,wide.shape,0)
    bit=1
    while bit<wide.shape[0]:
        out=jnp.where((row & bit)!=0,pltpu.roll(out,n-bit,1),out)
        bit*=2
    return out

FWD_PAIRS = 6
BWD_PAIRS = 3


def pair_spec(nrow, pairs):
    return pl.BlockSpec((nrow, 2 * HEAD_DIM * pairs), lambda p, *_: (0, p))


def full_spec(shape):
    return pl.BlockSpec(shape, lambda p, *_: (0,) * len(shape))


def lead_spec(pairs, shape):
    return pl.BlockSpec((pairs,) + shape, lambda p, *_: (p, 0, 0))


def attn_fwd(lo, nb, q, k, v, segq, segk, w):
    L, D = q.shape
    nblk = L // BLK
    every = D // (2 * HEAD_DIM)
    pairs = FWD_PAIRS
    return pl.pallas_call(
        functools.partial(fwd_kernel, nblk, pairs),
        grid_spec=pltpu.PrefetchScalarGridSpec(
            num_scalar_prefetch=2,
            grid=(every // pairs,),
            in_specs=[pair_spec(L, pairs)] * 3 + [full_spec((L, 128))] * 2 + [lead_spec(pairs, (2, 512))],
            out_specs=[pair_spec(L, pairs), lead_spec(pairs, (nblk, 2 * BLK))],
            scratch_shapes=[
                pltpu.VMEM((2 * HEAD_DIM * pairs, L), jnp.bfloat16),
                pltpu.VMEM(((2 * nblk - 1) * BLK, 2 * BLK * pairs), jnp.float32),
            ],
        ),
        out_shape=[
            jax.ShapeDtypeStruct((L, D), jnp.bfloat16),
            jax.ShapeDtypeStruct((every, nblk, 2 * BLK), jnp.float32),
        ],
        compiler_params=pltpu.CompilerParams(vmem_limit_bytes=60 * 2**20),
        cost_estimate=pl.CostEstimate(flops=2 * 10**9, bytes_accessed=8 * 2**20, transcendentals=6 * 10**6),
    )(lo, nb, q, k, v, segq, segk, w)


def attn_bwd(lo, nb, q, k, v, do, ctx, lse, segq, segk, w):
    L, D = q.shape
    nblk = L // BLK
    every = D // (2 * HEAD_DIM)
    pairs = BWD_PAIRS
    rows = (2 * nblk - 1) * BLK
    return pl.pallas_call(
        functools.partial(bwd_kernel, nblk, pairs),
        grid_spec=pltpu.PrefetchScalarGridSpec(
            num_scalar_prefetch=2,
            grid=(every // pairs,),
            in_specs=[pair_spec(L, pairs)] * 5
            + [lead_spec(pairs, (nblk, 2 * BLK))]
            + [full_spec((L, 128))] * 2
            + [lead_spec(pairs, (2, 512))],
            out_specs=[pair_spec(L, pairs)] * 3 + [lead_spec(pairs, (2, 512)), lead_spec(pairs, (2, 256))],
            scratch_shapes=[
                pltpu.VMEM((2 * HEAD_DIM * pairs, L), jnp.bfloat16),
                pltpu.VMEM((rows, 2 * BLK * pairs), jnp.float32),
                pltpu.VMEM((rows, 2 * BLK * pairs), jnp.float32),
                pltpu.VMEM((L, 2 * HEAD_DIM * pairs), jnp.float32),
                pltpu.VMEM((L, 2 * HEAD_DIM * pairs), jnp.float32),
            ],
        ),
        out_shape=[jax.ShapeDtypeStruct((L, D), jnp.bfloat16)] * 3
        + [jax.ShapeDtypeStruct((every, 2, 512), jnp.float32), jax.ShapeDtypeStruct((every, 2, 256), jnp.float32)],
        compiler_params=pltpu.CompilerParams(vmem_limit_bytes=60 * 2**20),
        cost_estimate=pl.CostEstimate(flops=4 * 10**9, bytes_accessed=16 * 2**20, transcendentals=6 * 10**6),
    )(lo, nb, q, k, v, do, ctx, lse, segq, segk, w)


def seg_arrays(seg):
    L=seg.shape[0]; nblk=L//BLK
    ids=jnp.arange(128,dtype=jnp.int32)
    segq=(seg[:,None]==ids[None,:]).astype(jnp.bfloat16)
    segk=jnp.where((seg[:,None]!=ids[None,:])&(ids[None,:]<16),-BIG,0.0).astype(jnp.bfloat16)
    sb=seg.reshape(nblk,BLK)
    first=jnp.sum((seg[None,:]<sb[:,:1]).astype(jnp.int32),axis=1)
    last=jnp.sum((seg[None,:]<=sb[:,-1:]).astype(jnp.int32),axis=1)
    lo=first//BLK
    nb=(last+BLK-1)//BLK-lo
    return segq,segk,lo.astype(jnp.int32),nb.astype(jnp.int32)

def bias_lanes(table):
    off=-(jnp.arange(512,dtype=jnp.int32)-256)
    oh=(bucket_index(off)[None,:]==jnp.arange(table.shape[0],dtype=jnp.int32)[:,None]).astype(jnp.bfloat16)
    w=lax.dot_general(table,oh,(((0,),(0,)),((),())),preferred_element_type=jnp.float32)
    return w.reshape(-1,2,512)

def table_grad(near,far,buckets):
    off=-(jnp.arange(512,dtype=jnp.int32)-256)
    oh=(bucket_index(off)[:,None]==jnp.arange(buckets,dtype=jnp.int32)[None,:]).astype(jnp.float32)
    n=jnp.einsum("hx,xb->bh",near.reshape(-1,512),oh,precision=lax.Precision.HIGHEST)
    f=far.reshape(-1,2,128).sum(-1)
    ids=jnp.arange(buckets,dtype=jnp.int32)[:,None]
    return n+jnp.where(ids==15,f[None,:,0],0)+jnp.where(ids==31,f[None,:,1],0)

TILE=256
def gelu_parts(x):
    c=0.7978845608028654
    x2=x*x
    t=jnp.tanh(x*(c+(c*0.044715)*x2))
    half=0.5*(1.0+t)
    slope=half+0.5*x*(1.0-t*t)*(c+(3*c*0.044715)*x2)
    return x*half,slope

def expert_kernel(count, parts, *refs):
    rows=refs[:count]; cots=refs[count:2*count]
    wi_refs=refs[2*count:2*count+parts]; wo_refs=refs[2*count+parts:2*count+2*parts]
    refs=refs[2*count+2*parts:]
    outs=refs[:count]; act_ref,db_ref,dg_ref=refs[count:count+3]
    x_ref,c_ref,wi_buf,wo_buf,acc_ref,dga_ref,act_buf,db_buf,w_sem,o_sem=refs[count+3:]
    block=wi_refs[0].shape[1]
    per=block//TILE
    total=parts*per
    for k in range(parts):
        pltpu.make_async_copy(wi_refs[k],wi_buf.at[k],w_sem.at[0,k]).start()
        pltpu.make_async_copy(wo_refs[k],wo_buf.at[k],w_sem.at[1,k]).start()
    first=0
    for i in range(count):
        n=rows[i].shape[0]
        x_ref[first:first+n,:]=rows[i][...]
        c_ref[first:first+n,:]=cots[i][...]
        first+=n
    acc_ref[...]=jnp.zeros_like(acc_ref)
    dga_ref[...]=jnp.zeros_like(dga_ref)
    def out_copies(step,slot):
        cols=pl.ds(pl.multiple_of(step*TILE,TILE),TILE)
        return (pltpu.make_async_copy(act_buf.at[slot],act_ref.at[:,cols],o_sem.at[0,slot]),
                pltpu.make_async_copy(db_buf.at[slot],db_ref.at[:,cols],o_sem.at[1,slot]))
    for k in range(parts):
        pltpu.make_async_copy(wi_refs[k],wi_buf.at[k],w_sem.at[0,k]).wait()
        pltpu.make_async_copy(wo_refs[k],wo_buf.at[k],w_sem.at[1,k]).wait()
        def body(c,_):
            step=k*per+c
            slot=lax.rem(step,2)
            @pl.when(step>=2)
            def _():
                for cp in out_copies(step-2,slot): cp.wait()
            cols=pl.ds(pl.multiple_of(c*TILE,TILE),TILE)
            wi=wi_buf[k,:,cols]
            wo=wo_buf[k,cols,:]
            before=dot_nn(x_ref[...],wi)
            up=dot_nt(c_ref[...],wo)
            active,slope=gelu_parts(before)
            prod=active*up
            dga_ref[...]+=prod[:,:128]+prod[:,128:]
            act_buf[slot]=active.astype(jnp.bfloat16)
            db=(up*slope).astype(jnp.bfloat16)
            db_buf[slot]=db
            acc_ref[...]+=dot_nt(db,wi)
            for cp in out_copies(step,slot): cp.start()
            return 0
        lax.fori_loop(0,per,body,0)
    first=0
    for i in range(count):
        n=rows[i].shape[0]
        outs[i][...]=acc_ref[first:first+n,:].astype(jnp.bfloat16)
        first+=n
    ones=jnp.ones((8,128),jnp.bfloat16)
    sums=dga_ref[...]
    hi=sums.astype(jnp.bfloat16)
    rest=sums-hi.astype(jnp.float32)
    mid=rest.astype(jnp.bfloat16)
    low=(rest-mid.astype(jnp.float32)).astype(jnp.bfloat16)
    dg_ref[...]=dot_nt(ones,hi)+dot_nt(ones,mid)+dot_nt(ones,low)
    for step in (total-2,total-1):
        for cp in out_copies(step,step%2): cp.wait()

def expert_half(rows,cots,w_ins,w_outs):
    count=len(rows); parts=len(w_ins)
    width,block=w_ins[0].shape
    R=sum(r.shape[0] for r in rows)
    vm=pl.BlockSpec(memory_space=pltpu.VMEM); hb=pl.BlockSpec(memory_space=pl.ANY)
    outs=pl.pallas_call(functools.partial(expert_kernel,count,parts),
        in_specs=[vm]*(2*count)+[hb]*(2*parts),
        out_specs=[vm]*count+[hb,hb,vm],
        out_shape=[jax.ShapeDtypeStruct(r.shape,jnp.bfloat16) for r in rows]+[jax.ShapeDtypeStruct((R,parts*block),jnp.bfloat16)]*2+[jax.ShapeDtypeStruct((8,R),jnp.float32)],
        scratch_shapes=[pltpu.VMEM((R,width),jnp.bfloat16)]*2+[pltpu.VMEM((parts,width,block),jnp.bfloat16),pltpu.VMEM((parts,block,width),jnp.bfloat16),
            pltpu.VMEM((R,width),jnp.float32),pltpu.VMEM((R,128),jnp.float32),pltpu.VMEM((2,R,TILE),jnp.bfloat16),pltpu.VMEM((2,R,TILE),jnp.bfloat16),
            pltpu.SemaphoreType.DMA((2,parts)),pltpu.SemaphoreType.DMA((2,2))],
        compiler_params=pltpu.CompilerParams(vmem_limit_bytes=48*2**20),
        cost_estimate=pl.CostEstimate(flops=6*R*width*parts*block,bytes_accessed=20*2**20,transcendentals=R*parts*block))(*rows,*cots,*w_ins,*w_outs)
    return outs[:count],outs[count],outs[count+1],outs[count+2][0]

MESH = pl.DeviceIdType.MESH


def shard_peer(bit):
    return (lax.axis_index("expert"), lax.axis_index("shard") ^ bit)


def expert_peer(bit):
    return (lax.axis_index("expert") ^ bit, lax.axis_index("shard"))


def greet(peers):
    barrier = pltpu.get_barrier_semaphore()
    for peer in peers:
        pl.semaphore_signal(barrier, inc=1, device_id=peer, device_id_type=MESH)
    pl.semaphore_wait(barrier, len(peers))


def send(src, dst, send_sem, recv_sem, peer):
    copy = pltpu.make_async_remote_copy(
        src_ref=src, dst_ref=dst, send_sem=send_sem, recv_sem=recv_sem, device_id=peer, device_id_type=MESH
    )
    copy.start()
    return copy


def project_kernel(x_ref, small_in, q_in, k_in, v_in, o_in, q_ref, k_ref, v_ref, normed_ref, small_ref, all_ref,
                   small_buf, w_buf, unit_ref, sem_send, sem_recv, sem_own, sem_out):
    shard = lax.axis_index("shard")
    own = q_in.shape[0]

    def rows(bit):
        return pl.ds(pl.multiple_of((shard ^ bit) * own, 64), own)

    ins = [small_in, q_in, k_in, v_in, o_in]
    bufs = [small_buf] + [w_buf.at[i] for i in range(4)]
    count = len(ins)
    locals_ = []
    for i in range(count):
        copy = pltpu.make_async_copy(ins[i], bufs[i].at[rows(0)], sem_own.at[i])
        copy.start()
        locals_.append(copy)
    greet([shard_peer(1), shard_peer(2)])
    far, near, passed = [], [], []
    for i in range(count):
        far.append(send(ins[i], bufs[i].at[rows(0)], sem_send.at[0, i], sem_recv.at[0, i], shard_peer(2)))
    for i in range(count):
        near.append(send(ins[i], bufs[i].at[rows(0)], sem_send.at[1, i], sem_recv.at[1, i], shard_peer(1)))
    length, width = x_ref.shape
    tile = 256

    def unit(t, _):
        r = pl.ds(pl.multiple_of(t * tile, tile), tile)
        x = x_ref[r, :].astype(jnp.float32)
        unit_ref[r, :] = x * lax.rsqrt(jnp.mean(x * x, axis=-1, keepdims=True) + 1e-6)
        return 0

    lax.fori_loop(0, length // tile, unit, 0)

    def finish(i):
        far[i].wait_recv()
        passed.append(
            send(bufs[i].at[rows(2)], bufs[i].at[rows(2)], sem_send.at[2, i], sem_recv.at[2, i], shard_peer(1))
        )
        locals_[i].wait()
        near[i].wait_recv()
        passed[i].wait_recv()

    finish(0)
    small = small_buf[...]
    small_ref[...] = small
    gain = jnp.concatenate(
        [small[c * 128 : (c + 1) * 128, :].astype(jnp.float32).T[0:1] for c in range(width // 128)], axis=1
    )

    def norm(t, _):
        r = pl.ds(pl.multiple_of(t * tile, tile), tile)
        normed_ref[r, :] = (unit_ref[r, :] * gain).astype(jnp.bfloat16)
        return 0

    lax.fori_loop(0, length // tile, norm, 0)
    outs = []
    for i, out in ((1, q_ref), (2, k_ref), (3, v_ref)):
        finish(i)
        copy = pltpu.make_async_copy(w_buf.at[i - 1], all_ref.at[i - 1], sem_out.at[i - 1])
        copy.start()
        outs.append(copy)

        def project(t, _):
            r = pl.ds(pl.multiple_of(t * tile, tile), tile)
            y = dot_nn(normed_ref[r, :], w_buf[i - 1]).astype(jnp.bfloat16)
            if i == 1:
                y = (y.astype(jnp.float32) * HEAD_DIM**-0.5).astype(jnp.bfloat16)
            out[r, :] = y
            return 0

        lax.fori_loop(0, length // tile, project, 0)
    finish(4)
    copy = pltpu.make_async_copy(w_buf.at[3], all_ref.at[3], sem_out.at[3])
    copy.start()
    outs.append(copy)
    for c in outs:
        c.wait()
    for c in far + near + passed:
        c.wait_send()


def project(x, small, weights):
    length, width = x.shape
    own = small.shape[0]
    vm = pl.BlockSpec(memory_space=pltpu.VMEM)
    hb = pl.BlockSpec(memory_space=pl.ANY)
    bf = jnp.bfloat16
    return pl.pallas_call(
        project_kernel,
        in_specs=[vm] + [hb] * 5,
        out_specs=[vm] * 5 + [hb],
        out_shape=[jax.ShapeDtypeStruct((length, width), bf)] * 4
        + [jax.ShapeDtypeStruct((width, 128), bf), jax.ShapeDtypeStruct((4, width, width), bf)],
        scratch_shapes=[
            pltpu.VMEM((width, 128), bf),
            pltpu.VMEM((4, width, width), bf),
            pltpu.VMEM((length, width), jnp.float32),
            pltpu.SemaphoreType.DMA((3, 5)),
            pltpu.SemaphoreType.DMA((3, 5)),
            pltpu.SemaphoreType.DMA((5,)),
            pltpu.SemaphoreType.DMA((4,)),
        ],
        compiler_params=pltpu.CompilerParams(collective_id=0, has_side_effects=True, vmem_limit_bytes=60 * 2**20),
        cost_estimate=pl.CostEstimate(flops=4 * 10**9, bytes_accessed=20 * 2**20, transcendentals=0),
    )(x, small, *weights)


def gate_columns(line, count, width):
    column = jnp.broadcast_to(line, (128, 256)).T[:count]
    return jnp.concatenate([column] * (width // 128), axis=1)


def experts_kernel(
    size, cap, tile,
    rows_in, gate_in, cot_in, own_in, far_in,
    back_out, dgate_out, mine_out, other_out, result_out,
    rows, gates, cots, weights, active, d_before, total, d_gate, back, d_gates, back_in, d_gates_in,
    gated, gated_t, g_send, g_recv, stage, result,
    w_sem, wr_sem, row_send, row_recv, gate_send, gate_recv, back_send, back_recv, dg_send, dg_recv,
    g_sem_send, g_sem_recv, cot_sem, out_sem, res_sem, back_sem, dgb_sem,
):
    width = weights.shape[2]
    block = weights.shape[3]
    per = block // tile
    group = 2
    count = group * cap

    me = lax.axis_index("expert")

    def part(k):
        return pl.ds(k * cap, cap)

    local = [
        pltpu.make_async_copy(own_in, weights.at[0], w_sem.at[0]),
        pltpu.make_async_copy(far_in, weights.at[2], w_sem.at[1]),
        pltpu.make_async_copy(rows_in.at[me], rows.at[part(0)], w_sem.at[2]),
        pltpu.make_async_copy(gate_in.at[me], gates.at[0], w_sem.at[3]),
    ]
    local += [pltpu.make_async_copy(cot_in.at[me ^ k], cots.at[part(k)], cot_sem.at[k]) for k in range(size)]
    for c in local:
        c.start()
    greet([expert_peer(k) for k in range(1, size)] + [shard_peer(1)])
    sent = []
    arrive = {}
    order = sorted(range(1, size), key=lambda k: (-(k >> 1) if k > 1 else 0))
    for k in order:
        arrive[k] = [
            send(gate_in.at[me ^ k], gates.at[k], gate_send.at[k], gate_recv.at[k], expert_peer(k)),
            send(rows_in.at[me ^ k], rows.at[part(k)], row_send.at[k], row_recv.at[k], expert_peer(k)),
        ]
        sent += arrive[k]
    moved = [
        send(own_in, weights.at[1], wr_sem.at[0, 0], wr_sem.at[1, 0], shard_peer(1)),
        send(far_in, weights.at[3], wr_sem.at[0, 1], wr_sem.at[1, 1], shard_peer(1)),
    ]
    sent += moved
    d_gates[...] = jnp.zeros_like(d_gates)
    for c in local:
        c.wait()
    for c in moved:
        c.wait_recv()
    ones = jnp.ones((8, 128), jnp.bfloat16)
    returned = {}
    groups = size // group
    for i in range(groups):
        g = i ^ (i >> 1)
        mine = slice(g * count, (g + 1) * count)
        for k in range(group * g, group * (g + 1)):
            if k:
                for c in arrive[k]:
                    c.wait_recv()
        total[...] = jnp.zeros_like(total)
        d_gate[...] = jnp.zeros_like(d_gate)

        def step(t, _):
            kk = t // per
            cols = pl.ds(pl.multiple_of(lax.rem(t, per) * tile, tile), tile)
            where = pl.ds(pl.multiple_of(t * tile, tile), tile)
            wi = weights[kk, 0, :, cols]
            wo = weights[kk, 1, cols, :]
            before = dot_nn(rows[mine, :], wi)
            up = dot_nt(cots[mine, :], wo)
            value, slope = gelu_parts(before)
            prod = value * up
            d_gate[...] += sum(prod[:, c * 128 : (c + 1) * 128] for c in range(tile // 128))
            active[mine, where] = value.astype(jnp.bfloat16)
            db = (up * slope).astype(jnp.bfloat16)
            d_before[mine, where] = db
            total[...] += dot_nt(db, wi)
            return 0

        lax.fori_loop(0, weights.shape[0] * per, step, 0)
        back[mine, :] = total[...].astype(jnp.bfloat16)
        for k in range(group * g, group * (g + 1)):
            sums = d_gate[(k - group * g) * cap : (k - group * g + 1) * cap, :]
            hi = sums.astype(jnp.bfloat16)
            rest = sums - hi.astype(jnp.float32)
            mid = rest.astype(jnp.bfloat16)
            low = (rest - mid.astype(jnp.float32)).astype(jnp.bfloat16)
            d_gates[k, :, 0:cap] = dot_nt(ones, hi) + dot_nt(ones, mid) + dot_nt(ones, low)
            if k:
                returned[k] = [
                    send(d_gates.at[k], d_gates_in.at[k], dg_send.at[k], dg_recv.at[k], expert_peer(k)),
                    send(back.at[part(k)], back_in.at[part(k)], back_send.at[k], back_recv.at[k], expert_peer(k)),
                ]
                sent += returned[k]
    for k in range(size):
        column = gate_columns(gates[k, 0:1, :], cap, width)
        gated[k * cap : (k + 1) * cap, :] = (cots[k * cap : (k + 1) * cap, :].astype(jnp.float32) * column).astype(jnp.bfloat16)
        scaled = rows[k * cap : (k + 1) * cap, :].astype(jnp.float32) * column
        result[k * cap : (k + 1) * cap, :] = scaled.astype(jnp.bfloat16)
    every = size * cap
    for c in range(width // 128):
        for r in range(every // 128):
            gated_t[c * 128 : (c + 1) * 128, r * 128 : (r + 1) * 128] = (
                result[r * 128 : (r + 1) * 128, c * 128 : (c + 1) * 128].astype(jnp.float32).T.astype(jnp.bfloat16)
            )
    strip = 256
    exchanged = []
    finals = []
    for n, kk in enumerate((1, 3, 2, 0)):
        def outer(t, _):
            where = pl.ds(pl.multiple_of(kk * block + t * strip, strip), strip)
            out = pl.ds(pl.multiple_of(t * strip, strip), strip)
            y = dot_tn(active[:, where], gated[...])
            if n < 2:
                g_send[n, 1, out, :] = y.astype(jnp.bfloat16)
            else:
                stage[1, out, :] = y
            return 0

        def inner(t, _):
            out = pl.ds(pl.multiple_of(t * strip, strip), strip)
            y = dot_nn(gated_t[out, :], d_before[:, kk * block : (kk + 1) * block])
            if n < 2:
                g_send[n, 0, out, :] = y.astype(jnp.bfloat16)
            else:
                stage[0, out, :] = y
            return 0

        lax.fori_loop(0, block // strip, outer, 0)
        lax.fori_loop(0, width // strip, inner, 0)
        if n < 2:
            c = send(g_send.at[n], g_recv.at[n], g_sem_send.at[n], g_sem_recv.at[n], shard_peer(1))
            exchanged.append(c)
            sent.append(c)
        else:
            m = 1 if kk == 2 else 0
            exchanged[m].wait_recv()
            if kk == 2:
                exchanged[1].wait_send()
                def add(t, _):
                    out = pl.ds(pl.multiple_of(t * strip, strip), strip)
                    for h in range(2):
                        g_send[1, h, out, :] = (stage[h, out, :] + g_recv[m, h, out, :].astype(jnp.float32)).astype(jnp.bfloat16)
                    return 0
                lax.fori_loop(0, block // strip, add, 0)
                c = pltpu.make_async_copy(g_send.at[1], other_out, out_sem.at[0])
            else:
                def add(t, _):
                    out = pl.ds(pl.multiple_of(t * strip, strip), strip)
                    for h in range(2):
                        stage[h, out, :] = stage[h, out, :] + g_recv[m, h, out, :].astype(jnp.float32)
                    return 0
                lax.fori_loop(0, block // strip, add, 0)
                c = pltpu.make_async_copy(stage, mine_out, out_sem.at[1])
            c.start()
            finals.append(c)

    def produce(r, _):
        span = pl.ds(pl.multiple_of(r * cap, 16), cap)
        y = sum(dot_nn(active[span, kk * block : (kk + 1) * block], weights[kk, 1]) for kk in range(4))
        result[span, :] = y.astype(jnp.bfloat16)
        return 0

    lax.fori_loop(0, size, produce, 0)
    for k in range(size):
        c = pltpu.make_async_copy(result.at[part(k)], result_out.at[me ^ k], res_sem.at[k])
        c.start()
        finals.append(c)
    back_in[part(0), :] = back[part(0), :]
    d_gates_in[0] = d_gates[0]
    for k in range(size):
        if k:
            for c in returned[k]:
                c.wait_recv()
        for c in (
            pltpu.make_async_copy(back_in.at[part(k)], back_out.at[me ^ k], back_sem.at[k]),
            pltpu.make_async_copy(d_gates_in.at[k], dgate_out.at[me ^ k], dgb_sem.at[k]),
        ):
            c.start()
            finals.append(c)
    for c in finals:
        c.wait()
    for c in sent:
        if c is not exchanged[1]:
            c.wait_send()


def run_experts(rows, gates, cots, own, far):
    size, cap, width = rows.shape
    block = own.shape[2]
    bf = jnp.bfloat16
    f32 = jnp.float32
    every = size * cap
    hb = pl.BlockSpec(memory_space=pl.ANY)
    vm = pltpu.VMEM
    dma = pltpu.SemaphoreType.DMA
    return pl.pallas_call(
        functools.partial(experts_kernel, size, cap, 256),
        in_specs=[hb] * 5,
        out_specs=[hb] * 5,
        out_shape=[
            jax.ShapeDtypeStruct((size, cap, width), bf),
            jax.ShapeDtypeStruct((size, 8, 256), f32),
            jax.ShapeDtypeStruct((2, width, block), f32),
            jax.ShapeDtypeStruct((2, width, block), bf),
            jax.ShapeDtypeStruct((size, cap, width), bf),
        ],
        scratch_shapes=[
            vm((every, width), bf),
            vm((size, 8, 256), f32),
            vm((every, width), bf),
            vm((4, 2, width, block), bf),
            vm((every, 4 * block), bf),
            vm((every, 4 * block), bf),
            vm((2 * cap, width), f32),
            vm((2 * cap, 128), f32),
            vm((every, width), bf),
            vm((size, 8, 256), f32),
            vm((every, width), bf),
            vm((size, 8, 256), f32),
            vm((every, width), bf),
            vm((width, every), bf),
            vm((2, 2, width, block), bf),
            vm((2, 2, width, block), bf),
            vm((2, width, block), f32),
            vm((every, width), bf),
            dma((4,)),
            dma((2, 2)),
        ]
        + [dma((size,))] * 8
        + [dma((2,)), dma((2,)), dma((size,)), dma((2,)), dma((size,)), dma((size,)), dma((size,))],
        compiler_params=pltpu.CompilerParams(collective_id=1, has_side_effects=True, vmem_limit_bytes=60 * 2**20),
        cost_estimate=pl.CostEstimate(flops=36 * 10**9, bytes_accessed=30 * 2**20, transcendentals=4 * 10**6),
    )(rows, gates, cots, own, far)


class Reduction:
    def __init__(self, index, partial, near, far_send, far_recv, full, x_send, x_recv, half, z_send, z_recv, piece, result, send_sems, recv_sems):
        self.partial, self.near, self.far_send, self.far_recv = partial, near, far_send, far_recv
        self.full, self.x_send, self.x_recv, self.half = full, x_send, x_recv, half
        self.z_send, self.z_recv, self.piece, self.result = z_send, z_recv, piece, result
        self.index, self.send_sems, self.recv_sems = index, send_sems, recv_sems
        self.own = full.shape[0]
        self.width = full.shape[1]
        self.type = partial.dtype
        self.copies = {}

    def block(self, bit):
        return pl.ds(pl.multiple_of((lax.axis_index("shard") ^ bit) * self.own, self.own & -self.own), self.own)

    def half_rows(self, bit):
        rows = self.own // 2
        return pl.ds(pl.multiple_of(((lax.axis_index("expert") & 1) ^ bit) * rows, rows & -rows), rows)

    def quarter(self, step):
        j = (lax.axis_index("expert") >> 1) ^ step
        rows = self.own // 2
        if self.type == jnp.float32:
            return (pl.ds(pl.multiple_of(j * (rows // 4), 8), rows // 4), slice(None))
        return (
            pl.ds(pl.multiple_of((j >> 1) * (rows // 2), 16), rows // 2),
            pl.ds(pl.multiple_of((j & 1) * (self.width // 2), 128), self.width // 2),
        )

    def go(self, slot, src, dst, peer):
        self.copies[slot] = send(src, dst, self.send_sems.at[self.index, slot], self.recv_sems.at[self.index, slot], peer)

    def core(self):
        self.go(0, self.partial.at[self.block(3)], self.near.at[1], shard_peer(1))
        self.go(1, self.partial.at[self.block(1)], self.near.at[0], shard_peer(1))

    def y(self):
        self.copies[0].wait_recv()
        other = self.partial[self.block(2), :].astype(jnp.float32) + self.near[1].astype(jnp.float32)
        self.far_send[...] = other.astype(self.type)
        self.go(2, self.far_send, self.far_recv, shard_peer(2))
        self.copies[1].wait_recv()
        self.full[...] = self.partial[self.block(0), :].astype(jnp.float32) + self.near[0].astype(jnp.float32)

    def x(self):
        self.copies[2].wait_recv()
        self.full[...] += self.far_recv[...].astype(jnp.float32)
        self.x_send[...] = self.full[self.half_rows(1), :].astype(self.type)
        self.go(3, self.x_send, self.x_recv, expert_peer(1))

    def z(self):
        self.copies[3].wait_recv()
        self.half[...] = self.own_half() + self.x_recv[...].astype(jnp.float32)
        self.z_send[...] = self.half[...].astype(self.type)
        for step in (2, 3, 1):
            self.go(3 + step, self.z_send.at[self.quarter(step)], self.z_recv.at[step - 1], expert_peer(2 * step))

    def own_half(self):
        return self.full[self.half_rows(0), :]

    def spread(self):
        for step in (1, 2, 3):
            self.copies[3 + step].wait_recv()
        rows, cols = self.quarter(0)
        total = self.half[rows, cols]
        for step in (1, 2, 3):
            total = total + self.z_recv[step - 1].astype(jnp.float32)
        self.piece[...] = total.astype(self.type)
        target = self.place()
        for step in (2, 3, 1):
            self.go(6 + step, self.piece, self.result.at[target], expert_peer(2 * step))
        self.result[target] = self.piece[...]

    def place(self):
        j = lax.axis_index("expert") >> 1
        first = (lax.axis_index("expert") & 1) * (self.own // 2)
        rows = self.own // 2
        if self.type == jnp.float32:
            return (pl.ds(pl.multiple_of(first + j * (rows // 4), 8), rows // 4), slice(None))
        return (
            pl.ds(pl.multiple_of(first + (j >> 1) * (rows // 2), 16), rows // 2),
            pl.ds(pl.multiple_of((j & 1) * (self.width // 2), 128), self.width // 2),
        )

    def cross(self):
        for step in (1, 2, 3):
            self.copies[6 + step].wait_recv()
        self.go(10, self.result.at[self.half_rows(0)], self.result.at[self.half_rows(0)], expert_peer(1))

    def finish(self, out):
        self.copies[10].wait_recv()
        out[...] = self.result[...].astype(jnp.float32)

    def drain(self):
        for c in self.copies.values():
            c.wait_send()


class Crossed(Reduction):
    other = None

    def y(self):
        rows = self.own // 2
        self.copies[0].wait_recv()
        self.other[...] = self.partial[self.block(2), :].astype(jnp.float32) + self.near[1].astype(jnp.float32)
        self.far_send[rows:, :] = self.other[self.half_rows(1), :].astype(self.type)
        self.copies[1].wait_recv()
        self.full[...] = self.partial[self.block(0), :].astype(jnp.float32) + self.near[0].astype(jnp.float32)
        self.far_send[:rows, :] = self.full[self.half_rows(1), :].astype(self.type)
        self.go(2, self.far_send, self.far_recv, expert_peer(1))

    def x(self):
        rows = self.own // 2
        self.copies[2].wait_recv()
        other = self.other[self.half_rows(0), :] + self.far_recv[rows:, :].astype(jnp.float32)
        self.x_send[...] = other.astype(self.type)
        self.go(3, self.x_send, self.x_recv, shard_peer(2))

    def own_half(self):
        return self.full[self.half_rows(0), :] + self.far_recv[: self.own // 2, :].astype(jnp.float32)


def tail_kernel(
    normed_in, dq_in, dk_in, dv_in, context_in, d_branch_in, weights_in, tokens_in, d_resid_in, small, extra,
    o_out, q_out, k_out, v_out, s_out, tokens_out,
    normed, dq, dk, dv, context, d_branch, weights, tokens, d_resid,
    normed_t, p_ref, near, far_send, far_recv, full, x_send, x_recv, half, z_send, z_recv, piece, result, other,
    ps, s_near, s_far_send, s_far_recv, s_full, s_x_send, s_x_recv, s_half, s_z_send, s_z_recv, s_piece, s_result,
    send_sems, recv_sems, load_sems,
):
    length, width = normed.shape
    tile = 256
    loads = [
        pltpu.make_async_copy(src, dst, load_sems.at[i])
        for i, (src, dst) in enumerate(
            (
                (context_in, context),
                (d_branch_in, d_branch),
                (normed_in, normed),
                (dq_in, dq),
                (dk_in, dk),
                (dv_in, dv),
                (weights_in.at[0:3], weights),
                (tokens_in, tokens),
                (d_resid_in, d_resid),
            )
        )
    ]
    for c in loads:
        c.start()
    greet([shard_peer(1), shard_peer(2)] + [expert_peer(k) for k in (1, 2, 4, 6)])
    work = []
    for m in range(4):
        w = (Crossed if m % 2 else Reduction)(
            m, p_ref.at[m], near.at[m], far_send.at[m], far_recv.at[m], full.at[m], x_send.at[m], x_recv.at[m],
            half.at[m], z_send.at[m], z_recv.at[m], piece.at[m], result.at[m], send_sems, recv_sems,
        )
        if m % 2:
            w.other = other.at[m // 2]
        work.append(w)
    o, q, k, v = work
    s = Reduction(
        4, ps, s_near, s_far_send, s_far_recv, s_full, s_x_send, s_x_recv, s_half, s_z_send, s_z_recv, s_piece,
        s_result, send_sems, recv_sems,
    )

    def strips(m, make):
        def body(t, _):
            r = pl.ds(pl.multiple_of(t * tile, tile), tile)
            p_ref[m, r, :] = make(r).astype(jnp.bfloat16)
            return 0

        lax.fori_loop(0, width // tile, body, 0)

    loads[0].wait()
    loads[1].wait()
    strips(0, lambda r: dot_tn(context[:, r], d_branch[...]))
    o.core()
    loads[2].wait()
    for c in range(width // 128):
        for t in range(length // 128):
            normed_t[c * 128 : (c + 1) * 128, t * 128 : (t + 1) * 128] = (
                normed[t * 128 : (t + 1) * 128, c * 128 : (c + 1) * 128].astype(jnp.float32).T.astype(jnp.bfloat16)
            )
    o.y()
    loads[3].wait()
    strips(1, lambda r: dot_nn(normed_t[r, :], dq[...]))
    q.core()
    loads[4].wait()
    strips(2, lambda r: dot_nn(normed_t[r, :], dk[...]))
    k.core()
    q.y()
    loads[5].wait()
    strips(3, lambda r: dot_nn(normed_t[r, :], dv[...]))
    v.core()
    k.y()
    head = small[...].astype(jnp.float32)
    gain = jnp.concatenate([head[c * 128 : (c + 1) * 128, :].T[0:1] for c in range(width // 128)], axis=1)
    for c in loads[6:]:
        c.wait()

    def back(t, total):
        r = pl.ds(pl.multiple_of(t * tile, tile), tile)
        grad = dot_nt(dq[r, :], weights[0]) + dot_nt(dk[r, :], weights[1]) + dot_nt(dv[r, :], weights[2])
        x = tokens[r, :].astype(jnp.float32)
        scale = lax.rsqrt(jnp.mean(x * x, axis=-1, keepdims=True) + 1e-6)
        unit = x * scale
        pulled = grad * gain
        shift = jnp.mean(unit * pulled, axis=-1, keepdims=True)
        tokens_out[r, :] = (d_resid[r, :] + scale * (pulled - unit * shift)).astype(jnp.bfloat16)
        return total + jnp.sum(grad * unit, axis=0, keepdims=True)

    def some(first, last, total):
        return lax.fori_loop(first, last, back, total)

    total = some(0, 1, jnp.zeros((1, width), jnp.float32))
    v.y()
    o.x()
    total = some(1, 2, total)
    q.x()
    o.z()
    total = some(2, 3, total)
    q.z()
    o.spread()
    total = some(3, length // tile, total)
    lane = lax.broadcasted_iota(jnp.int32, (128, 128), 1)
    for c in range(width // 128):
        column = jnp.broadcast_to(total[:, c * 128 : (c + 1) * 128], (128, 128)).T
        ps[c * 128 : (c + 1) * 128, :] = jnp.where(lane == 0, column, extra[c * 128 : (c + 1) * 128, :])
    s.core()
    k.x()
    q.spread()
    o.cross()
    s.y()
    v.x()
    k.z()
    q.cross()
    s.x()
    v.z()
    k.spread()
    s.z()
    v.spread()
    k.cross()
    s.spread()
    o.finish(o_out)
    v.cross()
    q.finish(q_out)
    s.cross()
    k.finish(k_out)
    v.finish(v_out)
    s.finish(s_out)
    for w in work + [s]:
        w.drain()


def run_tail(normed, dq, dk, dv, context, d_branch, weights, tokens, d_resid, small, extra):
    length, width = normed.shape
    own = width // 4
    bf = jnp.bfloat16
    f32 = jnp.float32
    vm = pltpu.VMEM
    mem = pl.BlockSpec(memory_space=pltpu.VMEM)
    h = own // 2
    return pl.pallas_call(
        tail_kernel,
        in_specs=[pl.BlockSpec(memory_space=pl.ANY)] * 9 + [mem] * 2,
        out_specs=[mem] * 6,
        out_shape=[jax.ShapeDtypeStruct((own, width), f32)] * 4
        + [jax.ShapeDtypeStruct((own, 128), f32), jax.ShapeDtypeStruct((length, width), bf)],
        scratch_shapes=[vm((length, width), bf)] * 6
        + [
            vm((3, width, width), bf),
            vm((length, width), bf),
            vm((length, width), f32),
            vm((width, length), bf),
            vm((4, width, width), bf),
            vm((4, 2, own, width), bf),
            vm((4, own, width), bf),
            vm((4, own, width), bf),
            vm((4, own, width), f32),
            vm((4, h, width), bf),
            vm((4, h, width), bf),
            vm((4, h, width), f32),
            vm((4, h, width), bf),
            vm((4, 3, h // 2, width // 2), bf),
            vm((4, h // 2, width // 2), bf),
            vm((4, own, width), bf),
            vm((2, own, width), f32),
            vm((width, 128), f32),
            vm((2, own, 128), f32),
            vm((own, 128), f32),
            vm((own, 128), f32),
            vm((own, 128), f32),
            vm((h, 128), f32),
            vm((h, 128), f32),
            vm((h, 128), f32),
            vm((h, 128), f32),
            vm((3, h // 4, 128), f32),
            vm((h // 4, 128), f32),
            vm((own, 128), f32),
            pltpu.SemaphoreType.DMA((5, 11)),
            pltpu.SemaphoreType.DMA((5, 11)),
            pltpu.SemaphoreType.DMA((9,)),
        ],
        compiler_params=pltpu.CompilerParams(collective_id=2, has_side_effects=True, vmem_limit_bytes=60 * 2**20),
        cost_estimate=pl.CostEstimate(flops=9 * 10**9, bytes_accessed=20 * 2**20, transcendentals=0),
    )(normed, dq, dk, dv, context, d_branch, weights, tokens, d_resid, small, extra)

EPS = 1e-06
BF = jnp.bfloat16
F32 = jnp.float32


def dot_tn(a, b):
    return lax.dot_general(a, b, (((0,), (0,)), ((), ())), preferred_element_type=F32)


def swap(value, axis, size, bit):
    return lax.ppermute(value, axis, [(i, i ^ bit) for i in range(size)])


def direct(size):
    return size <= 8 and size & (size - 1) == 0


def exchange(blocks):
    return lax.all_to_all(blocks, "expert", split_axis=0, concat_axis=0, tiled=True)


def gather_shards(value, size):
    if size == 4:
        far = swap(value, "shard", size, 2)
        near = swap(value, "shard", size, 1)
        return [value, near, far, swap(far, "shard", size, 1)]
    return [value] + [swap(value, "shard", size, k) for k in range(1, size)]


def reduce_shards(blocks, size):
    if size == 4:
        near1 = swap(blocks[3].astype(BF), "shard", size, 1)
        near0 = swap(blocks[1].astype(BF), "shard", size, 1)
        other = swap((blocks[2].astype(F32) + near1.astype(F32)).astype(BF), "shard", size, 2)
        return blocks[0].astype(F32) + near0.astype(F32) + other.astype(F32)
    total = blocks[0].astype(F32)
    for k in range(1, size):
        total = total + swap(blocks[k].astype(BF), "shard", size, k).astype(F32)
    return total


def experts_by_collectives(row_blocks, gate_slots, cot_blocks, inner, outer, size, shards, cap):
    inners = gather_shards(inner, shards)
    outers = gather_shards(outer, shards)
    cells, width = size * cap, row_blocks.shape[2]
    rows = exchange(row_blocks).reshape(cells, width)
    cots = cot_blocks.reshape(cells, width)
    gates = exchange(gate_slots.reshape(size, cap)).reshape(cells, 1)
    half = cells // 2
    parts = [expert_half([rows[i : i + half]], [cots[i : i + half]], inners, outers) for i in (0, half)]
    back, active, d_before, d_gate = (
        jnp.concatenate([p[0][0] if i == 0 else p[i] for p in parts], axis=0) for i in range(4)
    )
    back = exchange(back.reshape(size, cap, width)).reshape(cells, width)
    d_gate = exchange(d_gate.reshape(size, cap)).reshape(cells)
    d_out = (cots.astype(F32) * gates).astype(BF)
    gated = (rows.astype(F32) * gates).astype(BF)
    block = inner.shape[1]
    spans = [slice(k * block, (k + 1) * block) for k in range(shards)]
    grad_outer = reduce_shards([dot_tn(active[:, p], d_out) for p in spans], shards)
    grad_inner = reduce_shards([dot_tn(gated, d_before[:, p]) for p in spans], shards)
    result = dot_nn(active, jnp.concatenate(outers, axis=0)).astype(BF).reshape(size, cap, width)
    result = exchange(result).reshape(cells, width)
    return back, d_gate, grad_inner, grad_outer, result


def per_device(
    tokens,
    segments,
    routes,
    order,
    gain_attn,
    w_query,
    w_key,
    w_value,
    w_output,
    rel_bias,
    gain_ffn,
    w_router,
    w_in,
    w_out,
    cotangent,
):
    seq_count, length, width = tokens.shape
    total = seq_count * length
    experts = lax.axis_size("expert")
    shards = lax.axis_size("shard")
    me = lax.axis_index("expert")
    my_shard = lax.axis_index("shard")
    capacity = (5 * total + 4 * experts - 1) // (4 * experts)
    cells = experts * capacity
    heads = rel_bias.shape[1]
    own = w_query.shape[0]
    own_buckets = rel_bias.shape[0]
    buckets = own_buckets * shards
    small = jnp.concatenate([gain_attn[:, None], gain_ffn[:, None], w_router], axis=1)
    small = jnp.pad(small, ((0, 0), (0, 128 - small.shape[1])))
    small = lax.dynamic_update_slice(small, rel_bias, (0, 128 - heads))
    route = routes.reshape(total)
    ranks = (jnp.arange(seq_count, dtype=jnp.int32)[:, None] * length + order).reshape(total)
    same_route = route[:, None] == route[None, :]
    earlier = ranks[None, :] < ranks[:, None]
    slot = jnp.sum((same_route & earlier).astype(jnp.int32), axis=1)
    kept = slot < capacity
    place = jnp.where(kept, route * capacity + slot, -1)
    spread = (jnp.arange(cells, dtype=jnp.int32)[:, None] == place[None, :]).astype(BF)
    chosen = (route[:, None] == jnp.arange(experts, dtype=jnp.int32)[None, :]).astype(F32)

    def to_blocks(values):
        return dot_nn(spread, values).astype(BF).reshape(experts, capacity, width)

    cot = cotangent.reshape(total, width)
    cot_blocks = exchange(to_blocks(cot))
    query, key, value, normed_low, small_all, weights_all = project(
        tokens.reshape(total, width), small, (w_query, w_key, w_value, w_output)
    )
    query_all, key_all, value_all, output_all = (weights_all[i] for i in range(4))
    own_pair = jnp.concatenate([w_in, w_out], axis=0)
    own_pair, query = lax.optimization_barrier((own_pair, query))
    far_pair = swap(own_pair, "shard", shards, 2)
    inputs = tokens.reshape(total, width).astype(F32)
    gain_two = small_all[:, 1].astype(F32)
    router_all = small_all[:, 2 : 2 + experts]
    table = small_all[:, 128 - heads :].reshape(shards, own, heads)[:, :own_buckets]
    table = table.reshape(buckets, heads)
    bias = bias_lanes(table)
    seg = [seg_arrays(segments[i]) for i in range(seq_count)]
    rows_of = [slice(i * length, (i + 1) * length) for i in range(seq_count)]
    forward = [
        attn_fwd(s[2], s[3], query[r], key[r], value[r], s[0], s[1], bias)
        for s, r in zip(seg, rows_of)
    ]
    context = jnp.concatenate([f[0] for f in forward], axis=0) if seq_count > 1 else forward[0][0]
    resid = inputs + dot_nn(context, output_all)
    scale_two = lax.rsqrt(jnp.mean(resid * resid, axis=-1, keepdims=True) + EPS)
    unit_two = resid * scale_two
    normed_two_low = (unit_two * gain_two).astype(BF)
    logits = dot_nn(normed_two_low, router_all)
    probs = jax.nn.softmax(logits, axis=-1)
    gate = jnp.sum(probs * chosen, axis=-1)
    keep_weight = kept.astype(F32)
    keep_gate = gate * keep_weight
    gate_slots = jnp.sum(jnp.where(place[None, :] == jnp.arange(cells)[:, None], gate[None, :], 0), axis=1)
    row_blocks = to_blocks(normed_two_low)
    if direct(experts):
        gate_lines = jnp.pad(gate_slots.reshape(experts, 1, capacity), ((0, 0), (0, 7), (0, 256 - capacity)))
        back, gate_back, mine, other, expert_out = run_experts(
            row_blocks, gate_lines, cot_blocks, own_pair, far_pair
        )
        back = back.reshape(cells, width)
        gate_cells = gate_back[:, 0, :capacity].reshape(cells)
        grads = mine + swap(other, "shard", shards, 2).astype(F32)
        grad_inner, grad_outer = grads[0], grads[1]
        out_cells = exchange(expert_out).reshape(cells, width)
    else:
        back, gate_cells, grad_inner, grad_outer, out_cells = experts_by_collectives(
            row_blocks, gate_slots, cot_blocks, w_in[0], w_out[0], experts, shards, capacity
        )
    upstream = cot.astype(F32)
    d_rows = dot_tn(spread, back)
    d_gate = jnp.sum(
        jnp.where(place[:, None] == jnp.arange(cells)[None, :], gate_cells[None, :], 0), axis=1
    )
    d_logits = (probs * (d_gate[:, None] * chosen - (d_gate * gate)[:, None])).astype(BF)
    d_router = dot_tn(normed_two_low, d_logits)
    d_normed_two = dot_nt(d_logits, router_all) + keep_gate[:, None] * d_rows
    d_gain_two = jnp.sum(d_normed_two * unit_two, axis=0)
    pulled = gain_two * d_normed_two
    d_resid = upstream + scale_two * (
        pulled - unit_two * jnp.mean(unit_two * pulled, axis=-1, keepdims=True)
    )
    d_branch = d_resid.astype(BF)
    d_context = dot_nt(d_branch, output_all).astype(BF)
    backward = [
        attn_bwd(s[2], s[3], query[r], key[r], value[r], d_context[r], f[0], f[1], s[0], s[1], bias)
        for s, r, f in zip(seg, rows_of, forward)
    ]
    d_query, d_key, d_value = (
        jnp.concatenate([b[i] for b in backward], axis=0) if seq_count > 1 else backward[0][i]
        for i in range(3)
    )
    d_table = sum(table_grad(b[3], b[4], buckets) for b in backward)
    tail = jnp.concatenate([jnp.zeros_like(d_gain_two)[:, None], d_gain_two[:, None], d_router], axis=1)
    tail = jnp.pad(tail, ((0, 0), (0, 128 - tail.shape[1]))).reshape(shards, own, 128)
    tail = lax.dynamic_update_slice(
        tail, d_table.reshape(shards, own_buckets, heads), (0, 0, 128 - heads)
    ).reshape(width, 128)
    flat_tokens = tokens.reshape(total, width)
    if experts == 8 and shards == 4:
        sum_output, sum_query, sum_key, sum_value, sums, d_tokens = run_tail(
            normed_low, d_query, d_key, d_value, context, d_branch, weights_all, flat_tokens, d_resid, small_all, tail
        )
    else:
        d_normed = (
            dot_nt(d_query, query_all) + dot_nt(d_key, key_all) + dot_nt(d_value, value_all)
        )
        inputs_again = flat_tokens.astype(F32)
        scale_one = lax.rsqrt(jnp.mean(inputs_again * inputs_again, axis=-1, keepdims=True) + EPS)
        unit_one = inputs_again * scale_one
        tail = tail.at[:, 0].set(jnp.sum(d_normed * unit_one, axis=0))
        pulled_one = small_all[:, 0].astype(F32) * d_normed
        d_tokens = d_resid + scale_one * (
            pulled_one - unit_one * jnp.mean(unit_one * pulled_one, axis=-1, keepdims=True)
        )
        pairs = ((context, d_branch), (normed_low, d_query), (normed_low, d_key), (normed_low, d_value))
        parts = [dot_tn(left, right) for left, right in pairs] + [tail]
        sum_output, sum_query, sum_key, sum_value, sums = (
            lax.psum(
                reduce_shards(
                    [lax.dynamic_slice_in_dim(p, (my_shard ^ k) * own, own, 0) for k in range(shards)], shards
                ),
                "expert",
            )
            for p in parts
        )
    arrived = dot_tn(spread, out_cells)
    mixed = resid + keep_gate[:, None] * arrived
    return (
        mixed.astype(BF).reshape(tokens.shape),
        d_tokens.astype(BF).reshape(tokens.shape),
        sums[:, 0],
        sum_query,
        sum_key,
        sum_value,
        sum_output,
        sums[:own_buckets, 128 - heads :],
        sums[:, 1],
        sums[:, 2 : 2 + experts],
        grad_inner[None],
        grad_outer[None],
    )


def solution(mesh):
    in_specs = (
        P(("expert", "shard"), None, None),
        P(("expert", "shard"), None),
        P(("expert", "shard"), None, None),
        P(("expert", "shard"), None),
        P("shard"),
        P("shard", None),
        P("shard", None),
        P("shard", None),
        P("shard", None),
        P("shard", None),
        P("shard"),
        P("shard", None),
        P("expert", None, "shard"),
        P("expert", "shard", None),
        P(("expert", "shard"), None, None),
    )
    out_specs = (
        P(("expert", "shard"), None, None),
        P(("expert", "shard"), None, None),
        P("shard"),
        P("shard", None),
        P("shard", None),
        P("shard", None),
        P("shard", None),
        P("shard", None),
        P("shard"),
        P("shard", None),
        P("expert", None, "shard"),
        P("expert", "shard", None),
    )
    return jax.shard_map(
        per_device, mesh=mesh, in_specs=in_specs, out_specs=out_specs, check_vma=False
    )
```

```python
import functools

import jax
import jax.numpy as jnp
from jax import lax
from jax.experimental import pallas as pl
from jax.experimental.pallas import tpu as pltpu
from jax.sharding import PartitionSpec as P
HEAD_DIM=64
BLK=128
EDGES = (12, 16, 23, 32, 46, 64, 91)
BIG=1e9
def bucket_index(offset):
    magnitude = jnp.abs(offset)
    far = 8 + sum(((magnitude >= edge).astype(jnp.int32) for edge in EDGES))
    near = jnp.where(magnitude < 8, magnitude, far)
    return near + 16 * (offset > 0).astype(jnp.int32)

def dot_nt(a,b): return lax.dot_general(a,b,(((1,),(1,)),((),())),preferred_element_type=jnp.float32)
def dot_nn(a,b): return lax.dot_general(a,b,(((1,),(0,)),((),())),preferred_element_type=jnp.float32)

def head_mask():
    lane=lax.broadcasted_iota(jnp.int32,(BLK,2*HEAD_DIM),1)
    return (lane<HEAD_DIM).astype(jnp.float32).astype(jnp.bfloat16)

def build_bias(w_ref, bias_ref, nblk, pairs):
    rows = (2 * nblk - 1) * BLK
    near = (nblk - 2) * BLK
    for j in range(pairs):
        for h in range(2):
            c = slice((2 * j + h) * BLK, (2 * j + h + 1) * BLK)
            w = w_ref[j, h : h + 1, :]
            bias_ref[0:near, c] = jnp.broadcast_to(w[:, 511:512], (near, BLK))
            bias_ref[near + 3 * BLK : rows, c] = jnp.broadcast_to(w[:, 0:1], (near, BLK))
            r = pltpu.roll(jnp.broadcast_to(w, (BLK, 512)), 0, 1, stride=1, stride_axis=0)
            bias_ref[near : near + BLK, c] = r[:, 384:512]
            bias_ref[near + BLK : near + 2 * BLK, c] = r[:, 256:384]
            bias_ref[near + 2 * BLK : near + 3 * BLK, c] = r[:, 128:256]


def by_width(nblk, count, run):
    for n in range(1, nblk + 1):

        @pl.when(count == n)
        def _():
            run(n * BLK)


def pair_of(block, mask):
    return jnp.concatenate([block * mask, block * (1 - mask)], axis=0)


def flip(src_ref, dst_ref, nblk, pairs):
    for j in range(pairs):
        c = slice(j * BLK, (j + 1) * BLK)
        for b in range(nblk):
            s = slice(b * BLK, (b + 1) * BLK)
            dst_ref[c, s] = src_ref[s, c].astype(jnp.float32).T.astype(jnp.bfloat16)


def join_heads(wide):
    return jnp.concatenate([wide[:HEAD_DIM, :BLK], wide[HEAD_DIM:, BLK:]], axis=0)


def fwd_kernel(nblk, pairs, lo_ref, nb_ref, q_ref, k_ref, v_ref, segq_ref, segk_ref, w_ref, ctx_ref, lse_ref, vt_ref, bias_ref):
    build_bias(w_ref, bias_ref, nblk, pairs)
    flip(v_ref, vt_ref, nblk, pairs)
    mask = head_mask()
    lanes = [slice(j * BLK, (j + 1) * BLK) for j in range(pairs)]
    both = [slice(2 * j * BLK, 2 * (j + 1) * BLK) for j in range(pairs)]

    def body(qb, _):
        rows = pl.ds(pl.multiple_of(qb * BLK, BLK), BLK)
        lob = lo_ref[qb]
        sq = segq_ref[rows, :]
        sq = jnp.concatenate([sq, sq], axis=0)
        q_cat = [jnp.concatenate([pair_of(q_ref[rows, c], mask), sq], axis=1) for c in lanes]

        def run(W):
            ks = pl.ds(pl.multiple_of(lob * BLK, BLK), W)
            bs = pl.ds(pl.multiple_of((lob - qb + nblk - 1) * BLK, BLK), W)
            sk = segk_ref[ks, :]
            st = [
                dot_nt(jnp.concatenate([k_ref[ks, c], sk], axis=1), q) + bias_ref[bs, d]
                for c, d, q in zip(lanes, both, q_cat)
            ]
            m = [jnp.max(x, axis=0, keepdims=True) for x in st]
            e = [jnp.exp(x - y) for x, y in zip(st, m)]
            l = [jnp.sum(x, axis=0, keepdims=True) for x in e]
            ot = [dot_nn(vt_ref[c, ks], x.astype(jnp.bfloat16)) / y for c, x, y in zip(lanes, e, l)]
            for j, c in enumerate(lanes):
                ctx_ref[rows, c] = join_heads(ot[j]).T.astype(jnp.bfloat16)
                lse_ref[j, pl.ds(qb, 1), :] = m[j] + jnp.log(l[j])

        by_width(nblk, nb_ref[qb], run)
        return 0

    lax.fori_loop(0, nblk, body, 0)


def bwd_kernel(
    nblk, pairs, lo_ref, nb_ref, q_ref, k_ref, v_ref, do_ref, ctx_ref, lse_ref, segq_ref, segk_ref, w_ref,
    dq_ref, dk_ref, dv_ref, near_ref, far_ref, kt_ref, bias_ref, acc_ref, dka_ref, dva_ref,
):
    build_bias(w_ref, bias_ref, nblk, pairs)
    flip(k_ref, kt_ref, nblk, pairs)
    acc_ref[...] = jnp.zeros_like(acc_ref)
    dka_ref[...] = jnp.zeros_like(dka_ref)
    dva_ref[...] = jnp.zeros_like(dva_ref)
    mask = head_mask()
    lanes = [slice(j * BLK, (j + 1) * BLK) for j in range(pairs)]
    both = [slice(2 * j * BLK, 2 * (j + 1) * BLK) for j in range(pairs)]
    row = lax.broadcasted_iota(jnp.int32, (16, 2 * HEAD_DIM), 0)
    lane = lax.broadcasted_iota(jnp.int32, (16, 2 * HEAD_DIM), 1)
    pick = ((lane // HEAD_DIM) == row).astype(jnp.float32).astype(jnp.bfloat16)

    def body(qb, _):
        rows = pl.ds(pl.multiple_of(qb * BLK, BLK), BLK)
        lob = lo_ref[qb]
        sq = segq_ref[rows, :]
        sq = jnp.concatenate([sq, sq], axis=0)
        q2 = [pair_of(q_ref[rows, c], mask) for c in lanes]
        q_cat = [jnp.concatenate([q, sq], axis=1) for q in q2]
        do2 = [pair_of(do_ref[rows, c], mask) for c in lanes]
        delta = []
        for c in lanes:
            prod = do_ref[rows, c].astype(jnp.float32) * ctx_ref[rows, c].astype(jnp.float32)
            hi = prod.astype(jnp.bfloat16)
            low = (prod - hi.astype(jnp.float32)).astype(jnp.bfloat16)
            dl = dot_nt(pick, hi) + dot_nt(pick, low)
            delta.append(jnp.concatenate([dl[0:1], dl[1:2]], axis=1))
        lse = [lse_ref[j, pl.ds(qb, 1), :] for j in range(pairs)]

        def run(W):
            ks = pl.ds(pl.multiple_of(lob * BLK, BLK), W)
            bs = pl.ds(pl.multiple_of((lob - qb + nblk - 1) * BLK, BLK), W)
            sk = segk_ref[ks, :]
            st = [dot_nt(jnp.concatenate([k_ref[ks, c], sk], axis=1), q) for c, q in zip(lanes, q_cat)]
            dp = [dot_nt(v_ref[ks, c], d) for c, d in zip(lanes, do2)]
            p = [jnp.exp(x + bias_ref[bs, d] - y) for x, d, y in zip(st, both, lse)]
            ds = [x * (y - z) for x, y, z in zip(p, dp, delta)]
            dsb = [x.astype(jnp.bfloat16) for x in ds]
            for j, (c, d) in enumerate(zip(lanes, both)):
                acc_ref[bs, d] += ds[j]
                dva_ref[ks, c] += dot_nn(p[j].astype(jnp.bfloat16), do2[j])
                dka_ref[ks, c] += dot_nn(dsb[j], q2[j])
                dqt = join_heads(dot_nn(kt_ref[c, ks], dsb[j])) * (HEAD_DIM**-0.5)
                dq_ref[rows, c] = dqt.T.astype(jnp.bfloat16)

        by_width(nblk, nb_ref[qb], run)
        return 0

    lax.fori_loop(0, nblk, body, 0)
    dk_ref[...] = dka_ref[...].astype(jnp.bfloat16)
    dv_ref[...] = dva_ref[...].astype(jnp.bfloat16)
    near = (nblk - 2) * BLK
    total = (2 * nblk - 1) * BLK
    for j in range(pairs):
        for h in range(2):
            c = slice((2 * j + h) * BLK, (2 * j + h + 1) * BLK)
            wide = jnp.concatenate(
                [
                    jnp.zeros((BLK, BLK), jnp.float32),
                    acc_ref[near + 2 * BLK : near + 3 * BLK, c],
                    acc_ref[near + BLK : near + 2 * BLK, c],
                    acc_ref[near : near + BLK, c],
                ],
                axis=1,
            )
            near_ref[j, h : h + 1, :] = jnp.sum(unroll_rows(wide), axis=0, keepdims=True)
            low = jnp.sum(acc_ref[0:near, c], axis=0, keepdims=True)
            high = jnp.sum(acc_ref[near + 3 * BLK : total, c], axis=0, keepdims=True)
            far_ref[j, h : h + 1, :] = jnp.concatenate([low, high], axis=1)


def unroll_rows(wide):
    n=wide.shape[1]
    out=wide
    row=lax.broadcasted_iota(jnp.int32,wide.shape,0)
    bit=1
    while bit<wide.shape[0]:
        out=jnp.where((row & bit)!=0,pltpu.roll(out,n-bit,1),out)
        bit*=2
    return out

FWD_PAIRS = 6
BWD_PAIRS = 3


def pair_spec(nrow, pairs):
    return pl.BlockSpec((nrow, 2 * HEAD_DIM * pairs), lambda p, *_: (0, p))


def full_spec(shape):
    return pl.BlockSpec(shape, lambda p, *_: (0,) * len(shape))


def lead_spec(pairs, shape):
    return pl.BlockSpec((pairs,) + shape, lambda p, *_: (p, 0, 0))


def attn_fwd(lo, nb, q, k, v, segq, segk, w):
    L, D = q.shape
    nblk = L // BLK
    every = D // (2 * HEAD_DIM)
    pairs = FWD_PAIRS
    return pl.pallas_call(
        functools.partial(fwd_kernel, nblk, pairs),
        grid_spec=pltpu.PrefetchScalarGridSpec(
            num_scalar_prefetch=2,
            grid=(every // pairs,),
            in_specs=[pair_spec(L, pairs)] * 3 + [full_spec((L, 128))] * 2 + [lead_spec(pairs, (2, 512))],
            out_specs=[pair_spec(L, pairs), lead_spec(pairs, (nblk, 2 * BLK))],
            scratch_shapes=[
                pltpu.VMEM((2 * HEAD_DIM * pairs, L), jnp.bfloat16),
                pltpu.VMEM(((2 * nblk - 1) * BLK, 2 * BLK * pairs), jnp.float32),
            ],
        ),
        out_shape=[
            jax.ShapeDtypeStruct((L, D), jnp.bfloat16),
            jax.ShapeDtypeStruct((every, nblk, 2 * BLK), jnp.float32),
        ],
        compiler_params=pltpu.CompilerParams(vmem_limit_bytes=60 * 2**20),
        cost_estimate=pl.CostEstimate(flops=2 * 10**9, bytes_accessed=8 * 2**20, transcendentals=6 * 10**6),
    )(lo, nb, q, k, v, segq, segk, w)


def attn_bwd(lo, nb, q, k, v, do, ctx, lse, segq, segk, w):
    L, D = q.shape
    nblk = L // BLK
    every = D // (2 * HEAD_DIM)
    pairs = BWD_PAIRS
    rows = (2 * nblk - 1) * BLK
    return pl.pallas_call(
        functools.partial(bwd_kernel, nblk, pairs),
        grid_spec=pltpu.PrefetchScalarGridSpec(
            num_scalar_prefetch=2,
            grid=(every // pairs,),
            in_specs=[pair_spec(L, pairs)] * 5
            + [lead_spec(pairs, (nblk, 2 * BLK))]
            + [full_spec((L, 128))] * 2
            + [lead_spec(pairs, (2, 512))],
            out_specs=[pair_spec(L, pairs)] * 3 + [lead_spec(pairs, (2, 512)), lead_spec(pairs, (2, 256))],
            scratch_shapes=[
                pltpu.VMEM((2 * HEAD_DIM * pairs, L), jnp.bfloat16),
                pltpu.VMEM((rows, 2 * BLK * pairs), jnp.float32),
                pltpu.VMEM((rows, 2 * BLK * pairs), jnp.float32),
                pltpu.VMEM((L, 2 * HEAD_DIM * pairs), jnp.float32),
                pltpu.VMEM((L, 2 * HEAD_DIM * pairs), jnp.float32),
            ],
        ),
        out_shape=[jax.ShapeDtypeStruct((L, D), jnp.bfloat16)] * 3
        + [jax.ShapeDtypeStruct((every, 2, 512), jnp.float32), jax.ShapeDtypeStruct((every, 2, 256), jnp.float32)],
        compiler_params=pltpu.CompilerParams(vmem_limit_bytes=60 * 2**20),
        cost_estimate=pl.CostEstimate(flops=4 * 10**9, bytes_accessed=16 * 2**20, transcendentals=6 * 10**6),
    )(lo, nb, q, k, v, do, ctx, lse, segq, segk, w)


def seg_arrays(seg):
    L=seg.shape[0]; nblk=L//BLK
    ids=jnp.arange(128,dtype=jnp.int32)
    segq=(seg[:,None]==ids[None,:]).astype(jnp.bfloat16)
    segk=jnp.where((seg[:,None]!=ids[None,:])&(ids[None,:]<16),-BIG,0.0).astype(jnp.bfloat16)
    sb=seg.reshape(nblk,BLK)
    first=jnp.sum((seg[None,:]<sb[:,:1]).astype(jnp.int32),axis=1)
    last=jnp.sum((seg[None,:]<=sb[:,-1:]).astype(jnp.int32),axis=1)
    lo=first//BLK
    nb=(last+BLK-1)//BLK-lo
    return segq,segk,lo.astype(jnp.int32),nb.astype(jnp.int32)

def bias_lanes(table):
    off=-(jnp.arange(512,dtype=jnp.int32)-256)
    oh=(bucket_index(off)[None,:]==jnp.arange(table.shape[0],dtype=jnp.int32)[:,None]).astype(jnp.bfloat16)
    w=lax.dot_general(table,oh,(((0,),(0,)),((),())),preferred_element_type=jnp.float32)
    return w.reshape(-1,2,512)

def table_grad(near,far,buckets):
    off=-(jnp.arange(512,dtype=jnp.int32)-256)
    oh=(bucket_index(off)[:,None]==jnp.arange(buckets,dtype=jnp.int32)[None,:]).astype(jnp.float32)
    n=jnp.einsum("hx,xb->bh",near.reshape(-1,512),oh,precision=lax.Precision.HIGHEST)
    f=far.reshape(-1,2,128).sum(-1)
    ids=jnp.arange(buckets,dtype=jnp.int32)[:,None]
    return n+jnp.where(ids==15,f[None,:,0],0)+jnp.where(ids==31,f[None,:,1],0)

TILE=256
def gelu_parts(x):
    c=0.7978845608028654
    x2=x*x
    t=jnp.tanh(x*(c+(c*0.044715)*x2))
    half=0.5*(1.0+t)
    slope=half+0.5*x*(1.0-t*t)*(c+(3*c*0.044715)*x2)
    return x*half,slope

def expert_kernel(count, parts, *refs):
    rows=refs[:count]; cots=refs[count:2*count]
    wi_refs=refs[2*count:2*count+parts]; wo_refs=refs[2*count+parts:2*count+2*parts]
    refs=refs[2*count+2*parts:]
    outs=refs[:count]; act_ref,db_ref,dg_ref=refs[count:count+3]
    x_ref,c_ref,wi_buf,wo_buf,acc_ref,dga_ref,act_buf,db_buf,w_sem,o_sem=refs[count+3:]
    block=wi_refs[0].shape[1]
    per=block//TILE
    total=parts*per
    for k in range(parts):
        pltpu.make_async_copy(wi_refs[k],wi_buf.at[k],w_sem.at[0,k]).start()
        pltpu.make_async_copy(wo_refs[k],wo_buf.at[k],w_sem.at[1,k]).start()
    first=0
    for i in range(count):
        n=rows[i].shape[0]
        x_ref[first:first+n,:]=rows[i][...]
        c_ref[first:first+n,:]=cots[i][...]
        first+=n
    acc_ref[...]=jnp.zeros_like(acc_ref)
    dga_ref[...]=jnp.zeros_like(dga_ref)
    def out_copies(step,slot):
        cols=pl.ds(pl.multiple_of(step*TILE,TILE),TILE)
        return (pltpu.make_async_copy(act_buf.at[slot],act_ref.at[:,cols],o_sem.at[0,slot]),
                pltpu.make_async_copy(db_buf.at[slot],db_ref.at[:,cols],o_sem.at[1,slot]))
    for k in range(parts):
        pltpu.make_async_copy(wi_refs[k],wi_buf.at[k],w_sem.at[0,k]).wait()
        pltpu.make_async_copy(wo_refs[k],wo_buf.at[k],w_sem.at[1,k]).wait()
        def body(c,_):
            step=k*per+c
            slot=lax.rem(step,2)
            @pl.when(step>=2)
            def _():
                for cp in out_copies(step-2,slot): cp.wait()
            cols=pl.ds(pl.multiple_of(c*TILE,TILE),TILE)
            wi=wi_buf[k,:,cols]
            wo=wo_buf[k,cols,:]
            before=dot_nn(x_ref[...],wi)
            up=dot_nt(c_ref[...],wo)
            active,slope=gelu_parts(before)
            prod=active*up
            dga_ref[...]+=prod[:,:128]+prod[:,128:]
            act_buf[slot]=active.astype(jnp.bfloat16)
            db=(up*slope).astype(jnp.bfloat16)
            db_buf[slot]=db
            acc_ref[...]+=dot_nt(db,wi)
            for cp in out_copies(step,slot): cp.start()
            return 0
        lax.fori_loop(0,per,body,0)
    first=0
    for i in range(count):
        n=rows[i].shape[0]
        outs[i][...]=acc_ref[first:first+n,:].astype(jnp.bfloat16)
        first+=n
    ones=jnp.ones((8,128),jnp.bfloat16)
    sums=dga_ref[...]
    hi=sums.astype(jnp.bfloat16)
    rest=sums-hi.astype(jnp.float32)
    mid=rest.astype(jnp.bfloat16)
    low=(rest-mid.astype(jnp.float32)).astype(jnp.bfloat16)
    dg_ref[...]=dot_nt(ones,hi)+dot_nt(ones,mid)+dot_nt(ones,low)
    for step in (total-2,total-1):
        for cp in out_copies(step,step%2): cp.wait()

def expert_half(rows,cots,w_ins,w_outs):
    count=len(rows); parts=len(w_ins)
    width,block=w_ins[0].shape
    R=sum(r.shape[0] for r in rows)
    vm=pl.BlockSpec(memory_space=pltpu.VMEM); hb=pl.BlockSpec(memory_space=pl.ANY)
    outs=pl.pallas_call(functools.partial(expert_kernel,count,parts),
        in_specs=[vm]*(2*count)+[hb]*(2*parts),
        out_specs=[vm]*count+[hb,hb,vm],
        out_shape=[jax.ShapeDtypeStruct(r.shape,jnp.bfloat16) for r in rows]+[jax.ShapeDtypeStruct((R,parts*block),jnp.bfloat16)]*2+[jax.ShapeDtypeStruct((8,R),jnp.float32)],
        scratch_shapes=[pltpu.VMEM((R,width),jnp.bfloat16)]*2+[pltpu.VMEM((parts,width,block),jnp.bfloat16),pltpu.VMEM((parts,block,width),jnp.bfloat16),
            pltpu.VMEM((R,width),jnp.float32),pltpu.VMEM((R,128),jnp.float32),pltpu.VMEM((2,R,TILE),jnp.bfloat16),pltpu.VMEM((2,R,TILE),jnp.bfloat16),
            pltpu.SemaphoreType.DMA((2,parts)),pltpu.SemaphoreType.DMA((2,2))],
        compiler_params=pltpu.CompilerParams(vmem_limit_bytes=48*2**20),
        cost_estimate=pl.CostEstimate(flops=6*R*width*parts*block,bytes_accessed=20*2**20,transcendentals=R*parts*block))(*rows,*cots,*w_ins,*w_outs)
    return outs[:count],outs[count],outs[count+1],outs[count+2][0]

MESH = pl.DeviceIdType.MESH


def shard_peer(bit):
    return (lax.axis_index("expert"), lax.axis_index("shard") ^ bit)


def expert_peer(bit):
    return (lax.axis_index("expert") ^ bit, lax.axis_index("shard"))


def greet(peers):
    barrier = pltpu.get_barrier_semaphore()
    for peer in peers:
        pl.semaphore_signal(barrier, inc=1, device_id=peer, device_id_type=MESH)
    pl.semaphore_wait(barrier, len(peers))


def send(src, dst, send_sem, recv_sem, peer):
    copy = pltpu.make_async_remote_copy(
        src_ref=src, dst_ref=dst, send_sem=send_sem, recv_sem=recv_sem, device_id=peer, device_id_type=MESH
    )
    copy.start()
    return copy


def columns(line, block):
    return jnp.broadcast_to(line[:, block * 128 : (block + 1) * 128], (128, 128)).T


def project_kernel(
    experts, cap,
    route, order, x_in, cot_in, small_in, q_in, k_in, v_in, o_in,
    q_ref, k_ref, v_ref, normed_ref, small_ref, place_ref, cells_ref, all_ref,
    x_ref, cot_ref, small_buf, w_buf, unit_ref,
    sem_send, sem_recv, sem_own, sem_out, sem_load,
):
    shard = lax.axis_index("shard")
    side = lax.axis_index("expert") & 1
    own = q_in.shape[0]
    half = own // 2
    loads = [pltpu.make_async_copy(x_in, x_ref, sem_load.at[0]), pltpu.make_async_copy(cot_in, cot_ref, sem_load.at[1])]
    for c in loads:
        c.start()

    def rows(bit):
        return pl.ds(pl.multiple_of((shard ^ bit) * own, 64), own)

    def part(bit, other):
        return pl.ds(pl.multiple_of((shard ^ bit) * own + (side ^ other) * half, 32), half)

    mine = pl.ds(pl.multiple_of(side * half, 32), half)
    ins = [small_in, q_in, k_in, v_in, o_in]
    bufs = [small_buf] + [w_buf.at[i] for i in range(4)]
    count = len(ins)
    kept = []
    for i in range(count):
        copy = pltpu.make_async_copy(ins[i], bufs[i].at[rows(0)], sem_own.at[i])
        copy.start()
        kept.append(copy)
    greet([shard_peer(1), shard_peer(2)] + [expert_peer(1)])
    far, near, across, passed = [], [], [None] * count, [[] for _ in range(count)]
    for i in range(count):
        far.append(send(ins[i].at[mine], bufs[i].at[part(0, 0)], sem_send.at[0, i], sem_recv.at[0, i], shard_peer(2)))
    for i in range(count):
        near.append(send(ins[i], bufs[i].at[rows(0)], sem_send.at[1, i], sem_recv.at[1, i], shard_peer(1)))
    length, width = x_ref.shape
    tile = 512

    def unit(t, _):
        r = pl.ds(pl.multiple_of(t * tile, tile), tile)
        x = x_ref[r, :].astype(jnp.float32)
        unit_ref[r, :] = x * lax.rsqrt(jnp.mean(x * x, axis=-1, keepdims=True) + 1e-6)
        return 0

    def hop(i):
        far[i].wait_recv()
        here = bufs[i].at[part(2, 0)]
        across[i] = send(here, here, sem_send.at[2, i], sem_recv.at[2, i], expert_peer(1))
        passed[i].append(send(here, here, sem_send.at[3, i], sem_recv.at[3, i], shard_peer(1)))

    def finish(i):
        across[i].wait_recv()
        there = bufs[i].at[part(2, 1)]
        passed[i].append(send(there, there, sem_send.at[4, i], sem_recv.at[4, i], shard_peer(1)))
        kept[i].wait()
        near[i].wait_recv()
        for c in passed[i]:
            c.wait_recv()

    loads[0].wait()
    lax.fori_loop(0, length // tile, unit, 0)
    hop(0)
    keys = (route[...] * length + order[...]).astype(jnp.float32)
    starts = (route[...] * length).astype(jnp.float32)
    blocks = length // 128
    sides = [columns(keys, b) for b in range(blocks)]
    slots = []
    for t in range(blocks):
        s = slice(t * 128, (t + 1) * 128)
        sums = sum((c < keys[:, s]).astype(jnp.float32) - (c < starts[:, s]).astype(jnp.float32) for c in sides)
        slots.append(jnp.sum(sums, axis=0, keepdims=True))
    slot = jnp.concatenate(slots, axis=1).astype(jnp.int32)
    place = jnp.where(slot < cap, route[...] * cap + slot, -1)
    place_ref[...] = place
    loads[1].wait()
    step = 256

    def cells(t, _):
        r = pl.ds(pl.multiple_of(t * step, step), step)
        ids = lax.broadcasted_iota(jnp.int32, (step, length), 0) + t * step
        pick = (ids == place).astype(jnp.float32).astype(jnp.bfloat16)
        found = dot_nn(pick, cot_ref[...]).astype(jnp.bfloat16)
        cells_ref[r, :] = found
        return 0

    lax.fori_loop(0, cells_ref.shape[0] // step, cells, 0)
    hop(1)
    finish(0)
    small = small_buf[...]
    small_ref[...] = small
    gain = jnp.concatenate(
        [small[c * 128 : (c + 1) * 128, :].astype(jnp.float32).T[0:1] for c in range(width // 128)], axis=1
    )

    def norm(t, _):
        r = pl.ds(pl.multiple_of(t * tile, tile), tile)
        normed_ref[r, :] = (unit_ref[r, :] * gain).astype(jnp.bfloat16)
        return 0

    lax.fori_loop(0, length // tile, norm, 0)
    hop(2)
    outs = []

    def project_one(i, out):
        finish(i)
        copy = pltpu.make_async_copy(w_buf.at[i - 1], all_ref.at[i - 1], sem_out.at[i - 1])
        copy.start()
        outs.append(copy)

        def run(t, _):
            r = pl.ds(pl.multiple_of(t * tile, tile), tile)
            y = dot_nn(normed_ref[r, :], w_buf[i - 1]).astype(jnp.bfloat16)
            if i == 1:
                y = (y.astype(jnp.float32) * HEAD_DIM**-0.5).astype(jnp.bfloat16)
            out[r, :] = y
            return 0

        lax.fori_loop(0, length // tile, run, 0)

    hop(3)
    project_one(1, q_ref)
    hop(4)
    project_one(2, k_ref)
    project_one(3, v_ref)
    finish(4)
    copy = pltpu.make_async_copy(w_buf.at[3], all_ref.at[3], sem_out.at[3])
    copy.start()
    outs.append(copy)
    for c in outs:
        c.wait()
    for c in far + near + across + [c for p in passed for c in p]:
        c.wait_send()


def project(route, order, x, cot, small, weights, experts, cap):
    length, width = x.shape
    cells = experts * cap
    vm = pl.BlockSpec(memory_space=pltpu.VMEM)
    hb = pl.BlockSpec(memory_space=pl.ANY)
    bf = jnp.bfloat16
    shape = jax.ShapeDtypeStruct
    return pl.pallas_call(
        functools.partial(project_kernel, experts, cap),
        in_specs=[vm] * 2 + [hb] * 7,
        out_specs=[vm] * 7 + [hb],
        out_shape=[shape((length, width), bf)] * 4
        + [
            shape((width, 128), bf),
            shape((1, length), jnp.int32),
            shape((cells, width), bf),
            shape((4, width, width), bf),
        ],
        scratch_shapes=[
            pltpu.VMEM((length, width), bf),
            pltpu.VMEM((length, width), bf),
            pltpu.VMEM((width, 128), bf),
            pltpu.VMEM((4, width, width), bf),
            pltpu.VMEM((length, width), jnp.float32),
            pltpu.SemaphoreType.DMA((5, 5)),
            pltpu.SemaphoreType.DMA((5, 5)),
            pltpu.SemaphoreType.DMA((5,)),
            pltpu.SemaphoreType.DMA((4,)),
            pltpu.SemaphoreType.DMA((2,)),
        ],
        compiler_params=pltpu.CompilerParams(collective_id=0, has_side_effects=True, vmem_limit_bytes=60 * 2**20),
        cost_estimate=pl.CostEstimate(flops=6 * 10**9, bytes_accessed=20 * 2**20, transcendentals=0),
    )(route, order, x, cot, small, *weights)


def gate_columns(line, count, width):
    column = jnp.broadcast_to(line, (128, 256)).T[:count]
    return jnp.concatenate([column] * (width // 128), axis=1)


def experts_kernel(
    size, cap, tile,
    rows_in, gate_in, cot_in, inner_own, outer_own, inner_far,
    back_out, dgate_out, inner_out, outer_out, other_out, result_out,
    rows, gates, cots, weights, active, d_before, total, d_gate, back, d_gates, back_in, d_gates_in,
    gated_t, g_send, g_recv, far_recv, stage, result,
    w_sem, wr_sem, row_send, row_recv, gate_send, gate_recv, back_send, back_recv, dg_send, dg_recv,
    g_sem_send, g_sem_recv, cot_sem, out_sem, res_sem, back_sem, dgb_sem,
):
    width = weights.shape[2]
    block = weights.shape[3]
    per = block // tile
    group = 2
    count = group * cap
    me = lax.axis_index("expert")

    def part(k):
        return pl.ds(k * cap, cap)

    local = [
        pltpu.make_async_copy(inner_own, weights.at[0, 0], w_sem.at[0]),
        pltpu.make_async_copy(outer_own, weights.at[0, 1], w_sem.at[1]),
        pltpu.make_async_copy(inner_far, weights.at[2, 0], w_sem.at[2]),
        pltpu.make_async_copy(rows_in.at[me], rows.at[part(0)], w_sem.at[3]),
        pltpu.make_async_copy(gate_in.at[me], gates.at[0], w_sem.at[4]),
    ]
    local += [pltpu.make_async_copy(cot_in.at[me ^ k], cots.at[part(k)], cot_sem.at[k]) for k in range(size)]
    for c in local:
        c.start()
    greet([expert_peer(k) for k in range(1, size)] + [shard_peer(1), shard_peer(2)])
    sent = []
    arrive = {}
    outer_far = send(outer_own, weights.at[2, 1], wr_sem.at[0, 0], wr_sem.at[1, 0], shard_peer(2))

    def dispatch(k):
        arrive[k] = [
            send(gate_in.at[me ^ k], gates.at[k], gate_send.at[k], gate_recv.at[k], expert_peer(k)),
            send(rows_in.at[me ^ k], rows.at[part(k)], row_send.at[k], row_recv.at[k], expert_peer(k)),
        ]
        sent.append(arrive[k][0])

    for k in (4, 5, 6, 7, 2, 3, 1):
        dispatch(k)
    moved = [
        send(inner_own, weights.at[1, 0], wr_sem.at[0, 1], wr_sem.at[1, 1], shard_peer(1)),
        send(outer_own, weights.at[1, 1], wr_sem.at[0, 2], wr_sem.at[1, 2], shard_peer(1)),
        send(inner_far, weights.at[3, 0], wr_sem.at[0, 3], wr_sem.at[1, 3], shard_peer(1)),
    ]
    sent += moved + [outer_far]
    d_gates[...] = jnp.zeros_like(d_gates)
    for c in local:
        c.wait()
    for c in moved:
        c.wait_recv()
    ones = jnp.ones((8, 128), jnp.bfloat16)
    returned = {}
    groups = size // group

    def arrived(g):
        for k in range(group * g, group * (g + 1)):
            if k:
                for c in arrive[k]:
                    c.wait_recv()

    def forward_back(g, spot, first, last):
        mine = slice(g * count, (g + 1) * count)
        here = slice(spot * count, (spot + 1) * count)
        if first == 0:
            total[here, :] = jnp.zeros((count, width), jnp.float32)
            d_gate[here, :] = jnp.zeros((count, 128), jnp.float32)

        def step(t, _):
            kk = t // per
            cols = pl.ds(pl.multiple_of(lax.rem(t, per) * tile, tile), tile)
            where = pl.ds(pl.multiple_of(t * tile, tile), tile)
            wi = weights[kk, 0, :, cols]
            wo = weights[kk, 1, cols, :]
            before = dot_nn(rows[mine, :], wi)
            up = dot_nt(cots[mine, :], wo)
            value, slope = gelu_parts(before)
            prod = value * up
            d_gate[here, :] += sum(prod[:, c * 128 : (c + 1) * 128] for c in range(tile // 128))
            active[mine, where] = value.astype(jnp.bfloat16)
            db = (up * slope).astype(jnp.bfloat16)
            d_before[mine, where] = db
            total[here, :] += dot_nt(db, wi)
            return 0

        lax.fori_loop(first * per, last * per, step, 0)

    def give_back(g, spot):
        here = slice(spot * count, (spot + 1) * count)
        back[g * count : (g + 1) * count, :] = total[here, :].astype(jnp.bfloat16)
        for k in range(group * g, group * (g + 1)):
            start = spot * count + (k - group * g) * cap
            sums = d_gate[start : start + cap, :]
            hi = sums.astype(jnp.bfloat16)
            rest = sums - hi.astype(jnp.float32)
            mid = rest.astype(jnp.bfloat16)
            low = (rest - mid.astype(jnp.float32)).astype(jnp.bfloat16)
            d_gates[k, :, 0:cap] = dot_nt(ones, hi) + dot_nt(ones, mid) + dot_nt(ones, low)
            if k:
                returned[k] = [
                    send(d_gates.at[k], d_gates_in.at[k], dg_send.at[k], dg_recv.at[k], expert_peer(k)),
                    send(back.at[part(k)], back_in.at[part(k)], back_send.at[k], back_recv.at[k], expert_peer(k)),
                ]
                sent.extend(returned[k])

    arrived(0)
    forward_back(0, 0, 0, 2)
    arrived(1)
    forward_back(1, 1, 0, 2)
    outer_far.wait_recv()
    passed = send(weights.at[2, 1], weights.at[3, 1], wr_sem.at[0, 4], wr_sem.at[1, 4], shard_peer(1))
    sent.append(passed)
    passed.wait_recv()
    arrived(2)
    forward_back(2, 2, 0, 4)
    give_back(2, 2)
    forward_back(0, 0, 2, 4)
    give_back(0, 0)
    forward_back(1, 1, 2, 4)
    give_back(1, 1)
    arrived(3)
    forward_back(3, 2, 0, 4)
    give_back(3, 2)
    for k in range(size):
        span = slice(k * cap, (k + 1) * cap)
        column = gate_columns(gates[k, 0:1, :], cap, width)
        cots[span, :] = (cots[span, :].astype(jnp.float32) * column).astype(jnp.bfloat16)
        result[span, :] = (rows[span, :].astype(jnp.float32) * column).astype(jnp.bfloat16)
    every = size * cap
    for c in range(width // 128):
        for r in range(every // 128):
            gated_t[c * 128 : (c + 1) * 128, r * 128 : (r + 1) * 128] = (
                result[r * 128 : (r + 1) * 128, c * 128 : (c + 1) * 128].astype(jnp.float32).T.astype(jnp.bfloat16)
            )
    strip = block

    def inner(kk, out):
        return dot_nn(gated_t[out, :], d_before[:, kk * block : (kk + 1) * block])

    def outer(kk, out, t):
        return dot_tn(active[:, pl.ds(pl.multiple_of(kk * block + t * strip, strip), strip)], cots[...])

    def strips(body):
        def run(t, _):
            body(pl.ds(pl.multiple_of(t * strip, strip), strip), t)
            return 0

        lax.fori_loop(0, block // strip, run, 0)

    def chunk(h, kk, out, t):
        return inner(kk, out) if h == 0 else outer(kk, out, t)

    finals = []
    far_swap = None
    for h in range(2):
        shared = []
        for n, kk in enumerate((3, 1)):

            def give(out, t):
                g_send[h, n, out, :] = chunk(h, kk, out, t).astype(jnp.bfloat16)

            strips(give)
            c = send(g_send.at[h, n], g_recv.at[h, n], g_sem_send.at[h, n], g_sem_recv.at[h, n], shard_peer(1))
            shared.append(c)
        shared[0].wait_recv()
        shared[0].wait_send()

        def other(out, t):
            g_send[h, 0, out, :] = (chunk(h, 2, out, t) + g_recv[h, 0, out, :].astype(jnp.float32)).astype(jnp.bfloat16)

        strips(other)
        if h == 0:
            far_swap = send(g_send.at[0, 0], far_recv, g_sem_send.at[0, 2], g_sem_recv.at[0, 2], shard_peer(2))
            sent.append(far_swap)
        else:
            c = pltpu.make_async_copy(g_send.at[1, 0], other_out, out_sem.at[0])
            c.start()
            finals.append(c)
        shared[1].wait_recv()
        sent.append(shared[1])

        def keep(out, t):
            stage[h, out, :] = chunk(h, 0, out, t) + g_recv[h, 1, out, :].astype(jnp.float32)

        strips(keep)
    c = pltpu.make_async_copy(stage.at[1], outer_out, out_sem.at[1])
    c.start()
    finals.append(c)

    def produce(r, _):
        span = pl.ds(pl.multiple_of(r * 4 * cap, 16), 4 * cap)
        y = sum(dot_nn(active[span, kk * block : (kk + 1) * block], weights[kk, 1]) for kk in range(4))
        result[span, :] = y.astype(jnp.bfloat16)
        return 0

    lax.fori_loop(0, size // 4, produce, 0)
    for k in range(size):
        c = pltpu.make_async_copy(result.at[part(k)], result_out.at[me ^ k], res_sem.at[k])
        c.start()
        finals.append(c)
    back_in[part(0), :] = back[part(0), :]
    d_gates_in[0] = d_gates[0]
    far_swap.wait_recv()

    def join(out, t):
        stage[0, out, :] += far_recv[out, :].astype(jnp.float32)

    strips(join)
    c = pltpu.make_async_copy(stage.at[0], inner_out, out_sem.at[2])
    c.start()
    finals.append(c)
    for k in range(size):
        if k:
            for c in returned[k]:
                c.wait_recv()
        for c in (
            pltpu.make_async_copy(back_in.at[part(k)], back_out.at[me ^ k], back_sem.at[k]),
            pltpu.make_async_copy(d_gates_in.at[k], dgate_out.at[me ^ k], dgb_sem.at[k]),
        ):
            c.start()
            finals.append(c)
    for c in finals:
        c.wait()
    for k in range(1, size):
        arrive[k][1].wait_send()
    for c in sent:
        c.wait_send()


def run_experts(rows, gates, cots, inner_own, outer_own, inner_far):
    size, cap, width = rows.shape
    block = inner_own.shape[1]
    bf = jnp.bfloat16
    f32 = jnp.float32
    every = size * cap
    hb = pl.BlockSpec(memory_space=pl.ANY)
    vm = pltpu.VMEM
    dma = pltpu.SemaphoreType.DMA
    shape = jax.ShapeDtypeStruct
    return pl.pallas_call(
        functools.partial(experts_kernel, size, cap, block),
        in_specs=[hb] * 6,
        out_specs=[hb] * 6,
        out_shape=[
            shape((size, cap, width), bf),
            shape((size, 8, 256), f32),
            shape((width, block), f32),
            shape((block, width), f32),
            shape((block, width), bf),
            shape((size, cap, width), bf),
        ],
        scratch_shapes=[
            vm((every, width), bf),
            vm((size, 8, 256), f32),
            vm((every, width), bf),
            vm((4, 2, width, block), bf),
            vm((every, 4 * block), bf),
            vm((every, 4 * block), bf),
            vm((6 * cap, width), f32),
            vm((6 * cap, 128), f32),
            vm((every, width), bf),
            vm((size, 8, 256), f32),
            vm((every, width), bf),
            vm((size, 8, 256), f32),
            vm((width, every), bf),
            vm((2, 2, width, block), bf),
            vm((2, 2, width, block), bf),
            vm((width, block), bf),
            vm((2, width, block), f32),
            vm((every, width), bf),
            dma((5,)),
            dma((2, 5)),
        ]
        + [dma((size,))] * 8
        + [dma((2, 3)), dma((2, 3)), dma((size,)), dma((3,)), dma((size,)), dma((size,)), dma((size,))],
        compiler_params=pltpu.CompilerParams(collective_id=1, has_side_effects=True, vmem_limit_bytes=62 * 2**20),
        cost_estimate=pl.CostEstimate(flops=36 * 10**9, bytes_accessed=30 * 2**20, transcendentals=4 * 10**6),
    )(rows, gates, cots, inner_own, outer_own, inner_far)


class Reduction:
    def __init__(self, index, partial, near, far_send, far_recv, full, x_send, x_recv, half, z_send, z_recv, piece, result, send_sems, recv_sems):
        self.partial, self.near, self.far_send, self.far_recv = partial, near, far_send, far_recv
        self.full, self.x_send, self.x_recv, self.half = full, x_send, x_recv, half
        self.z_send, self.z_recv, self.piece, self.result = z_send, z_recv, piece, result
        self.index, self.send_sems, self.recv_sems = index, send_sems, recv_sems
        self.own = full.shape[0]
        self.width = full.shape[1]
        self.type = partial.dtype
        self.copies = {}

    def block(self, bit):
        return pl.ds(pl.multiple_of((lax.axis_index("shard") ^ bit) * self.own, self.own & -self.own), self.own)

    def half_rows(self, bit):
        rows = self.own // 2
        return pl.ds(pl.multiple_of(((lax.axis_index("expert") & 1) ^ bit) * rows, rows & -rows), rows)

    def quarter(self, step):
        j = (lax.axis_index("expert") >> 1) ^ step
        rows = self.own // 2
        if self.type == jnp.float32:
            return (pl.ds(pl.multiple_of(j * (rows // 4), 8), rows // 4), slice(None))
        return (
            pl.ds(pl.multiple_of((j >> 1) * (rows // 2), 16), rows // 2),
            pl.ds(pl.multiple_of((j & 1) * (self.width // 2), 128), self.width // 2),
        )

    def go(self, slot, src, dst, peer):
        self.copies[slot] = send(src, dst, self.send_sems.at[self.index, slot], self.recv_sems.at[self.index, slot], peer)

    def core(self):
        self.go(0, self.partial.at[self.block(3)], self.near.at[1], shard_peer(1))
        self.go(1, self.partial.at[self.block(1)], self.near.at[0], shard_peer(1))

    def y(self):
        self.copies[0].wait_recv()
        other = self.partial[self.block(2), :].astype(jnp.float32) + self.near[1].astype(jnp.float32)
        self.far_send[...] = other.astype(self.type)
        self.go(2, self.far_send, self.far_recv, shard_peer(2))
        self.copies[1].wait_recv()
        self.full[...] = self.partial[self.block(0), :].astype(jnp.float32) + self.near[0].astype(jnp.float32)

    def x(self):
        self.copies[2].wait_recv()
        self.full[...] += self.far_recv[...].astype(jnp.float32)
        self.x_send[...] = self.full[self.half_rows(1), :].astype(self.type)
        self.go(3, self.x_send, self.x_recv, expert_peer(1))

    def z(self):
        self.copies[3].wait_recv()
        self.half[...] = self.own_half() + self.x_recv[...].astype(jnp.float32)
        self.z_send[...] = self.half[...].astype(self.type)
        for step in (2, 3, 1):
            self.go(3 + step, self.z_send.at[self.quarter(step)], self.z_recv.at[step - 1], expert_peer(2 * step))

    def own_half(self):
        return self.full[self.half_rows(0), :]

    def spread(self):
        for step in (1, 2, 3):
            self.copies[3 + step].wait_recv()
        rows, cols = self.quarter(0)
        total = self.half[rows, cols]
        for step in (1, 2, 3):
            total = total + self.z_recv[step - 1].astype(jnp.float32)
        self.piece[...] = total.astype(self.type)
        target = self.place()
        for step in (2, 3, 1):
            self.go(6 + step, self.piece, self.result.at[target], expert_peer(2 * step))
        self.result[target] = self.piece[...]

    def place(self):
        j = lax.axis_index("expert") >> 1
        first = (lax.axis_index("expert") & 1) * (self.own // 2)
        rows = self.own // 2
        if self.type == jnp.float32:
            return (pl.ds(pl.multiple_of(first + j * (rows // 4), 8), rows // 4), slice(None))
        return (
            pl.ds(pl.multiple_of(first + (j >> 1) * (rows // 2), 16), rows // 2),
            pl.ds(pl.multiple_of((j & 1) * (self.width // 2), 128), self.width // 2),
        )

    def cross(self):
        for step in (1, 2, 3):
            self.copies[6 + step].wait_recv()
        self.go(10, self.result.at[self.half_rows(0)], self.result.at[self.half_rows(0)], expert_peer(1))

    def finish(self, out):
        self.copies[10].wait_recv()
        out[...] = self.result[...].astype(jnp.float32)

    def drain(self):
        for c in self.copies.values():
            c.wait_send()


class Crossed(Reduction):
    other = None

    def y(self):
        rows = self.own // 2
        self.copies[0].wait_recv()
        self.other[...] = self.partial[self.block(2), :].astype(jnp.float32) + self.near[1].astype(jnp.float32)
        self.far_send[rows:, :] = self.other[self.half_rows(1), :].astype(self.type)
        self.copies[1].wait_recv()
        self.full[...] = self.partial[self.block(0), :].astype(jnp.float32) + self.near[0].astype(jnp.float32)
        self.far_send[:rows, :] = self.full[self.half_rows(1), :].astype(self.type)
        self.go(2, self.far_send, self.far_recv, expert_peer(1))

    def x(self):
        rows = self.own // 2
        self.copies[2].wait_recv()
        other = self.other[self.half_rows(0), :] + self.far_recv[rows:, :].astype(jnp.float32)
        self.x_send[...] = other.astype(self.type)
        self.go(3, self.x_send, self.x_recv, shard_peer(2))

    def own_half(self):
        return self.full[self.half_rows(0), :] + self.far_recv[: self.own // 2, :].astype(jnp.float32)


def place_table(near, far, ps, own, heads):
    buckets = 32
    wide = near.shape[2]
    offset = wide // 2 - lax.broadcasted_iota(jnp.int32, (wide, buckets), 0)
    onehot = (bucket_index(offset) == lax.broadcasted_iota(jnp.int32, (wide, buckets), 1)).astype(jnp.float32)
    sums = jnp.concatenate([near[j] for j in range(near.shape[0])], axis=0)
    table = lax.dot_general(
        sums, onehot, (((1,), (0,)), ((), ())), preferred_element_type=jnp.float32, precision=lax.Precision.HIGHEST
    )
    ends = jnp.concatenate([far[j] for j in range(far.shape[0])], axis=0)
    low = jnp.sum(ends[:, :128], axis=1, keepdims=True)
    high = jnp.sum(ends[:, 128:], axis=1, keepdims=True)
    which = lax.broadcasted_iota(jnp.int32, (heads, buckets), 1)
    table = table + jnp.where(which == 15, low, 0.0) + jnp.where(which == 31, high, 0.0)
    part = buckets // 4
    square = jnp.concatenate([table, jnp.zeros((heads, 128 - buckets), jnp.float32)], axis=1)
    square = jnp.concatenate([jnp.zeros((128 - heads, 128), jnp.float32), square], axis=0).T
    lane = lax.broadcasted_iota(jnp.int32, (part, 128), 1)
    for j in range(4):
        r = slice(j * own, j * own + part)
        ps[r, :] = jnp.where(lane >= 128 - heads, square[j * part : (j + 1) * part, :], ps[r, :])


def tail_kernel(
    heads, experts,
    normed_in, dq_in, dk_in, dv_in, context_in, d_branch_in, weights_in, tokens_in, d_resid_in,
    cells_in, resid_in, small, extra, near_sums, far_sums, place, keep_gate,
    o_out, q_out, k_out, v_out, gain_out, gain_two_out, router_out, table_out, tokens_out, mixed_out,
    normed, dq, dk, dv, context, d_branch, weights, tokens, d_resid, cells, resid,
    normed_t, p_ref, near, far_send, far_recv, full, x_send, x_recv, half, z_send, z_recv, piece, result, other,
    ps, s_near, s_far_send, s_far_recv, s_full, s_x_send, s_x_recv, s_half, s_z_send, s_z_recv, s_piece, s_result,
    send_sems, recv_sems, load_sems,
):
    length, width = normed.shape
    tile = 256
    loads = [
        pltpu.make_async_copy(src, dst, load_sems.at[i])
        for i, (src, dst) in enumerate(
            (
                (context_in, context),
                (d_branch_in, d_branch),
                (normed_in, normed),
                (dq_in, dq),
                (dk_in, dk),
                (dv_in, dv),
                (weights_in.at[0:3], weights),
                (tokens_in, tokens),
                (d_resid_in, d_resid),
                (cells_in, cells),
                (resid_in, resid),
            )
        )
    ]
    for c in loads:
        c.start()
    greet([shard_peer(1), shard_peer(2)] + [expert_peer(k) for k in (1, 2, 4, 6)])
    work = []
    for m in range(4):
        w = (Crossed if m == 3 else Reduction)(
            m, p_ref.at[m], near.at[m], far_send.at[m], far_recv.at[m], full.at[m], x_send.at[m], x_recv.at[m],
            half.at[m], z_send.at[m], z_recv.at[m], piece.at[m], result.at[m], send_sems, recv_sems,
        )
        w.other = other
        work.append(w)
    o, q, k, v = work
    s = Reduction(
        4, ps, s_near, s_far_send, s_far_recv, s_full, s_x_send, s_x_recv, s_half, s_z_send, s_z_recv, s_piece,
        s_result, send_sems, recv_sems,
    )

    def strips(m, make):
        p_ref[m] = make(slice(None)).astype(jnp.bfloat16)

    loads[0].wait()
    loads[1].wait()
    strips(0, lambda r: dot_tn(context[...], d_branch[...]))
    o.core()
    loads[2].wait()
    for c in range(width // 128):
        for t in range(length // 128):
            normed_t[c * 128 : (c + 1) * 128, t * 128 : (t + 1) * 128] = (
                normed[t * 128 : (t + 1) * 128, c * 128 : (c + 1) * 128].astype(jnp.float32).T.astype(jnp.bfloat16)
            )
    o.y()
    loads[3].wait()
    strips(1, lambda r: dot_nn(normed_t[r, :], dq[...]))
    q.core()
    loads[4].wait()
    strips(2, lambda r: dot_nn(normed_t[r, :], dk[...]))
    q.y()
    k.core()
    loads[5].wait()
    strips(3, lambda r: dot_nn(normed_t[r, :], dv[...]))
    v.core()
    k.y()
    head = small[...].astype(jnp.float32)
    gain = jnp.concatenate([head[c * 128 : (c + 1) * 128, :].T[0:1] for c in range(width // 128)], axis=1)
    for c in loads[6:9]:
        c.wait()

    def back(t, total):
        r = pl.ds(pl.multiple_of(t * tile, tile), tile)
        grad = dot_nt(dq[r, :], weights[0]) + dot_nt(dk[r, :], weights[1]) + dot_nt(dv[r, :], weights[2])
        x = tokens[r, :].astype(jnp.float32)
        scale = lax.rsqrt(jnp.mean(x * x, axis=-1, keepdims=True) + 1e-6)
        unit = x * scale
        pulled = grad * gain
        shift = jnp.mean(unit * pulled, axis=-1, keepdims=True)
        tokens_out[r, :] = (d_resid[r, :] + scale * (pulled - unit * shift)).astype(jnp.bfloat16)
        return total + jnp.sum(grad * unit, axis=0, keepdims=True)

    def some(first, last, total):
        return lax.fori_loop(first, last, back, total)

    def mix(t, _):
        r = pl.ds(pl.multiple_of(t * tile, tile), tile)
        pick = (lax.broadcasted_iota(jnp.int32, (tile, cells.shape[0]), 1) == place[r, :]).astype(jnp.float32)
        arrived = dot_nn(pick.astype(jnp.bfloat16), cells[...])
        mixed_out[r, :] = (resid[r, :] + keep_gate[r, :] * arrived).astype(jnp.bfloat16)
        return 0

    v.y()
    total = some(0, 1, jnp.zeros((1, width), jnp.float32))
    o.x()
    total = some(1, 2, total)
    o.z()
    total = some(2, 3, total)
    q.x()
    total = some(3, length // tile, total)
    lane = lax.broadcasted_iota(jnp.int32, (128, 128), 1)
    for c in range(width // 128):
        column = jnp.broadcast_to(total[:, c * 128 : (c + 1) * 128], (128, 128)).T
        ps[c * 128 : (c + 1) * 128, :] = jnp.where(lane == 0, column, extra[c * 128 : (c + 1) * 128, :])
    place_table(near_sums, far_sums, ps, s.own, heads)
    s.core()
    o.spread()
    q.z()
    v.x()
    s.y()
    for c in loads[9:]:
        c.wait()
    lax.fori_loop(0, 1, mix, 0)
    k.x()
    o.cross()
    q.spread()
    s.x()
    lax.fori_loop(1, 2, mix, 0)
    v.z()
    k.z()
    lax.fori_loop(2, 3, mix, 0)
    s.z()
    q.cross()
    v.spread()
    k.spread()
    lax.fori_loop(3, length // tile, mix, 0)
    s.spread()
    o.finish(o_out)
    v.cross()
    k.cross()
    s.cross()
    q.finish(q_out)
    v.finish(v_out)
    k.finish(k_out)
    s.copies[10].wait_recv()
    final = s_result[...]
    pad = jnp.concatenate([final, jnp.zeros((256 - s.own, 128), jnp.float32)], axis=0)
    lines = jnp.concatenate([pad[:128, :].T, pad[128:, :].T], axis=1)
    gain_out[...] = lines[0:1, : s.own]
    gain_two_out[...] = lines[1:2, : s.own]
    router_out[...] = final[:, 2 : 2 + experts]
    table_out[...] = final[: table_out.shape[0], 128 - heads :]
    for w in work + [s]:
        w.drain()


def run_tail(
    normed, dq, dk, dv, context, d_branch, weights, tokens, d_resid, cells, resid, small, extra, near, far,
    place, keep_gate, experts, own_buckets,
):
    length, width = normed.shape
    own = width // 4
    heads = near.shape[0] * near.shape[1]
    bf = jnp.bfloat16
    f32 = jnp.float32
    vm = pltpu.VMEM
    hb = pl.BlockSpec(memory_space=pl.ANY)
    mem = pl.BlockSpec(memory_space=pltpu.VMEM)
    h = own // 2
    shape = jax.ShapeDtypeStruct
    return pl.pallas_call(
        functools.partial(tail_kernel, heads, experts),
        in_specs=[hb] * 11 + [mem] * 6,
        out_specs=[mem] * 10,
        out_shape=[shape((own, width), f32)] * 4
        + [
            shape((1, own), f32),
            shape((1, own), f32),
            shape((own, experts), f32),
            shape((own_buckets, heads), f32),
            shape((length, width), bf),
            shape((length, width), bf),
        ],
        scratch_shapes=[vm((length, width), bf)] * 6
        + [
            vm((3, width, width), bf),
            vm((length, width), bf),
            vm((length, width), f32),
            vm(cells.shape, bf),
            vm((length, width), f32),
            vm((width, length), bf),
            vm((4, width, width), bf),
            vm((4, 2, own, width), bf),
            vm((4, own, width), bf),
            vm((4, own, width), bf),
            vm((4, own, width), f32),
            vm((4, h, width), bf),
            vm((4, h, width), bf),
            vm((4, h, width), f32),
            vm((4, h, width), bf),
            vm((4, 3, h // 2, width // 2), bf),
            vm((4, h // 2, width // 2), bf),
            vm((4, own, width), bf),
            vm((own, width), f32),
            vm((width, 128), f32),
            vm((2, own, 128), f32),
            vm((own, 128), f32),
            vm((own, 128), f32),
            vm((own, 128), f32),
            vm((h, 128), f32),
            vm((h, 128), f32),
            vm((h, 128), f32),
            vm((h, 128), f32),
            vm((3, h // 4, 128), f32),
            vm((h // 4, 128), f32),
            vm((own, 128), f32),
            pltpu.SemaphoreType.DMA((5, 11)),
            pltpu.SemaphoreType.DMA((5, 11)),
            pltpu.SemaphoreType.DMA((11,)),
        ],
        compiler_params=pltpu.CompilerParams(collective_id=2, has_side_effects=True, vmem_limit_bytes=62 * 2**20),
        cost_estimate=pl.CostEstimate(flops=11 * 10**9, bytes_accessed=40 * 2**20, transcendentals=0),
    )(
        normed, dq, dk, dv, context, d_branch, weights, tokens, d_resid, cells, resid, small, extra, near,
        far, place, keep_gate,
    )


def finish_kernel(count, *refs):
    ins, (mine, other), outs = refs[:count], refs[count : count + 2], refs[count + 2 : 2 * count + 2]
    total = refs[2 * count + 2]
    add_a, add_b = refs[2 * count + 3 : 2 * count + 5]
    bufs = refs[2 * count + 5 : 3 * count + 5]
    in_sems, out_sems = refs[3 * count + 5 :]
    first = [pltpu.make_async_copy(mine, add_a, in_sems.at[count]), pltpu.make_async_copy(other, add_b, in_sems.at[count + 1])]
    loads = [pltpu.make_async_copy(ins[i], bufs[i], in_sems.at[i]) for i in range(count)]
    for c in first + loads:
        c.start()
    for c in first:
        c.wait()
    add_a[...] = add_a[...] + add_b[...].astype(jnp.float32)
    stores = [pltpu.make_async_copy(add_a, total, out_sems.at[count])]
    stores[0].start()
    for i in range(count):
        loads[i].wait()
        c = pltpu.make_async_copy(bufs[i], outs[i], out_sems.at[i])
        c.start()
        stores.append(c)
    for c in stores:
        c.wait()


def run_finish(results, mine, other):
    count = len(results)
    hb = pl.BlockSpec(memory_space=pl.ANY)
    return pl.pallas_call(
        functools.partial(finish_kernel, count),
        in_specs=[hb] * (count + 2),
        out_specs=[hb] * (count + 1),
        out_shape=[jax.ShapeDtypeStruct(r.shape, r.dtype) for r in results]
        + [jax.ShapeDtypeStruct(mine.shape, jnp.float32)],
        scratch_shapes=[pltpu.VMEM(mine.shape, jnp.float32), pltpu.VMEM(other.shape, jnp.bfloat16)]
        + [pltpu.VMEM(r.shape, r.dtype) for r in results]
        + [pltpu.SemaphoreType.DMA((count + 2,)), pltpu.SemaphoreType.DMA((count + 1,))],
        compiler_params=pltpu.CompilerParams(vmem_limit_bytes=62 * 2**20),
        cost_estimate=pl.CostEstimate(flops=10**6, bytes_accessed=24 * 2**20, transcendentals=0),
    )(*results, mine, other)

EPS = 1e-06
BF = jnp.bfloat16
F32 = jnp.float32


def dot_tn(a, b):
    return lax.dot_general(a, b, (((0,), (0,)), ((), ())), preferred_element_type=F32)


def swap(value, axis, size, bit):
    return lax.ppermute(value, axis, [(i, i ^ bit) for i in range(size)])


def direct(size):
    return size == 8


def exchange(blocks):
    return lax.all_to_all(blocks, "expert", split_axis=0, concat_axis=0, tiled=True)


def gather_shards(value, size):
    if size == 4:
        far = swap(value, "shard", size, 2)
        near = swap(value, "shard", size, 1)
        return [value, near, far, swap(far, "shard", size, 1)]
    return [value] + [swap(value, "shard", size, k) for k in range(1, size)]


def reduce_shards(blocks, size):
    if size == 4:
        near1 = swap(blocks[3].astype(BF), "shard", size, 1)
        near0 = swap(blocks[1].astype(BF), "shard", size, 1)
        other = swap((blocks[2].astype(F32) + near1.astype(F32)).astype(BF), "shard", size, 2)
        return blocks[0].astype(F32) + near0.astype(F32) + other.astype(F32)
    total = blocks[0].astype(F32)
    for k in range(1, size):
        total = total + swap(blocks[k].astype(BF), "shard", size, k).astype(F32)
    return total


def experts_by_collectives(row_blocks, gate_slots, cot_blocks, inner, outer, size, shards, cap):
    inners = gather_shards(inner, shards)
    outers = gather_shards(outer, shards)
    cells, width = size * cap, row_blocks.shape[2]
    rows = exchange(row_blocks).reshape(cells, width)
    cots = cot_blocks.reshape(cells, width)
    gates = exchange(gate_slots.reshape(size, cap)).reshape(cells, 1)
    half = cells // 2
    parts = [expert_half([rows[i : i + half]], [cots[i : i + half]], inners, outers) for i in (0, half)]
    back, active, d_before, d_gate = (
        jnp.concatenate([p[0][0] if i == 0 else p[i] for p in parts], axis=0) for i in range(4)
    )
    back = exchange(back.reshape(size, cap, width)).reshape(cells, width)
    d_gate = exchange(d_gate.reshape(size, cap)).reshape(cells)
    d_out = (cots.astype(F32) * gates).astype(BF)
    gated = (rows.astype(F32) * gates).astype(BF)
    block = inner.shape[1]
    spans = [slice(k * block, (k + 1) * block) for k in range(shards)]
    grad_outer = reduce_shards([dot_tn(active[:, p], d_out) for p in spans], shards)
    grad_inner = reduce_shards([dot_tn(gated, d_before[:, p]) for p in spans], shards)
    result = dot_nn(active, jnp.concatenate(outers, axis=0)).astype(BF).reshape(size, cap, width)
    result = exchange(result).reshape(cells, width)
    return back, d_gate, grad_inner, grad_outer, result


def per_device(
    tokens,
    segments,
    routes,
    order,
    gain_attn,
    w_query,
    w_key,
    w_value,
    w_output,
    rel_bias,
    gain_ffn,
    w_router,
    w_in,
    w_out,
    cotangent,
):
    seq_count, length, width = tokens.shape
    total = seq_count * length
    experts = lax.axis_size("expert")
    shards = lax.axis_size("shard")
    me = lax.axis_index("expert")
    my_shard = lax.axis_index("shard")
    capacity = (5 * total + 4 * experts - 1) // (4 * experts)
    cells = experts * capacity
    heads = rel_bias.shape[1]
    own = w_query.shape[0]
    own_buckets = rel_bias.shape[0]
    buckets = own_buckets * shards
    small = jnp.concatenate([gain_attn[:, None], gain_ffn[:, None], w_router], axis=1)
    small = jnp.pad(small, ((0, 0), (0, 128 - small.shape[1])))
    small = lax.dynamic_update_slice(small, rel_bias, (0, 128 - heads))
    route = routes.reshape(total)
    chosen = (route[:, None] == jnp.arange(experts, dtype=jnp.int32)[None, :]).astype(F32)
    cot = cotangent.reshape(total, width)
    ranks = (jnp.arange(seq_count, dtype=jnp.int32)[:, None] * length + order).reshape(1, total)
    query, key, value, normed_low, small_all, place_line, cot_cells, weights_all = project(
        routes.reshape(1, total), ranks, tokens.reshape(total, width), cot, small,
        (w_query, w_key, w_value, w_output), experts, capacity,
    )
    place = place_line[0]
    kept = place >= 0
    spread = (jnp.arange(cells, dtype=jnp.int32)[:, None] == place[None, :]).astype(BF)

    def to_blocks(values):
        return dot_nn(spread, values).astype(BF).reshape(experts, capacity, width)

    cot_blocks = exchange(cot_cells.reshape(experts, capacity, width))
    query_all, key_all, value_all, output_all = (weights_all[i] for i in range(4))
    inner_own, outer_own = w_in[0], w_out[0]
    if direct(experts):
        inner_own, query = lax.optimization_barrier((inner_own, query))
        inner_far = swap(inner_own, "shard", shards, 2)
    inputs = tokens.reshape(total, width).astype(F32)
    gain_two = small_all[:, 1].astype(F32)
    router_all = small_all[:, 2 : 2 + experts]
    table = small_all[:, 128 - heads :].reshape(shards, own, heads)[:, :own_buckets]
    table = table.reshape(buckets, heads)
    bias = bias_lanes(table)
    seg = [seg_arrays(segments[i]) for i in range(seq_count)]
    rows_of = [slice(i * length, (i + 1) * length) for i in range(seq_count)]
    forward = [
        attn_fwd(s[2], s[3], query[r], key[r], value[r], s[0], s[1], bias)
        for s, r in zip(seg, rows_of)
    ]
    context = jnp.concatenate([f[0] for f in forward], axis=0) if seq_count > 1 else forward[0][0]
    resid = inputs + dot_nn(context, output_all)
    scale_two = lax.rsqrt(jnp.mean(resid * resid, axis=-1, keepdims=True) + EPS)
    unit_two = resid * scale_two
    normed_two_low = (unit_two * gain_two).astype(BF)
    logits = dot_nn(normed_two_low, router_all)
    probs = jax.nn.softmax(logits, axis=-1)
    gate = jnp.sum(probs * chosen, axis=-1)
    keep_weight = kept.astype(F32)
    keep_gate = gate * keep_weight
    gate_slots = jnp.sum(jnp.where(place[None, :] == jnp.arange(cells)[:, None], gate[None, :], 0), axis=1)
    row_blocks = to_blocks(normed_two_low)
    if direct(experts):
        gate_lines = jnp.pad(gate_slots.reshape(experts, 1, capacity), ((0, 0), (0, 7), (0, 256 - capacity)))
        back, gate_back, grad_inner, outer_mine, outer_other, expert_out = run_experts(
            row_blocks, gate_lines, cot_blocks, inner_own, outer_own, inner_far
        )
        back = back.reshape(cells, width)
        gate_cells = gate_back[:, 0, :capacity].reshape(cells)
        outer_other = swap(outer_other, "shard", shards, 2)
        out_cells = exchange(expert_out).reshape(cells, width)
    else:
        back, gate_cells, grad_inner, grad_outer, out_cells = experts_by_collectives(
            row_blocks, gate_slots, cot_blocks, w_in[0], w_out[0], experts, shards, capacity
        )
    upstream = cot.astype(F32)
    d_rows = dot_tn(spread, back)
    d_gate = jnp.sum(
        jnp.where(place[:, None] == jnp.arange(cells)[None, :], gate_cells[None, :], 0), axis=1
    )
    d_logits = (probs * (d_gate[:, None] * chosen - (d_gate * gate)[:, None])).astype(BF)
    d_router = dot_tn(normed_two_low, d_logits)
    d_normed_two = dot_nt(d_logits, router_all) + keep_gate[:, None] * d_rows
    d_gain_two = jnp.sum(d_normed_two * unit_two, axis=0)
    pulled = gain_two * d_normed_two
    d_resid = upstream + scale_two * (
        pulled - unit_two * jnp.mean(unit_two * pulled, axis=-1, keepdims=True)
    )
    d_branch = d_resid.astype(BF)
    d_context = dot_nt(d_branch, output_all).astype(BF)
    backward = [
        attn_bwd(s[2], s[3], query[r], key[r], value[r], d_context[r], f[0], f[1], s[0], s[1], bias)
        for s, r, f in zip(seg, rows_of, forward)
    ]
    d_query, d_key, d_value = (
        jnp.concatenate([b[i] for b in backward], axis=0) if seq_count > 1 else backward[0][i]
        for i in range(3)
    )
    tail = jnp.concatenate([jnp.zeros_like(d_gain_two)[:, None], d_gain_two[:, None], d_router], axis=1)
    tail = jnp.pad(tail, ((0, 0), (0, 128 - tail.shape[1])))
    flat_tokens = tokens.reshape(total, width)
    if direct(experts):
        near_sums, far_sums = backward[0][3], backward[0][4]
        (
            sum_output, sum_query, sum_key, sum_value, sum_gain, sum_gain_two, sum_router, sum_table,
            d_tokens, mixed,
        ) = run_tail(
            normed_low, d_query, d_key, d_value, context, d_branch, weights_all, flat_tokens, d_resid, out_cells, resid,
            small_all, tail, near_sums, far_sums, place[:, None], keep_gate[:, None], experts, own_buckets,
        )
        sum_output, sum_query, sum_key, sum_value, d_tokens, mixed, grad_inner, grad_outer = run_finish(
            [sum_output, sum_query, sum_key, sum_value, d_tokens, mixed, grad_inner], outer_mine, outer_other
        )
        return (
            mixed.reshape(tokens.shape),
            d_tokens.reshape(tokens.shape),
            sum_gain[0],
            sum_query,
            sum_key,
            sum_value,
            sum_output,
            sum_table,
            sum_gain_two[0],
            sum_router,
            grad_inner[None],
            grad_outer[None],
        )
    d_table = sum(table_grad(b[3], b[4], buckets) for b in backward)
    tail = lax.dynamic_update_slice(
        tail.reshape(shards, own, 128), d_table.reshape(shards, own_buckets, heads), (0, 0, 128 - heads)
    ).reshape(width, 128)
    if True:
        d_normed = (
            dot_nt(d_query, query_all) + dot_nt(d_key, key_all) + dot_nt(d_value, value_all)
        )
        inputs_again = flat_tokens.astype(F32)
        scale_one = lax.rsqrt(jnp.mean(inputs_again * inputs_again, axis=-1, keepdims=True) + EPS)
        unit_one = inputs_again * scale_one
        tail = tail.at[:, 0].set(jnp.sum(d_normed * unit_one, axis=0))
        pulled_one = small_all[:, 0].astype(F32) * d_normed
        d_tokens = d_resid + scale_one * (
            pulled_one - unit_one * jnp.mean(unit_one * pulled_one, axis=-1, keepdims=True)
        )
        pairs = ((context, d_branch), (normed_low, d_query), (normed_low, d_key), (normed_low, d_value))
        parts = [dot_tn(left, right) for left, right in pairs] + [tail]
        sum_output, sum_query, sum_key, sum_value, sums = (
            lax.psum(
                reduce_shards(
                    [lax.dynamic_slice_in_dim(p, (my_shard ^ k) * own, own, 0) for k in range(shards)], shards
                ),
                "expert",
            )
            for p in parts
        )
    arrived = dot_tn(spread, out_cells)
    mixed = resid + keep_gate[:, None] * arrived
    return (
        mixed.astype(BF).reshape(tokens.shape),
        d_tokens.astype(BF).reshape(tokens.shape),
        sums[:, 0],
        sum_query,
        sum_key,
        sum_value,
        sum_output,
        sums[:own_buckets, 128 - heads :],
        sums[:, 1],
        sums[:, 2 : 2 + experts],
        grad_inner[None],
        grad_outer[None],
    )


def solution(mesh):
    in_specs = (
        P(("expert", "shard"), None, None),
        P(("expert", "shard"), None),
        P(("expert", "shard"), None, None),
        P(("expert", "shard"), None),
        P("shard"),
        P("shard", None),
        P("shard", None),
        P("shard", None),
        P("shard", None),
        P("shard", None),
        P("shard"),
        P("shard", None),
        P("expert", None, "shard"),
        P("expert", "shard", None),
        P(("expert", "shard"), None, None),
    )
    out_specs = (
        P(("expert", "shard"), None, None),
        P(("expert", "shard"), None, None),
        P("shard"),
        P("shard", None),
        P("shard", None),
        P("shard", None),
        P("shard", None),
        P("shard", None),
        P("shard"),
        P("shard", None),
        P("expert", None, "shard"),
        P("expert", "shard", None),
    )
    return jax.shard_map(
        per_device, mesh=mesh, in_specs=in_specs, out_specs=out_specs, check_vma=False
    )
```

```python
import functools

import jax
import jax.numpy as jnp
from jax import lax
from jax.experimental import pallas as pl
from jax.experimental.pallas import tpu as pltpu
from jax.sharding import PartitionSpec as P
HEAD_DIM=64
BLK=128
EDGES = (12, 16, 23, 32, 46, 64, 91)
BIG=1e9
def bucket_index(offset):
    magnitude = jnp.abs(offset)
    far = 8 + sum(((magnitude >= edge).astype(jnp.int32) for edge in EDGES))
    near = jnp.where(magnitude < 8, magnitude, far)
    return near + 16 * (offset > 0).astype(jnp.int32)

def dot_nt(a,b): return lax.dot_general(a,b,(((1,),(1,)),((),())),preferred_element_type=jnp.float32)
def dot_nn(a,b): return lax.dot_general(a,b,(((1,),(0,)),((),())),preferred_element_type=jnp.float32)

def head_mask():
    lane=lax.broadcasted_iota(jnp.int32,(BLK,2*HEAD_DIM),1)
    return (lane<HEAD_DIM).astype(jnp.float32).astype(jnp.bfloat16)

def build_bias(w_ref, bias_ref, nblk, pairs):
    rows = (2 * nblk - 1) * BLK
    near = (nblk - 2) * BLK
    for j in range(pairs):
        for h in range(2):
            c = slice((2 * j + h) * BLK, (2 * j + h + 1) * BLK)
            w = w_ref[j, h : h + 1, :]
            bias_ref[0:near, c] = jnp.broadcast_to(w[:, 511:512], (near, BLK))
            bias_ref[near + 3 * BLK : rows, c] = jnp.broadcast_to(w[:, 0:1], (near, BLK))
            r = pltpu.roll(jnp.broadcast_to(w, (BLK, 512)), 0, 1, stride=1, stride_axis=0)
            bias_ref[near : near + BLK, c] = r[:, 384:512]
            bias_ref[near + BLK : near + 2 * BLK, c] = r[:, 256:384]
            bias_ref[near + 2 * BLK : near + 3 * BLK, c] = r[:, 128:256]


def by_width(nblk, count, run):
    for n in range(1, nblk + 1):

        @pl.when(count == n)
        def _():
            run(n * BLK)


def pair_of(block, mask):
    return jnp.concatenate([block * mask, block * (1 - mask)], axis=0)


def flip(src_ref, dst_ref, nblk, pairs):
    for j in range(pairs):
        c = slice(j * BLK, (j + 1) * BLK)
        for b in range(nblk):
            s = slice(b * BLK, (b + 1) * BLK)
            dst_ref[c, s] = src_ref[s, c].astype(jnp.float32).T.astype(jnp.bfloat16)


def join_heads(wide):
    return jnp.concatenate([wide[:HEAD_DIM, :BLK], wide[HEAD_DIM:, BLK:]], axis=0)


def fwd_kernel(nblk, pairs, lo_ref, nb_ref, q_ref, k_ref, v_ref, segq_ref, segk_ref, w_ref, ctx_ref, lse_ref, vt_ref, bias_ref):
    build_bias(w_ref, bias_ref, nblk, pairs)
    flip(v_ref, vt_ref, nblk, pairs)
    mask = head_mask()
    lanes = [slice(j * BLK, (j + 1) * BLK) for j in range(pairs)]
    both = [slice(2 * j * BLK, 2 * (j + 1) * BLK) for j in range(pairs)]

    def body(qb, _):
        rows = pl.ds(pl.multiple_of(qb * BLK, BLK), BLK)
        lob = lo_ref[qb]
        sq = segq_ref[rows, :]
        sq = jnp.concatenate([sq, sq], axis=0)
        q_cat = [jnp.concatenate([pair_of(q_ref[rows, c], mask), sq], axis=1) for c in lanes]

        def run(W):
            ks = pl.ds(pl.multiple_of(lob * BLK, BLK), W)
            bs = pl.ds(pl.multiple_of((lob - qb + nblk - 1) * BLK, BLK), W)
            sk = segk_ref[ks, :]
            st = [
                dot_nt(jnp.concatenate([k_ref[ks, c], sk], axis=1), q) + bias_ref[bs, d]
                for c, d, q in zip(lanes, both, q_cat)
            ]
            m = [jnp.max(x, axis=0, keepdims=True) for x in st]
            e = [jnp.exp(x - y) for x, y in zip(st, m)]
            l = [jnp.sum(x, axis=0, keepdims=True) for x in e]
            ot = [dot_nn(vt_ref[c, ks], x.astype(jnp.bfloat16)) / y for c, x, y in zip(lanes, e, l)]
            for j, c in enumerate(lanes):
                ctx_ref[rows, c] = join_heads(ot[j]).T.astype(jnp.bfloat16)
                lse_ref[j, pl.ds(qb, 1), :] = m[j] + jnp.log(l[j])

        by_width(nblk, nb_ref[qb], run)
        return 0

    lax.fori_loop(0, nblk, body, 0)


def bwd_kernel(
    nblk, pairs, lo_ref, nb_ref, q_ref, k_ref, v_ref, do_ref, ctx_ref, lse_ref, segq_ref, segk_ref, w_ref,
    dq_ref, dk_ref, dv_ref, near_ref, far_ref, kt_ref, bias_ref, acc_ref, dka_ref, dva_ref,
):
    build_bias(w_ref, bias_ref, nblk, pairs)
    flip(k_ref, kt_ref, nblk, pairs)
    acc_ref[...] = jnp.zeros_like(acc_ref)
    dka_ref[...] = jnp.zeros_like(dka_ref)
    dva_ref[...] = jnp.zeros_like(dva_ref)
    mask = head_mask()
    lanes = [slice(j * BLK, (j + 1) * BLK) for j in range(pairs)]
    both = [slice(2 * j * BLK, 2 * (j + 1) * BLK) for j in range(pairs)]
    row = lax.broadcasted_iota(jnp.int32, (16, 2 * HEAD_DIM), 0)
    lane = lax.broadcasted_iota(jnp.int32, (16, 2 * HEAD_DIM), 1)
    pick = ((lane // HEAD_DIM) == row).astype(jnp.float32).astype(jnp.bfloat16)

    def body(qb, _):
        rows = pl.ds(pl.multiple_of(qb * BLK, BLK), BLK)
        lob = lo_ref[qb]
        sq = segq_ref[rows, :]
        sq = jnp.concatenate([sq, sq], axis=0)
        q2 = [pair_of(q_ref[rows, c], mask) for c in lanes]
        q_cat = [jnp.concatenate([q, sq], axis=1) for q in q2]
        do2 = [pair_of(do_ref[rows, c], mask) for c in lanes]
        delta = []
        for c in lanes:
            prod = do_ref[rows, c].astype(jnp.float32) * ctx_ref[rows, c].astype(jnp.float32)
            hi = prod.astype(jnp.bfloat16)
            low = (prod - hi.astype(jnp.float32)).astype(jnp.bfloat16)
            dl = dot_nt(pick, hi) + dot_nt(pick, low)
            delta.append(jnp.concatenate([dl[0:1], dl[1:2]], axis=1))
        lse = [lse_ref[j, pl.ds(qb, 1), :] for j in range(pairs)]

        def run(W):
            ks = pl.ds(pl.multiple_of(lob * BLK, BLK), W)
            bs = pl.ds(pl.multiple_of((lob - qb + nblk - 1) * BLK, BLK), W)
            sk = segk_ref[ks, :]
            st = [dot_nt(jnp.concatenate([k_ref[ks, c], sk], axis=1), q) for c, q in zip(lanes, q_cat)]
            dp = [dot_nt(v_ref[ks, c], d) for c, d in zip(lanes, do2)]
            p = [jnp.exp(x + bias_ref[bs, d] - y) for x, d, y in zip(st, both, lse)]
            ds = [x * (y - z) for x, y, z in zip(p, dp, delta)]
            dsb = [x.astype(jnp.bfloat16) for x in ds]
            for j, (c, d) in enumerate(zip(lanes, both)):
                acc_ref[bs, d] += ds[j]
                dva_ref[ks, c] += dot_nn(p[j].astype(jnp.bfloat16), do2[j])
                dka_ref[ks, c] += dot_nn(dsb[j], q2[j])
                dqt = join_heads(dot_nn(kt_ref[c, ks], dsb[j])) * (HEAD_DIM**-0.5)
                dq_ref[rows, c] = dqt.T.astype(jnp.bfloat16)

        by_width(nblk, nb_ref[qb], run)
        return 0

    lax.fori_loop(0, nblk, body, 0)
    dk_ref[...] = dka_ref[...].astype(jnp.bfloat16)
    dv_ref[...] = dva_ref[...].astype(jnp.bfloat16)
    near = (nblk - 2) * BLK
    total = (2 * nblk - 1) * BLK
    for j in range(pairs):
        for h in range(2):
            c = slice((2 * j + h) * BLK, (2 * j + h + 1) * BLK)
            wide = jnp.concatenate(
                [
                    jnp.zeros((BLK, BLK), jnp.float32),
                    acc_ref[near + 2 * BLK : near + 3 * BLK, c],
                    acc_ref[near + BLK : near + 2 * BLK, c],
                    acc_ref[near : near + BLK, c],
                ],
                axis=1,
            )
            near_ref[j, h : h + 1, :] = jnp.sum(unroll_rows(wide), axis=0, keepdims=True)
            low = jnp.sum(acc_ref[0:near, c], axis=0, keepdims=True)
            high = jnp.sum(acc_ref[near + 3 * BLK : total, c], axis=0, keepdims=True)
            far_ref[j, h : h + 1, :] = jnp.concatenate([low, high], axis=1)


def unroll_rows(wide):
    n=wide.shape[1]
    out=wide
    row=lax.broadcasted_iota(jnp.int32,wide.shape,0)
    bit=1
    while bit<wide.shape[0]:
        out=jnp.where((row & bit)!=0,pltpu.roll(out,n-bit,1),out)
        bit*=2
    return out

FWD_PAIRS = 6
BWD_PAIRS = 3


def pair_spec(nrow, pairs):
    return pl.BlockSpec((nrow, 2 * HEAD_DIM * pairs), lambda p, *_: (0, p))


def full_spec(shape):
    return pl.BlockSpec(shape, lambda p, *_: (0,) * len(shape))


def lead_spec(pairs, shape):
    return pl.BlockSpec((pairs,) + shape, lambda p, *_: (p, 0, 0))


def attn_fwd(lo, nb, q, k, v, segq, segk, w):
    L, D = q.shape
    nblk = L // BLK
    every = D // (2 * HEAD_DIM)
    pairs = FWD_PAIRS
    return pl.pallas_call(
        functools.partial(fwd_kernel, nblk, pairs),
        grid_spec=pltpu.PrefetchScalarGridSpec(
            num_scalar_prefetch=2,
            grid=(every // pairs,),
            in_specs=[pair_spec(L, pairs)] * 3 + [full_spec((L, 128))] * 2 + [lead_spec(pairs, (2, 512))],
            out_specs=[pair_spec(L, pairs), lead_spec(pairs, (nblk, 2 * BLK))],
            scratch_shapes=[
                pltpu.VMEM((2 * HEAD_DIM * pairs, L), jnp.bfloat16),
                pltpu.VMEM(((2 * nblk - 1) * BLK, 2 * BLK * pairs), jnp.float32),
            ],
        ),
        out_shape=[
            jax.ShapeDtypeStruct((L, D), jnp.bfloat16),
            jax.ShapeDtypeStruct((every, nblk, 2 * BLK), jnp.float32),
        ],
        compiler_params=pltpu.CompilerParams(vmem_limit_bytes=60 * 2**20),
        cost_estimate=pl.CostEstimate(flops=2 * 10**9, bytes_accessed=8 * 2**20, transcendentals=6 * 10**6),
    )(lo, nb, q, k, v, segq, segk, w)


def attn_bwd(lo, nb, q, k, v, do, ctx, lse, segq, segk, w):
    L, D = q.shape
    nblk = L // BLK
    every = D // (2 * HEAD_DIM)
    pairs = BWD_PAIRS
    rows = (2 * nblk - 1) * BLK
    return pl.pallas_call(
        functools.partial(bwd_kernel, nblk, pairs),
        grid_spec=pltpu.PrefetchScalarGridSpec(
            num_scalar_prefetch=2,
            grid=(every // pairs,),
            in_specs=[pair_spec(L, pairs)] * 5
            + [lead_spec(pairs, (nblk, 2 * BLK))]
            + [full_spec((L, 128))] * 2
            + [lead_spec(pairs, (2, 512))],
            out_specs=[pair_spec(L, pairs)] * 3 + [lead_spec(pairs, (2, 512)), lead_spec(pairs, (2, 256))],
            scratch_shapes=[
                pltpu.VMEM((2 * HEAD_DIM * pairs, L), jnp.bfloat16),
                pltpu.VMEM((rows, 2 * BLK * pairs), jnp.float32),
                pltpu.VMEM((rows, 2 * BLK * pairs), jnp.float32),
                pltpu.VMEM((L, 2 * HEAD_DIM * pairs), jnp.float32),
                pltpu.VMEM((L, 2 * HEAD_DIM * pairs), jnp.float32),
            ],
        ),
        out_shape=[jax.ShapeDtypeStruct((L, D), jnp.bfloat16)] * 3
        + [jax.ShapeDtypeStruct((every, 2, 512), jnp.float32), jax.ShapeDtypeStruct((every, 2, 256), jnp.float32)],
        compiler_params=pltpu.CompilerParams(vmem_limit_bytes=60 * 2**20),
        cost_estimate=pl.CostEstimate(flops=4 * 10**9, bytes_accessed=16 * 2**20, transcendentals=6 * 10**6),
    )(lo, nb, q, k, v, do, ctx, lse, segq, segk, w)


def seg_arrays(seg):
    L=seg.shape[0]; nblk=L//BLK
    ids=jnp.arange(128,dtype=jnp.int32)
    segq=(seg[:,None]==ids[None,:]).astype(jnp.bfloat16)
    segk=jnp.where((seg[:,None]!=ids[None,:])&(ids[None,:]<16),-BIG,0.0).astype(jnp.bfloat16)
    sb=seg.reshape(nblk,BLK)
    first=jnp.sum((seg[None,:]<sb[:,:1]).astype(jnp.int32),axis=1)
    last=jnp.sum((seg[None,:]<=sb[:,-1:]).astype(jnp.int32),axis=1)
    lo=first//BLK
    nb=(last+BLK-1)//BLK-lo
    return segq,segk,lo.astype(jnp.int32),nb.astype(jnp.int32)

def bias_lanes(table):
    off=-(jnp.arange(512,dtype=jnp.int32)-256)
    oh=(bucket_index(off)[None,:]==jnp.arange(table.shape[0],dtype=jnp.int32)[:,None]).astype(jnp.bfloat16)
    w=lax.dot_general(table,oh,(((0,),(0,)),((),())),preferred_element_type=jnp.float32)
    return w.reshape(-1,2,512)

def table_grad(near,far,buckets):
    off=-(jnp.arange(512,dtype=jnp.int32)-256)
    oh=(bucket_index(off)[:,None]==jnp.arange(buckets,dtype=jnp.int32)[None,:]).astype(jnp.float32)
    n=jnp.einsum("hx,xb->bh",near.reshape(-1,512),oh,precision=lax.Precision.HIGHEST)
    f=far.reshape(-1,2,128).sum(-1)
    ids=jnp.arange(buckets,dtype=jnp.int32)[:,None]
    return n+jnp.where(ids==15,f[None,:,0],0)+jnp.where(ids==31,f[None,:,1],0)

TILE=256
def gelu_parts(x):
    c=0.7978845608028654
    x2=x*x
    t=jnp.tanh(x*(c+(c*0.044715)*x2))
    half=0.5*(1.0+t)
    slope=half+0.5*x*(1.0-t*t)*(c+(3*c*0.044715)*x2)
    return x*half,slope

def expert_kernel(count, parts, *refs):
    rows=refs[:count]; cots=refs[count:2*count]
    wi_refs=refs[2*count:2*count+parts]; wo_refs=refs[2*count+parts:2*count+2*parts]
    refs=refs[2*count+2*parts:]
    outs=refs[:count]; act_ref,db_ref,dg_ref=refs[count:count+3]
    x_ref,c_ref,wi_buf,wo_buf,acc_ref,dga_ref,act_buf,db_buf,w_sem,o_sem=refs[count+3:]
    block=wi_refs[0].shape[1]
    per=block//TILE
    total=parts*per
    for k in range(parts):
        pltpu.make_async_copy(wi_refs[k],wi_buf.at[k],w_sem.at[0,k]).start()
        pltpu.make_async_copy(wo_refs[k],wo_buf.at[k],w_sem.at[1,k]).start()
    first=0
    for i in range(count):
        n=rows[i].shape[0]
        x_ref[first:first+n,:]=rows[i][...]
        c_ref[first:first+n,:]=cots[i][...]
        first+=n
    acc_ref[...]=jnp.zeros_like(acc_ref)
    dga_ref[...]=jnp.zeros_like(dga_ref)
    def out_copies(step,slot):
        cols=pl.ds(pl.multiple_of(step*TILE,TILE),TILE)
        return (pltpu.make_async_copy(act_buf.at[slot],act_ref.at[:,cols],o_sem.at[0,slot]),
                pltpu.make_async_copy(db_buf.at[slot],db_ref.at[:,cols],o_sem.at[1,slot]))
    for k in range(parts):
        pltpu.make_async_copy(wi_refs[k],wi_buf.at[k],w_sem.at[0,k]).wait()
        pltpu.make_async_copy(wo_refs[k],wo_buf.at[k],w_sem.at[1,k]).wait()
        def body(c,_):
            step=k*per+c
            slot=lax.rem(step,2)
            @pl.when(step>=2)
            def _():
                for cp in out_copies(step-2,slot): cp.wait()
            cols=pl.ds(pl.multiple_of(c*TILE,TILE),TILE)
            wi=wi_buf[k,:,cols]
            wo=wo_buf[k,cols,:]
            before=dot_nn(x_ref[...],wi)
            up=dot_nt(c_ref[...],wo)
            active,slope=gelu_parts(before)
            prod=active*up
            dga_ref[...]+=prod[:,:128]+prod[:,128:]
            act_buf[slot]=active.astype(jnp.bfloat16)
            db=(up*slope).astype(jnp.bfloat16)
            db_buf[slot]=db
            acc_ref[...]+=dot_nt(db,wi)
            for cp in out_copies(step,slot): cp.start()
            return 0
        lax.fori_loop(0,per,body,0)
    first=0
    for i in range(count):
        n=rows[i].shape[0]
        outs[i][...]=acc_ref[first:first+n,:].astype(jnp.bfloat16)
        first+=n
    ones=jnp.ones((8,128),jnp.bfloat16)
    sums=dga_ref[...]
    hi=sums.astype(jnp.bfloat16)
    rest=sums-hi.astype(jnp.float32)
    mid=rest.astype(jnp.bfloat16)
    low=(rest-mid.astype(jnp.float32)).astype(jnp.bfloat16)
    dg_ref[...]=dot_nt(ones,hi)+dot_nt(ones,mid)+dot_nt(ones,low)
    for step in (total-2,total-1):
        for cp in out_copies(step,step%2): cp.wait()

def expert_half(rows,cots,w_ins,w_outs):
    count=len(rows); parts=len(w_ins)
    width,block=w_ins[0].shape
    R=sum(r.shape[0] for r in rows)
    vm=pl.BlockSpec(memory_space=pltpu.VMEM); hb=pl.BlockSpec(memory_space=pl.ANY)
    outs=pl.pallas_call(functools.partial(expert_kernel,count,parts),
        in_specs=[vm]*(2*count)+[hb]*(2*parts),
        out_specs=[vm]*count+[hb,hb,vm],
        out_shape=[jax.ShapeDtypeStruct(r.shape,jnp.bfloat16) for r in rows]+[jax.ShapeDtypeStruct((R,parts*block),jnp.bfloat16)]*2+[jax.ShapeDtypeStruct((8,R),jnp.float32)],
        scratch_shapes=[pltpu.VMEM((R,width),jnp.bfloat16)]*2+[pltpu.VMEM((parts,width,block),jnp.bfloat16),pltpu.VMEM((parts,block,width),jnp.bfloat16),
            pltpu.VMEM((R,width),jnp.float32),pltpu.VMEM((R,128),jnp.float32),pltpu.VMEM((2,R,TILE),jnp.bfloat16),pltpu.VMEM((2,R,TILE),jnp.bfloat16),
            pltpu.SemaphoreType.DMA((2,parts)),pltpu.SemaphoreType.DMA((2,2))],
        compiler_params=pltpu.CompilerParams(vmem_limit_bytes=48*2**20),
        cost_estimate=pl.CostEstimate(flops=6*R*width*parts*block,bytes_accessed=20*2**20,transcendentals=R*parts*block))(*rows,*cots,*w_ins,*w_outs)
    return outs[:count],outs[count],outs[count+1],outs[count+2][0]

MESH = pl.DeviceIdType.MESH


def shard_peer(bit):
    return (lax.axis_index("expert"), lax.axis_index("shard") ^ bit)


def expert_peer(bit):
    return (lax.axis_index("expert") ^ bit, lax.axis_index("shard"))


def greet(peers):
    barrier = pltpu.get_barrier_semaphore()
    for peer in peers:
        pl.semaphore_signal(barrier, inc=1, device_id=peer, device_id_type=MESH)
    pl.semaphore_wait(barrier, len(peers))


def send(src, dst, send_sem, recv_sem, peer):
    copy = pltpu.make_async_remote_copy(
        src_ref=src, dst_ref=dst, send_sem=send_sem, recv_sem=recv_sem, device_id=peer, device_id_type=MESH
    )
    copy.start()
    return copy


def columns(line, block):
    return jnp.broadcast_to(line[:, block * 128 : (block + 1) * 128], (128, 128)).T


def project_kernel(
    x_in, small_in, q_in, k_in, v_in, o_in,
    q_ref, k_ref, v_ref, normed_ref, small_ref, all_ref,
    x_ref, small_buf, w_buf, unit_ref,
    sem_send, sem_recv, sem_own, sem_out, sem_load,
):
    shard = lax.axis_index("shard")
    own = q_in.shape[0]
    load = pltpu.make_async_copy(x_in, x_ref, sem_load.at[0])
    load.start()

    def rows(bit):
        return pl.ds(pl.multiple_of((shard ^ bit) * own, 64), own)

    ins = [small_in, q_in, k_in, v_in, o_in]
    bufs = [small_buf] + [w_buf.at[i] for i in range(4)]
    count = len(ins)
    kept = []
    for i in range(count):
        copy = pltpu.make_async_copy(ins[i], bufs[i].at[rows(0)], sem_own.at[i])
        copy.start()
        kept.append(copy)
    greet([shard_peer(1), shard_peer(2)])
    far, near, passed = [], [], [None] * count
    for i in range(count):
        far.append(send(ins[i], bufs[i].at[rows(0)], sem_send.at[0, i], sem_recv.at[0, i], shard_peer(2)))
    for i in range(count):
        near.append(send(ins[i], bufs[i].at[rows(0)], sem_send.at[1, i], sem_recv.at[1, i], shard_peer(1)))
    length, width = x_ref.shape
    tile = 512

    def unit(t, _):
        r = pl.ds(pl.multiple_of(t * tile, tile), tile)
        x = x_ref[r, :].astype(jnp.float32)
        unit_ref[r, :] = x * lax.rsqrt(jnp.mean(x * x, axis=-1, keepdims=True) + 1e-6)
        return 0

    def hop(i):
        far[i].wait_recv()
        here = bufs[i].at[rows(2)]
        passed[i] = send(here, here, sem_send.at[2, i], sem_recv.at[2, i], shard_peer(1))

    def finish(i):
        kept[i].wait()
        near[i].wait_recv()
        passed[i].wait_recv()

    load.wait()
    lax.fori_loop(0, length // tile, unit, 0)
    hop(0)
    hop(1)
    finish(0)
    small = small_buf[...]
    small_ref[...] = small
    gain = jnp.concatenate(
        [small[c * 128 : (c + 1) * 128, :].astype(jnp.float32).T[0:1] for c in range(width // 128)], axis=1
    )

    def norm(t, _):
        r = pl.ds(pl.multiple_of(t * tile, tile), tile)
        normed_ref[r, :] = (unit_ref[r, :] * gain).astype(jnp.bfloat16)
        return 0

    lax.fori_loop(0, length // tile, norm, 0)
    outs = []

    def project_one(i, out):
        finish(i)
        copy = pltpu.make_async_copy(w_buf.at[i - 1], all_ref.at[i - 1], sem_out.at[i - 1])
        copy.start()
        outs.append(copy)

        def run(t, _):
            r = pl.ds(pl.multiple_of(t * tile, tile), tile)
            y = dot_nn(normed_ref[r, :], w_buf[i - 1]).astype(jnp.bfloat16)
            if i == 1:
                y = (y.astype(jnp.float32) * HEAD_DIM**-0.5).astype(jnp.bfloat16)
            out[r, :] = y
            return 0

        lax.fori_loop(0, length // tile, run, 0)

    project_one(1, q_ref)
    hop(2)
    project_one(2, k_ref)
    hop(3)
    project_one(3, v_ref)
    hop(4)
    finish(4)
    copy = pltpu.make_async_copy(w_buf.at[3], all_ref.at[3], sem_out.at[3])
    copy.start()
    outs.append(copy)
    for c in outs:
        c.wait()
    for c in far + near + passed:
        c.wait_send()


def project(x, small, weights):
    length, width = x.shape
    vm = pl.BlockSpec(memory_space=pltpu.VMEM)
    hb = pl.BlockSpec(memory_space=pl.ANY)
    bf = jnp.bfloat16
    shape = jax.ShapeDtypeStruct
    return pl.pallas_call(
        project_kernel,
        in_specs=[hb] * 6,
        out_specs=[vm] * 5 + [hb],
        out_shape=[shape((length, width), bf)] * 4 + [shape((width, 128), bf), shape((4, width, width), bf)],
        scratch_shapes=[
            pltpu.VMEM((length, width), bf),
            pltpu.VMEM((width, 128), bf),
            pltpu.VMEM((4, width, width), bf),
            pltpu.VMEM((length, width), jnp.float32),
            pltpu.SemaphoreType.DMA((3, 5)),
            pltpu.SemaphoreType.DMA((3, 5)),
            pltpu.SemaphoreType.DMA((5,)),
            pltpu.SemaphoreType.DMA((4,)),
            pltpu.SemaphoreType.DMA((1,)),
        ],
        compiler_params=pltpu.CompilerParams(collective_id=0, has_side_effects=True, vmem_limit_bytes=62 * 2**20),
        cost_estimate=pl.CostEstimate(flops=6 * 10**9, bytes_accessed=20 * 2**20, transcendentals=0),
    )(x, small, *weights)


def slot_kernel(cap, route, order, cot, place_ref, cells_ref):
    length = cot.shape[0]
    keys = (route[...] * length + order[...]).astype(jnp.float32)
    starts = (route[...] * length).astype(jnp.float32)
    blocks = length // 128
    sides = [columns(keys, b) for b in range(blocks)]
    slots = []
    for t in range(blocks):
        s = slice(t * 128, (t + 1) * 128)
        sums = sum((c < keys[:, s]).astype(jnp.float32) - (c < starts[:, s]).astype(jnp.float32) for c in sides)
        slots.append(jnp.sum(sums, axis=0, keepdims=True))
    slot = jnp.concatenate(slots, axis=1).astype(jnp.int32)
    place = jnp.where(slot < cap, route[...] * cap + slot, -1)
    place_ref[...] = place
    step = 640
    for t in range(cells_ref.shape[0] // step):
        ids = lax.broadcasted_iota(jnp.int32, (step, length), 0) + t * step
        pick = (ids == place).astype(jnp.float32).astype(jnp.bfloat16)
        cells_ref[t * step : (t + 1) * step, :] = dot_nn(pick, cot[...]).astype(jnp.bfloat16)


def find_slots(route, order, cot, cells, cap):
    length, width = cot.shape
    vm = pl.BlockSpec(memory_space=pltpu.VMEM)
    return pl.pallas_call(
        functools.partial(slot_kernel, cap),
        in_specs=[vm] * 3,
        out_specs=[vm] * 2,
        out_shape=[jax.ShapeDtypeStruct((1, length), jnp.int32), jax.ShapeDtypeStruct((cells, width), jnp.bfloat16)],
        compiler_params=pltpu.CompilerParams(vmem_limit_bytes=62 * 2**20),
        cost_estimate=pl.CostEstimate(flops=2 * 10**9, bytes_accessed=4 * 2**20, transcendentals=0),
    )(route, order, cot)


def gate_columns(line, count, width):
    column = jnp.broadcast_to(line, (128, 256)).T[:count]
    return jnp.concatenate([column] * (width // 128), axis=1)


def experts_kernel(
    size, cap, tile,
    rows_in, gate_in, cot_in, inner_own, outer_own, inner_far,
    back_out, dgate_out, inner_out, outer_out, other_out, result_out,
    rows, gates, cots, weights, active, d_before, total, d_gate, back, d_gates, back_in, d_gates_in,
    gated_t, g_send, g_recv, far_recv, stage, result,
    w_sem, wr_sem, row_send, row_recv, gate_send, gate_recv, back_send, back_recv, dg_send, dg_recv,
    g_sem_send, g_sem_recv, cot_sem, out_sem, res_sem, back_sem, dgb_sem,
):
    width = weights.shape[2]
    block = weights.shape[3]
    per = block // tile
    group = 2
    count = group * cap
    me = lax.axis_index("expert")

    def part(k):
        return pl.ds(k * cap, cap)

    local = [
        pltpu.make_async_copy(inner_own, weights.at[0, 0], w_sem.at[0]),
        pltpu.make_async_copy(outer_own, weights.at[0, 1], w_sem.at[1]),
        pltpu.make_async_copy(inner_far, weights.at[2, 0], w_sem.at[2]),
        pltpu.make_async_copy(rows_in.at[me], rows.at[part(0)], w_sem.at[3]),
        pltpu.make_async_copy(gate_in.at[me], gates.at[0], w_sem.at[4]),
    ]
    local += [pltpu.make_async_copy(cot_in.at[me ^ k], cots.at[part(k)], cot_sem.at[k]) for k in range(size)]
    for c in local:
        c.start()
    greet([expert_peer(k) for k in range(1, size)] + [shard_peer(1), shard_peer(2)])
    sent = []
    arrive = {}
    outer_far = send(outer_own, weights.at[2, 1], wr_sem.at[0, 0], wr_sem.at[1, 0], shard_peer(2))

    def dispatch(k):
        arrive[k] = [
            send(gate_in.at[me ^ k], gates.at[k], gate_send.at[k], gate_recv.at[k], expert_peer(k)),
            send(rows_in.at[me ^ k], rows.at[part(k)], row_send.at[k], row_recv.at[k], expert_peer(k)),
        ]
        sent.append(arrive[k][0])

    for k in (4, 5, 6, 7, 2, 3, 1):
        dispatch(k)
    moved = [
        send(inner_own, weights.at[1, 0], wr_sem.at[0, 1], wr_sem.at[1, 1], shard_peer(1)),
        send(outer_own, weights.at[1, 1], wr_sem.at[0, 2], wr_sem.at[1, 2], shard_peer(1)),
        send(inner_far, weights.at[3, 0], wr_sem.at[0, 3], wr_sem.at[1, 3], shard_peer(1)),
    ]
    sent += moved + [outer_far]
    d_gates[...] = jnp.zeros_like(d_gates)
    for c in local:
        c.wait()
    for c in moved:
        c.wait_recv()
    ones = jnp.ones((8, 128), jnp.bfloat16)
    returned = {}
    groups = size // group

    def arrived(g):
        for k in range(group * g, group * (g + 1)):
            if k:
                for c in arrive[k]:
                    c.wait_recv()

    def forward_back(g, spot, first, last):
        mine = slice(g * count, (g + 1) * count)
        here = slice(spot * count, (spot + 1) * count)
        if first == 0:
            total[here, :] = jnp.zeros((count, width), jnp.float32)
            d_gate[here, :] = jnp.zeros((count, 128), jnp.float32)

        def step(t, _):
            kk = t // per
            cols = pl.ds(pl.multiple_of(lax.rem(t, per) * tile, tile), tile)
            where = pl.ds(pl.multiple_of(t * tile, tile), tile)
            wi = weights[kk, 0, :, cols]
            wo = weights[kk, 1, cols, :]
            before = dot_nn(rows[mine, :], wi)
            up = dot_nt(cots[mine, :], wo)
            value, slope = gelu_parts(before)
            prod = value * up
            d_gate[here, :] += sum(prod[:, c * 128 : (c + 1) * 128] for c in range(tile // 128))
            active[mine, where] = value.astype(jnp.bfloat16)
            db = (up * slope).astype(jnp.bfloat16)
            d_before[mine, where] = db
            total[here, :] += dot_nt(db, wi)
            return 0

        lax.fori_loop(first * per, last * per, step, 0)

    def give_back(g, spot):
        here = slice(spot * count, (spot + 1) * count)
        back[g * count : (g + 1) * count, :] = total[here, :].astype(jnp.bfloat16)
        for k in range(group * g, group * (g + 1)):
            start = spot * count + (k - group * g) * cap
            sums = d_gate[start : start + cap, :]
            hi = sums.astype(jnp.bfloat16)
            rest = sums - hi.astype(jnp.float32)
            mid = rest.astype(jnp.bfloat16)
            low = (rest - mid.astype(jnp.float32)).astype(jnp.bfloat16)
            d_gates[k, :, 0:cap] = dot_nt(ones, hi) + dot_nt(ones, mid) + dot_nt(ones, low)
            if k:
                returned[k] = [
                    send(d_gates.at[k], d_gates_in.at[k], dg_send.at[k], dg_recv.at[k], expert_peer(k)),
                    send(back.at[part(k)], back_in.at[part(k)], back_send.at[k], back_recv.at[k], expert_peer(k)),
                ]
                sent.extend(returned[k])

    arrived(0)
    forward_back(0, 0, 0, 2)
    arrived(1)
    forward_back(1, 1, 0, 2)
    outer_far.wait_recv()
    passed = send(weights.at[2, 1], weights.at[3, 1], wr_sem.at[0, 4], wr_sem.at[1, 4], shard_peer(1))
    sent.append(passed)
    passed.wait_recv()
    arrived(2)
    forward_back(2, 2, 0, 4)
    give_back(2, 2)
    forward_back(0, 0, 2, 4)
    give_back(0, 0)
    forward_back(1, 1, 2, 4)
    give_back(1, 1)
    arrived(3)
    forward_back(3, 2, 0, 4)
    give_back(3, 2)
    for k in range(size):
        span = slice(k * cap, (k + 1) * cap)
        column = gate_columns(gates[k, 0:1, :], cap, width)
        cots[span, :] = (cots[span, :].astype(jnp.float32) * column).astype(jnp.bfloat16)
        result[span, :] = (rows[span, :].astype(jnp.float32) * column).astype(jnp.bfloat16)
    every = size * cap
    for c in range(width // 128):
        for r in range(every // 128):
            gated_t[c * 128 : (c + 1) * 128, r * 128 : (r + 1) * 128] = (
                result[r * 128 : (r + 1) * 128, c * 128 : (c + 1) * 128].astype(jnp.float32).T.astype(jnp.bfloat16)
            )
    strip = block

    def inner(kk, out):
        return dot_nn(gated_t[out, :], d_before[:, kk * block : (kk + 1) * block])

    def outer(kk, out, t):
        return dot_tn(active[:, pl.ds(pl.multiple_of(kk * block + t * strip, strip), strip)], cots[...])

    def strips(body):
        def run(t, _):
            body(pl.ds(pl.multiple_of(t * strip, strip), strip), t)
            return 0

        lax.fori_loop(0, block // strip, run, 0)

    def chunk(h, kk, out, t):
        return inner(kk, out) if h == 0 else outer(kk, out, t)

    finals = []
    far_swap = None
    for h in range(2):
        shared = []
        for n, kk in enumerate((3, 1)):

            def give(out, t):
                g_send[h, n, out, :] = chunk(h, kk, out, t).astype(jnp.bfloat16)

            strips(give)
            c = send(g_send.at[h, n], g_recv.at[h, n], g_sem_send.at[h, n], g_sem_recv.at[h, n], shard_peer(1))
            shared.append(c)
        shared[0].wait_recv()
        shared[0].wait_send()

        def other(out, t):
            g_send[h, 0, out, :] = (chunk(h, 2, out, t) + g_recv[h, 0, out, :].astype(jnp.float32)).astype(jnp.bfloat16)

        strips(other)
        if h == 0:
            far_swap = send(g_send.at[0, 0], far_recv, g_sem_send.at[0, 2], g_sem_recv.at[0, 2], shard_peer(2))
            sent.append(far_swap)
        else:
            c = pltpu.make_async_copy(g_send.at[1, 0], other_out, out_sem.at[0])
            c.start()
            finals.append(c)
        shared[1].wait_recv()
        sent.append(shared[1])

        def keep(out, t):
            stage[h, out, :] = chunk(h, 0, out, t) + g_recv[h, 1, out, :].astype(jnp.float32)

        strips(keep)
    c = pltpu.make_async_copy(stage.at[1], outer_out, out_sem.at[1])
    c.start()
    finals.append(c)

    def produce(r, _):
        span = pl.ds(pl.multiple_of(r * 4 * cap, 16), 4 * cap)
        y = sum(dot_nn(active[span, kk * block : (kk + 1) * block], weights[kk, 1]) for kk in range(4))
        result[span, :] = y.astype(jnp.bfloat16)
        return 0

    lax.fori_loop(0, size // 4, produce, 0)
    for k in range(size):
        c = pltpu.make_async_copy(result.at[part(k)], result_out.at[me ^ k], res_sem.at[k])
        c.start()
        finals.append(c)
    back_in[part(0), :] = back[part(0), :]
    d_gates_in[0] = d_gates[0]
    far_swap.wait_recv()

    def join(out, t):
        stage[0, out, :] += far_recv[out, :].astype(jnp.float32)

    strips(join)
    c = pltpu.make_async_copy(stage.at[0], inner_out, out_sem.at[2])
    c.start()
    finals.append(c)
    for k in range(size):
        if k:
            for c in returned[k]:
                c.wait_recv()
        for c in (
            pltpu.make_async_copy(back_in.at[part(k)], back_out.at[me ^ k], back_sem.at[k]),
            pltpu.make_async_copy(d_gates_in.at[k], dgate_out.at[me ^ k], dgb_sem.at[k]),
        ):
            c.start()
            finals.append(c)
    for c in finals:
        c.wait()
    for k in range(1, size):
        arrive[k][1].wait_send()
    for c in sent:
        c.wait_send()


def run_experts(rows, gates, cots, inner_own, outer_own, inner_far):
    size, cap, width = rows.shape
    block = inner_own.shape[1]
    bf = jnp.bfloat16
    f32 = jnp.float32
    every = size * cap
    hb = pl.BlockSpec(memory_space=pl.ANY)
    vm = pltpu.VMEM
    dma = pltpu.SemaphoreType.DMA
    shape = jax.ShapeDtypeStruct
    return pl.pallas_call(
        functools.partial(experts_kernel, size, cap, block),
        in_specs=[hb] * 6,
        out_specs=[hb] * 6,
        out_shape=[
            shape((size, cap, width), bf),
            shape((size, 8, 256), f32),
            shape((width, block), f32),
            shape((block, width), f32),
            shape((block, width), bf),
            shape((size, cap, width), bf),
        ],
        scratch_shapes=[
            vm((every, width), bf),
            vm((size, 8, 256), f32),
            vm((every, width), bf),
            vm((4, 2, width, block), bf),
            vm((every, 4 * block), bf),
            vm((every, 4 * block), bf),
            vm((6 * cap, width), f32),
            vm((6 * cap, 128), f32),
            vm((every, width), bf),
            vm((size, 8, 256), f32),
            vm((every, width), bf),
            vm((size, 8, 256), f32),
            vm((width, every), bf),
            vm((2, 2, width, block), bf),
            vm((2, 2, width, block), bf),
            vm((width, block), bf),
            vm((2, width, block), f32),
            vm((every, width), bf),
            dma((5,)),
            dma((2, 5)),
        ]
        + [dma((size,))] * 8
        + [dma((2, 3)), dma((2, 3)), dma((size,)), dma((3,)), dma((size,)), dma((size,)), dma((size,))],
        compiler_params=pltpu.CompilerParams(collective_id=1, has_side_effects=True, vmem_limit_bytes=62 * 2**20),
        cost_estimate=pl.CostEstimate(flops=36 * 10**9, bytes_accessed=30 * 2**20, transcendentals=4 * 10**6),
    )(rows, gates, cots, inner_own, outer_own, inner_far)


def turned(small, width):
    return jnp.concatenate(
        [small[c * 128 : (c + 1) * 128, :].astype(jnp.float32).T for c in range(width // 128)], axis=1
    )


def three_parts(line):
    hi = line.astype(jnp.bfloat16)
    rest = line - hi.astype(jnp.float32)
    mid = rest.astype(jnp.bfloat16)
    low = rest - mid.astype(jnp.float32)
    none = jnp.zeros((5, line.shape[1]), jnp.float32)
    parts = jnp.concatenate([hi.astype(jnp.float32), mid.astype(jnp.float32), low, none], axis=0)
    return parts.astype(jnp.bfloat16)


def pick_cells(place, first, tile, cells):
    out = []
    for b in range(first // 128, (first + tile) // 128):
        column = columns(place, b)
        lane = lax.broadcasted_iota(jnp.int32, (128, 128), 1).astype(jnp.float32)
        out.append(
            jnp.concatenate([(column == lane + 128.0 * j).astype(jnp.float32) for j in range(cells // 128)], axis=1)
        )
    return jnp.concatenate(out, axis=0).astype(jnp.bfloat16)


def spread_column(line, first, tile, width):
    return jnp.concatenate(
        [
            jnp.concatenate([columns(line, b)] * (width // 128), axis=1)
            for b in range(first // 128, (first + tile) // 128)
        ],
        axis=0,
    )


def route_kernel(
    cap, context_in, tokens_in, weights_in, small, route, place,
    resid_out, cells_out, gate_out, probs_out,
    context, tokens, w_out, normed, sems,
):
    length, width = normed.shape
    experts = probs_out.shape[0]
    loads = [
        pltpu.make_async_copy(weights_in.at[3], w_out, sems.at[0]),
        pltpu.make_async_copy(context_in, context, sems.at[1]),
        pltpu.make_async_copy(tokens_in, tokens, sems.at[2]),
    ]
    for c in loads:
        c.start()
    lines = turned(small, width)
    gain = lines[1:2]
    for c in loads:
        c.wait()
    tile = 512
    for t in range(length // tile):
        r = slice(t * tile, (t + 1) * tile)
        resid = tokens[r, :].astype(jnp.float32) + dot_nn(context[r, :], w_out[...])
        resid_out[r, :] = resid
        scale = lax.rsqrt(jnp.mean(resid * resid, axis=-1, keepdims=True) + 1e-6)
        normed[r, :] = (resid * scale * gain).astype(jnp.bfloat16)
    logits = dot_nt(lines.astype(jnp.bfloat16), normed[...])[2 : 2 + experts]
    top = jnp.exp(logits - jnp.max(logits, axis=0, keepdims=True))
    probs = top / jnp.sum(top, axis=0, keepdims=True)
    probs_out[...] = probs
    which = lax.broadcasted_iota(jnp.int32, probs.shape, 0)
    gate = jnp.sum(jnp.where(which == route[...], probs, 0.0), axis=0, keepdims=True)
    parts = three_parts(gate)
    gate_out[...] = jnp.zeros_like(gate_out)
    for k in range(experts):
        ids = lax.broadcasted_iota(jnp.int32, (cap, length), 0) + k * cap
        pick = (ids == place[...]).astype(jnp.float32).astype(jnp.bfloat16)
        cells_out[k] = dot_nn(pick, normed[...]).astype(jnp.bfloat16)
        found = dot_nt(parts, pick)
        gate_out[k, :, 0:cap] = jnp.broadcast_to(jnp.sum(found, axis=0, keepdims=True), (8, cap))


def run_route(context, tokens, weights, small, route, place, experts, cap):
    length, width = tokens.shape
    bf, f32 = jnp.bfloat16, jnp.float32
    vm = pl.BlockSpec(memory_space=pltpu.VMEM)
    hb = pl.BlockSpec(memory_space=pl.ANY)
    shape = jax.ShapeDtypeStruct
    return pl.pallas_call(
        functools.partial(route_kernel, cap),
        in_specs=[hb] * 3 + [vm] * 3,
        out_specs=[vm] * 4,
        out_shape=[
            shape((length, width), f32),
            shape((experts, cap, width), bf),
            shape((experts, 8, 256), f32),
            shape((experts, length), f32),
        ],
        scratch_shapes=[
            pltpu.VMEM((length, width), bf),
            pltpu.VMEM((length, width), bf),
            pltpu.VMEM((width, width), bf),
            pltpu.VMEM((length, width), bf),
            pltpu.SemaphoreType.DMA((3,)),
        ],
        compiler_params=pltpu.CompilerParams(vmem_limit_bytes=62 * 2**20),
        cost_estimate=pl.CostEstimate(flops=4 * 10**9, bytes_accessed=16 * 2**20, transcendentals=0),
    )(context, tokens, weights, small, route, place)


def unroute_kernel(
    cap, back_in, d_gate_in, resid_in, cot_in, weights_in, context_in, small, route, place, probs,
    d_context, d_resid, extra, keep_out, grad_out,
    back, resid, cot, w_out, context, d_branch, sems,
):
    length, width = resid.shape
    experts = probs.shape[0]
    cells = experts * cap
    loads = [pltpu.make_async_copy(back_in.at[k], back.at[pl.ds(k * cap, cap)], sems.at[4 + k]) for k in range(experts)]
    loads += [
        pltpu.make_async_copy(resid_in, resid, sems.at[0]),
        pltpu.make_async_copy(cot_in, cot, sems.at[1]),
        pltpu.make_async_copy(weights_in.at[3], w_out, sems.at[2]),
        pltpu.make_async_copy(context_in, context, sems.at[3]),
    ]
    for c in loads:
        c.start()
    lines = turned(small, width)
    gain = lines[1:2]
    low_lines = lines.astype(jnp.bfloat16)
    which = lax.broadcasted_iota(jnp.int32, probs.shape, 0)
    chosen = (which == route[...]).astype(jnp.float32)
    gate = jnp.sum(probs[...] * chosen, axis=0, keepdims=True)
    keep = jnp.where(place[...] >= 0, gate, 0.0)
    keep_out[...] = keep
    places = place[...].astype(jnp.float32)
    parts = three_parts(jnp.concatenate([d_gate_in[k, 0:1, 0:cap] for k in range(experts)], axis=1))
    for c in loads:
        c.wait()
    tile = 256
    grads = jnp.zeros((128, width), jnp.float32)
    gains = jnp.zeros((1, width), jnp.float32)
    for t in range(length // tile):
        r = slice(t * tile, (t + 1) * tile)
        pick = pick_cells(places, t * tile, tile, cells)
        d_rows = dot_nn(pick, back[...])
        d_gate = jnp.sum(dot_nt(parts, pick), axis=0, keepdims=True)
        d_logits = probs[:, r] * (chosen[:, r] - gate[:, r]) * d_gate
        padded = jnp.concatenate(
            [
                jnp.zeros((2, tile), jnp.float32),
                d_logits.astype(jnp.bfloat16).astype(jnp.float32),
                jnp.zeros((126 - experts, tile), jnp.float32),
            ],
            axis=0,
        )
        d_normed = dot_nn(padded.T.astype(jnp.bfloat16), low_lines) + spread_column(keep, t * tile, tile, width) * d_rows
        x = resid[r, :]
        scale = lax.rsqrt(jnp.mean(x * x, axis=-1, keepdims=True) + 1e-6)
        unit = x * scale
        grads = grads + dot_nn(padded.astype(jnp.bfloat16), (unit * gain).astype(jnp.bfloat16))
        gains = gains + jnp.sum(d_normed * unit, axis=0, keepdims=True)
        pulled = gain * d_normed
        out = cot[r, :].astype(jnp.float32) + scale * (
            pulled - unit * jnp.mean(unit * pulled, axis=-1, keepdims=True)
        )
        d_resid[r, :] = out
        low = out.astype(jnp.bfloat16)
        d_branch[r, :] = low
        d_context[r, :] = dot_nt(low, w_out[...]).astype(jnp.bfloat16)
    grad_out[...] = dot_tn(context[...], d_branch[...]).astype(jnp.bfloat16)
    row = lax.broadcasted_iota(jnp.int32, (128, width), 0)
    extra[...] = jnp.where(row == 1, gains, grads)


def run_unroute(back, d_gate, resid, cot, weights, context, small, route, place, probs):
    experts, cap, width = back.shape
    length = resid.shape[0]
    bf, f32 = jnp.bfloat16, jnp.float32
    vm = pl.BlockSpec(memory_space=pltpu.VMEM)
    hb = pl.BlockSpec(memory_space=pl.ANY)
    shape = jax.ShapeDtypeStruct
    return pl.pallas_call(
        functools.partial(unroute_kernel, cap),
        in_specs=[hb, vm, hb, hb, hb, hb] + [vm] * 4,
        out_specs=[vm] * 5,
        out_shape=[
            shape((length, width), bf),
            shape((length, width), f32),
            shape((128, width), f32),
            shape((1, length), f32),
            shape((width, width), bf),
        ],
        scratch_shapes=[
            pltpu.VMEM((experts * cap, width), bf),
            pltpu.VMEM((length, width), f32),
            pltpu.VMEM((length, width), bf),
            pltpu.VMEM((width, width), bf),
            pltpu.VMEM((length, width), bf),
            pltpu.VMEM((length, width), bf),
            pltpu.SemaphoreType.DMA((4 + experts,)),
        ],
        compiler_params=pltpu.CompilerParams(vmem_limit_bytes=62 * 2**20),
        cost_estimate=pl.CostEstimate(flops=4 * 10**9, bytes_accessed=18 * 2**20, transcendentals=0),
    )(back, d_gate, resid, cot, weights, context, small, route, place, probs)


class Reduction:
    def __init__(self, index, partial, near, far_send, far_recv, full, x_send, x_recv, half, z_send, z_recv, piece, result, send_sems, recv_sems):
        self.partial, self.near, self.far_send, self.far_recv = partial, near, far_send, far_recv
        self.full, self.x_send, self.x_recv, self.half = full, x_send, x_recv, half
        self.z_send, self.z_recv, self.piece, self.result = z_send, z_recv, piece, result
        self.index, self.send_sems, self.recv_sems = index, send_sems, recv_sems
        self.own = full.shape[0]
        self.width = full.shape[1]
        self.type = partial.dtype
        self.copies = {}

    def block(self, bit):
        return pl.ds(pl.multiple_of((lax.axis_index("shard") ^ bit) * self.own, self.own & -self.own), self.own)

    def half_rows(self, bit):
        rows = self.own // 2
        return pl.ds(pl.multiple_of(((lax.axis_index("expert") & 1) ^ bit) * rows, rows & -rows), rows)

    def quarter(self, step):
        j = (lax.axis_index("expert") >> 1) ^ step
        rows = self.own // 2
        if self.type == jnp.float32:
            return (pl.ds(pl.multiple_of(j * (rows // 4), 8), rows // 4), slice(None))
        return (
            pl.ds(pl.multiple_of((j >> 1) * (rows // 2), 16), rows // 2),
            pl.ds(pl.multiple_of((j & 1) * (self.width // 2), 128), self.width // 2),
        )

    def go(self, slot, src, dst, peer):
        self.copies[slot] = send(src, dst, self.send_sems.at[self.index, slot], self.recv_sems.at[self.index, slot], peer)

    def core(self):
        self.go(0, self.partial.at[self.block(3)], self.near.at[1], shard_peer(1))
        self.go(1, self.partial.at[self.block(1)], self.near.at[0], shard_peer(1))

    def y(self):
        self.copies[0].wait_recv()
        other = self.partial[self.block(2), :].astype(jnp.float32) + self.near[1].astype(jnp.float32)
        self.far_send[...] = other.astype(self.type)
        self.go(2, self.far_send, self.far_recv, shard_peer(2))
        self.copies[1].wait_recv()
        self.full[...] = self.partial[self.block(0), :].astype(jnp.float32) + self.near[0].astype(jnp.float32)

    def x(self):
        self.copies[2].wait_recv()
        self.full[...] += self.far_recv[...].astype(jnp.float32)
        self.x_send[...] = self.full[self.half_rows(1), :].astype(self.type)
        self.go(3, self.x_send, self.x_recv, expert_peer(1))

    def z(self):
        self.copies[3].wait_recv()
        self.half[...] = self.own_half() + self.x_recv[...].astype(jnp.float32)
        self.z_send[...] = self.half[...].astype(self.type)
        for step in (2, 3, 1):
            self.go(3 + step, self.z_send.at[self.quarter(step)], self.z_recv.at[step - 1], expert_peer(2 * step))

    def own_half(self):
        return self.full[self.half_rows(0), :]

    def spread(self):
        for step in (1, 2, 3):
            self.copies[3 + step].wait_recv()
        rows, cols = self.quarter(0)
        total = self.half[rows, cols]
        for step in (1, 2, 3):
            total = total + self.z_recv[step - 1].astype(jnp.float32)
        self.piece[...] = total.astype(self.type)
        target = self.place()
        for step in (2, 3, 1):
            self.go(6 + step, self.piece, self.result.at[target], expert_peer(2 * step))
        self.result[target] = self.piece[...]

    def place(self):
        j = lax.axis_index("expert") >> 1
        first = (lax.axis_index("expert") & 1) * (self.own // 2)
        rows = self.own // 2
        if self.type == jnp.float32:
            return (pl.ds(pl.multiple_of(first + j * (rows // 4), 8), rows // 4), slice(None))
        return (
            pl.ds(pl.multiple_of(first + (j >> 1) * (rows // 2), 16), rows // 2),
            pl.ds(pl.multiple_of((j & 1) * (self.width // 2), 128), self.width // 2),
        )

    def cross(self):
        for step in (1, 2, 3):
            self.copies[6 + step].wait_recv()
        self.go(10, self.result.at[self.half_rows(0)], self.result.at[self.half_rows(0)], expert_peer(1))

    def finish(self, out):
        self.copies[10].wait_recv()
        out[...] = self.result[...].astype(jnp.float32)

    def drain(self):
        for c in self.copies.values():
            c.wait_send()


class Crossed(Reduction):
    other = None

    def y(self):
        rows = self.own // 2
        self.copies[0].wait_recv()
        self.other[...] = self.partial[self.block(2), :].astype(jnp.float32) + self.near[1].astype(jnp.float32)
        self.far_send[rows:, :] = self.other[self.half_rows(1), :].astype(self.type)
        self.copies[1].wait_recv()
        self.full[...] = self.partial[self.block(0), :].astype(jnp.float32) + self.near[0].astype(jnp.float32)
        self.far_send[:rows, :] = self.full[self.half_rows(1), :].astype(self.type)
        self.go(2, self.far_send, self.far_recv, expert_peer(1))

    def x(self):
        rows = self.own // 2
        self.copies[2].wait_recv()
        other = self.other[self.half_rows(0), :] + self.far_recv[rows:, :].astype(jnp.float32)
        self.x_send[...] = other.astype(self.type)
        self.go(3, self.x_send, self.x_recv, shard_peer(2))

    def own_half(self):
        return self.full[self.half_rows(0), :] + self.far_recv[: self.own // 2, :].astype(jnp.float32)


def place_table(near, far, ps, own, heads):
    buckets = 32
    wide = near.shape[2]
    offset = wide // 2 - lax.broadcasted_iota(jnp.int32, (wide, buckets), 0)
    onehot = (bucket_index(offset) == lax.broadcasted_iota(jnp.int32, (wide, buckets), 1)).astype(jnp.float32)
    sums = jnp.concatenate([near[j] for j in range(near.shape[0])], axis=0)
    table = lax.dot_general(
        sums, onehot, (((1,), (0,)), ((), ())), preferred_element_type=jnp.float32, precision=lax.Precision.HIGHEST
    )
    ends = jnp.concatenate([far[j] for j in range(far.shape[0])], axis=0)
    low = jnp.sum(ends[:, :128], axis=1, keepdims=True)
    high = jnp.sum(ends[:, 128:], axis=1, keepdims=True)
    which = lax.broadcasted_iota(jnp.int32, (heads, buckets), 1)
    table = table + jnp.where(which == 15, low, 0.0) + jnp.where(which == 31, high, 0.0)
    part = buckets // 4
    square = jnp.concatenate([table, jnp.zeros((heads, 128 - buckets), jnp.float32)], axis=1)
    square = jnp.concatenate([jnp.zeros((128 - heads, 128), jnp.float32), square], axis=0).T
    lane = lax.broadcasted_iota(jnp.int32, (part, 128), 1)
    for j in range(4):
        r = slice(j * own, j * own + part)
        ps[r, :] = jnp.where(lane >= 128 - heads, square[j * part : (j + 1) * part, :], ps[r, :])


def tail_kernel(
    heads, experts,
    normed_in, dq_in, dk_in, dv_in, p_in, weights_in, tokens_in, d_resid_in,
    cells_in, resid_in, small, extra, near_sums, far_sums, place, keep_gate,
    o_out, q_out, k_out, v_out, gain_out, gain_two_out, router_out, table_out, tokens_out, mixed_out,
    normed, dq, dk, dv, weights, tokens, d_resid, cells, resid,
    normed_t, p_ref, near, far_send, far_recv, full, x_send, x_recv, half, z_send, z_recv, piece, result, other,
    ps, s_near, s_far_send, s_far_recv, s_full, s_x_send, s_x_recv, s_half, s_z_send, s_z_recv, s_piece, s_result,
    send_sems, recv_sems, load_sems,
):
    length, width = normed.shape
    tile = 256
    loads = [
        pltpu.make_async_copy(src, dst, load_sems.at[i])
        for i, (src, dst) in enumerate(
            (
                (p_in, p_ref.at[0]),
                (weights_in.at[0:3], weights),
                (normed_in, normed),
                (dq_in, dq),
                (dk_in, dk),
                (dv_in, dv),
                (tokens_in, tokens),
                (d_resid_in, d_resid),
                (resid_in, resid),
            )
        )
    ]
    cap = cells_in.shape[1]
    loads += [
        pltpu.make_async_copy(cells_in.at[k], cells.at[pl.ds(k * cap, cap)], load_sems.at[11 + k])
        for k in range(cells_in.shape[0])
    ]
    for c in loads:
        c.start()
    greet([shard_peer(1), shard_peer(2)] + [expert_peer(k) for k in (1, 2, 4, 6)])
    work = []
    for m in range(4):
        w = (Crossed if m >= 2 else Reduction)(
            m, p_ref.at[m], near.at[m], far_send.at[m], far_recv.at[m], full.at[m], x_send.at[m], x_recv.at[m],
            half.at[m], z_send.at[m], z_recv.at[m], piece.at[m], result.at[m], send_sems, recv_sems,
        )
        w.other = other.at[m % 2]
        work.append(w)
    o, q, k, v = work
    s = Reduction(
        4, ps, s_near, s_far_send, s_far_recv, s_full, s_x_send, s_x_recv, s_half, s_z_send, s_z_recv, s_piece,
        s_result, send_sems, recv_sems,
    )

    def strips(m, make):
        p_ref[m] = make(slice(None)).astype(jnp.bfloat16)

    loads[0].wait()
    o.core()
    loads[2].wait()
    for c in range(width // 128):
        for t in range(length // 128):
            normed_t[c * 128 : (c + 1) * 128, t * 128 : (t + 1) * 128] = (
                normed[t * 128 : (t + 1) * 128, c * 128 : (c + 1) * 128].astype(jnp.float32).T.astype(jnp.bfloat16)
            )
    o.y()
    loads[3].wait()
    strips(1, lambda r: dot_nn(normed_t[r, :], dq[...]))
    q.core()
    loads[4].wait()
    strips(2, lambda r: dot_nn(normed_t[r, :], dk[...]))
    q.y()
    k.core()
    loads[5].wait()
    strips(3, lambda r: dot_nn(normed_t[r, :], dv[...]))
    v.core()
    k.y()
    head = small[...].astype(jnp.float32)
    gain = jnp.concatenate([head[c * 128 : (c + 1) * 128, :].T[0:1] for c in range(width // 128)], axis=1)
    for c in [loads[1]] + loads[6:8]:
        c.wait()

    def back(t, total):
        r = pl.ds(pl.multiple_of(t * tile, tile), tile)
        grad = dot_nt(dq[r, :], weights[0]) + dot_nt(dk[r, :], weights[1]) + dot_nt(dv[r, :], weights[2])
        x = tokens[r, :].astype(jnp.float32)
        scale = lax.rsqrt(jnp.mean(x * x, axis=-1, keepdims=True) + 1e-6)
        unit = x * scale
        pulled = grad * gain
        shift = jnp.mean(unit * pulled, axis=-1, keepdims=True)
        tokens_out[r, :] = (d_resid[r, :] + scale * (pulled - unit * shift)).astype(jnp.bfloat16)
        return total + jnp.sum(grad * unit, axis=0, keepdims=True)

    def some(first, last, total):
        return lax.fori_loop(first, last, back, total)

    def mix(t):
        r = slice(t * tile, (t + 1) * tile)
        arrived = dot_nn(pick_cells(places, t * tile, tile, cells.shape[0]), cells[...])
        mixed_out[r, :] = (resid[r, :] + spread_column(keep_gate, t * tile, tile, width) * arrived).astype(jnp.bfloat16)

    places = place[...].astype(jnp.float32)
    total = some(0, 1, jnp.zeros((1, width), jnp.float32))
    o.x()
    v.y()
    total = some(1, 3, total)
    k.x()
    total = some(3, length // tile, total)
    q.x()
    lane = lax.broadcasted_iota(jnp.int32, (128, 128), 1)
    for c in range(width // 128):
        column = jnp.broadcast_to(total[:, c * 128 : (c + 1) * 128], (128, 128)).T
        ps[c * 128 : (c + 1) * 128, :] = jnp.where(lane == 0, column, extra[:, c * 128 : (c + 1) * 128].T)
    place_table(near_sums, far_sums, ps, s.own, heads)
    s.core()
    o.z()
    k.z()
    s.y()
    for c in loads[8:]:
        c.wait()
    mix(0)
    o.spread()
    v.x()
    q.z()
    s.x()
    mix(1)
    k.spread()
    o.cross()
    v.z()
    s.z()
    mix(2)
    k.cross()
    q.spread()
    v.spread()
    s.spread()
    mix(3)
    o.finish(o_out)
    q.cross()
    v.cross()
    s.cross()
    k.finish(k_out)
    q.finish(q_out)
    v.finish(v_out)
    s.copies[10].wait_recv()
    final = s_result[...]
    pad = jnp.concatenate([final, jnp.zeros((256 - s.own, 128), jnp.float32)], axis=0)
    lines = jnp.concatenate([pad[:128, :].T, pad[128:, :].T], axis=1)
    gain_out[...] = lines[0:1, : s.own]
    gain_two_out[...] = lines[1:2, : s.own]
    router_out[...] = final[:, 2 : 2 + experts]
    table_out[...] = final[: table_out.shape[0], 128 - heads :]
    for w in work + [s]:
        w.drain()


def run_tail(
    normed, dq, dk, dv, partial, weights, tokens, d_resid, cells, resid, small, extra, near, far,
    place, keep_gate, experts, own_buckets,
):
    length, width = normed.shape
    own = width // 4
    heads = near.shape[0] * near.shape[1]
    bf = jnp.bfloat16
    f32 = jnp.float32
    vm = pltpu.VMEM
    hb = pl.BlockSpec(memory_space=pl.ANY)
    mem = pl.BlockSpec(memory_space=pltpu.VMEM)
    h = own // 2
    shape = jax.ShapeDtypeStruct
    return pl.pallas_call(
        functools.partial(tail_kernel, heads, experts),
        in_specs=[hb] * 10 + [mem] * 6,
        out_specs=[mem] * 10,
        out_shape=[shape((own, width), f32)] * 4
        + [
            shape((1, own), f32),
            shape((1, own), f32),
            shape((own, experts), f32),
            shape((own_buckets, heads), f32),
            shape((length, width), bf),
            shape((length, width), bf),
        ],
        scratch_shapes=[vm((length, width), bf)] * 4
        + [
            vm((3, width, width), bf),
            vm((length, width), bf),
            vm((length, width), f32),
            vm((cells.shape[0] * cells.shape[1], width), bf),
            vm((length, width), f32),
            vm((width, length), bf),
            vm((4, width, width), bf),
            vm((4, 2, own, width), bf),
            vm((4, own, width), bf),
            vm((4, own, width), bf),
            vm((4, own, width), f32),
            vm((4, h, width), bf),
            vm((4, h, width), bf),
            vm((4, h, width), f32),
            vm((4, h, width), bf),
            vm((4, 3, h // 2, width // 2), bf),
            vm((4, h // 2, width // 2), bf),
            vm((4, own, width), bf),
            vm((2, own, width), f32),
            vm((width, 128), f32),
            vm((2, own, 128), f32),
            vm((own, 128), f32),
            vm((own, 128), f32),
            vm((own, 128), f32),
            vm((h, 128), f32),
            vm((h, 128), f32),
            vm((h, 128), f32),
            vm((h, 128), f32),
            vm((3, h // 4, 128), f32),
            vm((h // 4, 128), f32),
            vm((own, 128), f32),
            pltpu.SemaphoreType.DMA((5, 11)),
            pltpu.SemaphoreType.DMA((5, 11)),
            pltpu.SemaphoreType.DMA((20,)),
        ],
        compiler_params=pltpu.CompilerParams(collective_id=2, has_side_effects=True, vmem_limit_bytes=62 * 2**20),
        cost_estimate=pl.CostEstimate(flops=11 * 10**9, bytes_accessed=40 * 2**20, transcendentals=0),
    )(
        normed, dq, dk, dv, partial, weights, tokens, d_resid, cells, resid, small, extra, near,
        far, place, keep_gate,
    )


def finish_kernel(count, *refs):
    ins, (mine, other), outs = refs[:count], refs[count : count + 2], refs[count + 2 : 2 * count + 2]
    total = refs[2 * count + 2]
    add_a, add_b = refs[2 * count + 3 : 2 * count + 5]
    bufs = refs[2 * count + 5 : 3 * count + 5]
    in_sems, out_sems = refs[3 * count + 5 :]
    first = [pltpu.make_async_copy(mine, add_a, in_sems.at[count]), pltpu.make_async_copy(other, add_b, in_sems.at[count + 1])]
    loads = [pltpu.make_async_copy(ins[i], bufs[i], in_sems.at[i]) for i in range(count)]
    for c in first + loads:
        c.start()
    for c in first:
        c.wait()
    add_a[...] = add_a[...] + add_b[...].astype(jnp.float32)
    stores = [pltpu.make_async_copy(add_a, total, out_sems.at[count])]
    stores[0].start()
    for i in range(count):
        loads[i].wait()
        c = pltpu.make_async_copy(bufs[i], outs[i], out_sems.at[i])
        c.start()
        stores.append(c)
    for c in stores:
        c.wait()


def run_finish(results, mine, other):
    count = len(results)
    hb = pl.BlockSpec(memory_space=pl.ANY)
    return pl.pallas_call(
        functools.partial(finish_kernel, count),
        in_specs=[hb] * (count + 2),
        out_specs=[hb] * (count + 1),
        out_shape=[jax.ShapeDtypeStruct(r.shape, r.dtype) for r in results]
        + [jax.ShapeDtypeStruct(mine.shape, jnp.float32)],
        scratch_shapes=[pltpu.VMEM(mine.shape, jnp.float32), pltpu.VMEM(other.shape, jnp.bfloat16)]
        + [pltpu.VMEM(r.shape, r.dtype) for r in results]
        + [pltpu.SemaphoreType.DMA((count + 2,)), pltpu.SemaphoreType.DMA((count + 1,))],
        compiler_params=pltpu.CompilerParams(vmem_limit_bytes=62 * 2**20),
        cost_estimate=pl.CostEstimate(flops=10**6, bytes_accessed=24 * 2**20, transcendentals=0),
    )(*results, mine, other)

EPS = 1e-06
BF = jnp.bfloat16
F32 = jnp.float32


def dot_tn(a, b):
    return lax.dot_general(a, b, (((0,), (0,)), ((), ())), preferred_element_type=F32)


def swap(value, axis, size, bit):
    return lax.ppermute(value, axis, [(i, i ^ bit) for i in range(size)])


def direct(size):
    return size == 8


def exchange(blocks):
    return lax.all_to_all(blocks, "expert", split_axis=0, concat_axis=0, tiled=True)


def gather_shards(value, size):
    if size == 4:
        far = swap(value, "shard", size, 2)
        near = swap(value, "shard", size, 1)
        return [value, near, far, swap(far, "shard", size, 1)]
    return [value] + [swap(value, "shard", size, k) for k in range(1, size)]


def reduce_shards(blocks, size):
    if size == 4:
        near1 = swap(blocks[3].astype(BF), "shard", size, 1)
        near0 = swap(blocks[1].astype(BF), "shard", size, 1)
        other = swap((blocks[2].astype(F32) + near1.astype(F32)).astype(BF), "shard", size, 2)
        return blocks[0].astype(F32) + near0.astype(F32) + other.astype(F32)
    total = blocks[0].astype(F32)
    for k in range(1, size):
        total = total + swap(blocks[k].astype(BF), "shard", size, k).astype(F32)
    return total


def experts_by_collectives(row_blocks, gate_slots, cot_blocks, inner, outer, size, shards, cap):
    inners = gather_shards(inner, shards)
    outers = gather_shards(outer, shards)
    cells, width = size * cap, row_blocks.shape[2]
    rows = exchange(row_blocks).reshape(cells, width)
    cots = cot_blocks.reshape(cells, width)
    gates = exchange(gate_slots.reshape(size, cap)).reshape(cells, 1)
    half = cells // 2
    parts = [expert_half([rows[i : i + half]], [cots[i : i + half]], inners, outers) for i in (0, half)]
    back, active, d_before, d_gate = (
        jnp.concatenate([p[0][0] if i == 0 else p[i] for p in parts], axis=0) for i in range(4)
    )
    back = exchange(back.reshape(size, cap, width)).reshape(cells, width)
    d_gate = exchange(d_gate.reshape(size, cap)).reshape(cells)
    d_out = (cots.astype(F32) * gates).astype(BF)
    gated = (rows.astype(F32) * gates).astype(BF)
    block = inner.shape[1]
    spans = [slice(k * block, (k + 1) * block) for k in range(shards)]
    grad_outer = reduce_shards([dot_tn(active[:, p], d_out) for p in spans], shards)
    grad_inner = reduce_shards([dot_tn(gated, d_before[:, p]) for p in spans], shards)
    result = dot_nn(active, jnp.concatenate(outers, axis=0)).astype(BF).reshape(size, cap, width)
    result = exchange(result).reshape(cells, width)
    return back, d_gate, grad_inner, grad_outer, result


def finish_direct(
    tokens, routes, cotangent, context, weights, small, place, cot_blocks, inner_own, outer_own, inner_far,
    capacity, query, key, value, normed, forward, seg, bias, own_buckets,
):
    experts = lax.axis_size("expert")
    shards = lax.axis_size("shard")
    total, width = normed.shape
    route = routes.reshape(1, total)
    flat = tokens.reshape(total, width)
    resid, row_blocks, gate_lines, probs = run_route(context, flat, weights, small, route, place, experts, capacity)
    back, gate_back, grad_inner, outer_mine, outer_other, expert_out = run_experts(
        row_blocks, gate_lines, cot_blocks, inner_own, outer_own, inner_far
    )
    outer_other = swap(outer_other, "shard", shards, 2)
    out_cells = exchange(expert_out)
    d_context, d_resid, extra, keep, partial = run_unroute(
        back, gate_back, resid, cotangent.reshape(total, width), weights, context, small, route, place, probs
    )
    d_query, d_key, d_value, near_sums, far_sums = attn_bwd(
        seg[0][2], seg[0][3], query, key, value, d_context, context, forward[0][1], seg[0][0], seg[0][1], bias
    )
    (
        sum_output, sum_query, sum_key, sum_value, sum_gain, sum_gain_two, sum_router, sum_table, d_tokens, mixed,
    ) = run_tail(
        normed, d_query, d_key, d_value, partial, weights, flat, d_resid, out_cells, resid,
        small, extra, near_sums, far_sums, place, keep, experts, own_buckets,
    )
    sum_output, sum_query, sum_key, sum_value, d_tokens, mixed, grad_inner, grad_outer = run_finish(
        [sum_output, sum_query, sum_key, sum_value, d_tokens, mixed, grad_inner], outer_mine, outer_other
    )
    return (
        mixed.reshape(tokens.shape),
        d_tokens.reshape(tokens.shape),
        sum_gain[0],
        sum_query,
        sum_key,
        sum_value,
        sum_output,
        sum_table,
        sum_gain_two[0],
        sum_router,
        grad_inner[None],
        grad_outer[None],
    )


def per_device(
    tokens,
    segments,
    routes,
    order,
    gain_attn,
    w_query,
    w_key,
    w_value,
    w_output,
    rel_bias,
    gain_ffn,
    w_router,
    w_in,
    w_out,
    cotangent,
):
    seq_count, length, width = tokens.shape
    total = seq_count * length
    experts = lax.axis_size("expert")
    shards = lax.axis_size("shard")
    me = lax.axis_index("expert")
    my_shard = lax.axis_index("shard")
    capacity = (5 * total + 4 * experts - 1) // (4 * experts)
    cells = experts * capacity
    heads = rel_bias.shape[1]
    own = w_query.shape[0]
    own_buckets = rel_bias.shape[0]
    buckets = own_buckets * shards
    small = jnp.concatenate([gain_attn[:, None], gain_ffn[:, None], w_router], axis=1)
    small = jnp.pad(small, ((0, 0), (0, 128 - small.shape[1])))
    small = lax.dynamic_update_slice(small, rel_bias, (0, 128 - heads))
    route = routes.reshape(total)
    chosen = (route[:, None] == jnp.arange(experts, dtype=jnp.int32)[None, :]).astype(F32)
    cot = cotangent.reshape(total, width)
    ranks = (jnp.arange(seq_count, dtype=jnp.int32)[:, None] * length + order).reshape(1, total)
    place_line, cot_cells = find_slots(routes.reshape(1, total), ranks, cot, cells, capacity)
    cot_blocks = exchange(cot_cells.reshape(experts, capacity, width))
    query, key, value, normed_low, small_all, weights_all = project(
        tokens.reshape(total, width), small, (w_query, w_key, w_value, w_output)
    )
    place = place_line[0]
    kept = place >= 0
    spread = (jnp.arange(cells, dtype=jnp.int32)[:, None] == place[None, :]).astype(BF)

    def to_blocks(values):
        return dot_nn(spread, values).astype(BF).reshape(experts, capacity, width)

    query_all, key_all, value_all, output_all = (weights_all[i] for i in range(4))
    inner_own, outer_own = w_in[0], w_out[0]
    if direct(experts):
        inner_own, query = lax.optimization_barrier((inner_own, query))
        inner_far = swap(inner_own, "shard", shards, 2)
    inputs = tokens.reshape(total, width).astype(F32)
    gain_two = small_all[:, 1].astype(F32)
    router_all = small_all[:, 2 : 2 + experts]
    table = small_all[:, 128 - heads :].reshape(shards, own, heads)[:, :own_buckets]
    table = table.reshape(buckets, heads)
    bias = bias_lanes(table)
    seg = [seg_arrays(segments[i]) for i in range(seq_count)]
    rows_of = [slice(i * length, (i + 1) * length) for i in range(seq_count)]
    forward = [
        attn_fwd(s[2], s[3], query[r], key[r], value[r], s[0], s[1], bias)
        for s, r in zip(seg, rows_of)
    ]
    context = jnp.concatenate([f[0] for f in forward], axis=0) if seq_count > 1 else forward[0][0]
    if direct(experts):
        return finish_direct(
            tokens, routes, cotangent, context, weights_all, small_all, place_line, cot_blocks, inner_own, outer_own,
            inner_far, capacity, query, key, value, normed_low, forward, seg, bias, own_buckets,
        )
    resid = inputs + dot_nn(context, output_all)
    scale_two = lax.rsqrt(jnp.mean(resid * resid, axis=-1, keepdims=True) + EPS)
    unit_two = resid * scale_two
    normed_two_low = (unit_two * gain_two).astype(BF)
    logits = dot_nn(normed_two_low, router_all)
    probs = jax.nn.softmax(logits, axis=-1)
    gate = jnp.sum(probs * chosen, axis=-1)
    keep_weight = kept.astype(F32)
    keep_gate = gate * keep_weight
    gate_slots = jnp.sum(jnp.where(place[None, :] == jnp.arange(cells)[:, None], gate[None, :], 0), axis=1)
    row_blocks = to_blocks(normed_two_low)
    back, gate_cells, grad_inner, grad_outer, out_cells = experts_by_collectives(
        row_blocks, gate_slots, cot_blocks, w_in[0], w_out[0], experts, shards, capacity
    )
    upstream = cot.astype(F32)
    d_rows = dot_tn(spread, back)
    d_gate = jnp.sum(
        jnp.where(place[:, None] == jnp.arange(cells)[None, :], gate_cells[None, :], 0), axis=1
    )
    d_logits = (probs * (d_gate[:, None] * chosen - (d_gate * gate)[:, None])).astype(BF)
    d_router = dot_tn(normed_two_low, d_logits)
    d_normed_two = dot_nt(d_logits, router_all) + keep_gate[:, None] * d_rows
    d_gain_two = jnp.sum(d_normed_two * unit_two, axis=0)
    pulled = gain_two * d_normed_two
    d_resid = upstream + scale_two * (
        pulled - unit_two * jnp.mean(unit_two * pulled, axis=-1, keepdims=True)
    )
    d_branch = d_resid.astype(BF)
    d_context = dot_nt(d_branch, output_all).astype(BF)
    backward = [
        attn_bwd(s[2], s[3], query[r], key[r], value[r], d_context[r], f[0], f[1], s[0], s[1], bias)
        for s, r, f in zip(seg, rows_of, forward)
    ]
    d_query, d_key, d_value = (
        jnp.concatenate([b[i] for b in backward], axis=0) if seq_count > 1 else backward[0][i]
        for i in range(3)
    )
    tail = jnp.concatenate([jnp.zeros_like(d_gain_two)[:, None], d_gain_two[:, None], d_router], axis=1)
    tail = jnp.pad(tail, ((0, 0), (0, 128 - tail.shape[1])))
    flat_tokens = tokens.reshape(total, width)
    d_table = sum(table_grad(b[3], b[4], buckets) for b in backward)
    tail = lax.dynamic_update_slice(
        tail.reshape(shards, own, 128), d_table.reshape(shards, own_buckets, heads), (0, 0, 128 - heads)
    ).reshape(width, 128)
    if True:
        d_normed = (
            dot_nt(d_query, query_all) + dot_nt(d_key, key_all) + dot_nt(d_value, value_all)
        )
        inputs_again = flat_tokens.astype(F32)
        scale_one = lax.rsqrt(jnp.mean(inputs_again * inputs_again, axis=-1, keepdims=True) + EPS)
        unit_one = inputs_again * scale_one
        tail = tail.at[:, 0].set(jnp.sum(d_normed * unit_one, axis=0))
        pulled_one = small_all[:, 0].astype(F32) * d_normed
        d_tokens = d_resid + scale_one * (
            pulled_one - unit_one * jnp.mean(unit_one * pulled_one, axis=-1, keepdims=True)
        )
        pairs = ((context, d_branch), (normed_low, d_query), (normed_low, d_key), (normed_low, d_value))
        parts = [dot_tn(left, right) for left, right in pairs] + [tail]
        sum_output, sum_query, sum_key, sum_value, sums = (
            lax.psum(
                reduce_shards(
                    [lax.dynamic_slice_in_dim(p, (my_shard ^ k) * own, own, 0) for k in range(shards)], shards
                ),
                "expert",
            )
            for p in parts
        )
    arrived = dot_tn(spread, out_cells)
    mixed = resid + keep_gate[:, None] * arrived
    return (
        mixed.astype(BF).reshape(tokens.shape),
        d_tokens.astype(BF).reshape(tokens.shape),
        sums[:, 0],
        sum_query,
        sum_key,
        sum_value,
        sum_output,
        sums[:own_buckets, 128 - heads :],
        sums[:, 1],
        sums[:, 2 : 2 + experts],
        grad_inner[None],
        grad_outer[None],
    )


def solution(mesh):
    in_specs = (
        P(("expert", "shard"), None, None),
        P(("expert", "shard"), None),
        P(("expert", "shard"), None, None),
        P(("expert", "shard"), None),
        P("shard"),
        P("shard", None),
        P("shard", None),
        P("shard", None),
        P("shard", None),
        P("shard", None),
        P("shard"),
        P("shard", None),
        P("expert", None, "shard"),
        P("expert", "shard", None),
        P(("expert", "shard"), None, None),
    )
    out_specs = (
        P(("expert", "shard"), None, None),
        P(("expert", "shard"), None, None),
        P("shard"),
        P("shard", None),
        P("shard", None),
        P("shard", None),
        P("shard", None),
        P("shard", None),
        P("shard"),
        P("shard", None),
        P("expert", None, "shard"),
        P("expert", "shard", None),
    )
    return jax.shard_map(
        per_device, mesh=mesh, in_specs=in_specs, out_specs=out_specs, check_vma=False
    )
```

```python
import functools

import jax
import jax.numpy as jnp
from jax import lax
from jax.experimental import pallas as pl
from jax.experimental.pallas import tpu as pltpu
from jax.sharding import PartitionSpec as P
HEAD_DIM=64
BLK=128
EDGES = (12, 16, 23, 32, 46, 64, 91)
BIG=1e9
def bucket_index(offset):
    magnitude = jnp.abs(offset)
    far = 8 + sum(((magnitude >= edge).astype(jnp.int32) for edge in EDGES))
    near = jnp.where(magnitude < 8, magnitude, far)
    return near + 16 * (offset > 0).astype(jnp.int32)

def dot_nt(a,b): return lax.dot_general(a,b,(((1,),(1,)),((),())),preferred_element_type=jnp.float32)
def dot_nn(a,b): return lax.dot_general(a,b,(((1,),(0,)),((),())),preferred_element_type=jnp.float32)

def head_mask():
    lane=lax.broadcasted_iota(jnp.int32,(BLK,2*HEAD_DIM),1)
    return (lane<HEAD_DIM).astype(jnp.float32).astype(jnp.bfloat16)

def build_bias(w_ref, bias_ref, nblk, pairs):
    rows = (2 * nblk - 1) * BLK
    near = (nblk - 2) * BLK
    for j in range(pairs):
        for h in range(2):
            c = slice((2 * j + h) * BLK, (2 * j + h + 1) * BLK)
            w = w_ref[j, h : h + 1, :]
            bias_ref[0:near, c] = jnp.broadcast_to(w[:, 511:512], (near, BLK))
            bias_ref[near + 3 * BLK : rows, c] = jnp.broadcast_to(w[:, 0:1], (near, BLK))
            r = pltpu.roll(jnp.broadcast_to(w, (BLK, 512)), 0, 1, stride=1, stride_axis=0)
            bias_ref[near : near + BLK, c] = r[:, 384:512]
            bias_ref[near + BLK : near + 2 * BLK, c] = r[:, 256:384]
            bias_ref[near + 2 * BLK : near + 3 * BLK, c] = r[:, 128:256]


def by_width(nblk, count, run):
    for n in range(1, nblk + 1):

        @pl.when(count == n)
        def _():
            run(n * BLK)


def pair_of(block, mask):
    return jnp.concatenate([block * mask, block * (1 - mask)], axis=0)


def flip(src_ref, dst_ref, nblk, pairs):
    for j in range(pairs):
        c = slice(j * BLK, (j + 1) * BLK)
        for b in range(nblk):
            s = slice(b * BLK, (b + 1) * BLK)
            dst_ref[c, s] = src_ref[s, c].astype(jnp.float32).T.astype(jnp.bfloat16)


def join_heads(wide):
    return jnp.concatenate([wide[:HEAD_DIM, :BLK], wide[HEAD_DIM:, BLK:]], axis=0)


def fwd_kernel(nblk, pairs, lo_ref, nb_ref, q_ref, k_ref, v_ref, segq_ref, segk_ref, w_ref, ctx_ref, lse_ref, vt_ref, bias_ref):
    build_bias(w_ref, bias_ref, nblk, pairs)
    flip(v_ref, vt_ref, nblk, pairs)
    mask = head_mask()
    lanes = [slice(j * BLK, (j + 1) * BLK) for j in range(pairs)]
    both = [slice(2 * j * BLK, 2 * (j + 1) * BLK) for j in range(pairs)]

    def body(qb, _):
        rows = pl.ds(pl.multiple_of(qb * BLK, BLK), BLK)
        lob = lo_ref[qb]
        sq = segq_ref[rows, :]
        sq = jnp.concatenate([sq, sq], axis=0)
        q_cat = [jnp.concatenate([pair_of(q_ref[rows, c], mask), sq], axis=1) for c in lanes]

        def run(W):
            ks = pl.ds(pl.multiple_of(lob * BLK, BLK), W)
            bs = pl.ds(pl.multiple_of((lob - qb + nblk - 1) * BLK, BLK), W)
            sk = segk_ref[ks, :]
            st = [
                dot_nt(jnp.concatenate([k_ref[ks, c], sk], axis=1), q) + bias_ref[bs, d]
                for c, d, q in zip(lanes, both, q_cat)
            ]
            m = [jnp.max(x, axis=0, keepdims=True) for x in st]
            e = [jnp.exp(x - y) for x, y in zip(st, m)]
            l = [jnp.sum(x, axis=0, keepdims=True) for x in e]
            ot = [dot_nn(vt_ref[c, ks], x.astype(jnp.bfloat16)) / y for c, x, y in zip(lanes, e, l)]
            for j, c in enumerate(lanes):
                ctx_ref[rows, c] = join_heads(ot[j]).T.astype(jnp.bfloat16)
                lse_ref[j, pl.ds(qb, 1), :] = m[j] + jnp.log(l[j])

        by_width(nblk, nb_ref[qb], run)
        return 0

    lax.fori_loop(0, nblk, body, 0)


def bwd_kernel(
    nblk, pairs, lo_ref, nb_ref, q_ref, k_ref, v_ref, do_ref, ctx_ref, lse_ref, segq_ref, segk_ref, w_ref,
    dq_ref, dk_ref, dv_ref, near_ref, far_ref, kt_ref, bias_ref, acc_ref, dka_ref, dva_ref,
):
    build_bias(w_ref, bias_ref, nblk, pairs)
    flip(k_ref, kt_ref, nblk, pairs)
    acc_ref[...] = jnp.zeros_like(acc_ref)
    dka_ref[...] = jnp.zeros_like(dka_ref)
    dva_ref[...] = jnp.zeros_like(dva_ref)
    mask = head_mask()
    lanes = [slice(j * BLK, (j + 1) * BLK) for j in range(pairs)]
    both = [slice(2 * j * BLK, 2 * (j + 1) * BLK) for j in range(pairs)]
    row = lax.broadcasted_iota(jnp.int32, (16, 2 * HEAD_DIM), 0)
    lane = lax.broadcasted_iota(jnp.int32, (16, 2 * HEAD_DIM), 1)
    pick = ((lane // HEAD_DIM) == row).astype(jnp.float32).astype(jnp.bfloat16)

    def body(qb, _):
        rows = pl.ds(pl.multiple_of(qb * BLK, BLK), BLK)
        lob = lo_ref[qb]
        sq = segq_ref[rows, :]
        sq = jnp.concatenate([sq, sq], axis=0)
        q2 = [pair_of(q_ref[rows, c], mask) for c in lanes]
        q_cat = [jnp.concatenate([q, sq], axis=1) for q in q2]
        do2 = [pair_of(do_ref[rows, c], mask) for c in lanes]
        delta = []
        for c in lanes:
            prod = do_ref[rows, c].astype(jnp.float32) * ctx_ref[rows, c].astype(jnp.float32)
            hi = prod.astype(jnp.bfloat16)
            low = (prod - hi.astype(jnp.float32)).astype(jnp.bfloat16)
            dl = dot_nt(pick, hi) + dot_nt(pick, low)
            delta.append(jnp.concatenate([dl[0:1], dl[1:2]], axis=1))
        lse = [lse_ref[j, pl.ds(qb, 1), :] for j in range(pairs)]

        def run(W):
            ks = pl.ds(pl.multiple_of(lob * BLK, BLK), W)
            bs = pl.ds(pl.multiple_of((lob - qb + nblk - 1) * BLK, BLK), W)
            sk = segk_ref[ks, :]
            st = [dot_nt(jnp.concatenate([k_ref[ks, c], sk], axis=1), q) for c, q in zip(lanes, q_cat)]
            dp = [dot_nt(v_ref[ks, c], d) for c, d in zip(lanes, do2)]
            p = [jnp.exp(x + bias_ref[bs, d] - y) for x, d, y in zip(st, both, lse)]
            ds = [x * (y - z) for x, y, z in zip(p, dp, delta)]
            dsb = [x.astype(jnp.bfloat16) for x in ds]
            for j, (c, d) in enumerate(zip(lanes, both)):
                acc_ref[bs, d] += ds[j]
                dva_ref[ks, c] += dot_nn(p[j].astype(jnp.bfloat16), do2[j])
                dka_ref[ks, c] += dot_nn(dsb[j], q2[j])
                dqt = join_heads(dot_nn(kt_ref[c, ks], dsb[j])) * (HEAD_DIM**-0.5)
                dq_ref[rows, c] = dqt.T.astype(jnp.bfloat16)

        by_width(nblk, nb_ref[qb], run)
        return 0

    lax.fori_loop(0, nblk, body, 0)
    dk_ref[...] = dka_ref[...].astype(jnp.bfloat16)
    dv_ref[...] = dva_ref[...].astype(jnp.bfloat16)
    near = (nblk - 2) * BLK
    total = (2 * nblk - 1) * BLK
    for j in range(pairs):
        for h in range(2):
            c = slice((2 * j + h) * BLK, (2 * j + h + 1) * BLK)
            wide = jnp.concatenate(
                [
                    jnp.zeros((BLK, BLK), jnp.float32),
                    acc_ref[near + 2 * BLK : near + 3 * BLK, c],
                    acc_ref[near + BLK : near + 2 * BLK, c],
                    acc_ref[near : near + BLK, c],
                ],
                axis=1,
            )
            near_ref[j, h : h + 1, :] = jnp.sum(unroll_rows(wide), axis=0, keepdims=True)
            low = jnp.sum(acc_ref[0:near, c], axis=0, keepdims=True)
            high = jnp.sum(acc_ref[near + 3 * BLK : total, c], axis=0, keepdims=True)
            far_ref[j, h : h + 1, :] = jnp.concatenate([low, high], axis=1)


def unroll_rows(wide):
    n=wide.shape[1]
    out=wide
    row=lax.broadcasted_iota(jnp.int32,wide.shape,0)
    bit=1
    while bit<wide.shape[0]:
        out=jnp.where((row & bit)!=0,pltpu.roll(out,n-bit,1),out)
        bit*=2
    return out

FWD_PAIRS = 6
BWD_PAIRS = 3


def pair_spec(nrow, pairs):
    return pl.BlockSpec((nrow, 2 * HEAD_DIM * pairs), lambda p, *_: (0, p))


def full_spec(shape):
    return pl.BlockSpec(shape, lambda p, *_: (0,) * len(shape))


def lead_spec(pairs, shape):
    return pl.BlockSpec((pairs,) + shape, lambda p, *_: (p, 0, 0))


def attn_fwd(lo, nb, q, k, v, segq, segk, w):
    L, D = q.shape
    nblk = L // BLK
    every = D // (2 * HEAD_DIM)
    pairs = FWD_PAIRS
    return pl.pallas_call(
        functools.partial(fwd_kernel, nblk, pairs),
        grid_spec=pltpu.PrefetchScalarGridSpec(
            num_scalar_prefetch=2,
            grid=(every // pairs,),
            in_specs=[pair_spec(L, pairs)] * 3 + [full_spec((L, 128))] * 2 + [lead_spec(pairs, (2, 512))],
            out_specs=[pair_spec(L, pairs), lead_spec(pairs, (nblk, 2 * BLK))],
            scratch_shapes=[
                pltpu.VMEM((2 * HEAD_DIM * pairs, L), jnp.bfloat16),
                pltpu.VMEM(((2 * nblk - 1) * BLK, 2 * BLK * pairs), jnp.float32),
            ],
        ),
        out_shape=[
            jax.ShapeDtypeStruct((L, D), jnp.bfloat16),
            jax.ShapeDtypeStruct((every, nblk, 2 * BLK), jnp.float32),
        ],
        compiler_params=pltpu.CompilerParams(vmem_limit_bytes=60 * 2**20),
        cost_estimate=pl.CostEstimate(flops=2 * 10**9, bytes_accessed=8 * 2**20, transcendentals=6 * 10**6),
    )(lo, nb, q, k, v, segq, segk, w)


def attn_bwd(lo, nb, q, k, v, do, ctx, lse, segq, segk, w):
    L, D = q.shape
    nblk = L // BLK
    every = D // (2 * HEAD_DIM)
    pairs = BWD_PAIRS
    rows = (2 * nblk - 1) * BLK
    return pl.pallas_call(
        functools.partial(bwd_kernel, nblk, pairs),
        grid_spec=pltpu.PrefetchScalarGridSpec(
            num_scalar_prefetch=2,
            grid=(every // pairs,),
            in_specs=[pair_spec(L, pairs)] * 5
            + [lead_spec(pairs, (nblk, 2 * BLK))]
            + [full_spec((L, 128))] * 2
            + [lead_spec(pairs, (2, 512))],
            out_specs=[pair_spec(L, pairs)] * 3 + [lead_spec(pairs, (2, 512)), lead_spec(pairs, (2, 256))],
            scratch_shapes=[
                pltpu.VMEM((2 * HEAD_DIM * pairs, L), jnp.bfloat16),
                pltpu.VMEM((rows, 2 * BLK * pairs), jnp.float32),
                pltpu.VMEM((rows, 2 * BLK * pairs), jnp.float32),
                pltpu.VMEM((L, 2 * HEAD_DIM * pairs), jnp.float32),
                pltpu.VMEM((L, 2 * HEAD_DIM * pairs), jnp.float32),
            ],
        ),
        out_shape=[jax.ShapeDtypeStruct((L, D), jnp.bfloat16)] * 3
        + [jax.ShapeDtypeStruct((every, 2, 512), jnp.float32), jax.ShapeDtypeStruct((every, 2, 256), jnp.float32)],
        compiler_params=pltpu.CompilerParams(vmem_limit_bytes=60 * 2**20),
        cost_estimate=pl.CostEstimate(flops=4 * 10**9, bytes_accessed=16 * 2**20, transcendentals=6 * 10**6),
    )(lo, nb, q, k, v, do, ctx, lse, segq, segk, w)


def seg_ranges(seg):
    L = seg.shape[0]
    nblk = L // BLK
    sb = seg.reshape(nblk, BLK)
    first = jnp.sum((seg[None, :] < sb[:, :1]).astype(jnp.int32), axis=1)
    last = jnp.sum((seg[None, :] <= sb[:, -1:]).astype(jnp.int32), axis=1)
    lo = first // BLK
    nb = (last + BLK - 1) // BLK - lo
    return lo.astype(jnp.int32), nb.astype(jnp.int32)


def table_grad(near,far,buckets):
    off=-(jnp.arange(512,dtype=jnp.int32)-256)
    oh=(bucket_index(off)[:,None]==jnp.arange(buckets,dtype=jnp.int32)[None,:]).astype(jnp.float32)
    n=jnp.einsum("hx,xb->bh",near.reshape(-1,512),oh,precision=lax.Precision.HIGHEST)
    f=far.reshape(-1,2,128).sum(-1)
    ids=jnp.arange(buckets,dtype=jnp.int32)[:,None]
    return n+jnp.where(ids==15,f[None,:,0],0)+jnp.where(ids==31,f[None,:,1],0)

TILE=256
def gelu_parts(x):
    c=0.7978845608028654
    x2=x*x
    t=jnp.tanh(x*(c+(c*0.044715)*x2))
    half=0.5*(1.0+t)
    slope=half+0.5*x*(1.0-t*t)*(c+(3*c*0.044715)*x2)
    return x*half,slope

def expert_kernel(count, parts, *refs):
    rows=refs[:count]; cots=refs[count:2*count]
    wi_refs=refs[2*count:2*count+parts]; wo_refs=refs[2*count+parts:2*count+2*parts]
    refs=refs[2*count+2*parts:]
    outs=refs[:count]; act_ref,db_ref,dg_ref=refs[count:count+3]
    x_ref,c_ref,wi_buf,wo_buf,acc_ref,dga_ref,act_buf,db_buf,w_sem,o_sem=refs[count+3:]
    block=wi_refs[0].shape[1]
    per=block//TILE
    total=parts*per
    for k in range(parts):
        pltpu.make_async_copy(wi_refs[k],wi_buf.at[k],w_sem.at[0,k]).start()
        pltpu.make_async_copy(wo_refs[k],wo_buf.at[k],w_sem.at[1,k]).start()
    first=0
    for i in range(count):
        n=rows[i].shape[0]
        x_ref[first:first+n,:]=rows[i][...]
        c_ref[first:first+n,:]=cots[i][...]
        first+=n
    acc_ref[...]=jnp.zeros_like(acc_ref)
    dga_ref[...]=jnp.zeros_like(dga_ref)
    def out_copies(step,slot):
        cols=pl.ds(pl.multiple_of(step*TILE,TILE),TILE)
        return (pltpu.make_async_copy(act_buf.at[slot],act_ref.at[:,cols],o_sem.at[0,slot]),
                pltpu.make_async_copy(db_buf.at[slot],db_ref.at[:,cols],o_sem.at[1,slot]))
    for k in range(parts):
        pltpu.make_async_copy(wi_refs[k],wi_buf.at[k],w_sem.at[0,k]).wait()
        pltpu.make_async_copy(wo_refs[k],wo_buf.at[k],w_sem.at[1,k]).wait()
        def body(c,_):
            step=k*per+c
            slot=lax.rem(step,2)
            @pl.when(step>=2)
            def _():
                for cp in out_copies(step-2,slot): cp.wait()
            cols=pl.ds(pl.multiple_of(c*TILE,TILE),TILE)
            wi=wi_buf[k,:,cols]
            wo=wo_buf[k,cols,:]
            before=dot_nn(x_ref[...],wi)
            up=dot_nt(c_ref[...],wo)
            active,slope=gelu_parts(before)
            prod=active*up
            dga_ref[...]+=prod[:,:128]+prod[:,128:]
            act_buf[slot]=active.astype(jnp.bfloat16)
            db=(up*slope).astype(jnp.bfloat16)
            db_buf[slot]=db
            acc_ref[...]+=dot_nt(db,wi)
            for cp in out_copies(step,slot): cp.start()
            return 0
        lax.fori_loop(0,per,body,0)
    first=0
    for i in range(count):
        n=rows[i].shape[0]
        outs[i][...]=acc_ref[first:first+n,:].astype(jnp.bfloat16)
        first+=n
    ones=jnp.ones((8,128),jnp.bfloat16)
    sums=dga_ref[...]
    hi=sums.astype(jnp.bfloat16)
    rest=sums-hi.astype(jnp.float32)
    mid=rest.astype(jnp.bfloat16)
    low=(rest-mid.astype(jnp.float32)).astype(jnp.bfloat16)
    dg_ref[...]=dot_nt(ones,hi)+dot_nt(ones,mid)+dot_nt(ones,low)
    for step in (total-2,total-1):
        for cp in out_copies(step,step%2): cp.wait()

def expert_half(rows,cots,w_ins,w_outs):
    count=len(rows); parts=len(w_ins)
    width,block=w_ins[0].shape
    R=sum(r.shape[0] for r in rows)
    vm=pl.BlockSpec(memory_space=pltpu.VMEM); hb=pl.BlockSpec(memory_space=pl.ANY)
    outs=pl.pallas_call(functools.partial(expert_kernel,count,parts),
        in_specs=[vm]*(2*count)+[hb]*(2*parts),
        out_specs=[vm]*count+[hb,hb,vm],
        out_shape=[jax.ShapeDtypeStruct(r.shape,jnp.bfloat16) for r in rows]+[jax.ShapeDtypeStruct((R,parts*block),jnp.bfloat16)]*2+[jax.ShapeDtypeStruct((8,R),jnp.float32)],
        scratch_shapes=[pltpu.VMEM((R,width),jnp.bfloat16)]*2+[pltpu.VMEM((parts,width,block),jnp.bfloat16),pltpu.VMEM((parts,block,width),jnp.bfloat16),
            pltpu.VMEM((R,width),jnp.float32),pltpu.VMEM((R,128),jnp.float32),pltpu.VMEM((2,R,TILE),jnp.bfloat16),pltpu.VMEM((2,R,TILE),jnp.bfloat16),
            pltpu.SemaphoreType.DMA((2,parts)),pltpu.SemaphoreType.DMA((2,2))],
        compiler_params=pltpu.CompilerParams(vmem_limit_bytes=48*2**20),
        cost_estimate=pl.CostEstimate(flops=6*R*width*parts*block,bytes_accessed=20*2**20,transcendentals=R*parts*block))(*rows,*cots,*w_ins,*w_outs)
    return outs[:count],outs[count],outs[count+1],outs[count+2][0]

MESH = pl.DeviceIdType.MESH


def shard_peer(bit):
    return (lax.axis_index("expert"), lax.axis_index("shard") ^ bit)


def expert_peer(bit):
    return (lax.axis_index("expert") ^ bit, lax.axis_index("shard"))


def greet(peers):
    barrier = pltpu.get_barrier_semaphore()
    for peer in peers:
        pl.semaphore_signal(barrier, inc=1, device_id=peer, device_id_type=MESH)
    pl.semaphore_wait(barrier, len(peers))


def send(src, dst, send_sem, recv_sem, peer):
    copy = pltpu.make_async_remote_copy(
        src_ref=src, dst_ref=dst, send_sem=send_sem, recv_sem=recv_sem, device_id=peer, device_id_type=MESH
    )
    copy.start()
    return copy


def columns(line, block):
    return jnp.broadcast_to(line[:, block * 128 : (block + 1) * 128], (128, 128)).T


def project_kernel(
    heads, x_in, small_in, q_in, k_in, v_in, o_in, segments,
    q_ref, k_ref, v_ref, normed_ref, small_ref, segq_ref, segk_ref, bias_ref, all_ref,
    x_ref, small_buf, w_buf, unit_ref,
    sem_send, sem_recv, sem_own, sem_out, sem_load,
):
    shard = lax.axis_index("shard")
    own = q_in.shape[0]
    load = pltpu.make_async_copy(x_in, x_ref, sem_load.at[0])
    load.start()

    def rows(bit):
        return pl.ds(pl.multiple_of((shard ^ bit) * own, 64), own)

    ins = [small_in, q_in, k_in, v_in, o_in]
    bufs = [small_buf] + [w_buf.at[i] for i in range(4)]
    count = len(ins)
    kept = []
    for i in range(count):
        copy = pltpu.make_async_copy(ins[i], bufs[i].at[rows(0)], sem_own.at[i])
        copy.start()
        kept.append(copy)
    greet([shard_peer(1), shard_peer(2)])
    far, near, passed = [], [], [None] * count
    for i in range(count):
        far.append(send(ins[i], bufs[i].at[rows(0)], sem_send.at[0, i], sem_recv.at[0, i], shard_peer(2)))
    for i in range(count):
        near.append(send(ins[i], bufs[i].at[rows(0)], sem_send.at[1, i], sem_recv.at[1, i], shard_peer(1)))
    length, width = x_ref.shape
    tile = 512

    def unit(t, _):
        r = pl.ds(pl.multiple_of(t * tile, tile), tile)
        x = x_ref[r, :].astype(jnp.float32)
        unit_ref[r, :] = x * lax.rsqrt(jnp.mean(x * x, axis=-1, keepdims=True) + 1e-6)
        return 0

    def hop(i):
        far[i].wait_recv()
        here = bufs[i].at[rows(2)]
        passed[i] = send(here, here, sem_send.at[2, i], sem_recv.at[2, i], shard_peer(1))

    def finish(i):
        kept[i].wait()
        near[i].wait_recv()
        passed[i].wait_recv()

    load.wait()
    lax.fori_loop(0, length // tile, unit, 0)
    documents = segments[...].astype(jnp.float32)
    ids = lax.broadcasted_iota(jnp.int32, (128, 128), 1).astype(jnp.float32)
    for b in range(length // 128):
        r = slice(b * 128, (b + 1) * 128)
        same = (columns(documents, b) == ids).astype(jnp.float32)
        segq_ref[r, :] = same.astype(jnp.bfloat16)
        segk_ref[r, :] = jnp.where(ids < 16.0, (same - 1.0) * BIG, 0.0).astype(jnp.bfloat16)
    hop(0)
    hop(1)
    finish(0)
    small = small_buf[...]
    small_ref[...] = small
    gain = jnp.concatenate(
        [small[c * 128 : (c + 1) * 128, :].astype(jnp.float32).T[0:1] for c in range(width // 128)], axis=1
    )

    buckets = 32
    part = buckets // 4
    table = jnp.concatenate([small[j * own : j * own + part, :].astype(jnp.float32) for j in range(4)], axis=0)
    table = jnp.concatenate([table, jnp.zeros((128 - buckets, 128), jnp.float32)], axis=0).T
    wide = bias_ref.shape[2]
    offset = wide // 2 - lax.broadcasted_iota(jnp.int32, (128, wide), 1)
    onehot = (bucket_index(offset) == lax.broadcasted_iota(jnp.int32, (128, wide), 0)).astype(jnp.float32)
    lines = dot_nn(table.astype(jnp.bfloat16), onehot.astype(jnp.bfloat16))
    for p in range(heads // 2):
        bias_ref[p] = lines[128 - heads + 2 * p : 130 - heads + 2 * p]

    def norm(t, _):
        r = pl.ds(pl.multiple_of(t * tile, tile), tile)
        normed_ref[r, :] = (unit_ref[r, :] * gain).astype(jnp.bfloat16)
        return 0

    lax.fori_loop(0, length // tile, norm, 0)
    outs = []

    def project_one(i, out):
        finish(i)
        copy = pltpu.make_async_copy(w_buf.at[i - 1], all_ref.at[i - 1], sem_out.at[i - 1])
        copy.start()
        outs.append(copy)

        def run(t, _):
            r = pl.ds(pl.multiple_of(t * tile, tile), tile)
            y = dot_nn(normed_ref[r, :], w_buf[i - 1]).astype(jnp.bfloat16)
            if i == 1:
                y = (y.astype(jnp.float32) * HEAD_DIM**-0.5).astype(jnp.bfloat16)
            out[r, :] = y
            return 0

        lax.fori_loop(0, length // tile, run, 0)

    project_one(1, q_ref)
    hop(2)
    project_one(2, k_ref)
    hop(3)
    project_one(3, v_ref)
    hop(4)
    finish(4)
    copy = pltpu.make_async_copy(w_buf.at[3], all_ref.at[3], sem_out.at[3])
    copy.start()
    outs.append(copy)
    for c in outs:
        c.wait()
    for c in far + near + passed:
        c.wait_send()


def project(x, small, weights, segments, heads):
    length, width = x.shape
    vm = pl.BlockSpec(memory_space=pltpu.VMEM)
    hb = pl.BlockSpec(memory_space=pl.ANY)
    bf = jnp.bfloat16
    shape = jax.ShapeDtypeStruct
    return pl.pallas_call(
        functools.partial(project_kernel, heads),
        in_specs=[hb] * 6 + [vm],
        out_specs=[vm] * 8 + [hb],
        out_shape=[shape((length, width), bf)] * 4 + [shape((width, 128), bf), shape((length, 128), bf), shape((length, 128), bf), shape((heads // 2, 2, 512), jnp.float32)]
        + [shape((4, width, width), bf)],
        scratch_shapes=[
            pltpu.VMEM((length, width), bf),
            pltpu.VMEM((width, 128), bf),
            pltpu.VMEM((4, width, width), bf),
            pltpu.VMEM((length, width), jnp.float32),
            pltpu.SemaphoreType.DMA((3, 5)),
            pltpu.SemaphoreType.DMA((3, 5)),
            pltpu.SemaphoreType.DMA((5,)),
            pltpu.SemaphoreType.DMA((4,)),
            pltpu.SemaphoreType.DMA((1,)),
        ],
        compiler_params=pltpu.CompilerParams(collective_id=0, has_side_effects=True, vmem_limit_bytes=62 * 2**20),
        cost_estimate=pl.CostEstimate(flops=6 * 10**9, bytes_accessed=20 * 2**20, transcendentals=0),
    )(x, small, *weights, segments)


def slot_kernel(cap, route, order, cot, place_ref, cells_ref):
    length = cot.shape[0]
    keys = (route[...] * length + order[...]).astype(jnp.float32)
    starts = (route[...] * length).astype(jnp.float32)
    blocks = length // 128
    sides = [columns(keys, b) for b in range(blocks)]
    slots = []
    for t in range(blocks):
        s = slice(t * 128, (t + 1) * 128)
        sums = sum((c < keys[:, s]).astype(jnp.float32) - (c < starts[:, s]).astype(jnp.float32) for c in sides)
        slots.append(jnp.sum(sums, axis=0, keepdims=True))
    slot = jnp.concatenate(slots, axis=1).astype(jnp.int32)
    place = jnp.where(slot < cap, route[...] * cap + slot, -1)
    place_ref[...] = place
    step = 640
    for t in range(cells_ref.shape[0] // step):
        ids = lax.broadcasted_iota(jnp.int32, (step, length), 0) + t * step
        pick = (ids == place).astype(jnp.float32).astype(jnp.bfloat16)
        cells_ref[t * step : (t + 1) * step, :] = dot_nn(pick, cot[...]).astype(jnp.bfloat16)


def find_slots(route, order, cot, cells, cap):
    length, width = cot.shape
    vm = pl.BlockSpec(memory_space=pltpu.VMEM)
    return pl.pallas_call(
        functools.partial(slot_kernel, cap),
        in_specs=[vm] * 3,
        out_specs=[vm] * 2,
        out_shape=[jax.ShapeDtypeStruct((1, length), jnp.int32), jax.ShapeDtypeStruct((cells, width), jnp.bfloat16)],
        compiler_params=pltpu.CompilerParams(vmem_limit_bytes=62 * 2**20),
        cost_estimate=pl.CostEstimate(flops=2 * 10**9, bytes_accessed=4 * 2**20, transcendentals=0),
    )(route, order, cot)


def gate_columns(line, count, width):
    column = jnp.broadcast_to(line, (128, 256)).T[:count]
    return jnp.concatenate([column] * (width // 128), axis=1)


def experts_kernel(
    size, cap, tile,
    rows_in, gate_in, cot_in, inner_own, outer_own, inner_far,
    back_out, dgate_out, mine_out, other_out, result_out,
    rows, gates, cots, weights, active, d_before, total, d_gate, back, d_gates, back_in, d_gates_in,
    gated_t, g_send, g_recv, stage, result,
    w_sem, wr_sem, row_send, row_recv, gate_send, gate_recv, back_send, back_recv, dg_send, dg_recv,
    g_sem_send, g_sem_recv, cot_sem, out_sem, res_sem, back_sem, dgb_sem,
):
    width = weights.shape[2]
    block = weights.shape[3]
    per = block // tile
    group = 2
    count = group * cap
    me = lax.axis_index("expert")

    def part(k):
        return pl.ds(k * cap, cap)

    local = [
        pltpu.make_async_copy(inner_own, weights.at[0, 0], w_sem.at[0]),
        pltpu.make_async_copy(outer_own, weights.at[0, 1], w_sem.at[1]),
        pltpu.make_async_copy(inner_far, weights.at[2, 0], w_sem.at[2]),
        pltpu.make_async_copy(rows_in.at[me], rows.at[part(0)], w_sem.at[3]),
        pltpu.make_async_copy(gate_in.at[me], gates.at[0], w_sem.at[4]),
    ]
    local += [pltpu.make_async_copy(cot_in.at[me ^ k], cots.at[part(k)], cot_sem.at[k]) for k in range(size)]
    for c in local:
        c.start()
    greet([expert_peer(k) for k in range(1, size)] + [shard_peer(1), shard_peer(2)])
    sent = []
    arrive = {}
    outer_far = send(outer_own, weights.at[2, 1], wr_sem.at[0, 0], wr_sem.at[1, 0], shard_peer(2))

    def dispatch(k):
        arrive[k] = [
            send(gate_in.at[me ^ k], gates.at[k], gate_send.at[k], gate_recv.at[k], expert_peer(k)),
            send(rows_in.at[me ^ k], rows.at[part(k)], row_send.at[k], row_recv.at[k], expert_peer(k)),
        ]
        sent.append(arrive[k][0])

    for k in (4, 5, 6, 7, 2, 3, 1):
        dispatch(k)
    moved = [
        send(inner_own, weights.at[1, 0], wr_sem.at[0, 1], wr_sem.at[1, 1], shard_peer(1)),
        send(outer_own, weights.at[1, 1], wr_sem.at[0, 2], wr_sem.at[1, 2], shard_peer(1)),
        send(inner_far, weights.at[3, 0], wr_sem.at[0, 3], wr_sem.at[1, 3], shard_peer(1)),
    ]
    sent += moved + [outer_far]
    d_gates[...] = jnp.zeros_like(d_gates)
    for c in local:
        c.wait()
    for c in moved:
        c.wait_recv()
    ones = jnp.ones((8, 128), jnp.bfloat16)
    returned = {}
    groups = size // group

    def arrived(g):
        for k in range(group * g, group * (g + 1)):
            if k:
                for c in arrive[k]:
                    c.wait_recv()

    def forward_back(g, spot, first, last):
        mine = slice(g * count, (g + 1) * count)
        here = slice(spot * count, (spot + 1) * count)
        if first == 0:
            total[here, :] = jnp.zeros((count, width), jnp.float32)
            d_gate[here, :] = jnp.zeros((count, 128), jnp.float32)

        def step(t, _):
            kk = t // per
            cols = pl.ds(pl.multiple_of(lax.rem(t, per) * tile, tile), tile)
            where = pl.ds(pl.multiple_of(t * tile, tile), tile)
            wi = weights[kk, 0, :, cols]
            wo = weights[kk, 1, cols, :]
            before = dot_nn(rows[mine, :], wi)
            up = dot_nt(cots[mine, :], wo)
            value, slope = gelu_parts(before)
            prod = value * up
            d_gate[here, :] += sum(prod[:, c * 128 : (c + 1) * 128] for c in range(tile // 128))
            active[mine, where] = value.astype(jnp.bfloat16)
            db = (up * slope).astype(jnp.bfloat16)
            d_before[mine, where] = db
            total[here, :] += dot_nt(db, wi)
            return 0

        lax.fori_loop(first * per, last * per, step, 0)

    def give_back(g, spot):
        here = slice(spot * count, (spot + 1) * count)
        back[g * count : (g + 1) * count, :] = total[here, :].astype(jnp.bfloat16)
        for k in range(group * g, group * (g + 1)):
            start = spot * count + (k - group * g) * cap
            sums = d_gate[start : start + cap, :]
            hi = sums.astype(jnp.bfloat16)
            rest = sums - hi.astype(jnp.float32)
            mid = rest.astype(jnp.bfloat16)
            low = (rest - mid.astype(jnp.float32)).astype(jnp.bfloat16)
            d_gates[k, :, 0:cap] = dot_nt(ones, hi) + dot_nt(ones, mid) + dot_nt(ones, low)
            if k:
                returned[k] = [
                    send(d_gates.at[k], d_gates_in.at[k], dg_send.at[k], dg_recv.at[k], expert_peer(k)),
                    send(back.at[part(k)], back_in.at[part(k)], back_send.at[k], back_recv.at[k], expert_peer(k)),
                ]
                sent.extend(returned[k])

    arrived(0)
    forward_back(0, 0, 0, 2)
    arrived(1)
    forward_back(1, 1, 0, 2)
    outer_far.wait_recv()
    passed = send(weights.at[2, 1], weights.at[3, 1], wr_sem.at[0, 4], wr_sem.at[1, 4], shard_peer(1))
    sent.append(passed)
    passed.wait_recv()
    for i in range(2):
        forward_back(i, i, 2, 4)
        give_back(i, i)
    for i in range(2, groups):
        arrived(i)
        forward_back(i, 2, 0, 4)
        give_back(i, 2)
    for k in range(size):
        span = slice(k * cap, (k + 1) * cap)
        column = gate_columns(gates[k, 0:1, :], cap, width)
        cots[span, :] = (cots[span, :].astype(jnp.float32) * column).astype(jnp.bfloat16)
        result[span, :] = (rows[span, :].astype(jnp.float32) * column).astype(jnp.bfloat16)
    every = size * cap
    for c in range(width // 128):
        for r in range(every // 128):
            gated_t[c * 128 : (c + 1) * 128, r * 128 : (r + 1) * 128] = (
                result[r * 128 : (r + 1) * 128, c * 128 : (c + 1) * 128].astype(jnp.float32).T.astype(jnp.bfloat16)
            )
    strip = block

    def inner(kk, out):
        return dot_nn(gated_t[out, :], d_before[:, kk * block : (kk + 1) * block])

    def outer(kk, out, t):
        return dot_tn(active[:, pl.ds(pl.multiple_of(kk * block + t * strip, strip), strip)], cots[...])

    def strips(body):
        def run(t, _):
            body(pl.ds(pl.multiple_of(t * strip, strip), strip), t)
            return 0

        lax.fori_loop(0, block // strip, run, 0)

    def chunk(h, kk, out, t):
        return inner(kk, out) if h == 0 else outer(kk, out, t)

    finals = []
    for h in range(2):
        shared = []
        for n, kk in enumerate((3, 1)):

            def give(out, t):
                g_send[h, n, out, :] = chunk(h, kk, out, t).astype(jnp.bfloat16)

            strips(give)
            c = send(g_send.at[h, n], g_recv.at[h, n], g_sem_send.at[h, n], g_sem_recv.at[h, n], shard_peer(1))
            shared.append(c)
        shared[0].wait_recv()
        shared[0].wait_send()

        def other(out, t):
            g_send[h, 0, out, :] = (chunk(h, 2, out, t) + g_recv[h, 0, out, :].astype(jnp.float32)).astype(jnp.bfloat16)

        strips(other)
        c = pltpu.make_async_copy(g_send.at[h, 0], other_out.at[h], out_sem.at[0, h])
        c.start()
        finals.append(c)
        shared[1].wait_recv()
        sent.append(shared[1])

        def keep(out, t):
            stage[h, out, :] = chunk(h, 0, out, t) + g_recv[h, 1, out, :].astype(jnp.float32)

        strips(keep)
        c = pltpu.make_async_copy(stage.at[h], mine_out.at[h], out_sem.at[1, h])
        c.start()
        finals.append(c)

    def produce(r, _):
        span = pl.ds(pl.multiple_of(r * 4 * cap, 16), 4 * cap)
        y = sum(dot_nn(active[span, kk * block : (kk + 1) * block], weights[kk, 1]) for kk in range(4))
        result[span, :] = y.astype(jnp.bfloat16)
        return 0

    lax.fori_loop(0, size // 4, produce, 0)
    for k in range(size):
        c = pltpu.make_async_copy(result.at[part(k)], result_out.at[me ^ k], res_sem.at[k])
        c.start()
        finals.append(c)
    back_in[part(0), :] = back[part(0), :]
    d_gates_in[0] = d_gates[0]
    for k in range(size):
        if k:
            for c in returned[k]:
                c.wait_recv()
        for c in (
            pltpu.make_async_copy(back_in.at[part(k)], back_out.at[me ^ k], back_sem.at[k]),
            pltpu.make_async_copy(d_gates_in.at[k], dgate_out.at[me ^ k], dgb_sem.at[k]),
        ):
            c.start()
            finals.append(c)
    for c in finals:
        c.wait()
    for k in range(1, size):
        arrive[k][1].wait_send()
    for c in sent:
        c.wait_send()


def run_experts(rows, gates, cots, inner_own, outer_own, inner_far):
    size, cap, width = rows.shape
    block = inner_own.shape[1]
    bf = jnp.bfloat16
    f32 = jnp.float32
    every = size * cap
    hb = pl.BlockSpec(memory_space=pl.ANY)
    vm = pltpu.VMEM
    dma = pltpu.SemaphoreType.DMA
    shape = jax.ShapeDtypeStruct
    return pl.pallas_call(
        functools.partial(experts_kernel, size, cap, block),
        in_specs=[hb] * 6,
        out_specs=[hb] * 5,
        out_shape=[
            shape((size, cap, width), bf),
            shape((size, 8, 256), f32),
            shape((2, width, block), f32),
            shape((2, width, block), bf),
            shape((size, cap, width), bf),
        ],
        scratch_shapes=[
            vm((every, width), bf),
            vm((size, 8, 256), f32),
            vm((every, width), bf),
            vm((4, 2, width, block), bf),
            vm((every, 4 * block), bf),
            vm((every, 4 * block), bf),
            vm((6 * cap, width), f32),
            vm((6 * cap, 128), f32),
            vm((every, width), bf),
            vm((size, 8, 256), f32),
            vm((every, width), bf),
            vm((size, 8, 256), f32),
            vm((width, every), bf),
            vm((2, 2, width, block), bf),
            vm((2, 2, width, block), bf),
            vm((2, width, block), f32),
            vm((every, width), bf),
            dma((5,)),
            dma((2, 5)),
        ]
        + [dma((size,))] * 8
        + [dma((2, 2)), dma((2, 2)), dma((size,)), dma((2, 2)), dma((size,)), dma((size,)), dma((size,))],
        compiler_params=pltpu.CompilerParams(collective_id=1, has_side_effects=True, vmem_limit_bytes=62 * 2**20),
        cost_estimate=pl.CostEstimate(flops=36 * 10**9, bytes_accessed=30 * 2**20, transcendentals=4 * 10**6),
    )(rows, gates, cots, inner_own, outer_own, inner_far)


def turned(small, width):
    return jnp.concatenate(
        [small[c * 128 : (c + 1) * 128, :].astype(jnp.float32).T for c in range(width // 128)], axis=1
    )


def three_parts(line):
    hi = line.astype(jnp.bfloat16)
    rest = line - hi.astype(jnp.float32)
    mid = rest.astype(jnp.bfloat16)
    low = rest - mid.astype(jnp.float32)
    none = jnp.zeros((5, line.shape[1]), jnp.float32)
    parts = jnp.concatenate([hi.astype(jnp.float32), mid.astype(jnp.float32), low, none], axis=0)
    return parts.astype(jnp.bfloat16)


def pick_cells(place, first, tile, cells):
    out = []
    for b in range(first // 128, (first + tile) // 128):
        column = columns(place, b)
        lane = lax.broadcasted_iota(jnp.int32, (128, 128), 1).astype(jnp.float32)
        out.append(
            jnp.concatenate([(column == lane + 128.0 * j).astype(jnp.float32) for j in range(cells // 128)], axis=1)
        )
    return jnp.concatenate(out, axis=0).astype(jnp.bfloat16)


def spread_column(line, first, tile, width):
    return jnp.concatenate(
        [
            jnp.concatenate([columns(line, b)] * (width // 128), axis=1)
            for b in range(first // 128, (first + tile) // 128)
        ],
        axis=0,
    )


def route_kernel(
    cap, context_in, tokens_in, weights_in, small, route, place,
    resid_out, cells_out, gate_out, probs_out,
    context, tokens, w_out, normed, sems,
):
    length, width = normed.shape
    experts = probs_out.shape[0]
    loads = [
        pltpu.make_async_copy(weights_in.at[3], w_out, sems.at[0]),
        pltpu.make_async_copy(context_in, context, sems.at[1]),
        pltpu.make_async_copy(tokens_in, tokens, sems.at[2]),
    ]
    for c in loads:
        c.start()
    lines = turned(small, width)
    gain = lines[1:2]
    for c in loads:
        c.wait()
    tile = 512
    for t in range(length // tile):
        r = slice(t * tile, (t + 1) * tile)
        resid = tokens[r, :].astype(jnp.float32) + dot_nn(context[r, :], w_out[...])
        resid_out[r, :] = resid
        scale = lax.rsqrt(jnp.mean(resid * resid, axis=-1, keepdims=True) + 1e-6)
        normed[r, :] = (resid * scale * gain).astype(jnp.bfloat16)
    logits = dot_nt(lines.astype(jnp.bfloat16), normed[...])[2 : 2 + experts]
    top = jnp.exp(logits - jnp.max(logits, axis=0, keepdims=True))
    probs = top / jnp.sum(top, axis=0, keepdims=True)
    probs_out[...] = probs
    which = lax.broadcasted_iota(jnp.int32, probs.shape, 0)
    gate = jnp.sum(jnp.where(which == route[...], probs, 0.0), axis=0, keepdims=True)
    parts = three_parts(gate)
    gate_out[...] = jnp.zeros_like(gate_out)
    for k in range(experts):
        ids = lax.broadcasted_iota(jnp.int32, (cap, length), 0) + k * cap
        pick = (ids == place[...]).astype(jnp.float32).astype(jnp.bfloat16)
        cells_out[k] = dot_nn(pick, normed[...]).astype(jnp.bfloat16)
        found = dot_nt(parts, pick)
        gate_out[k, :, 0:cap] = jnp.broadcast_to(jnp.sum(found, axis=0, keepdims=True), (8, cap))


def run_route(context, tokens, weights, small, route, place, experts, cap):
    length, width = tokens.shape
    bf, f32 = jnp.bfloat16, jnp.float32
    vm = pl.BlockSpec(memory_space=pltpu.VMEM)
    hb = pl.BlockSpec(memory_space=pl.ANY)
    shape = jax.ShapeDtypeStruct
    return pl.pallas_call(
        functools.partial(route_kernel, cap),
        in_specs=[hb] * 3 + [vm] * 3,
        out_specs=[vm] * 4,
        out_shape=[
            shape((length, width), f32),
            shape((experts, cap, width), bf),
            shape((experts, 8, 256), f32),
            shape((experts, length), f32),
        ],
        scratch_shapes=[
            pltpu.VMEM((length, width), bf),
            pltpu.VMEM((length, width), bf),
            pltpu.VMEM((width, width), bf),
            pltpu.VMEM((length, width), bf),
            pltpu.SemaphoreType.DMA((3,)),
        ],
        compiler_params=pltpu.CompilerParams(vmem_limit_bytes=62 * 2**20),
        cost_estimate=pl.CostEstimate(flops=4 * 10**9, bytes_accessed=16 * 2**20, transcendentals=0),
    )(context, tokens, weights, small, route, place)


def unroute_kernel(
    cap, back_in, d_gate_in, resid_in, cot_in, weights_in, context_in, small, route, place, probs,
    d_context, d_resid, extra, keep_out, grad_out,
    back, resid, cot, w_out, context, d_branch, sems,
):
    length, width = resid.shape
    experts = probs.shape[0]
    cells = experts * cap
    loads = [pltpu.make_async_copy(back_in.at[k], back.at[pl.ds(k * cap, cap)], sems.at[4 + k]) for k in range(experts)]
    loads += [
        pltpu.make_async_copy(resid_in, resid, sems.at[0]),
        pltpu.make_async_copy(cot_in, cot, sems.at[1]),
        pltpu.make_async_copy(weights_in.at[3], w_out, sems.at[2]),
        pltpu.make_async_copy(context_in, context, sems.at[3]),
    ]
    for c in loads:
        c.start()
    lines = turned(small, width)
    gain = lines[1:2]
    low_lines = lines.astype(jnp.bfloat16)
    which = lax.broadcasted_iota(jnp.int32, probs.shape, 0)
    chosen = (which == route[...]).astype(jnp.float32)
    gate = jnp.sum(probs[...] * chosen, axis=0, keepdims=True)
    keep = jnp.where(place[...] >= 0, gate, 0.0)
    keep_out[...] = keep
    places = place[...].astype(jnp.float32)
    parts = three_parts(jnp.concatenate([d_gate_in[k, 0:1, 0:cap] for k in range(experts)], axis=1))
    for c in loads[: experts + 3]:
        c.wait()
    tile = 256
    grads = jnp.zeros((128, width), jnp.float32)
    gains = jnp.zeros((1, width), jnp.float32)
    for t in range(length // tile):
        r = slice(t * tile, (t + 1) * tile)
        pick = pick_cells(places, t * tile, tile, cells)
        d_rows = dot_nn(pick, back[...])
        d_gate = jnp.sum(dot_nt(parts, pick), axis=0, keepdims=True)
        d_logits = probs[:, r] * (chosen[:, r] - gate[:, r]) * d_gate
        padded = jnp.concatenate(
            [
                jnp.zeros((2, tile), jnp.float32),
                d_logits.astype(jnp.bfloat16).astype(jnp.float32),
                jnp.zeros((126 - experts, tile), jnp.float32),
            ],
            axis=0,
        )
        d_normed = dot_nn(padded.T.astype(jnp.bfloat16), low_lines) + spread_column(keep, t * tile, tile, width) * d_rows
        x = resid[r, :]
        scale = lax.rsqrt(jnp.mean(x * x, axis=-1, keepdims=True) + 1e-6)
        unit = x * scale
        grads = grads + dot_nn(padded.astype(jnp.bfloat16), (unit * gain).astype(jnp.bfloat16))
        gains = gains + jnp.sum(d_normed * unit, axis=0, keepdims=True)
        pulled = gain * d_normed
        out = cot[r, :].astype(jnp.float32) + scale * (
            pulled - unit * jnp.mean(unit * pulled, axis=-1, keepdims=True)
        )
        d_resid[r, :] = out
        low = out.astype(jnp.bfloat16)
        d_branch[r, :] = low
        d_context[r, :] = dot_nt(low, w_out[...]).astype(jnp.bfloat16)
    loads[experts + 3].wait()
    grad_out[...] = dot_tn(context[...], d_branch[...]).astype(jnp.bfloat16)
    row = lax.broadcasted_iota(jnp.int32, (128, width), 0)
    extra[...] = jnp.where(row == 1, gains, grads)


def run_unroute(back, d_gate, resid, cot, weights, context, small, route, place, probs):
    experts, cap, width = back.shape
    length = resid.shape[0]
    bf, f32 = jnp.bfloat16, jnp.float32
    vm = pl.BlockSpec(memory_space=pltpu.VMEM)
    hb = pl.BlockSpec(memory_space=pl.ANY)
    shape = jax.ShapeDtypeStruct
    return pl.pallas_call(
        functools.partial(unroute_kernel, cap),
        in_specs=[hb, vm, hb, hb, hb, hb] + [vm] * 4,
        out_specs=[vm] * 5,
        out_shape=[
            shape((length, width), bf),
            shape((length, width), f32),
            shape((128, width), f32),
            shape((1, length), f32),
            shape((width, width), bf),
        ],
        scratch_shapes=[
            pltpu.VMEM((experts * cap, width), bf),
            pltpu.VMEM((length, width), f32),
            pltpu.VMEM((length, width), bf),
            pltpu.VMEM((width, width), bf),
            pltpu.VMEM((length, width), bf),
            pltpu.VMEM((length, width), bf),
            pltpu.SemaphoreType.DMA((4 + experts,)),
        ],
        compiler_params=pltpu.CompilerParams(vmem_limit_bytes=62 * 2**20),
        cost_estimate=pl.CostEstimate(flops=4 * 10**9, bytes_accessed=18 * 2**20, transcendentals=0),
    )(back, d_gate, resid, cot, weights, context, small, route, place, probs)


class Reduction:
    def __init__(self, index, partial, near, far_send, far_recv, full, x_send, x_recv, half, z_send, z_recv, piece, result, send_sems, recv_sems):
        self.partial, self.near, self.far_send, self.far_recv = partial, near, far_send, far_recv
        self.full, self.x_send, self.x_recv, self.half = full, x_send, x_recv, half
        self.z_send, self.z_recv, self.piece, self.result = z_send, z_recv, piece, result
        self.index, self.send_sems, self.recv_sems = index, send_sems, recv_sems
        self.own = full.shape[0]
        self.width = full.shape[1]
        self.type = partial.dtype
        self.copies = {}

    def block(self, bit):
        return pl.ds(pl.multiple_of((lax.axis_index("shard") ^ bit) * self.own, self.own & -self.own), self.own)

    def half_rows(self, bit):
        rows = self.own // 2
        return pl.ds(pl.multiple_of(((lax.axis_index("expert") & 1) ^ bit) * rows, rows & -rows), rows)

    def quarter(self, step):
        j = (lax.axis_index("expert") >> 1) ^ step
        rows = self.own // 2
        if self.type == jnp.float32:
            return (pl.ds(pl.multiple_of(j * (rows // 4), 8), rows // 4), slice(None))
        return (
            pl.ds(pl.multiple_of((j >> 1) * (rows // 2), 16), rows // 2),
            pl.ds(pl.multiple_of((j & 1) * (self.width // 2), 128), self.width // 2),
        )

    def go(self, slot, src, dst, peer):
        self.copies[slot] = send(src, dst, self.send_sems.at[self.index, slot], self.recv_sems.at[self.index, slot], peer)

    def core(self):
        self.go(0, self.partial.at[self.block(3)], self.near.at[1], shard_peer(1))
        self.go(1, self.partial.at[self.block(1)], self.near.at[0], shard_peer(1))

    def y(self):
        self.copies[0].wait_recv()
        other = self.partial[self.block(2), :].astype(jnp.float32) + self.near[1].astype(jnp.float32)
        self.far_send[...] = other.astype(self.type)
        self.go(2, self.far_send, self.far_recv, shard_peer(2))
        self.copies[1].wait_recv()
        self.full[...] = self.partial[self.block(0), :].astype(jnp.float32) + self.near[0].astype(jnp.float32)

    def x(self):
        self.copies[2].wait_recv()
        self.full[...] += self.far_recv[...].astype(jnp.float32)
        self.x_send[...] = self.full[self.half_rows(1), :].astype(self.type)
        self.go(3, self.x_send, self.x_recv, expert_peer(1))

    def z(self):
        self.copies[3].wait_recv()
        self.half[...] = self.own_half() + self.x_recv[...].astype(jnp.float32)
        self.z_send[...] = self.half[...].astype(self.type)
        for step in (2, 3, 1):
            self.go(3 + step, self.z_send.at[self.quarter(step)], self.z_recv.at[step - 1], expert_peer(2 * step))

    def own_half(self):
        return self.full[self.half_rows(0), :]

    def spread(self):
        for step in (1, 2, 3):
            self.copies[3 + step].wait_recv()
        rows, cols = self.quarter(0)
        total = self.half[rows, cols]
        for step in (1, 2, 3):
            total = total + self.z_recv[step - 1].astype(jnp.float32)
        self.piece[...] = total.astype(self.type)
        target = self.place()
        for step in (2, 3, 1):
            self.go(6 + step, self.piece, self.result.at[target], expert_peer(2 * step))
        self.result[target] = self.piece[...]

    def place(self):
        j = lax.axis_index("expert") >> 1
        first = (lax.axis_index("expert") & 1) * (self.own // 2)
        rows = self.own // 2
        if self.type == jnp.float32:
            return (pl.ds(pl.multiple_of(first + j * (rows // 4), 8), rows // 4), slice(None))
        return (
            pl.ds(pl.multiple_of(first + (j >> 1) * (rows // 2), 16), rows // 2),
            pl.ds(pl.multiple_of((j & 1) * (self.width // 2), 128), self.width // 2),
        )

    def cross(self):
        for step in (1, 2, 3):
            self.copies[6 + step].wait_recv()
        self.go(10, self.result.at[self.half_rows(0)], self.result.at[self.half_rows(0)], expert_peer(1))

    def finish(self, out):
        self.copies[10].wait_recv()
        out[...] = self.result[...].astype(jnp.float32)

    def drain(self):
        for c in self.copies.values():
            c.wait_send()


class Crossed(Reduction):
    other = None

    def y(self):
        rows = self.own // 2
        self.copies[0].wait_recv()
        self.other[...] = self.partial[self.block(2), :].astype(jnp.float32) + self.near[1].astype(jnp.float32)
        self.far_send[rows:, :] = self.other[self.half_rows(1), :].astype(self.type)
        self.copies[1].wait_recv()
        self.full[...] = self.partial[self.block(0), :].astype(jnp.float32) + self.near[0].astype(jnp.float32)
        self.far_send[:rows, :] = self.full[self.half_rows(1), :].astype(self.type)
        self.go(2, self.far_send, self.far_recv, expert_peer(1))

    def x(self):
        rows = self.own // 2
        self.copies[2].wait_recv()
        other = self.other[self.half_rows(0), :] + self.far_recv[rows:, :].astype(jnp.float32)
        self.x_send[...] = other.astype(self.type)
        self.go(3, self.x_send, self.x_recv, shard_peer(2))

    def own_half(self):
        return self.full[self.half_rows(0), :] + self.far_recv[: self.own // 2, :].astype(jnp.float32)


def place_table(near, far, ps, own, heads):
    buckets = 32
    wide = near.shape[2]
    offset = wide // 2 - lax.broadcasted_iota(jnp.int32, (wide, buckets), 0)
    onehot = (bucket_index(offset) == lax.broadcasted_iota(jnp.int32, (wide, buckets), 1)).astype(jnp.float32)
    sums = jnp.concatenate([near[j] for j in range(near.shape[0])], axis=0)
    table = lax.dot_general(
        sums, onehot, (((1,), (0,)), ((), ())), preferred_element_type=jnp.float32, precision=lax.Precision.HIGHEST
    )
    ends = jnp.concatenate([far[j] for j in range(far.shape[0])], axis=0)
    low = jnp.sum(ends[:, :128], axis=1, keepdims=True)
    high = jnp.sum(ends[:, 128:], axis=1, keepdims=True)
    which = lax.broadcasted_iota(jnp.int32, (heads, buckets), 1)
    table = table + jnp.where(which == 15, low, 0.0) + jnp.where(which == 31, high, 0.0)
    part = buckets // 4
    square = jnp.concatenate([table, jnp.zeros((heads, 128 - buckets), jnp.float32)], axis=1)
    square = jnp.concatenate([jnp.zeros((128 - heads, 128), jnp.float32), square], axis=0).T
    lane = lax.broadcasted_iota(jnp.int32, (part, 128), 1)
    for j in range(4):
        r = slice(j * own, j * own + part)
        ps[r, :] = jnp.where(lane >= 128 - heads, square[j * part : (j + 1) * part, :], ps[r, :])


def tail_kernel(
    heads, experts,
    normed_in, dq_in, dk_in, dv_in, p_in, weights_in, tokens_in, d_resid_in,
    cells_in, resid_in, small, extra, near_sums, far_sums, place, keep_gate,
    o_out, q_out, k_out, v_out, gain_out, gain_two_out, router_out, table_out, tokens_out, mixed_out,
    normed, dq, dk, dv, weights, tokens, d_resid, cells, resid,
    normed_t, p_ref, near, far_send, far_recv, full, x_send, x_recv, half, z_send, z_recv, piece, result, other,
    ps, s_near, s_far_send, s_far_recv, s_full, s_x_send, s_x_recv, s_half, s_z_send, s_z_recv, s_piece, s_result,
    send_sems, recv_sems, load_sems,
):
    length, width = normed.shape
    tile = 256
    loads = [
        pltpu.make_async_copy(src, dst, load_sems.at[i])
        for i, (src, dst) in enumerate(
            (
                (p_in, p_ref.at[0]),
                (weights_in.at[0:3], weights),
                (normed_in, normed),
                (dq_in, dq),
                (dk_in, dk),
                (dv_in, dv),
                (tokens_in, tokens),
                (d_resid_in, d_resid),
                (resid_in, resid),
            )
        )
    ]
    cap = cells_in.shape[1]
    loads += [
        pltpu.make_async_copy(cells_in.at[k], cells.at[pl.ds(k * cap, cap)], load_sems.at[11 + k])
        for k in range(cells_in.shape[0])
    ]
    for c in loads:
        c.start()
    greet([shard_peer(1), shard_peer(2)] + [expert_peer(k) for k in (1, 2, 4, 6)])
    work = []
    for m in range(4):
        w = (Crossed if m >= 2 else Reduction)(
            m, p_ref.at[m], near.at[m], far_send.at[m], far_recv.at[m], full.at[m], x_send.at[m], x_recv.at[m],
            half.at[m], z_send.at[m], z_recv.at[m], piece.at[m], result.at[m], send_sems, recv_sems,
        )
        w.other = other.at[m % 2]
        work.append(w)
    o, q, k, v = work
    s = Reduction(
        4, ps, s_near, s_far_send, s_far_recv, s_full, s_x_send, s_x_recv, s_half, s_z_send, s_z_recv, s_piece,
        s_result, send_sems, recv_sems,
    )

    def strips(m, make):
        p_ref[m] = make(slice(None)).astype(jnp.bfloat16)

    loads[0].wait()
    o.core()
    loads[2].wait()
    for c in range(width // 128):
        for t in range(length // 128):
            normed_t[c * 128 : (c + 1) * 128, t * 128 : (t + 1) * 128] = (
                normed[t * 128 : (t + 1) * 128, c * 128 : (c + 1) * 128].astype(jnp.float32).T.astype(jnp.bfloat16)
            )
    o.y()
    loads[3].wait()
    strips(1, lambda r: dot_nn(normed_t[r, :], dq[...]))
    q.core()
    loads[4].wait()
    strips(2, lambda r: dot_nn(normed_t[r, :], dk[...]))
    q.y()
    k.core()
    loads[5].wait()
    strips(3, lambda r: dot_nn(normed_t[r, :], dv[...]))
    v.core()
    k.y()
    head = small[...].astype(jnp.float32)
    gain = jnp.concatenate([head[c * 128 : (c + 1) * 128, :].T[0:1] for c in range(width // 128)], axis=1)
    for c in [loads[1]] + loads[6:8]:
        c.wait()

    def back(t, total):
        r = pl.ds(pl.multiple_of(t * tile, tile), tile)
        grad = dot_nt(dq[r, :], weights[0]) + dot_nt(dk[r, :], weights[1]) + dot_nt(dv[r, :], weights[2])
        x = tokens[r, :].astype(jnp.float32)
        scale = lax.rsqrt(jnp.mean(x * x, axis=-1, keepdims=True) + 1e-6)
        unit = x * scale
        pulled = grad * gain
        shift = jnp.mean(unit * pulled, axis=-1, keepdims=True)
        tokens_out[r, :] = (d_resid[r, :] + scale * (pulled - unit * shift)).astype(jnp.bfloat16)
        return total + jnp.sum(grad * unit, axis=0, keepdims=True)

    def some(first, last, total):
        return lax.fori_loop(first, last, back, total)

    def mix(t):
        r = slice(t * tile, (t + 1) * tile)
        arrived = dot_nn(pick_cells(places, t * tile, tile, cells.shape[0]), cells[...])
        mixed_out[r, :] = (resid[r, :] + spread_column(keep_gate, t * tile, tile, width) * arrived).astype(jnp.bfloat16)

    places = place[...].astype(jnp.float32)
    total = some(0, 1, jnp.zeros((1, width), jnp.float32))
    o.x()
    v.y()
    total = some(1, 3, total)
    k.x()
    total = some(3, length // tile, total)
    q.x()
    lane = lax.broadcasted_iota(jnp.int32, (128, 128), 1)
    for c in range(width // 128):
        column = jnp.broadcast_to(total[:, c * 128 : (c + 1) * 128], (128, 128)).T
        ps[c * 128 : (c + 1) * 128, :] = jnp.where(lane == 0, column, extra[:, c * 128 : (c + 1) * 128].T)
    place_table(near_sums, far_sums, ps, s.own, heads)
    s.core()
    o.z()
    k.z()
    s.y()
    for c in loads[8:]:
        c.wait()
    mix(0)
    o.spread()
    v.x()
    q.z()
    s.x()
    mix(1)
    k.spread()
    o.cross()
    v.z()
    s.z()
    mix(2)
    k.cross()
    q.spread()
    v.spread()
    s.spread()
    mix(3)
    o.finish(o_out)
    q.cross()
    v.cross()
    s.cross()
    k.finish(k_out)
    q.finish(q_out)
    v.finish(v_out)
    s.copies[10].wait_recv()
    final = s_result[...]
    pad = jnp.concatenate([final, jnp.zeros((256 - s.own, 128), jnp.float32)], axis=0)
    lines = jnp.concatenate([pad[:128, :].T, pad[128:, :].T], axis=1)
    gain_out[...] = lines[0:1, : s.own]
    gain_two_out[...] = lines[1:2, : s.own]
    router_out[...] = lines[2 : 2 + experts, : s.own]
    table_out[...] = final[: table_out.shape[0], 128 - heads :]
    for w in work + [s]:
        w.drain()


def run_tail(
    normed, dq, dk, dv, partial, weights, tokens, d_resid, cells, resid, small, extra, near, far,
    place, keep_gate, experts, own_buckets,
):
    length, width = normed.shape
    own = width // 4
    heads = near.shape[0] * near.shape[1]
    bf = jnp.bfloat16
    f32 = jnp.float32
    vm = pltpu.VMEM
    hb = pl.BlockSpec(memory_space=pl.ANY)
    mem = pl.BlockSpec(memory_space=pltpu.VMEM)
    h = own // 2
    shape = jax.ShapeDtypeStruct
    return pl.pallas_call(
        functools.partial(tail_kernel, heads, experts),
        in_specs=[hb] * 10 + [mem] * 6,
        out_specs=[mem] * 10,
        out_shape=[shape((own, width), f32)] * 4
        + [
            shape((1, own), f32),
            shape((1, own), f32),
            shape((experts, own), f32),
            shape((own_buckets, heads), f32),
            shape((length, width), bf),
            shape((length, width), bf),
        ],
        scratch_shapes=[vm((length, width), bf)] * 4
        + [
            vm((3, width, width), bf),
            vm((length, width), bf),
            vm((length, width), f32),
            vm((cells.shape[0] * cells.shape[1], width), bf),
            vm((length, width), f32),
            vm((width, length), bf),
            vm((4, width, width), bf),
            vm((4, 2, own, width), bf),
            vm((4, own, width), bf),
            vm((4, own, width), bf),
            vm((4, own, width), f32),
            vm((4, h, width), bf),
            vm((4, h, width), bf),
            vm((4, h, width), f32),
            vm((4, h, width), bf),
            vm((4, 3, h // 2, width // 2), bf),
            vm((4, h // 2, width // 2), bf),
            vm((4, own, width), bf),
            vm((2, own, width), f32),
            vm((width, 128), f32),
            vm((2, own, 128), f32),
            vm((own, 128), f32),
            vm((own, 128), f32),
            vm((own, 128), f32),
            vm((h, 128), f32),
            vm((h, 128), f32),
            vm((h, 128), f32),
            vm((h, 128), f32),
            vm((3, h // 4, 128), f32),
            vm((h // 4, 128), f32),
            vm((own, 128), f32),
            pltpu.SemaphoreType.DMA((5, 11)),
            pltpu.SemaphoreType.DMA((5, 11)),
            pltpu.SemaphoreType.DMA((20,)),
        ],
        compiler_params=pltpu.CompilerParams(collective_id=2, has_side_effects=True, vmem_limit_bytes=62 * 2**20),
        cost_estimate=pl.CostEstimate(flops=11 * 10**9, bytes_accessed=40 * 2**20, transcendentals=0),
    )(
        normed, dq, dk, dv, partial, weights, tokens, d_resid, cells, resid, small, extra, near,
        far, place, keep_gate,
    )


def finish_kernel(count, *refs):
    ins, (mine, other), outs = refs[:count], refs[count : count + 2], refs[count + 2 : 2 * count + 2]
    totals = refs[2 * count + 2 : 2 * count + 4]
    add_a, add_b = refs[2 * count + 4 : 2 * count + 6]
    bufs = refs[2 * count + 6 : 3 * count + 6]
    in_sems, out_sems = refs[3 * count + 6 :]
    first = [pltpu.make_async_copy(mine, add_a, in_sems.at[count]), pltpu.make_async_copy(other, add_b, in_sems.at[count + 1])]
    loads = [pltpu.make_async_copy(ins[i], bufs[i], in_sems.at[i]) for i in range(count)]
    for c in first + loads:
        c.start()
    for c in first:
        c.wait()
    add_a[...] = add_a[...] + add_b[...].astype(jnp.float32)
    stores = [pltpu.make_async_copy(add_a.at[h], totals[h], out_sems.at[count + h]) for h in range(2)]
    for c in stores:
        c.start()
    for i in range(count):
        loads[i].wait()
        c = pltpu.make_async_copy(bufs[i], outs[i], out_sems.at[i])
        c.start()
        stores.append(c)
    for c in stores:
        c.wait()


def run_finish(results, mine, other):
    count = len(results)
    hb = pl.BlockSpec(memory_space=pl.ANY)
    return pl.pallas_call(
        functools.partial(finish_kernel, count),
        in_specs=[hb] * (count + 2),
        out_specs=[hb] * (count + 2),
        out_shape=[jax.ShapeDtypeStruct(r.shape, r.dtype) for r in results]
        + [jax.ShapeDtypeStruct(mine.shape[1:], jnp.float32)] * 2,
        scratch_shapes=[pltpu.VMEM(mine.shape, jnp.float32), pltpu.VMEM(other.shape, jnp.bfloat16)]
        + [pltpu.VMEM(r.shape, r.dtype) for r in results]
        + [pltpu.SemaphoreType.DMA((count + 2,)), pltpu.SemaphoreType.DMA((count + 2,))],
        compiler_params=pltpu.CompilerParams(vmem_limit_bytes=62 * 2**20),
        cost_estimate=pl.CostEstimate(flops=10**6, bytes_accessed=24 * 2**20, transcendentals=0),
    )(*results, mine, other)

EPS = 1e-06
BF = jnp.bfloat16
F32 = jnp.float32


def dot_tn(a, b):
    return lax.dot_general(a, b, (((0,), (0,)), ((), ())), preferred_element_type=F32)


def swap(value, axis, size, bit):
    return lax.ppermute(value, axis, [(i, i ^ bit) for i in range(size)])


def direct(size):
    return size == 8


def exchange(blocks):
    return lax.all_to_all(blocks, "expert", split_axis=0, concat_axis=0, tiled=True)


def gather_shards(value, size):
    if size == 4:
        far = swap(value, "shard", size, 2)
        near = swap(value, "shard", size, 1)
        return [value, near, far, swap(far, "shard", size, 1)]
    return [value] + [swap(value, "shard", size, k) for k in range(1, size)]


def reduce_shards(blocks, size):
    if size == 4:
        near1 = swap(blocks[3].astype(BF), "shard", size, 1)
        near0 = swap(blocks[1].astype(BF), "shard", size, 1)
        other = swap((blocks[2].astype(F32) + near1.astype(F32)).astype(BF), "shard", size, 2)
        return blocks[0].astype(F32) + near0.astype(F32) + other.astype(F32)
    total = blocks[0].astype(F32)
    for k in range(1, size):
        total = total + swap(blocks[k].astype(BF), "shard", size, k).astype(F32)
    return total


def experts_by_collectives(row_blocks, gate_slots, cot_blocks, inner, outer, size, shards, cap):
    inners = gather_shards(inner, shards)
    outers = gather_shards(outer, shards)
    cells, width = size * cap, row_blocks.shape[2]
    rows = exchange(row_blocks).reshape(cells, width)
    cots = cot_blocks.reshape(cells, width)
    gates = exchange(gate_slots.reshape(size, cap)).reshape(cells, 1)
    half = cells // 2
    parts = [expert_half([rows[i : i + half]], [cots[i : i + half]], inners, outers) for i in (0, half)]
    back, active, d_before, d_gate = (
        jnp.concatenate([p[0][0] if i == 0 else p[i] for p in parts], axis=0) for i in range(4)
    )
    back = exchange(back.reshape(size, cap, width)).reshape(cells, width)
    d_gate = exchange(d_gate.reshape(size, cap)).reshape(cells)
    d_out = (cots.astype(F32) * gates).astype(BF)
    gated = (rows.astype(F32) * gates).astype(BF)
    block = inner.shape[1]
    spans = [slice(k * block, (k + 1) * block) for k in range(shards)]
    grad_outer = reduce_shards([dot_tn(active[:, p], d_out) for p in spans], shards)
    grad_inner = reduce_shards([dot_tn(gated, d_before[:, p]) for p in spans], shards)
    result = dot_nn(active, jnp.concatenate(outers, axis=0)).astype(BF).reshape(size, cap, width)
    result = exchange(result).reshape(cells, width)
    return back, d_gate, grad_inner, grad_outer, result


def finish_direct(
    tokens, routes, cotangent, context, weights, small, place, cot_blocks, inner_own, outer_own, inner_far,
    capacity, query, key, value, normed, forward, seg, bias, own_buckets,
):
    experts = lax.axis_size("expert")
    shards = lax.axis_size("shard")
    total, width = normed.shape
    route = routes.reshape(1, total)
    flat = tokens.reshape(total, width)
    resid, row_blocks, gate_lines, probs = run_route(context, flat, weights, small, route, place, experts, capacity)
    back, gate_back, mine, other, expert_out = run_experts(
        row_blocks, gate_lines, cot_blocks, inner_own, outer_own, inner_far
    )
    other = swap(other, "shard", shards, 2)
    out_cells = exchange(expert_out)
    d_context, d_resid, extra, keep, partial = run_unroute(
        back, gate_back, resid, cotangent.reshape(total, width), weights, context, small, route, place, probs
    )
    d_query, d_key, d_value, near_sums, far_sums = attn_bwd(
        seg[0][2], seg[0][3], query, key, value, d_context, context, forward[0][1], seg[0][0], seg[0][1], bias
    )
    (
        sum_output, sum_query, sum_key, sum_value, sum_gain, sum_gain_two, sum_router, sum_table, d_tokens, mixed,
    ) = run_tail(
        normed, d_query, d_key, d_value, partial, weights, flat, d_resid, out_cells, resid,
        small, extra, near_sums, far_sums, place, keep, experts, own_buckets,
    )
    (
        sum_output, sum_query, sum_key, sum_value, d_tokens, mixed, sum_gain, sum_gain_two, sum_router, sum_table,
        grad_inner, grad_outer,
    ) = run_finish(
        [sum_output, sum_query, sum_key, sum_value, d_tokens, mixed, sum_gain, sum_gain_two, sum_router, sum_table],
        mine, other,
    )
    return (
        mixed.reshape(tokens.shape),
        d_tokens.reshape(tokens.shape),
        sum_gain[0],
        sum_query,
        sum_key,
        sum_value,
        sum_output,
        sum_table,
        sum_gain_two[0],
        sum_router.T,
        grad_inner[None],
        grad_outer[None],
    )


def per_device(
    tokens,
    segments,
    routes,
    order,
    gain_attn,
    w_query,
    w_key,
    w_value,
    w_output,
    rel_bias,
    gain_ffn,
    w_router,
    w_in,
    w_out,
    cotangent,
):
    seq_count, length, width = tokens.shape
    total = seq_count * length
    experts = lax.axis_size("expert")
    shards = lax.axis_size("shard")
    me = lax.axis_index("expert")
    my_shard = lax.axis_index("shard")
    capacity = (5 * total + 4 * experts - 1) // (4 * experts)
    cells = experts * capacity
    heads = rel_bias.shape[1]
    own = w_query.shape[0]
    own_buckets = rel_bias.shape[0]
    buckets = own_buckets * shards
    small = jnp.concatenate([gain_attn[:, None], gain_ffn[:, None], w_router], axis=1)
    small = jnp.pad(small, ((0, 0), (0, 128 - small.shape[1])))
    small = lax.dynamic_update_slice(small, rel_bias, (0, 128 - heads))
    route = routes.reshape(total)
    chosen = (route[:, None] == jnp.arange(experts, dtype=jnp.int32)[None, :]).astype(F32)
    cot = cotangent.reshape(total, width)
    ranks = (jnp.arange(seq_count, dtype=jnp.int32)[:, None] * length + order).reshape(1, total)
    place_line, cot_cells = find_slots(routes.reshape(1, total), ranks, cot, cells, capacity)
    cot_blocks = exchange(cot_cells.reshape(experts, capacity, width))
    query, key, value, normed_low, small_all, seg_query, seg_key, bias, weights_all = project(
        tokens.reshape(total, width), small, (w_query, w_key, w_value, w_output), segments.reshape(1, total), heads
    )
    place = place_line[0]
    kept = place >= 0
    spread = (jnp.arange(cells, dtype=jnp.int32)[:, None] == place[None, :]).astype(BF)

    def to_blocks(values):
        return dot_nn(spread, values).astype(BF).reshape(experts, capacity, width)

    query_all, key_all, value_all, output_all = (weights_all[i] for i in range(4))
    inner_own, outer_own = w_in[0], w_out[0]
    if direct(experts):
        inner_own, query = lax.optimization_barrier((inner_own, query))
        inner_far = swap(inner_own, "shard", shards, 2)
    inputs = tokens.reshape(total, width).astype(F32)
    gain_two = small_all[:, 1].astype(F32)
    router_all = small_all[:, 2 : 2 + experts]
    rows_of = [slice(i * length, (i + 1) * length) for i in range(seq_count)]
    seg = [(seg_query[r], seg_key[r]) + seg_ranges(segments[i]) for i, r in enumerate(rows_of)]
    forward = [
        attn_fwd(s[2], s[3], query[r], key[r], value[r], s[0], s[1], bias)
        for s, r in zip(seg, rows_of)
    ]
    context = jnp.concatenate([f[0] for f in forward], axis=0) if seq_count > 1 else forward[0][0]
    if direct(experts):
        return finish_direct(
            tokens, routes, cotangent, context, weights_all, small_all, place_line, cot_blocks, inner_own, outer_own,
            inner_far, capacity, query, key, value, normed_low, forward, seg, bias, own_buckets,
        )
    resid = inputs + dot_nn(context, output_all)
    scale_two = lax.rsqrt(jnp.mean(resid * resid, axis=-1, keepdims=True) + EPS)
    unit_two = resid * scale_two
    normed_two_low = (unit_two * gain_two).astype(BF)
    logits = dot_nn(normed_two_low, router_all)
    probs = jax.nn.softmax(logits, axis=-1)
    gate = jnp.sum(probs * chosen, axis=-1)
    keep_weight = kept.astype(F32)
    keep_gate = gate * keep_weight
    gate_slots = jnp.sum(jnp.where(place[None, :] == jnp.arange(cells)[:, None], gate[None, :], 0), axis=1)
    row_blocks = to_blocks(normed_two_low)
    back, gate_cells, grad_inner, grad_outer, out_cells = experts_by_collectives(
        row_blocks, gate_slots, cot_blocks, w_in[0], w_out[0], experts, shards, capacity
    )
    upstream = cot.astype(F32)
    d_rows = dot_tn(spread, back)
    d_gate = jnp.sum(
        jnp.where(place[:, None] == jnp.arange(cells)[None, :], gate_cells[None, :], 0), axis=1
    )
    d_logits = (probs * (d_gate[:, None] * chosen - (d_gate * gate)[:, None])).astype(BF)
    d_router = dot_tn(normed_two_low, d_logits)
    d_normed_two = dot_nt(d_logits, router_all) + keep_gate[:, None] * d_rows
    d_gain_two = jnp.sum(d_normed_two * unit_two, axis=0)
    pulled = gain_two * d_normed_two
    d_resid = upstream + scale_two * (
        pulled - unit_two * jnp.mean(unit_two * pulled, axis=-1, keepdims=True)
    )
    d_branch = d_resid.astype(BF)
    d_context = dot_nt(d_branch, output_all).astype(BF)
    backward = [
        attn_bwd(s[2], s[3], query[r], key[r], value[r], d_context[r], f[0], f[1], s[0], s[1], bias)
        for s, r, f in zip(seg, rows_of, forward)
    ]
    d_query, d_key, d_value = (
        jnp.concatenate([b[i] for b in backward], axis=0) if seq_count > 1 else backward[0][i]
        for i in range(3)
    )
    tail = jnp.concatenate([jnp.zeros_like(d_gain_two)[:, None], d_gain_two[:, None], d_router], axis=1)
    tail = jnp.pad(tail, ((0, 0), (0, 128 - tail.shape[1])))
    flat_tokens = tokens.reshape(total, width)
    d_table = sum(table_grad(b[3], b[4], buckets) for b in backward)
    tail = lax.dynamic_update_slice(
        tail.reshape(shards, own, 128), d_table.reshape(shards, own_buckets, heads), (0, 0, 128 - heads)
    ).reshape(width, 128)
    if True:
        d_normed = (
            dot_nt(d_query, query_all) + dot_nt(d_key, key_all) + dot_nt(d_value, value_all)
        )
        inputs_again = flat_tokens.astype(F32)
        scale_one = lax.rsqrt(jnp.mean(inputs_again * inputs_again, axis=-1, keepdims=True) + EPS)
        unit_one = inputs_again * scale_one
        tail = tail.at[:, 0].set(jnp.sum(d_normed * unit_one, axis=0))
        pulled_one = small_all[:, 0].astype(F32) * d_normed
        d_tokens = d_resid + scale_one * (
            pulled_one - unit_one * jnp.mean(unit_one * pulled_one, axis=-1, keepdims=True)
        )
        pairs = ((context, d_branch), (normed_low, d_query), (normed_low, d_key), (normed_low, d_value))
        parts = [dot_tn(left, right) for left, right in pairs] + [tail]
        sum_output, sum_query, sum_key, sum_value, sums = (
            lax.psum(
                reduce_shards(
                    [lax.dynamic_slice_in_dim(p, (my_shard ^ k) * own, own, 0) for k in range(shards)], shards
                ),
                "expert",
            )
            for p in parts
        )
    arrived = dot_tn(spread, out_cells)
    mixed = resid + keep_gate[:, None] * arrived
    return (
        mixed.astype(BF).reshape(tokens.shape),
        d_tokens.astype(BF).reshape(tokens.shape),
        sums[:, 0],
        sum_query,
        sum_key,
        sum_value,
        sum_output,
        sums[:own_buckets, 128 - heads :],
        sums[:, 1],
        sums[:, 2 : 2 + experts],
        grad_inner[None],
        grad_outer[None],
    )


def solution(mesh):
    in_specs = (
        P(("expert", "shard"), None, None),
        P(("expert", "shard"), None),
        P(("expert", "shard"), None, None),
        P(("expert", "shard"), None),
        P("shard"),
        P("shard", None),
        P("shard", None),
        P("shard", None),
        P("shard", None),
        P("shard", None),
        P("shard"),
        P("shard", None),
        P("expert", None, "shard"),
        P("expert", "shard", None),
        P(("expert", "shard"), None, None),
    )
    out_specs = (
        P(("expert", "shard"), None, None),
        P(("expert", "shard"), None, None),
        P("shard"),
        P("shard", None),
        P("shard", None),
        P("shard", None),
        P("shard", None),
        P("shard", None),
        P("shard"),
        P("shard", None),
        P("expert", None, "shard"),
        P("expert", "shard", None),
    )
    return jax.shard_map(
        per_device, mesh=mesh, in_specs=in_specs, out_specs=out_specs, check_vma=False
    )
```

```python
import functools

import jax
import jax.numpy as jnp
from jax import lax
from jax.experimental import pallas as pl
from jax.experimental.pallas import tpu as pltpu
from jax.sharding import PartitionSpec as P
HEAD_DIM=64
BLK=128
EDGES = (12, 16, 23, 32, 46, 64, 91)
BIG=1e9
def bucket_index(offset):
    magnitude = jnp.abs(offset)
    far = 8 + sum(((magnitude >= edge).astype(jnp.int32) for edge in EDGES))
    near = jnp.where(magnitude < 8, magnitude, far)
    return near + 16 * (offset > 0).astype(jnp.int32)

def dot_nt(a,b): return lax.dot_general(a,b,(((1,),(1,)),((),())),preferred_element_type=jnp.float32)
def dot_nn(a,b): return lax.dot_general(a,b,(((1,),(0,)),((),())),preferred_element_type=jnp.float32)

def head_mask():
    lane=lax.broadcasted_iota(jnp.int32,(BLK,2*HEAD_DIM),1)
    return (lane<HEAD_DIM).astype(jnp.float32).astype(jnp.bfloat16)

def build_bias(w_ref, bias_ref, nblk, pairs):
    rows = (2 * nblk - 1) * BLK
    near = (nblk - 2) * BLK
    for j in range(pairs):
        for h in range(2):
            c = slice((2 * j + h) * BLK, (2 * j + h + 1) * BLK)
            w = w_ref[j, h : h + 1, :]
            bias_ref[0:near, c] = jnp.broadcast_to(w[:, 511:512], (near, BLK))
            bias_ref[near + 3 * BLK : rows, c] = jnp.broadcast_to(w[:, 0:1], (near, BLK))
            r = pltpu.roll(jnp.broadcast_to(w, (BLK, 512)), 0, 1, stride=1, stride_axis=0)
            bias_ref[near : near + BLK, c] = r[:, 384:512]
            bias_ref[near + BLK : near + 2 * BLK, c] = r[:, 256:384]
            bias_ref[near + 2 * BLK : near + 3 * BLK, c] = r[:, 128:256]


def by_width(nblk, count, run):
    for n in range(1, nblk + 1):

        @pl.when(count == n)
        def _():
            run(n * BLK)


def pair_of(block, mask):
    return jnp.concatenate([block * mask, block * (1 - mask)], axis=0)


def flip(src_ref, dst_ref, nblk, pairs):
    for j in range(pairs):
        c = slice(j * BLK, (j + 1) * BLK)
        for b in range(nblk):
            s = slice(b * BLK, (b + 1) * BLK)
            dst_ref[c, s] = src_ref[s, c].astype(jnp.float32).T.astype(jnp.bfloat16)


def join_heads(wide):
    return jnp.concatenate([wide[:HEAD_DIM, :BLK], wide[HEAD_DIM:, BLK:]], axis=0)


def fwd_kernel(nblk, pairs, lo_ref, nb_ref, q_ref, k_ref, v_ref, segq_ref, segk_ref, w_ref, ctx_ref, lse_ref, vt_ref, bias_ref):
    build_bias(w_ref, bias_ref, nblk, pairs)
    flip(v_ref, vt_ref, nblk, pairs)
    mask = head_mask()
    lanes = [slice(j * BLK, (j + 1) * BLK) for j in range(pairs)]
    both = [slice(2 * j * BLK, 2 * (j + 1) * BLK) for j in range(pairs)]

    def body(qb, _):
        rows = pl.ds(pl.multiple_of(qb * BLK, BLK), BLK)
        lob = lo_ref[qb]
        sq = segq_ref[rows, :]
        sq = jnp.concatenate([sq, sq], axis=0)
        q_cat = [jnp.concatenate([pair_of(q_ref[rows, c], mask), sq], axis=1) for c in lanes]

        def run(W):
            ks = pl.ds(pl.multiple_of(lob * BLK, BLK), W)
            bs = pl.ds(pl.multiple_of((lob - qb + nblk - 1) * BLK, BLK), W)
            sk = segk_ref[ks, :]
            st = [
                dot_nt(jnp.concatenate([k_ref[ks, c], sk], axis=1), q) + bias_ref[bs, d]
                for c, d, q in zip(lanes, both, q_cat)
            ]
            m = [jnp.max(x, axis=0, keepdims=True) for x in st]
            e = [jnp.exp(x - y) for x, y in zip(st, m)]
            l = [jnp.sum(x, axis=0, keepdims=True) for x in e]
            ot = [dot_nn(vt_ref[c, ks], x.astype(jnp.bfloat16)) / y for c, x, y in zip(lanes, e, l)]
            for j, c in enumerate(lanes):
                ctx_ref[rows, c] = join_heads(ot[j]).T.astype(jnp.bfloat16)
                lse_ref[j, pl.ds(qb, 1), :] = m[j] + jnp.log(l[j])

        by_width(nblk, nb_ref[qb], run)
        return 0

    lax.fori_loop(0, nblk, body, 0)


def bwd_kernel(
    nblk, pairs, lo_ref, nb_ref, q_ref, k_ref, v_ref, do_ref, ctx_ref, lse_ref, segq_ref, segk_ref, w_ref,
    dq_ref, dk_ref, dv_ref, near_ref, far_ref, kt_ref, bias_ref, acc_ref, dka_ref, dva_ref,
):
    build_bias(w_ref, bias_ref, nblk, pairs)
    flip(k_ref, kt_ref, nblk, pairs)
    acc_ref[...] = jnp.zeros_like(acc_ref)
    dka_ref[...] = jnp.zeros_like(dka_ref)
    dva_ref[...] = jnp.zeros_like(dva_ref)
    mask = head_mask()
    lanes = [slice(j * BLK, (j + 1) * BLK) for j in range(pairs)]
    both = [slice(2 * j * BLK, 2 * (j + 1) * BLK) for j in range(pairs)]
    row = lax.broadcasted_iota(jnp.int32, (16, 2 * HEAD_DIM), 0)
    lane = lax.broadcasted_iota(jnp.int32, (16, 2 * HEAD_DIM), 1)
    pick = ((lane // HEAD_DIM) == row).astype(jnp.float32).astype(jnp.bfloat16)

    def body(qb, _):
        rows = pl.ds(pl.multiple_of(qb * BLK, BLK), BLK)
        lob = lo_ref[qb]
        sq = segq_ref[rows, :]
        sq = jnp.concatenate([sq, sq], axis=0)
        q2 = [pair_of(q_ref[rows, c], mask) for c in lanes]
        q_cat = [jnp.concatenate([q, sq], axis=1) for q in q2]
        do2 = [pair_of(do_ref[rows, c], mask) for c in lanes]
        delta = []
        for c in lanes:
            prod = do_ref[rows, c].astype(jnp.float32) * ctx_ref[rows, c].astype(jnp.float32)
            hi = prod.astype(jnp.bfloat16)
            low = (prod - hi.astype(jnp.float32)).astype(jnp.bfloat16)
            dl = dot_nt(pick, hi) + dot_nt(pick, low)
            delta.append(jnp.concatenate([dl[0:1], dl[1:2]], axis=1))
        lse = [lse_ref[j, pl.ds(qb, 1), :] for j in range(pairs)]

        def run(W):
            ks = pl.ds(pl.multiple_of(lob * BLK, BLK), W)
            bs = pl.ds(pl.multiple_of((lob - qb + nblk - 1) * BLK, BLK), W)
            sk = segk_ref[ks, :]
            st = [dot_nt(jnp.concatenate([k_ref[ks, c], sk], axis=1), q) for c, q in zip(lanes, q_cat)]
            dp = [dot_nt(v_ref[ks, c], d) for c, d in zip(lanes, do2)]
            p = [jnp.exp(x + bias_ref[bs, d] - y) for x, d, y in zip(st, both, lse)]
            ds = [x * (y - z) for x, y, z in zip(p, dp, delta)]
            dsb = [x.astype(jnp.bfloat16) for x in ds]
            for j, (c, d) in enumerate(zip(lanes, both)):
                acc_ref[bs, d] += ds[j]
                dva_ref[ks, c] += dot_nn(p[j].astype(jnp.bfloat16), do2[j])
                dka_ref[ks, c] += dot_nn(dsb[j], q2[j])
                dqt = join_heads(dot_nn(kt_ref[c, ks], dsb[j])) * (HEAD_DIM**-0.5)
                dq_ref[rows, c] = dqt.T.astype(jnp.bfloat16)

        by_width(nblk, nb_ref[qb], run)
        return 0

    lax.fori_loop(0, nblk, body, 0)
    dk_ref[...] = dka_ref[...].astype(jnp.bfloat16)
    dv_ref[...] = dva_ref[...].astype(jnp.bfloat16)
    near = (nblk - 2) * BLK
    total = (2 * nblk - 1) * BLK
    for j in range(pairs):
        for h in range(2):
            c = slice((2 * j + h) * BLK, (2 * j + h + 1) * BLK)
            wide = jnp.concatenate(
                [
                    jnp.zeros((BLK, BLK), jnp.float32),
                    acc_ref[near + 2 * BLK : near + 3 * BLK, c],
                    acc_ref[near + BLK : near + 2 * BLK, c],
                    acc_ref[near : near + BLK, c],
                ],
                axis=1,
            )
            near_ref[j, h : h + 1, :] = jnp.sum(unroll_rows(wide), axis=0, keepdims=True)
            low = jnp.sum(acc_ref[0:near, c], axis=0, keepdims=True)
            high = jnp.sum(acc_ref[near + 3 * BLK : total, c], axis=0, keepdims=True)
            far_ref[j, h : h + 1, :] = jnp.concatenate([low, high], axis=1)


def unroll_rows(wide):
    n=wide.shape[1]
    out=wide
    row=lax.broadcasted_iota(jnp.int32,wide.shape,0)
    bit=1
    while bit<wide.shape[0]:
        out=jnp.where((row & bit)!=0,pltpu.roll(out,n-bit,1),out)
        bit*=2
    return out

FWD_PAIRS = 6
BWD_PAIRS = 3


def pair_spec(nrow, pairs):
    return pl.BlockSpec((nrow, 2 * HEAD_DIM * pairs), lambda p, *_: (0, p))


def full_spec(shape):
    return pl.BlockSpec(shape, lambda p, *_: (0,) * len(shape))


def lead_spec(pairs, shape):
    return pl.BlockSpec((pairs,) + shape, lambda p, *_: (p, 0, 0))


def attn_fwd(lo, nb, q, k, v, segq, segk, w):
    L, D = q.shape
    nblk = L // BLK
    every = D // (2 * HEAD_DIM)
    pairs = FWD_PAIRS
    return pl.pallas_call(
        functools.partial(fwd_kernel, nblk, pairs),
        grid_spec=pltpu.PrefetchScalarGridSpec(
            num_scalar_prefetch=2,
            grid=(every // pairs,),
            in_specs=[pair_spec(L, pairs)] * 3 + [full_spec((L, 128))] * 2 + [lead_spec(pairs, (2, 512))],
            out_specs=[pair_spec(L, pairs), lead_spec(pairs, (nblk, 2 * BLK))],
            scratch_shapes=[
                pltpu.VMEM((2 * HEAD_DIM * pairs, L), jnp.bfloat16),
                pltpu.VMEM(((2 * nblk - 1) * BLK, 2 * BLK * pairs), jnp.float32),
            ],
        ),
        out_shape=[
            jax.ShapeDtypeStruct((L, D), jnp.bfloat16),
            jax.ShapeDtypeStruct((every, nblk, 2 * BLK), jnp.float32),
        ],
        compiler_params=pltpu.CompilerParams(vmem_limit_bytes=63 * 2**20),
        cost_estimate=pl.CostEstimate(flops=2 * 10**9, bytes_accessed=8 * 2**20, transcendentals=6 * 10**6),
    )(lo, nb, q, k, v, segq, segk, w)


def attn_bwd(lo, nb, q, k, v, do, ctx, lse, segq, segk, w):
    L, D = q.shape
    nblk = L // BLK
    every = D // (2 * HEAD_DIM)
    pairs = BWD_PAIRS
    rows = (2 * nblk - 1) * BLK
    return pl.pallas_call(
        functools.partial(bwd_kernel, nblk, pairs),
        grid_spec=pltpu.PrefetchScalarGridSpec(
            num_scalar_prefetch=2,
            grid=(every // pairs,),
            in_specs=[pair_spec(L, pairs)] * 5
            + [lead_spec(pairs, (nblk, 2 * BLK))]
            + [full_spec((L, 128))] * 2
            + [lead_spec(pairs, (2, 512))],
            out_specs=[pair_spec(L, pairs)] * 3 + [lead_spec(pairs, (2, 512)), lead_spec(pairs, (2, 256))],
            scratch_shapes=[
                pltpu.VMEM((2 * HEAD_DIM * pairs, L), jnp.bfloat16),
                pltpu.VMEM((rows, 2 * BLK * pairs), jnp.float32),
                pltpu.VMEM((rows, 2 * BLK * pairs), jnp.float32),
                pltpu.VMEM((L, 2 * HEAD_DIM * pairs), jnp.float32),
                pltpu.VMEM((L, 2 * HEAD_DIM * pairs), jnp.float32),
            ],
        ),
        out_shape=[jax.ShapeDtypeStruct((L, D), jnp.bfloat16)] * 3
        + [jax.ShapeDtypeStruct((every, 2, 512), jnp.float32), jax.ShapeDtypeStruct((every, 2, 256), jnp.float32)],
        compiler_params=pltpu.CompilerParams(vmem_limit_bytes=63 * 2**20),
        cost_estimate=pl.CostEstimate(flops=4 * 10**9, bytes_accessed=16 * 2**20, transcendentals=6 * 10**6),
    )(lo, nb, q, k, v, do, ctx, lse, segq, segk, w)


def seg_ranges(seg):
    L = seg.shape[0]
    nblk = L // BLK
    sb = seg.reshape(nblk, BLK)
    first = jnp.sum((seg[None, :] < sb[:, :1]).astype(jnp.int32), axis=1)
    last = jnp.sum((seg[None, :] <= sb[:, -1:]).astype(jnp.int32), axis=1)
    lo = first // BLK
    nb = (last + BLK - 1) // BLK - lo
    return lo.astype(jnp.int32), nb.astype(jnp.int32)


def table_grad(near,far,buckets):
    off=-(jnp.arange(512,dtype=jnp.int32)-256)
    oh=(bucket_index(off)[:,None]==jnp.arange(buckets,dtype=jnp.int32)[None,:]).astype(jnp.float32)
    n=jnp.einsum("hx,xb->bh",near.reshape(-1,512),oh,precision=lax.Precision.HIGHEST)
    f=far.reshape(-1,2,128).sum(-1)
    ids=jnp.arange(buckets,dtype=jnp.int32)[:,None]
    return n+jnp.where(ids==15,f[None,:,0],0)+jnp.where(ids==31,f[None,:,1],0)

TILE=256
def gelu_parts(x):
    c=0.7978845608028654
    x2=x*x
    t=jnp.tanh(x*(c+(c*0.044715)*x2))
    half=0.5*(1.0+t)
    slope=half+0.5*x*(1.0-t*t)*(c+(3*c*0.044715)*x2)
    return x*half,slope

def expert_kernel(count, parts, *refs):
    rows=refs[:count]; cots=refs[count:2*count]
    wi_refs=refs[2*count:2*count+parts]; wo_refs=refs[2*count+parts:2*count+2*parts]
    refs=refs[2*count+2*parts:]
    outs=refs[:count]; act_ref,db_ref,dg_ref=refs[count:count+3]
    x_ref,c_ref,wi_buf,wo_buf,acc_ref,dga_ref,act_buf,db_buf,w_sem,o_sem=refs[count+3:]
    block=wi_refs[0].shape[1]
    per=block//TILE
    total=parts*per
    for k in range(parts):
        pltpu.make_async_copy(wi_refs[k],wi_buf.at[k],w_sem.at[0,k]).start()
        pltpu.make_async_copy(wo_refs[k],wo_buf.at[k],w_sem.at[1,k]).start()
    first=0
    for i in range(count):
        n=rows[i].shape[0]
        x_ref[first:first+n,:]=rows[i][...]
        c_ref[first:first+n,:]=cots[i][...]
        first+=n
    acc_ref[...]=jnp.zeros_like(acc_ref)
    dga_ref[...]=jnp.zeros_like(dga_ref)
    def out_copies(step,slot):
        cols=pl.ds(pl.multiple_of(step*TILE,TILE),TILE)
        return (pltpu.make_async_copy(act_buf.at[slot],act_ref.at[:,cols],o_sem.at[0,slot]),
                pltpu.make_async_copy(db_buf.at[slot],db_ref.at[:,cols],o_sem.at[1,slot]))
    for k in range(parts):
        pltpu.make_async_copy(wi_refs[k],wi_buf.at[k],w_sem.at[0,k]).wait()
        pltpu.make_async_copy(wo_refs[k],wo_buf.at[k],w_sem.at[1,k]).wait()
        def body(c,_):
            step=k*per+c
            slot=lax.rem(step,2)
            @pl.when(step>=2)
            def _():
                for cp in out_copies(step-2,slot): cp.wait()
            cols=pl.ds(pl.multiple_of(c*TILE,TILE),TILE)
            wi=wi_buf[k,:,cols]
            wo=wo_buf[k,cols,:]
            before=dot_nn(x_ref[...],wi)
            up=dot_nt(c_ref[...],wo)
            active,slope=gelu_parts(before)
            prod=active*up
            dga_ref[...]+=prod[:,:128]+prod[:,128:]
            act_buf[slot]=active.astype(jnp.bfloat16)
            db=(up*slope).astype(jnp.bfloat16)
            db_buf[slot]=db
            acc_ref[...]+=dot_nt(db,wi)
            for cp in out_copies(step,slot): cp.start()
            return 0
        lax.fori_loop(0,per,body,0)
    first=0
    for i in range(count):
        n=rows[i].shape[0]
        outs[i][...]=acc_ref[first:first+n,:].astype(jnp.bfloat16)
        first+=n
    ones=jnp.ones((8,128),jnp.bfloat16)
    sums=dga_ref[...]
    hi=sums.astype(jnp.bfloat16)
    rest=sums-hi.astype(jnp.float32)
    mid=rest.astype(jnp.bfloat16)
    low=(rest-mid.astype(jnp.float32)).astype(jnp.bfloat16)
    dg_ref[...]=dot_nt(ones,hi)+dot_nt(ones,mid)+dot_nt(ones,low)
    for step in (total-2,total-1):
        for cp in out_copies(step,step%2): cp.wait()

def expert_half(rows,cots,w_ins,w_outs):
    count=len(rows); parts=len(w_ins)
    width,block=w_ins[0].shape
    R=sum(r.shape[0] for r in rows)
    vm=pl.BlockSpec(memory_space=pltpu.VMEM); hb=pl.BlockSpec(memory_space=pl.ANY)
    outs=pl.pallas_call(functools.partial(expert_kernel,count,parts),
        in_specs=[vm]*(2*count)+[hb]*(2*parts),
        out_specs=[vm]*count+[hb,hb,vm],
        out_shape=[jax.ShapeDtypeStruct(r.shape,jnp.bfloat16) for r in rows]+[jax.ShapeDtypeStruct((R,parts*block),jnp.bfloat16)]*2+[jax.ShapeDtypeStruct((8,R),jnp.float32)],
        scratch_shapes=[pltpu.VMEM((R,width),jnp.bfloat16)]*2+[pltpu.VMEM((parts,width,block),jnp.bfloat16),pltpu.VMEM((parts,block,width),jnp.bfloat16),
            pltpu.VMEM((R,width),jnp.float32),pltpu.VMEM((R,128),jnp.float32),pltpu.VMEM((2,R,TILE),jnp.bfloat16),pltpu.VMEM((2,R,TILE),jnp.bfloat16),
            pltpu.SemaphoreType.DMA((2,parts)),pltpu.SemaphoreType.DMA((2,2))],
        compiler_params=pltpu.CompilerParams(vmem_limit_bytes=48*2**20),
        cost_estimate=pl.CostEstimate(flops=6*R*width*parts*block,bytes_accessed=20*2**20,transcendentals=R*parts*block))(*rows,*cots,*w_ins,*w_outs)
    return outs[:count],outs[count],outs[count+1],outs[count+2][0]

MESH = pl.DeviceIdType.MESH


def shard_peer(bit):
    return (lax.axis_index("expert"), lax.axis_index("shard") ^ bit)


def expert_peer(bit):
    return (lax.axis_index("expert") ^ bit, lax.axis_index("shard"))


def greet(peers):
    barrier = pltpu.get_barrier_semaphore()
    for peer in peers:
        pl.semaphore_signal(barrier, inc=1, device_id=peer, device_id_type=MESH)
    pl.semaphore_wait(barrier, len(peers))


def send(src, dst, send_sem, recv_sem, peer):
    copy = pltpu.make_async_remote_copy(
        src_ref=src, dst_ref=dst, send_sem=send_sem, recv_sem=recv_sem, device_id=peer, device_id_type=MESH
    )
    copy.start()
    return copy


def columns(line, block):
    return jnp.broadcast_to(line[:, block * 128 : (block + 1) * 128], (128, 128)).T


def project_kernel(
    heads, x_in, small_in, q_in, k_in, v_in, o_in, segments,
    q_ref, k_ref, v_ref, normed_ref, small_ref, segq_ref, segk_ref, bias_ref, all_ref,
    x_ref, small_buf, w_buf, unit_ref,
    sem_send, sem_recv, sem_own, sem_out, sem_load,
):
    shard = lax.axis_index("shard")
    own = q_in.shape[0]
    load = pltpu.make_async_copy(x_in, x_ref, sem_load.at[0])
    load.start()

    def rows(bit):
        return pl.ds(pl.multiple_of((shard ^ bit) * own, 64), own)

    ins = [small_in, q_in, k_in, v_in, o_in]
    bufs = [small_buf] + [w_buf.at[i] for i in range(4)]
    count = len(ins)
    kept = []
    for i in range(count):
        copy = pltpu.make_async_copy(ins[i], bufs[i].at[rows(0)], sem_own.at[i])
        copy.start()
        kept.append(copy)
    greet([shard_peer(1), shard_peer(2)])
    far, near, passed = [], [], [None] * count
    for i in range(count):
        far.append(send(ins[i], bufs[i].at[rows(0)], sem_send.at[0, i], sem_recv.at[0, i], shard_peer(2)))
    for i in range(count):
        near.append(send(ins[i], bufs[i].at[rows(0)], sem_send.at[1, i], sem_recv.at[1, i], shard_peer(1)))
    length, width = x_ref.shape
    tile = 512

    def unit(t, _):
        r = pl.ds(pl.multiple_of(t * tile, tile), tile)
        x = x_ref[r, :].astype(jnp.float32)
        unit_ref[r, :] = x * lax.rsqrt(jnp.mean(x * x, axis=-1, keepdims=True) + 1e-6)
        return 0

    def hop(i):
        far[i].wait_recv()
        here = bufs[i].at[rows(2)]
        passed[i] = send(here, here, sem_send.at[2, i], sem_recv.at[2, i], shard_peer(1))

    def finish(i):
        kept[i].wait()
        near[i].wait_recv()
        passed[i].wait_recv()

    load.wait()
    lax.fori_loop(0, length // tile, unit, 0)
    documents = segments[...].astype(jnp.float32)
    ids = lax.broadcasted_iota(jnp.int32, (128, 128), 1).astype(jnp.float32)
    for b in range(length // 128):
        r = slice(b * 128, (b + 1) * 128)
        same = (columns(documents, b) == ids).astype(jnp.float32)
        segq_ref[r, :] = same.astype(jnp.bfloat16)
        segk_ref[r, :] = jnp.where(ids < 16.0, (same - 1.0) * BIG, 0.0).astype(jnp.bfloat16)
    hop(0)
    hop(1)
    finish(0)
    small = small_buf[...]
    small_ref[...] = small
    gain = jnp.concatenate(
        [small[c * 128 : (c + 1) * 128, :].astype(jnp.float32).T[0:1] for c in range(width // 128)], axis=1
    )

    buckets = 32
    part = buckets // 4
    table = jnp.concatenate([small[j * own : j * own + part, :].astype(jnp.float32) for j in range(4)], axis=0)
    table = jnp.concatenate([table, jnp.zeros((128 - buckets, 128), jnp.float32)], axis=0).T
    wide = bias_ref.shape[2]
    offset = wide // 2 - lax.broadcasted_iota(jnp.int32, (128, wide), 1)
    onehot = (bucket_index(offset) == lax.broadcasted_iota(jnp.int32, (128, wide), 0)).astype(jnp.float32)
    lines = dot_nn(table.astype(jnp.bfloat16), onehot.astype(jnp.bfloat16))
    for p in range(heads // 2):
        bias_ref[p] = lines[128 - heads + 2 * p : 130 - heads + 2 * p]

    def norm(t, _):
        r = pl.ds(pl.multiple_of(t * tile, tile), tile)
        normed_ref[r, :] = (unit_ref[r, :] * gain).astype(jnp.bfloat16)
        return 0

    lax.fori_loop(0, length // tile, norm, 0)
    outs = []

    def project_one(i, out):
        finish(i)
        copy = pltpu.make_async_copy(w_buf.at[i - 1], all_ref.at[i - 1], sem_out.at[i - 1])
        copy.start()
        outs.append(copy)

        def run(t, _):
            r = pl.ds(pl.multiple_of(t * tile, tile), tile)
            y = dot_nn(normed_ref[r, :], w_buf[i - 1]).astype(jnp.bfloat16)
            if i == 1:
                y = (y.astype(jnp.float32) * HEAD_DIM**-0.5).astype(jnp.bfloat16)
            out[r, :] = y
            return 0

        lax.fori_loop(0, length // tile, run, 0)

    project_one(1, q_ref)
    hop(2)
    project_one(2, k_ref)
    hop(3)
    project_one(3, v_ref)
    hop(4)
    finish(4)
    copy = pltpu.make_async_copy(w_buf.at[3], all_ref.at[3], sem_out.at[3])
    copy.start()
    outs.append(copy)
    for c in outs:
        c.wait()
    for c in far + near + passed:
        c.wait_send()


def project(x, small, weights, segments, heads):
    length, width = x.shape
    vm = pl.BlockSpec(memory_space=pltpu.VMEM)
    hb = pl.BlockSpec(memory_space=pl.ANY)
    bf = jnp.bfloat16
    shape = jax.ShapeDtypeStruct
    return pl.pallas_call(
        functools.partial(project_kernel, heads),
        in_specs=[hb] * 6 + [vm],
        out_specs=[vm] * 8 + [hb],
        out_shape=[shape((length, width), bf)] * 4 + [shape((width, 128), bf), shape((length, 128), bf), shape((length, 128), bf), shape((heads // 2, 2, 512), jnp.float32)]
        + [shape((4, width, width), bf)],
        scratch_shapes=[
            pltpu.VMEM((length, width), bf),
            pltpu.VMEM((width, 128), bf),
            pltpu.VMEM((4, width, width), bf),
            pltpu.VMEM((length, width), jnp.float32),
            pltpu.SemaphoreType.DMA((3, 5)),
            pltpu.SemaphoreType.DMA((3, 5)),
            pltpu.SemaphoreType.DMA((5,)),
            pltpu.SemaphoreType.DMA((4,)),
            pltpu.SemaphoreType.DMA((1,)),
        ],
        compiler_params=pltpu.CompilerParams(collective_id=0, has_side_effects=True, vmem_limit_bytes=63 * 2**20),
        cost_estimate=pl.CostEstimate(flops=6 * 10**9, bytes_accessed=20 * 2**20, transcendentals=0),
    )(x, small, *weights, segments)


def slot_kernel(cap, route, order, cot, place_ref, cells_ref):
    length = cot.shape[0]
    keys = (route[...] * length + order[...]).astype(jnp.float32)
    starts = (route[...] * length).astype(jnp.float32)
    blocks = length // 128
    sides = [columns(keys, b) for b in range(blocks)]
    slots = []
    for t in range(blocks):
        s = slice(t * 128, (t + 1) * 128)
        sums = sum((c < keys[:, s]).astype(jnp.float32) - (c < starts[:, s]).astype(jnp.float32) for c in sides)
        slots.append(jnp.sum(sums, axis=0, keepdims=True))
    slot = jnp.concatenate(slots, axis=1).astype(jnp.int32)
    place = jnp.where(slot < cap, route[...] * cap + slot, -1)
    place_ref[...] = place
    step = 640
    for t in range(cells_ref.shape[0] // step):
        ids = lax.broadcasted_iota(jnp.int32, (step, length), 0) + t * step
        pick = (ids == place).astype(jnp.float32).astype(jnp.bfloat16)
        cells_ref[t * step : (t + 1) * step, :] = dot_nn(pick, cot[...]).astype(jnp.bfloat16)


def find_slots(route, order, cot, cells, cap):
    length, width = cot.shape
    vm = pl.BlockSpec(memory_space=pltpu.VMEM)
    return pl.pallas_call(
        functools.partial(slot_kernel, cap),
        in_specs=[vm] * 3,
        out_specs=[vm] * 2,
        out_shape=[jax.ShapeDtypeStruct((1, length), jnp.int32), jax.ShapeDtypeStruct((cells, width), jnp.bfloat16)],
        compiler_params=pltpu.CompilerParams(vmem_limit_bytes=63 * 2**20),
        cost_estimate=pl.CostEstimate(flops=2 * 10**9, bytes_accessed=4 * 2**20, transcendentals=0),
    )(route, order, cot)


def gate_columns(line, count, width):
    column = jnp.broadcast_to(line, (128, 256)).T[:count]
    return jnp.concatenate([column] * (width // 128), axis=1)


def experts_kernel(
    size, cap, tile,
    rows_in, gate_in, cot_in, inner_own, outer_own, inner_far,
    back_out, dgate_out, mine_out, other_out, result_out,
    rows, gates, cots, weights, active, d_before, total, d_gate, back, d_gates, back_in, d_gates_in,
    gated_t, g_send, g_recv, stage, result,
    w_sem, wr_sem, row_send, row_recv, gate_send, gate_recv, back_send, back_recv, dg_send, dg_recv,
    g_sem_send, g_sem_recv, cot_sem, out_sem, res_sem, back_sem, dgb_sem,
):
    width = weights.shape[2]
    block = weights.shape[3]
    per = block // tile
    group = 2
    count = group * cap
    me = lax.axis_index("expert")

    def part(k):
        return pl.ds(k * cap, cap)

    local = [
        pltpu.make_async_copy(inner_own, weights.at[0, 0], w_sem.at[0]),
        pltpu.make_async_copy(outer_own, weights.at[0, 1], w_sem.at[1]),
        pltpu.make_async_copy(inner_far, weights.at[2, 0], w_sem.at[2]),
        pltpu.make_async_copy(rows_in.at[me], rows.at[part(0)], w_sem.at[3]),
        pltpu.make_async_copy(gate_in.at[me], gates.at[0], w_sem.at[4]),
    ]
    local += [pltpu.make_async_copy(cot_in.at[me ^ k], cots.at[part(k)], cot_sem.at[k]) for k in range(size)]
    for c in local:
        c.start()
    greet([expert_peer(k) for k in range(1, size)] + [shard_peer(1), shard_peer(2)])
    sent = []
    arrive = {}
    outer_far = send(outer_own, weights.at[2, 1], wr_sem.at[0, 0], wr_sem.at[1, 0], shard_peer(2))

    def dispatch(k):
        arrive[k] = [
            send(gate_in.at[me ^ k], gates.at[k], gate_send.at[k], gate_recv.at[k], expert_peer(k)),
            send(rows_in.at[me ^ k], rows.at[part(k)], row_send.at[k], row_recv.at[k], expert_peer(k)),
        ]
        sent.append(arrive[k][0])

    for k in (4, 5, 6, 7, 2, 3, 1):
        dispatch(k)
    moved = [
        send(inner_own, weights.at[1, 0], wr_sem.at[0, 1], wr_sem.at[1, 1], shard_peer(1)),
        send(outer_own, weights.at[1, 1], wr_sem.at[0, 2], wr_sem.at[1, 2], shard_peer(1)),
        send(inner_far, weights.at[3, 0], wr_sem.at[0, 3], wr_sem.at[1, 3], shard_peer(1)),
    ]
    sent += moved + [outer_far]
    d_gates[...] = jnp.zeros_like(d_gates)
    for c in local:
        c.wait()
    for c in moved:
        c.wait_recv()
    ones = jnp.ones((8, 128), jnp.bfloat16)
    returned = {}

    def arrived(blocks):
        for k in blocks:
            if k:
                for c in arrive[k]:
                    c.wait_recv()

    def forward_back(blocks, spot, first, last):
        span = len(blocks) * cap
        mine = slice(blocks[0] * cap, blocks[0] * cap + span)
        here = slice(spot * count, spot * count + span)
        if first == 0:
            total[here, :] = jnp.zeros((span, width), jnp.float32)
            d_gate[here, :] = jnp.zeros((span, 128), jnp.float32)

        def step(t, _):
            kk = t // per
            cols = pl.ds(pl.multiple_of(lax.rem(t, per) * tile, tile), tile)
            where = pl.ds(pl.multiple_of(t * tile, tile), tile)
            wi = weights[kk, 0, :, cols]
            wo = weights[kk, 1, cols, :]
            before = dot_nn(rows[mine, :], wi)
            up = dot_nt(cots[mine, :], wo)
            value, slope = gelu_parts(before)
            prod = value * up
            d_gate[here, :] += sum(prod[:, c * 128 : (c + 1) * 128] for c in range(tile // 128))
            active[mine, where] = value.astype(jnp.bfloat16)
            db = (up * slope).astype(jnp.bfloat16)
            d_before[mine, where] = db
            total[here, :] += dot_nt(db, wi)
            return 0

        lax.fori_loop(first * per, last * per, step, 0)

    def give_back(blocks, spot):
        span = len(blocks) * cap
        here = slice(spot * count, spot * count + span)
        back[blocks[0] * cap : blocks[0] * cap + span, :] = total[here, :].astype(jnp.bfloat16)
        for k in blocks:
            start = spot * count + (k - blocks[0]) * cap
            sums = d_gate[start : start + cap, :]
            hi = sums.astype(jnp.bfloat16)
            rest = sums - hi.astype(jnp.float32)
            mid = rest.astype(jnp.bfloat16)
            low = (rest - mid.astype(jnp.float32)).astype(jnp.bfloat16)
            d_gates[k, :, 0:cap] = dot_nt(ones, hi) + dot_nt(ones, mid) + dot_nt(ones, low)
            if k:
                returned[k] = [
                    send(d_gates.at[k], d_gates_in.at[k], dg_send.at[k], dg_recv.at[k], expert_peer(k)),
                    send(back.at[part(k)], back_in.at[part(k)], back_send.at[k], back_recv.at[k], expert_peer(k)),
                ]
                sent.extend(returned[k])

    near = ((0, 1), (2, 3))
    for i, blocks in enumerate(near):
        arrived(blocks)
        forward_back(blocks, i, 0, 2)
    outer_far.wait_recv()
    passed = send(weights.at[2, 1], weights.at[3, 1], wr_sem.at[0, 4], wr_sem.at[1, 4], shard_peer(1))
    sent.append(passed)
    passed.wait_recv()
    for i, blocks in enumerate(near):
        forward_back(blocks, i, 2, 4)
        give_back(blocks, i)
    for blocks in ((4,), (5,), (6, 7)):
        arrived(blocks)
        forward_back(blocks, 2, 0, 4)
        give_back(blocks, 2)
    for k in range(size):
        span = slice(k * cap, (k + 1) * cap)
        column = gate_columns(gates[k, 0:1, :], cap, width)
        cots[span, :] = (cots[span, :].astype(jnp.float32) * column).astype(jnp.bfloat16)
        result[span, :] = (rows[span, :].astype(jnp.float32) * column).astype(jnp.bfloat16)
    every = size * cap
    for c in range(width // 128):
        for r in range(every // 128):
            gated_t[c * 128 : (c + 1) * 128, r * 128 : (r + 1) * 128] = (
                result[r * 128 : (r + 1) * 128, c * 128 : (c + 1) * 128].astype(jnp.float32).T.astype(jnp.bfloat16)
            )
    strip = block

    def inner(kk, out):
        return dot_nn(gated_t[out, :], d_before[:, kk * block : (kk + 1) * block])

    def outer(kk, out, t):
        return dot_tn(active[:, pl.ds(pl.multiple_of(kk * block + t * strip, strip), strip)], cots[...])

    def strips(body):
        def run(t, _):
            body(pl.ds(pl.multiple_of(t * strip, strip), strip), t)
            return 0

        lax.fori_loop(0, block // strip, run, 0)

    def chunk(h, kk, out, t):
        return inner(kk, out) if h == 0 else outer(kk, out, t)

    finals = []
    for h in range(2):
        shared = []
        for n, kk in enumerate((3, 1)):

            def give(out, t):
                g_send[h, n, out, :] = chunk(h, kk, out, t).astype(jnp.bfloat16)

            strips(give)
            c = send(g_send.at[h, n], g_recv.at[h, n], g_sem_send.at[h, n], g_sem_recv.at[h, n], shard_peer(1))
            shared.append(c)
        shared[0].wait_recv()
        shared[0].wait_send()

        def other(out, t):
            g_send[h, 0, out, :] = (chunk(h, 2, out, t) + g_recv[h, 0, out, :].astype(jnp.float32)).astype(jnp.bfloat16)

        strips(other)
        c = pltpu.make_async_copy(g_send.at[h, 0], other_out.at[h], out_sem.at[0, h])
        c.start()
        finals.append(c)
        shared[1].wait_recv()
        sent.append(shared[1])

        def keep(out, t):
            stage[h, out, :] = chunk(h, 0, out, t) + g_recv[h, 1, out, :].astype(jnp.float32)

        strips(keep)
        c = pltpu.make_async_copy(stage.at[h], mine_out.at[h], out_sem.at[1, h])
        c.start()
        finals.append(c)

    def produce(r, _):
        span = pl.ds(pl.multiple_of(r * 4 * cap, 16), 4 * cap)
        y = sum(dot_nn(active[span, kk * block : (kk + 1) * block], weights[kk, 1]) for kk in range(4))
        result[span, :] = y.astype(jnp.bfloat16)
        return 0

    lax.fori_loop(0, size // 4, produce, 0)
    for k in range(size):
        c = pltpu.make_async_copy(result.at[part(k)], result_out.at[me ^ k], res_sem.at[k])
        c.start()
        finals.append(c)
    back_in[part(0), :] = back[part(0), :]
    d_gates_in[0] = d_gates[0]
    for k in range(size):
        if k:
            for c in returned[k]:
                c.wait_recv()
        for c in (
            pltpu.make_async_copy(back_in.at[part(k)], back_out.at[me ^ k], back_sem.at[k]),
            pltpu.make_async_copy(d_gates_in.at[k], dgate_out.at[me ^ k], dgb_sem.at[k]),
        ):
            c.start()
            finals.append(c)
    for c in finals:
        c.wait()
    for k in range(1, size):
        arrive[k][1].wait_send()
    for c in sent:
        c.wait_send()


def run_experts(rows, gates, cots, inner_own, outer_own, inner_far):
    size, cap, width = rows.shape
    block = inner_own.shape[1]
    bf = jnp.bfloat16
    f32 = jnp.float32
    every = size * cap
    hb = pl.BlockSpec(memory_space=pl.ANY)
    vm = pltpu.VMEM
    dma = pltpu.SemaphoreType.DMA
    shape = jax.ShapeDtypeStruct
    return pl.pallas_call(
        functools.partial(experts_kernel, size, cap, block),
        in_specs=[hb] * 6,
        out_specs=[hb] * 5,
        out_shape=[
            shape((size, cap, width), bf),
            shape((size, 8, 256), f32),
            shape((2, width, block), f32),
            shape((2, width, block), bf),
            shape((size, cap, width), bf),
        ],
        scratch_shapes=[
            vm((every, width), bf),
            vm((size, 8, 256), f32),
            vm((every, width), bf),
            vm((4, 2, width, block), bf),
            vm((every, 4 * block), bf),
            vm((every, 4 * block), bf),
            vm((6 * cap, width), f32),
            vm((6 * cap, 128), f32),
            vm((every, width), bf),
            vm((size, 8, 256), f32),
            vm((every, width), bf),
            vm((size, 8, 256), f32),
            vm((width, every), bf),
            vm((2, 2, width, block), bf),
            vm((2, 2, width, block), bf),
            vm((2, width, block), f32),
            vm((every, width), bf),
            dma((5,)),
            dma((2, 5)),
        ]
        + [dma((size,))] * 8
        + [dma((2, 2)), dma((2, 2)), dma((size,)), dma((2, 2)), dma((size,)), dma((size,)), dma((size,))],
        compiler_params=pltpu.CompilerParams(collective_id=1, has_side_effects=True, vmem_limit_bytes=63 * 2**20),
        cost_estimate=pl.CostEstimate(flops=36 * 10**9, bytes_accessed=30 * 2**20, transcendentals=4 * 10**6),
    )(rows, gates, cots, inner_own, outer_own, inner_far)


def turned(small, width):
    return jnp.concatenate(
        [small[c * 128 : (c + 1) * 128, :].astype(jnp.float32).T for c in range(width // 128)], axis=1
    )


def three_parts(line):
    hi = line.astype(jnp.bfloat16)
    rest = line - hi.astype(jnp.float32)
    mid = rest.astype(jnp.bfloat16)
    low = rest - mid.astype(jnp.float32)
    none = jnp.zeros((5, line.shape[1]), jnp.float32)
    parts = jnp.concatenate([hi.astype(jnp.float32), mid.astype(jnp.float32), low, none], axis=0)
    return parts.astype(jnp.bfloat16)


def pick_cells(place, first, tile, cells):
    out = []
    for b in range(first // 128, (first + tile) // 128):
        column = columns(place, b)
        lane = lax.broadcasted_iota(jnp.int32, (128, 128), 1).astype(jnp.float32)
        out.append(
            jnp.concatenate([(column == lane + 128.0 * j).astype(jnp.float32) for j in range(cells // 128)], axis=1)
        )
    return jnp.concatenate(out, axis=0).astype(jnp.bfloat16)


def spread_column(line, first, tile, width):
    return jnp.concatenate(
        [
            jnp.concatenate([columns(line, b)] * (width // 128), axis=1)
            for b in range(first // 128, (first + tile) // 128)
        ],
        axis=0,
    )


def route_kernel(
    cap, context_in, tokens_in, weights_in, small, route, place,
    resid_out, cells_out, gate_out, probs_out,
    context, tokens, w_out, normed, sems,
):
    length, width = normed.shape
    experts = probs_out.shape[0]
    loads = [
        pltpu.make_async_copy(weights_in.at[3], w_out, sems.at[0]),
        pltpu.make_async_copy(context_in, context, sems.at[1]),
        pltpu.make_async_copy(tokens_in, tokens, sems.at[2]),
    ]
    for c in loads:
        c.start()
    lines = turned(small, width)
    gain = lines[1:2]
    for c in loads:
        c.wait()
    tile = 512
    for t in range(length // tile):
        r = slice(t * tile, (t + 1) * tile)
        resid = tokens[r, :].astype(jnp.float32) + dot_nn(context[r, :], w_out[...])
        resid_out[r, :] = resid
        scale = lax.rsqrt(jnp.mean(resid * resid, axis=-1, keepdims=True) + 1e-6)
        normed[r, :] = (resid * scale * gain).astype(jnp.bfloat16)
    logits = dot_nt(lines.astype(jnp.bfloat16), normed[...])[2 : 2 + experts]
    top = jnp.exp(logits - jnp.max(logits, axis=0, keepdims=True))
    probs = top / jnp.sum(top, axis=0, keepdims=True)
    probs_out[...] = probs
    which = lax.broadcasted_iota(jnp.int32, probs.shape, 0)
    gate = jnp.sum(jnp.where(which == route[...], probs, 0.0), axis=0, keepdims=True)
    parts = three_parts(gate)
    gate_out[...] = jnp.zeros_like(gate_out)
    for k in range(experts):
        ids = lax.broadcasted_iota(jnp.int32, (cap, length), 0) + k * cap
        pick = (ids == place[...]).astype(jnp.float32).astype(jnp.bfloat16)
        cells_out[k] = dot_nn(pick, normed[...]).astype(jnp.bfloat16)
        found = dot_nt(parts, pick)
        gate_out[k, :, 0:cap] = jnp.broadcast_to(jnp.sum(found, axis=0, keepdims=True), (8, cap))


def run_route(context, tokens, weights, small, route, place, experts, cap):
    length, width = tokens.shape
    bf, f32 = jnp.bfloat16, jnp.float32
    vm = pl.BlockSpec(memory_space=pltpu.VMEM)
    hb = pl.BlockSpec(memory_space=pl.ANY)
    shape = jax.ShapeDtypeStruct
    return pl.pallas_call(
        functools.partial(route_kernel, cap),
        in_specs=[hb] * 3 + [vm] * 3,
        out_specs=[vm] * 4,
        out_shape=[
            shape((length, width), f32),
            shape((experts, cap, width), bf),
            shape((experts, 8, 256), f32),
            shape((experts, length), f32),
        ],
        scratch_shapes=[
            pltpu.VMEM((length, width), bf),
            pltpu.VMEM((length, width), bf),
            pltpu.VMEM((width, width), bf),
            pltpu.VMEM((length, width), bf),
            pltpu.SemaphoreType.DMA((3,)),
        ],
        compiler_params=pltpu.CompilerParams(vmem_limit_bytes=63 * 2**20),
        cost_estimate=pl.CostEstimate(flops=4 * 10**9, bytes_accessed=16 * 2**20, transcendentals=0),
    )(context, tokens, weights, small, route, place)


def unroute_kernel(
    cap, back_in, d_gate_in, resid_in, cot_in, weights_in, context_in, small, route, place, probs,
    d_context_out, d_resid_out, extra, keep_out, grad_out,
    back, resid, cot, w_out, context, d_branch, d_context, d_resid, sems, tile_sems, out_sems,
):
    length, width = resid.shape
    experts = probs.shape[0]
    cells = experts * cap
    loads = [pltpu.make_async_copy(back_in.at[k], back.at[pl.ds(k * cap, cap)], sems.at[4 + k]) for k in range(experts)]
    tile = 512
    spans = [pl.ds(t * tile, tile) for t in range(length // tile)]
    loads.append(pltpu.make_async_copy(weights_in.at[3], w_out, sems.at[2]))
    last = pltpu.make_async_copy(context_in, context, sems.at[3])
    tiles = [
        [
            pltpu.make_async_copy(resid_in.at[r], resid.at[r], tile_sems.at[0, t]),
            pltpu.make_async_copy(cot_in.at[r], cot.at[r], tile_sems.at[1, t]),
        ]
        for t, r in enumerate(spans)
    ]
    for c in loads + [c for pair in tiles for c in pair] + [last]:
        c.start()
    lines = turned(small, width)
    gain = lines[1:2]
    low_lines = lines.astype(jnp.bfloat16)
    which = lax.broadcasted_iota(jnp.int32, probs.shape, 0)
    chosen = (which == route[...]).astype(jnp.float32)
    gate = jnp.sum(probs[...] * chosen, axis=0, keepdims=True)
    keep = jnp.where(place[...] >= 0, gate, 0.0)
    keep_out[...] = keep
    places = place[...].astype(jnp.float32)
    parts = three_parts(jnp.concatenate([d_gate_in[k, 0:1, 0:cap] for k in range(experts)], axis=1))
    for c in loads:
        c.wait()
    stores = []
    grads = jnp.zeros((128, width), jnp.float32)
    gains = jnp.zeros((1, width), jnp.float32)
    for t in range(length // tile):
        r = slice(t * tile, (t + 1) * tile)
        for c in tiles[t]:
            c.wait()
        pick = pick_cells(places, t * tile, tile, cells)
        d_rows = dot_nn(pick, back[...])
        d_gate = jnp.sum(dot_nt(parts, pick), axis=0, keepdims=True)
        d_logits = probs[:, r] * (chosen[:, r] - gate[:, r]) * d_gate
        padded = jnp.concatenate(
            [
                jnp.zeros((2, tile), jnp.float32),
                d_logits.astype(jnp.bfloat16).astype(jnp.float32),
                jnp.zeros((126 - experts, tile), jnp.float32),
            ],
            axis=0,
        )
        d_normed = dot_nn(padded.T.astype(jnp.bfloat16), low_lines) + spread_column(keep, t * tile, tile, width) * d_rows
        x = resid[r, :]
        scale = lax.rsqrt(jnp.mean(x * x, axis=-1, keepdims=True) + 1e-6)
        unit = x * scale
        grads = grads + dot_nn(padded.astype(jnp.bfloat16), (unit * gain).astype(jnp.bfloat16))
        gains = gains + jnp.sum(d_normed * unit, axis=0, keepdims=True)
        pulled = gain * d_normed
        out = cot[r, :].astype(jnp.float32) + scale * (
            pulled - unit * jnp.mean(unit * pulled, axis=-1, keepdims=True)
        )
        d_resid[r, :] = out
        low = out.astype(jnp.bfloat16)
        d_branch[r, :] = low
        d_context[r, :] = dot_nt(low, w_out[...]).astype(jnp.bfloat16)
        for h, (src, dst) in enumerate(((d_context, d_context_out), (d_resid, d_resid_out))):
            c = pltpu.make_async_copy(src.at[spans[t]], dst.at[spans[t]], out_sems.at[h, t])
            c.start()
            stores.append(c)
    last.wait()
    grad_out[...] = dot_tn(context[...], d_branch[...]).astype(jnp.bfloat16)
    row = lax.broadcasted_iota(jnp.int32, (128, width), 0)
    extra[...] = jnp.where(row == 1, gains, grads)
    for c in stores:
        c.wait()


def run_unroute(back, d_gate, resid, cot, weights, context, small, route, place, probs):
    experts, cap, width = back.shape
    length = resid.shape[0]
    bf, f32 = jnp.bfloat16, jnp.float32
    vm = pl.BlockSpec(memory_space=pltpu.VMEM)
    hb = pl.BlockSpec(memory_space=pl.ANY)
    shape = jax.ShapeDtypeStruct
    return pl.pallas_call(
        functools.partial(unroute_kernel, cap),
        in_specs=[hb, vm, hb, hb, hb, hb] + [vm] * 4,
        out_specs=[hb, hb] + [vm] * 3,
        out_shape=[
            shape((length, width), bf),
            shape((length, width), f32),
            shape((128, width), f32),
            shape((1, length), f32),
            shape((width, width), bf),
        ],
        scratch_shapes=[
            pltpu.VMEM((experts * cap, width), bf),
            pltpu.VMEM((length, width), f32),
            pltpu.VMEM((length, width), bf),
            pltpu.VMEM((width, width), bf),
            pltpu.VMEM((length, width), bf),
            pltpu.VMEM((length, width), bf),
            pltpu.VMEM((length, width), bf),
            pltpu.VMEM((length, width), f32),
            pltpu.SemaphoreType.DMA((4 + experts,)),
            pltpu.SemaphoreType.DMA((2, length // 256)),
            pltpu.SemaphoreType.DMA((2, length // 256)),
        ],
        compiler_params=pltpu.CompilerParams(vmem_limit_bytes=63 * 2**20),
        cost_estimate=pl.CostEstimate(flops=4 * 10**9, bytes_accessed=18 * 2**20, transcendentals=0),
    )(back, d_gate, resid, cot, weights, context, small, route, place, probs)


class Reduction:
    def __init__(self, index, partial, near, far_send, far_recv, full, x_send, x_recv, half, z_send, z_recv, piece, result, send_sems, recv_sems):
        self.partial, self.near, self.far_send, self.far_recv = partial, near, far_send, far_recv
        self.full, self.x_send, self.x_recv, self.half = full, x_send, x_recv, half
        self.z_send, self.z_recv, self.piece, self.result = z_send, z_recv, piece, result
        self.index, self.send_sems, self.recv_sems = index, send_sems, recv_sems
        self.own = full.shape[0]
        self.width = full.shape[1]
        self.type = partial.dtype
        self.copies = {}

    def block(self, bit):
        return pl.ds(pl.multiple_of((lax.axis_index("shard") ^ bit) * self.own, self.own & -self.own), self.own)

    def half_rows(self, bit):
        rows = self.own // 2
        return pl.ds(pl.multiple_of(((lax.axis_index("expert") & 1) ^ bit) * rows, rows & -rows), rows)

    def quarter(self, step):
        j = (lax.axis_index("expert") >> 1) ^ step
        rows = self.own // 2
        if self.type == jnp.float32:
            return (pl.ds(pl.multiple_of(j * (rows // 4), 8), rows // 4), slice(None))
        return (
            pl.ds(pl.multiple_of((j >> 1) * (rows // 2), 16), rows // 2),
            pl.ds(pl.multiple_of((j & 1) * (self.width // 2), 128), self.width // 2),
        )

    def go(self, slot, src, dst, peer):
        self.copies[slot] = send(src, dst, self.send_sems.at[self.index, slot], self.recv_sems.at[self.index, slot], peer)

    def core(self):
        self.go(0, self.partial.at[self.block(3)], self.near.at[1], shard_peer(1))
        self.go(1, self.partial.at[self.block(1)], self.near.at[0], shard_peer(1))

    def y(self):
        self.copies[0].wait_recv()
        other = self.partial[self.block(2), :].astype(jnp.float32) + self.near[1].astype(jnp.float32)
        self.far_send[...] = other.astype(self.type)
        self.go(2, self.far_send, self.far_recv, shard_peer(2))
        self.copies[1].wait_recv()
        self.full[...] = self.partial[self.block(0), :].astype(jnp.float32) + self.near[0].astype(jnp.float32)

    def x(self):
        self.copies[2].wait_recv()
        self.full[...] += self.far_recv[...].astype(jnp.float32)
        self.x_send[...] = self.full[self.half_rows(1), :].astype(self.type)
        self.go(3, self.x_send, self.x_recv, expert_peer(1))

    def z(self):
        self.copies[3].wait_recv()
        self.half[...] = self.own_half() + self.x_recv[...].astype(jnp.float32)
        self.z_send[...] = self.half[...].astype(self.type)
        for step in (2, 3, 1):
            self.go(3 + step, self.z_send.at[self.quarter(step)], self.z_recv.at[step - 1], expert_peer(2 * step))

    def own_half(self):
        return self.full[self.half_rows(0), :]

    def spread(self):
        for step in (1, 2, 3):
            self.copies[3 + step].wait_recv()
        rows, cols = self.quarter(0)
        total = self.half[rows, cols]
        for step in (1, 2, 3):
            total = total + self.z_recv[step - 1].astype(jnp.float32)
        self.piece[...] = total.astype(self.type)
        target = self.place()
        for step in (2, 3, 1):
            self.go(6 + step, self.piece, self.result.at[target], expert_peer(2 * step))
        self.result[target] = self.piece[...]

    def place(self):
        j = lax.axis_index("expert") >> 1
        first = (lax.axis_index("expert") & 1) * (self.own // 2)
        rows = self.own // 2
        if self.type == jnp.float32:
            return (pl.ds(pl.multiple_of(first + j * (rows // 4), 8), rows // 4), slice(None))
        return (
            pl.ds(pl.multiple_of(first + (j >> 1) * (rows // 2), 16), rows // 2),
            pl.ds(pl.multiple_of((j & 1) * (self.width // 2), 128), self.width // 2),
        )

    def cross(self):
        for step in (1, 2, 3):
            self.copies[6 + step].wait_recv()
        self.go(10, self.result.at[self.half_rows(0)], self.result.at[self.half_rows(0)], expert_peer(1))

    def finish(self, out):
        self.copies[10].wait_recv()
        out[...] = self.result[...].astype(jnp.float32)

    def drain(self):
        for c in self.copies.values():
            c.wait_send()


class Crossed(Reduction):
    other = None

    def y(self):
        rows = self.own // 2
        self.copies[0].wait_recv()
        self.other[...] = self.partial[self.block(2), :].astype(jnp.float32) + self.near[1].astype(jnp.float32)
        self.far_send[rows:, :] = self.other[self.half_rows(1), :].astype(self.type)
        self.copies[1].wait_recv()
        self.full[...] = self.partial[self.block(0), :].astype(jnp.float32) + self.near[0].astype(jnp.float32)
        self.far_send[:rows, :] = self.full[self.half_rows(1), :].astype(self.type)
        self.go(2, self.far_send, self.far_recv, expert_peer(1))

    def x(self):
        rows = self.own // 2
        self.copies[2].wait_recv()
        other = self.other[self.half_rows(0), :] + self.far_recv[rows:, :].astype(jnp.float32)
        self.x_send[...] = other.astype(self.type)
        self.go(3, self.x_send, self.x_recv, shard_peer(2))

    def own_half(self):
        return self.full[self.half_rows(0), :] + self.far_recv[: self.own // 2, :].astype(jnp.float32)


def place_table(near, far, ps, own, heads):
    buckets = 32
    wide = near.shape[2]
    offset = wide // 2 - lax.broadcasted_iota(jnp.int32, (wide, buckets), 0)
    onehot = (bucket_index(offset) == lax.broadcasted_iota(jnp.int32, (wide, buckets), 1)).astype(jnp.float32)
    sums = jnp.concatenate([near[j] for j in range(near.shape[0])], axis=0)
    table = lax.dot_general(
        sums, onehot, (((1,), (0,)), ((), ())), preferred_element_type=jnp.float32, precision=lax.Precision.HIGHEST
    )
    ends = jnp.concatenate([far[j] for j in range(far.shape[0])], axis=0)
    low = jnp.sum(ends[:, :128], axis=1, keepdims=True)
    high = jnp.sum(ends[:, 128:], axis=1, keepdims=True)
    which = lax.broadcasted_iota(jnp.int32, (heads, buckets), 1)
    table = table + jnp.where(which == 15, low, 0.0) + jnp.where(which == 31, high, 0.0)
    part = buckets // 4
    square = jnp.concatenate([table, jnp.zeros((heads, 128 - buckets), jnp.float32)], axis=1)
    square = jnp.concatenate([jnp.zeros((128 - heads, 128), jnp.float32), square], axis=0).T
    lane = lax.broadcasted_iota(jnp.int32, (part, 128), 1)
    for j in range(4):
        r = slice(j * own, j * own + part)
        ps[r, :] = jnp.where(lane >= 128 - heads, square[j * part : (j + 1) * part, :], ps[r, :])


def tail_kernel(
    heads, experts,
    normed_in, dq_in, dk_in, dv_in, p_in, weights_in, tokens_in, d_resid_in,
    cells_in, resid_in, small, extra, near_sums, far_sums, place, keep_gate,
    o_out, q_out, k_out, v_out, gain_out, gain_two_out, router_out, table_out, tokens_out, mixed_out,
    normed, dq, dk, dv, weights, tokens, d_resid, cells, resid,
    normed_t, p_ref, near, far_send, far_recv, full, x_send, x_recv, half, z_send, z_recv, piece, result, other,
    ps, s_near, s_far_send, s_far_recv, s_full, s_x_send, s_x_recv, s_half, s_z_send, s_z_recv, s_piece, s_result,
    send_sems, recv_sems, load_sems,
):
    length, width = normed.shape
    tile = 256
    loads = [
        pltpu.make_async_copy(src, dst, load_sems.at[i])
        for i, (src, dst) in enumerate(
            (
                (p_in, p_ref.at[0]),
                (weights_in.at[0:3], weights),
                (normed_in, normed),
                (dq_in, dq),
                (dk_in, dk),
                (dv_in, dv),
                (tokens_in, tokens),
                (d_resid_in, d_resid),
                (resid_in, resid),
            )
        )
    ]
    cap = cells_in.shape[1]
    loads += [
        pltpu.make_async_copy(cells_in.at[k], cells.at[pl.ds(k * cap, cap)], load_sems.at[11 + k])
        for k in range(cells_in.shape[0])
    ]
    for c in loads:
        c.start()
    greet([shard_peer(1), shard_peer(2)] + [expert_peer(k) for k in (1, 2, 4, 6)])
    work = []
    for m in range(4):
        w = (Crossed if m >= 2 else Reduction)(
            m, p_ref.at[m], near.at[m], far_send.at[m], far_recv.at[m], full.at[m], x_send.at[m], x_recv.at[m],
            half.at[m], z_send.at[m], z_recv.at[m], piece.at[m], result.at[m], send_sems, recv_sems,
        )
        w.other = other.at[m % 2]
        work.append(w)
    o, q, k, v = work
    s = Reduction(
        4, ps, s_near, s_far_send, s_far_recv, s_full, s_x_send, s_x_recv, s_half, s_z_send, s_z_recv, s_piece,
        s_result, send_sems, recv_sems,
    )

    def strips(m, make):
        p_ref[m] = make(slice(None)).astype(jnp.bfloat16)

    loads[0].wait()
    o.core()
    loads[2].wait()
    for c in range(width // 128):
        for t in range(length // 128):
            normed_t[c * 128 : (c + 1) * 128, t * 128 : (t + 1) * 128] = (
                normed[t * 128 : (t + 1) * 128, c * 128 : (c + 1) * 128].astype(jnp.float32).T.astype(jnp.bfloat16)
            )
    o.y()
    loads[3].wait()
    strips(1, lambda r: dot_nn(normed_t[r, :], dq[...]))
    q.core()
    loads[4].wait()
    strips(2, lambda r: dot_nn(normed_t[r, :], dk[...]))
    q.y()
    k.core()
    loads[5].wait()
    strips(3, lambda r: dot_nn(normed_t[r, :], dv[...]))
    v.core()
    k.y()
    head = small[...].astype(jnp.float32)
    gain = jnp.concatenate([head[c * 128 : (c + 1) * 128, :].T[0:1] for c in range(width // 128)], axis=1)
    for c in [loads[1]] + loads[6:8]:
        c.wait()

    def back(t, total):
        r = pl.ds(pl.multiple_of(t * tile, tile), tile)
        grad = dot_nt(dq[r, :], weights[0]) + dot_nt(dk[r, :], weights[1]) + dot_nt(dv[r, :], weights[2])
        x = tokens[r, :].astype(jnp.float32)
        scale = lax.rsqrt(jnp.mean(x * x, axis=-1, keepdims=True) + 1e-6)
        unit = x * scale
        pulled = grad * gain
        shift = jnp.mean(unit * pulled, axis=-1, keepdims=True)
        tokens_out[r, :] = (d_resid[r, :] + scale * (pulled - unit * shift)).astype(jnp.bfloat16)
        return total + jnp.sum(grad * unit, axis=0, keepdims=True)

    def some(first, last, total):
        return lax.fori_loop(first, last, back, total)

    def mix(t):
        r = slice(t * tile, (t + 1) * tile)
        arrived = dot_nn(pick_cells(places, t * tile, tile, cells.shape[0]), cells[...])
        mixed_out[r, :] = (resid[r, :] + spread_column(keep_gate, t * tile, tile, width) * arrived).astype(jnp.bfloat16)

    places = place[...].astype(jnp.float32)
    total = some(0, 1, jnp.zeros((1, width), jnp.float32))
    o.x()
    v.y()
    total = some(1, 3, total)
    k.x()
    total = some(3, length // tile, total)
    q.x()
    lane = lax.broadcasted_iota(jnp.int32, (128, 128), 1)
    for c in range(width // 128):
        column = jnp.broadcast_to(total[:, c * 128 : (c + 1) * 128], (128, 128)).T
        ps[c * 128 : (c + 1) * 128, :] = jnp.where(lane == 0, column, extra[:, c * 128 : (c + 1) * 128].T)
    place_table(near_sums, far_sums, ps, s.own, heads)
    s.core()
    o.z()
    k.z()
    s.y()
    for c in loads[8:]:
        c.wait()
    mix(0)
    o.spread()
    v.x()
    q.z()
    s.x()
    mix(1)
    k.spread()
    o.cross()
    v.z()
    s.z()
    mix(2)
    k.cross()
    q.spread()
    v.spread()
    s.spread()
    mix(3)
    o.finish(o_out)
    q.cross()
    v.cross()
    s.cross()
    k.finish(k_out)
    q.finish(q_out)
    v.finish(v_out)
    s.copies[10].wait_recv()
    final = s_result[...]
    pad = jnp.concatenate([final, jnp.zeros((256 - s.own, 128), jnp.float32)], axis=0)
    lines = jnp.concatenate([pad[:128, :].T, pad[128:, :].T], axis=1)
    gain_out[...] = lines[0:1, : s.own]
    gain_two_out[...] = lines[1:2, : s.own]
    router_out[...] = lines[2 : 2 + experts, : s.own]
    table_out[...] = final[: table_out.shape[0], 128 - heads :]
    for w in work + [s]:
        w.drain()


def run_tail(
    normed, dq, dk, dv, partial, weights, tokens, d_resid, cells, resid, small, extra, near, far,
    place, keep_gate, experts, own_buckets,
):
    length, width = normed.shape
    own = width // 4
    heads = near.shape[0] * near.shape[1]
    bf = jnp.bfloat16
    f32 = jnp.float32
    vm = pltpu.VMEM
    hb = pl.BlockSpec(memory_space=pl.ANY)
    mem = pl.BlockSpec(memory_space=pltpu.VMEM)
    h = own // 2
    shape = jax.ShapeDtypeStruct
    return pl.pallas_call(
        functools.partial(tail_kernel, heads, experts),
        in_specs=[hb] * 10 + [mem] * 6,
        out_specs=[mem] * 10,
        out_shape=[shape((own, width), f32)] * 4
        + [
            shape((1, own), f32),
            shape((1, own), f32),
            shape((experts, own), f32),
            shape((own_buckets, heads), f32),
            shape((length, width), bf),
            shape((length, width), bf),
        ],
        scratch_shapes=[vm((length, width), bf)] * 4
        + [
            vm((3, width, width), bf),
            vm((length, width), bf),
            vm((length, width), f32),
            vm((cells.shape[0] * cells.shape[1], width), bf),
            vm((length, width), f32),
            vm((width, length), bf),
            vm((4, width, width), bf),
            vm((4, 2, own, width), bf),
            vm((4, own, width), bf),
            vm((4, own, width), bf),
            vm((4, own, width), f32),
            vm((4, h, width), bf),
            vm((4, h, width), bf),
            vm((4, h, width), f32),
            vm((4, h, width), bf),
            vm((4, 3, h // 2, width // 2), bf),
            vm((4, h // 2, width // 2), bf),
            vm((4, own, width), bf),
            vm((2, own, width), f32),
            vm((width, 128), f32),
            vm((2, own, 128), f32),
            vm((own, 128), f32),
            vm((own, 128), f32),
            vm((own, 128), f32),
            vm((h, 128), f32),
            vm((h, 128), f32),
            vm((h, 128), f32),
            vm((h, 128), f32),
            vm((3, h // 4, 128), f32),
            vm((h // 4, 128), f32),
            vm((own, 128), f32),
            pltpu.SemaphoreType.DMA((5, 11)),
            pltpu.SemaphoreType.DMA((5, 11)),
            pltpu.SemaphoreType.DMA((20,)),
        ],
        compiler_params=pltpu.CompilerParams(collective_id=2, has_side_effects=True, vmem_limit_bytes=63 * 2**20),
        cost_estimate=pl.CostEstimate(flops=11 * 10**9, bytes_accessed=40 * 2**20, transcendentals=0),
    )(
        normed, dq, dk, dv, partial, weights, tokens, d_resid, cells, resid, small, extra, near,
        far, place, keep_gate,
    )


def finish_kernel(count, *refs):
    ins, (mine, other), outs = refs[:count], refs[count : count + 2], refs[count + 2 : 2 * count + 2]
    totals = refs[2 * count + 2 : 2 * count + 4]
    add_a, add_b = refs[2 * count + 4 : 2 * count + 6]
    bufs = refs[2 * count + 6 : 3 * count + 6]
    in_sems, out_sems = refs[3 * count + 6 :]
    first = [pltpu.make_async_copy(mine, add_a, in_sems.at[count]), pltpu.make_async_copy(other, add_b, in_sems.at[count + 1])]
    loads = [pltpu.make_async_copy(ins[i], bufs[i], in_sems.at[i]) for i in range(count)]
    for c in first + loads:
        c.start()
    for c in first:
        c.wait()
    add_a[...] = add_a[...] + add_b[...].astype(jnp.float32)
    stores = [pltpu.make_async_copy(add_a.at[h], totals[h], out_sems.at[count + h]) for h in range(2)]
    for c in stores:
        c.start()
    for i in range(count):
        loads[i].wait()
        c = pltpu.make_async_copy(bufs[i], outs[i], out_sems.at[i])
        c.start()
        stores.append(c)
    for c in stores:
        c.wait()


def run_finish(results, mine, other):
    count = len(results)
    hb = pl.BlockSpec(memory_space=pl.ANY)
    return pl.pallas_call(
        functools.partial(finish_kernel, count),
        in_specs=[hb] * (count + 2),
        out_specs=[hb] * (count + 2),
        out_shape=[jax.ShapeDtypeStruct(r.shape, r.dtype) for r in results]
        + [jax.ShapeDtypeStruct(mine.shape[1:], jnp.float32)] * 2,
        scratch_shapes=[pltpu.VMEM(mine.shape, jnp.float32), pltpu.VMEM(other.shape, jnp.bfloat16)]
        + [pltpu.VMEM(r.shape, r.dtype) for r in results]
        + [pltpu.SemaphoreType.DMA((count + 2,)), pltpu.SemaphoreType.DMA((count + 2,))],
        compiler_params=pltpu.CompilerParams(vmem_limit_bytes=63 * 2**20),
        cost_estimate=pl.CostEstimate(flops=10**6, bytes_accessed=24 * 2**20, transcendentals=0),
    )(*results, mine, other)

EPS = 1e-06
BF = jnp.bfloat16
F32 = jnp.float32


def dot_tn(a, b):
    return lax.dot_general(a, b, (((0,), (0,)), ((), ())), preferred_element_type=F32)


def swap(value, axis, size, bit):
    return lax.ppermute(value, axis, [(i, i ^ bit) for i in range(size)])


def direct(size):
    return size == 8


def exchange(blocks):
    return lax.all_to_all(blocks, "expert", split_axis=0, concat_axis=0, tiled=True)


def gather_shards(value, size):
    if size == 4:
        far = swap(value, "shard", size, 2)
        near = swap(value, "shard", size, 1)
        return [value, near, far, swap(far, "shard", size, 1)]
    return [value] + [swap(value, "shard", size, k) for k in range(1, size)]


def reduce_shards(blocks, size):
    if size == 4:
        near1 = swap(blocks[3].astype(BF), "shard", size, 1)
        near0 = swap(blocks[1].astype(BF), "shard", size, 1)
        other = swap((blocks[2].astype(F32) + near1.astype(F32)).astype(BF), "shard", size, 2)
        return blocks[0].astype(F32) + near0.astype(F32) + other.astype(F32)
    total = blocks[0].astype(F32)
    for k in range(1, size):
        total = total + swap(blocks[k].astype(BF), "shard", size, k).astype(F32)
    return total


def experts_by_collectives(row_blocks, gate_slots, cot_blocks, inner, outer, size, shards, cap):
    inners = gather_shards(inner, shards)
    outers = gather_shards(outer, shards)
    cells, width = size * cap, row_blocks.shape[2]
    rows = exchange(row_blocks).reshape(cells, width)
    cots = cot_blocks.reshape(cells, width)
    gates = exchange(gate_slots.reshape(size, cap)).reshape(cells, 1)
    half = cells // 2
    parts = [expert_half([rows[i : i + half]], [cots[i : i + half]], inners, outers) for i in (0, half)]
    back, active, d_before, d_gate = (
        jnp.concatenate([p[0][0] if i == 0 else p[i] for p in parts], axis=0) for i in range(4)
    )
    back = exchange(back.reshape(size, cap, width)).reshape(cells, width)
    d_gate = exchange(d_gate.reshape(size, cap)).reshape(cells)
    d_out = (cots.astype(F32) * gates).astype(BF)
    gated = (rows.astype(F32) * gates).astype(BF)
    block = inner.shape[1]
    spans = [slice(k * block, (k + 1) * block) for k in range(shards)]
    grad_outer = reduce_shards([dot_tn(active[:, p], d_out) for p in spans], shards)
    grad_inner = reduce_shards([dot_tn(gated, d_before[:, p]) for p in spans], shards)
    result = dot_nn(active, jnp.concatenate(outers, axis=0)).astype(BF).reshape(size, cap, width)
    result = exchange(result).reshape(cells, width)
    return back, d_gate, grad_inner, grad_outer, result


def finish_direct(
    tokens, routes, cotangent, context, weights, small, place, cot_blocks, inner_own, outer_own, inner_far,
    capacity, query, key, value, normed, forward, seg, bias, own_buckets,
):
    experts = lax.axis_size("expert")
    shards = lax.axis_size("shard")
    total, width = normed.shape
    route = routes.reshape(1, total)
    flat = tokens.reshape(total, width)
    resid, row_blocks, gate_lines, probs = run_route(context, flat, weights, small, route, place, experts, capacity)
    back, gate_back, mine, other, expert_out = run_experts(
        row_blocks, gate_lines, cot_blocks, inner_own, outer_own, inner_far
    )
    other = swap(other, "shard", shards, 2)
    out_cells = exchange(expert_out)
    d_context, d_resid, extra, keep, partial = run_unroute(
        back, gate_back, resid, cotangent.reshape(total, width), weights, context, small, route, place, probs
    )
    d_query, d_key, d_value, near_sums, far_sums = attn_bwd(
        seg[0][2], seg[0][3], query, key, value, d_context, context, forward[0][1], seg[0][0], seg[0][1], bias
    )
    (
        sum_output, sum_query, sum_key, sum_value, sum_gain, sum_gain_two, sum_router, sum_table, d_tokens, mixed,
    ) = run_tail(
        normed, d_query, d_key, d_value, partial, weights, flat, d_resid, out_cells, resid,
        small, extra, near_sums, far_sums, place, keep, experts, own_buckets,
    )
    (
        sum_output, sum_query, sum_key, sum_value, d_tokens, mixed, sum_gain, sum_gain_two, sum_router, sum_table,
        grad_inner, grad_outer,
    ) = run_finish(
        [sum_output, sum_query, sum_key, sum_value, d_tokens, mixed, sum_gain, sum_gain_two, sum_router, sum_table],
        mine, other,
    )
    return (
        mixed.reshape(tokens.shape),
        d_tokens.reshape(tokens.shape),
        sum_gain[0],
        sum_query,
        sum_key,
        sum_value,
        sum_output,
        sum_table,
        sum_gain_two[0],
        sum_router.T,
        grad_inner[None],
        grad_outer[None],
    )


def per_device(
    tokens,
    segments,
    routes,
    order,
    gain_attn,
    w_query,
    w_key,
    w_value,
    w_output,
    rel_bias,
    gain_ffn,
    w_router,
    w_in,
    w_out,
    cotangent,
):
    seq_count, length, width = tokens.shape
    total = seq_count * length
    experts = lax.axis_size("expert")
    shards = lax.axis_size("shard")
    me = lax.axis_index("expert")
    my_shard = lax.axis_index("shard")
    capacity = (5 * total + 4 * experts - 1) // (4 * experts)
    cells = experts * capacity
    heads = rel_bias.shape[1]
    own = w_query.shape[0]
    own_buckets = rel_bias.shape[0]
    buckets = own_buckets * shards
    small = jnp.concatenate([gain_attn[:, None], gain_ffn[:, None], w_router], axis=1)
    small = jnp.pad(small, ((0, 0), (0, 128 - small.shape[1])))
    small = lax.dynamic_update_slice(small, rel_bias, (0, 128 - heads))
    route = routes.reshape(total)
    chosen = (route[:, None] == jnp.arange(experts, dtype=jnp.int32)[None, :]).astype(F32)
    cot = cotangent.reshape(total, width)
    ranks = (jnp.arange(seq_count, dtype=jnp.int32)[:, None] * length + order).reshape(1, total)
    place_line, cot_cells = find_slots(routes.reshape(1, total), ranks, cot, cells, capacity)
    cot_blocks = exchange(cot_cells.reshape(experts, capacity, width))
    query, key, value, normed_low, small_all, seg_query, seg_key, bias, weights_all = project(
        tokens.reshape(total, width), small, (w_query, w_key, w_value, w_output), segments.reshape(1, total), heads
    )
    place = place_line[0]
    kept = place >= 0
    spread = (jnp.arange(cells, dtype=jnp.int32)[:, None] == place[None, :]).astype(BF)

    def to_blocks(values):
        return dot_nn(spread, values).astype(BF).reshape(experts, capacity, width)

    query_all, key_all, value_all, output_all = (weights_all[i] for i in range(4))
    inner_own, outer_own = w_in[0], w_out[0]
    if direct(experts):
        inner_own, query = lax.optimization_barrier((inner_own, query))
        inner_far = swap(inner_own, "shard", shards, 2)
    inputs = tokens.reshape(total, width).astype(F32)
    gain_two = small_all[:, 1].astype(F32)
    router_all = small_all[:, 2 : 2 + experts]
    rows_of = [slice(i * length, (i + 1) * length) for i in range(seq_count)]
    seg = [(seg_query[r], seg_key[r]) + seg_ranges(segments[i]) for i, r in enumerate(rows_of)]
    forward = [
        attn_fwd(s[2], s[3], query[r], key[r], value[r], s[0], s[1], bias)
        for s, r in zip(seg, rows_of)
    ]
    context = jnp.concatenate([f[0] for f in forward], axis=0) if seq_count > 1 else forward[0][0]
    if direct(experts):
        return finish_direct(
            tokens, routes, cotangent, context, weights_all, small_all, place_line, cot_blocks, inner_own, outer_own,
            inner_far, capacity, query, key, value, normed_low, forward, seg, bias, own_buckets,
        )
    resid = inputs + dot_nn(context, output_all)
    scale_two = lax.rsqrt(jnp.mean(resid * resid, axis=-1, keepdims=True) + EPS)
    unit_two = resid * scale_two
    normed_two_low = (unit_two * gain_two).astype(BF)
    logits = dot_nn(normed_two_low, router_all)
    probs = jax.nn.softmax(logits, axis=-1)
    gate = jnp.sum(probs * chosen, axis=-1)
    keep_weight = kept.astype(F32)
    keep_gate = gate * keep_weight
    gate_slots = jnp.sum(jnp.where(place[None, :] == jnp.arange(cells)[:, None], gate[None, :], 0), axis=1)
    row_blocks = to_blocks(normed_two_low)
    back, gate_cells, grad_inner, grad_outer, out_cells = experts_by_collectives(
        row_blocks, gate_slots, cot_blocks, w_in[0], w_out[0], experts, shards, capacity
    )
    upstream = cot.astype(F32)
    d_rows = dot_tn(spread, back)
    d_gate = jnp.sum(
        jnp.where(place[:, None] == jnp.arange(cells)[None, :], gate_cells[None, :], 0), axis=1
    )
    d_logits = (probs * (d_gate[:, None] * chosen - (d_gate * gate)[:, None])).astype(BF)
    d_router = dot_tn(normed_two_low, d_logits)
    d_normed_two = dot_nt(d_logits, router_all) + keep_gate[:, None] * d_rows
    d_gain_two = jnp.sum(d_normed_two * unit_two, axis=0)
    pulled = gain_two * d_normed_two
    d_resid = upstream + scale_two * (
        pulled - unit_two * jnp.mean(unit_two * pulled, axis=-1, keepdims=True)
    )
    d_branch = d_resid.astype(BF)
    d_context = dot_nt(d_branch, output_all).astype(BF)
    backward = [
        attn_bwd(s[2], s[3], query[r], key[r], value[r], d_context[r], f[0], f[1], s[0], s[1], bias)
        for s, r, f in zip(seg, rows_of, forward)
    ]
    d_query, d_key, d_value = (
        jnp.concatenate([b[i] for b in backward], axis=0) if seq_count > 1 else backward[0][i]
        for i in range(3)
    )
    tail = jnp.concatenate([jnp.zeros_like(d_gain_two)[:, None], d_gain_two[:, None], d_router], axis=1)
    tail = jnp.pad(tail, ((0, 0), (0, 128 - tail.shape[1])))
    flat_tokens = tokens.reshape(total, width)
    d_table = sum(table_grad(b[3], b[4], buckets) for b in backward)
    tail = lax.dynamic_update_slice(
        tail.reshape(shards, own, 128), d_table.reshape(shards, own_buckets, heads), (0, 0, 128 - heads)
    ).reshape(width, 128)
    if True:
        d_normed = (
            dot_nt(d_query, query_all) + dot_nt(d_key, key_all) + dot_nt(d_value, value_all)
        )
        inputs_again = flat_tokens.astype(F32)
        scale_one = lax.rsqrt(jnp.mean(inputs_again * inputs_again, axis=-1, keepdims=True) + EPS)
        unit_one = inputs_again * scale_one
        tail = tail.at[:, 0].set(jnp.sum(d_normed * unit_one, axis=0))
        pulled_one = small_all[:, 0].astype(F32) * d_normed
        d_tokens = d_resid + scale_one * (
            pulled_one - unit_one * jnp.mean(unit_one * pulled_one, axis=-1, keepdims=True)
        )
        pairs = ((context, d_branch), (normed_low, d_query), (normed_low, d_key), (normed_low, d_value))
        parts = [dot_tn(left, right) for left, right in pairs] + [tail]
        sum_output, sum_query, sum_key, sum_value, sums = (
            lax.psum(
                reduce_shards(
                    [lax.dynamic_slice_in_dim(p, (my_shard ^ k) * own, own, 0) for k in range(shards)], shards
                ),
                "expert",
            )
            for p in parts
        )
    arrived = dot_tn(spread, out_cells)
    mixed = resid + keep_gate[:, None] * arrived
    return (
        mixed.astype(BF).reshape(tokens.shape),
        d_tokens.astype(BF).reshape(tokens.shape),
        sums[:, 0],
        sum_query,
        sum_key,
        sum_value,
        sum_output,
        sums[:own_buckets, 128 - heads :],
        sums[:, 1],
        sums[:, 2 : 2 + experts],
        grad_inner[None],
        grad_outer[None],
    )


def solution(mesh):
    in_specs = (
        P(("expert", "shard"), None, None),
        P(("expert", "shard"), None),
        P(("expert", "shard"), None, None),
        P(("expert", "shard"), None),
        P("shard"),
        P("shard", None),
        P("shard", None),
        P("shard", None),
        P("shard", None),
        P("shard", None),
        P("shard"),
        P("shard", None),
        P("expert", None, "shard"),
        P("expert", "shard", None),
        P(("expert", "shard"), None, None),
    )
    out_specs = (
        P(("expert", "shard"), None, None),
        P(("expert", "shard"), None, None),
        P("shard"),
        P("shard", None),
        P("shard", None),
        P("shard", None),
        P("shard", None),
        P("shard", None),
        P("shard"),
        P("shard", None),
        P("expert", None, "shard"),
        P("expert", "shard", None),
    )
    return jax.shard_map(
        per_device, mesh=mesh, in_specs=in_specs, out_specs=out_specs, check_vma=False
    )
```

```python
import functools

import jax
import jax.numpy as jnp
from jax import lax
from jax.experimental import pallas as pl
from jax.experimental.pallas import tpu as pltpu
from jax.sharding import PartitionSpec as P
HEAD_DIM=64
BLK=128
EDGES = (12, 16, 23, 32, 46, 64, 91)
BIG=1e9
def bucket_index(offset):
    magnitude = jnp.abs(offset)
    far = 8 + sum(((magnitude >= edge).astype(jnp.int32) for edge in EDGES))
    near = jnp.where(magnitude < 8, magnitude, far)
    return near + 16 * (offset > 0).astype(jnp.int32)

def dot_nt(a,b): return lax.dot_general(a,b,(((1,),(1,)),((),())),preferred_element_type=jnp.float32)
def dot_nn(a,b): return lax.dot_general(a,b,(((1,),(0,)),((),())),preferred_element_type=jnp.float32)

def head_mask():
    lane=lax.broadcasted_iota(jnp.int32,(BLK,2*HEAD_DIM),1)
    return (lane<HEAD_DIM).astype(jnp.float32).astype(jnp.bfloat16)

def build_bias(w_ref, bias_ref, nblk, pairs):
    rows = (2 * nblk - 1) * BLK
    near = (nblk - 2) * BLK
    for j in range(pairs):
        for h in range(2):
            c = slice((2 * j + h) * BLK, (2 * j + h + 1) * BLK)
            w = w_ref[j, h : h + 1, :]
            bias_ref[0:near, c] = jnp.broadcast_to(w[:, 511:512], (near, BLK))
            bias_ref[near + 3 * BLK : rows, c] = jnp.broadcast_to(w[:, 0:1], (near, BLK))
            r = pltpu.roll(jnp.broadcast_to(w, (BLK, 512)), 0, 1, stride=1, stride_axis=0)
            bias_ref[near : near + BLK, c] = r[:, 384:512]
            bias_ref[near + BLK : near + 2 * BLK, c] = r[:, 256:384]
            bias_ref[near + 2 * BLK : near + 3 * BLK, c] = r[:, 128:256]


def by_width(nblk, count, run):
    for n in range(1, nblk + 1):

        @pl.when(count == n)
        def _():
            run(n * BLK)


def pair_of(block, mask):
    return jnp.concatenate([block * mask, block * (1 - mask)], axis=0)


def flip(src_ref, dst_ref, nblk, pairs):
    for j in range(pairs):
        c = slice(j * BLK, (j + 1) * BLK)
        for b in range(nblk):
            s = slice(b * BLK, (b + 1) * BLK)
            dst_ref[c, s] = src_ref[s, c].astype(jnp.float32).T.astype(jnp.bfloat16)


def join_heads(wide):
    return jnp.concatenate([wide[:HEAD_DIM, :BLK], wide[HEAD_DIM:, BLK:]], axis=0)


def fwd_kernel(nblk, pairs, lo_ref, nb_ref, q_ref, k_ref, v_ref, segq_ref, segk_ref, w_ref, ctx_ref, lse_ref, vt_ref, bias_ref):
    build_bias(w_ref, bias_ref, nblk, pairs)
    flip(v_ref, vt_ref, nblk, pairs)
    mask = head_mask()
    lanes = [slice(j * BLK, (j + 1) * BLK) for j in range(pairs)]
    both = [slice(2 * j * BLK, 2 * (j + 1) * BLK) for j in range(pairs)]

    def body(qb, _):
        rows = pl.ds(pl.multiple_of(qb * BLK, BLK), BLK)
        lob = lo_ref[qb]
        sq = segq_ref[rows, :]
        sq = jnp.concatenate([sq, sq], axis=0)
        q_cat = [jnp.concatenate([pair_of(q_ref[rows, c], mask), sq], axis=1) for c in lanes]

        def run(W):
            ks = pl.ds(pl.multiple_of(lob * BLK, BLK), W)
            bs = pl.ds(pl.multiple_of((lob - qb + nblk - 1) * BLK, BLK), W)
            sk = segk_ref[ks, :]
            st = [
                dot_nt(jnp.concatenate([k_ref[ks, c], sk], axis=1), q) + bias_ref[bs, d]
                for c, d, q in zip(lanes, both, q_cat)
            ]
            m = [jnp.max(x, axis=0, keepdims=True) for x in st]
            e = [jnp.exp(x - y) for x, y in zip(st, m)]
            l = [jnp.sum(x, axis=0, keepdims=True) for x in e]
            ot = [dot_nn(vt_ref[c, ks], x.astype(jnp.bfloat16)) / y for c, x, y in zip(lanes, e, l)]
            for j, c in enumerate(lanes):
                ctx_ref[rows, c] = join_heads(ot[j]).T.astype(jnp.bfloat16)
                lse_ref[j, pl.ds(qb, 1), :] = m[j] + jnp.log(l[j])

        by_width(nblk, nb_ref[qb], run)
        return 0

    lax.fori_loop(0, nblk, body, 0)


def bwd_kernel(
    nblk, pairs, lo_ref, nb_ref, q_ref, k_ref, v_ref, do_ref, ctx_ref, lse_ref, segq_ref, segk_ref, w_ref,
    dq_ref, dk_ref, dv_ref, near_ref, far_ref, kt_ref, bias_ref, acc_ref, dka_ref, dva_ref,
):
    build_bias(w_ref, bias_ref, nblk, pairs)
    flip(k_ref, kt_ref, nblk, pairs)
    acc_ref[...] = jnp.zeros_like(acc_ref)
    dka_ref[...] = jnp.zeros_like(dka_ref)
    dva_ref[...] = jnp.zeros_like(dva_ref)
    mask = head_mask()
    lanes = [slice(j * BLK, (j + 1) * BLK) for j in range(pairs)]
    both = [slice(2 * j * BLK, 2 * (j + 1) * BLK) for j in range(pairs)]
    row = lax.broadcasted_iota(jnp.int32, (16, 2 * HEAD_DIM), 0)
    lane = lax.broadcasted_iota(jnp.int32, (16, 2 * HEAD_DIM), 1)
    pick = ((lane // HEAD_DIM) == row).astype(jnp.float32).astype(jnp.bfloat16)

    def body(qb, _):
        rows = pl.ds(pl.multiple_of(qb * BLK, BLK), BLK)
        lob = lo_ref[qb]
        sq = segq_ref[rows, :]
        sq = jnp.concatenate([sq, sq], axis=0)
        q2 = [pair_of(q_ref[rows, c], mask) for c in lanes]
        q_cat = [jnp.concatenate([q, sq], axis=1) for q in q2]
        do2 = [pair_of(do_ref[rows, c], mask) for c in lanes]
        delta = []
        for c in lanes:
            prod = do_ref[rows, c].astype(jnp.float32) * ctx_ref[rows, c].astype(jnp.float32)
            hi = prod.astype(jnp.bfloat16)
            low = (prod - hi.astype(jnp.float32)).astype(jnp.bfloat16)
            dl = dot_nt(pick, hi) + dot_nt(pick, low)
            delta.append(jnp.concatenate([dl[0:1], dl[1:2]], axis=1))
        lse = [lse_ref[j, pl.ds(qb, 1), :] for j in range(pairs)]

        def run(W):
            ks = pl.ds(pl.multiple_of(lob * BLK, BLK), W)
            bs = pl.ds(pl.multiple_of((lob - qb + nblk - 1) * BLK, BLK), W)
            sk = segk_ref[ks, :]
            st = [dot_nt(jnp.concatenate([k_ref[ks, c], sk], axis=1), q) for c, q in zip(lanes, q_cat)]
            dp = [dot_nt(v_ref[ks, c], d) for c, d in zip(lanes, do2)]
            p = [jnp.exp(x + bias_ref[bs, d] - y) for x, d, y in zip(st, both, lse)]
            ds = [x * (y - z) for x, y, z in zip(p, dp, delta)]
            dsb = [x.astype(jnp.bfloat16) for x in ds]
            for j, (c, d) in enumerate(zip(lanes, both)):
                acc_ref[bs, d] += ds[j]
                dva_ref[ks, c] += dot_nn(p[j].astype(jnp.bfloat16), do2[j])
                dka_ref[ks, c] += dot_nn(dsb[j], q2[j])
                dqt = join_heads(dot_nn(kt_ref[c, ks], dsb[j])) * (HEAD_DIM**-0.5)
                dq_ref[rows, c] = dqt.T.astype(jnp.bfloat16)

        by_width(nblk, nb_ref[qb], run)
        return 0

    lax.fori_loop(0, nblk, body, 0)
    dk_ref[...] = dka_ref[...].astype(jnp.bfloat16)
    dv_ref[...] = dva_ref[...].astype(jnp.bfloat16)
    near = (nblk - 2) * BLK
    total = (2 * nblk - 1) * BLK
    for j in range(pairs):
        for h in range(2):
            c = slice((2 * j + h) * BLK, (2 * j + h + 1) * BLK)
            wide = jnp.concatenate(
                [
                    jnp.zeros((BLK, BLK), jnp.float32),
                    acc_ref[near + 2 * BLK : near + 3 * BLK, c],
                    acc_ref[near + BLK : near + 2 * BLK, c],
                    acc_ref[near : near + BLK, c],
                ],
                axis=1,
            )
            near_ref[j, h : h + 1, :] = jnp.sum(unroll_rows(wide), axis=0, keepdims=True)
            low = jnp.sum(acc_ref[0:near, c], axis=0, keepdims=True)
            high = jnp.sum(acc_ref[near + 3 * BLK : total, c], axis=0, keepdims=True)
            far_ref[j, h : h + 1, :] = jnp.concatenate([low, high], axis=1)


def unroll_rows(wide):
    n=wide.shape[1]
    out=wide
    row=lax.broadcasted_iota(jnp.int32,wide.shape,0)
    bit=1
    while bit<wide.shape[0]:
        out=jnp.where((row & bit)!=0,pltpu.roll(out,n-bit,1),out)
        bit*=2
    return out

FWD_PAIRS = 6
BWD_PAIRS = 3


def pair_spec(nrow, pairs):
    return pl.BlockSpec((nrow, 2 * HEAD_DIM * pairs), lambda p, *_: (0, p))


def full_spec(shape):
    return pl.BlockSpec(shape, lambda p, *_: (0,) * len(shape))


def lead_spec(pairs, shape):
    return pl.BlockSpec((pairs,) + shape, lambda p, *_: (p, 0, 0))


def attn_fwd(lo, nb, q, k, v, segq, segk, w):
    L, D = q.shape
    nblk = L // BLK
    every = D // (2 * HEAD_DIM)
    pairs = FWD_PAIRS
    return pl.pallas_call(
        functools.partial(fwd_kernel, nblk, pairs),
        grid_spec=pltpu.PrefetchScalarGridSpec(
            num_scalar_prefetch=2,
            grid=(every // pairs,),
            in_specs=[pair_spec(L, pairs)] * 3 + [full_spec((L, 128))] * 2 + [lead_spec(pairs, (2, 512))],
            out_specs=[pair_spec(L, pairs), lead_spec(pairs, (nblk, 2 * BLK))],
            scratch_shapes=[
                pltpu.VMEM((2 * HEAD_DIM * pairs, L), jnp.bfloat16),
                pltpu.VMEM(((2 * nblk - 1) * BLK, 2 * BLK * pairs), jnp.float32),
            ],
        ),
        out_shape=[
            jax.ShapeDtypeStruct((L, D), jnp.bfloat16),
            jax.ShapeDtypeStruct((every, nblk, 2 * BLK), jnp.float32),
        ],
        compiler_params=pltpu.CompilerParams(vmem_limit_bytes=63 * 2**20),
        cost_estimate=pl.CostEstimate(flops=2 * 10**9, bytes_accessed=8 * 2**20, transcendentals=6 * 10**6),
    )(lo, nb, q, k, v, segq, segk, w)


def attn_bwd(lo, nb, q, k, v, do, ctx, lse, segq, segk, w):
    L, D = q.shape
    nblk = L // BLK
    every = D // (2 * HEAD_DIM)
    pairs = BWD_PAIRS
    rows = (2 * nblk - 1) * BLK
    return pl.pallas_call(
        functools.partial(bwd_kernel, nblk, pairs),
        grid_spec=pltpu.PrefetchScalarGridSpec(
            num_scalar_prefetch=2,
            grid=(every // pairs,),
            in_specs=[pair_spec(L, pairs)] * 5
            + [lead_spec(pairs, (nblk, 2 * BLK))]
            + [full_spec((L, 128))] * 2
            + [lead_spec(pairs, (2, 512))],
            out_specs=[pair_spec(L, pairs)] * 3 + [lead_spec(pairs, (2, 512)), lead_spec(pairs, (2, 256))],
            scratch_shapes=[
                pltpu.VMEM((2 * HEAD_DIM * pairs, L), jnp.bfloat16),
                pltpu.VMEM((rows, 2 * BLK * pairs), jnp.float32),
                pltpu.VMEM((rows, 2 * BLK * pairs), jnp.float32),
                pltpu.VMEM((L, 2 * HEAD_DIM * pairs), jnp.float32),
                pltpu.VMEM((L, 2 * HEAD_DIM * pairs), jnp.float32),
            ],
        ),
        out_shape=[jax.ShapeDtypeStruct((L, D), jnp.bfloat16)] * 3
        + [jax.ShapeDtypeStruct((every, 2, 512), jnp.float32), jax.ShapeDtypeStruct((every, 2, 256), jnp.float32)],
        compiler_params=pltpu.CompilerParams(vmem_limit_bytes=63 * 2**20),
        cost_estimate=pl.CostEstimate(flops=4 * 10**9, bytes_accessed=16 * 2**20, transcendentals=6 * 10**6),
    )(lo, nb, q, k, v, do, ctx, lse, segq, segk, w)


def seg_ranges(seg):
    L = seg.shape[0]
    nblk = L // BLK
    sb = seg.reshape(nblk, BLK)
    first = jnp.sum((seg[None, :] < sb[:, :1]).astype(jnp.int32), axis=1)
    last = jnp.sum((seg[None, :] <= sb[:, -1:]).astype(jnp.int32), axis=1)
    lo = first // BLK
    nb = (last + BLK - 1) // BLK - lo
    return lo.astype(jnp.int32), nb.astype(jnp.int32)


def table_grad(near,far,buckets):
    off=-(jnp.arange(512,dtype=jnp.int32)-256)
    oh=(bucket_index(off)[:,None]==jnp.arange(buckets,dtype=jnp.int32)[None,:]).astype(jnp.float32)
    n=jnp.einsum("hx,xb->bh",near.reshape(-1,512),oh,precision=lax.Precision.HIGHEST)
    f=far.reshape(-1,2,128).sum(-1)
    ids=jnp.arange(buckets,dtype=jnp.int32)[:,None]
    return n+jnp.where(ids==15,f[None,:,0],0)+jnp.where(ids==31,f[None,:,1],0)

TILE=256
def gelu_parts(x):
    c=0.7978845608028654
    x2=x*x
    t=jnp.tanh(x*(c+(c*0.044715)*x2))
    half=0.5*(1.0+t)
    slope=half+0.5*x*(1.0-t*t)*(c+(3*c*0.044715)*x2)
    return x*half,slope

def expert_kernel(count, parts, *refs):
    rows=refs[:count]; cots=refs[count:2*count]
    wi_refs=refs[2*count:2*count+parts]; wo_refs=refs[2*count+parts:2*count+2*parts]
    refs=refs[2*count+2*parts:]
    outs=refs[:count]; act_ref,db_ref,dg_ref=refs[count:count+3]
    x_ref,c_ref,wi_buf,wo_buf,acc_ref,dga_ref,act_buf,db_buf,w_sem,o_sem=refs[count+3:]
    block=wi_refs[0].shape[1]
    per=block//TILE
    total=parts*per
    for k in range(parts):
        pltpu.make_async_copy(wi_refs[k],wi_buf.at[k],w_sem.at[0,k]).start()
        pltpu.make_async_copy(wo_refs[k],wo_buf.at[k],w_sem.at[1,k]).start()
    first=0
    for i in range(count):
        n=rows[i].shape[0]
        x_ref[first:first+n,:]=rows[i][...]
        c_ref[first:first+n,:]=cots[i][...]
        first+=n
    acc_ref[...]=jnp.zeros_like(acc_ref)
    dga_ref[...]=jnp.zeros_like(dga_ref)
    def out_copies(step,slot):
        cols=pl.ds(pl.multiple_of(step*TILE,TILE),TILE)
        return (pltpu.make_async_copy(act_buf.at[slot],act_ref.at[:,cols],o_sem.at[0,slot]),
                pltpu.make_async_copy(db_buf.at[slot],db_ref.at[:,cols],o_sem.at[1,slot]))
    for k in range(parts):
        pltpu.make_async_copy(wi_refs[k],wi_buf.at[k],w_sem.at[0,k]).wait()
        pltpu.make_async_copy(wo_refs[k],wo_buf.at[k],w_sem.at[1,k]).wait()
        def body(c,_):
            step=k*per+c
            slot=lax.rem(step,2)
            @pl.when(step>=2)
            def _():
                for cp in out_copies(step-2,slot): cp.wait()
            cols=pl.ds(pl.multiple_of(c*TILE,TILE),TILE)
            wi=wi_buf[k,:,cols]
            wo=wo_buf[k,cols,:]
            before=dot_nn(x_ref[...],wi)
            up=dot_nt(c_ref[...],wo)
            active,slope=gelu_parts(before)
            prod=active*up
            dga_ref[...]+=prod[:,:128]+prod[:,128:]
            act_buf[slot]=active.astype(jnp.bfloat16)
            db=(up*slope).astype(jnp.bfloat16)
            db_buf[slot]=db
            acc_ref[...]+=dot_nt(db,wi)
            for cp in out_copies(step,slot): cp.start()
            return 0
        lax.fori_loop(0,per,body,0)
    first=0
    for i in range(count):
        n=rows[i].shape[0]
        outs[i][...]=acc_ref[first:first+n,:].astype(jnp.bfloat16)
        first+=n
    ones=jnp.ones((8,128),jnp.bfloat16)
    sums=dga_ref[...]
    hi=sums.astype(jnp.bfloat16)
    rest=sums-hi.astype(jnp.float32)
    mid=rest.astype(jnp.bfloat16)
    low=(rest-mid.astype(jnp.float32)).astype(jnp.bfloat16)
    dg_ref[...]=dot_nt(ones,hi)+dot_nt(ones,mid)+dot_nt(ones,low)
    for step in (total-2,total-1):
        for cp in out_copies(step,step%2): cp.wait()

def expert_half(rows,cots,w_ins,w_outs):
    count=len(rows); parts=len(w_ins)
    width,block=w_ins[0].shape
    R=sum(r.shape[0] for r in rows)
    vm=pl.BlockSpec(memory_space=pltpu.VMEM); hb=pl.BlockSpec(memory_space=pl.ANY)
    outs=pl.pallas_call(functools.partial(expert_kernel,count,parts),
        in_specs=[vm]*(2*count)+[hb]*(2*parts),
        out_specs=[vm]*count+[hb,hb,vm],
        out_shape=[jax.ShapeDtypeStruct(r.shape,jnp.bfloat16) for r in rows]+[jax.ShapeDtypeStruct((R,parts*block),jnp.bfloat16)]*2+[jax.ShapeDtypeStruct((8,R),jnp.float32)],
        scratch_shapes=[pltpu.VMEM((R,width),jnp.bfloat16)]*2+[pltpu.VMEM((parts,width,block),jnp.bfloat16),pltpu.VMEM((parts,block,width),jnp.bfloat16),
            pltpu.VMEM((R,width),jnp.float32),pltpu.VMEM((R,128),jnp.float32),pltpu.VMEM((2,R,TILE),jnp.bfloat16),pltpu.VMEM((2,R,TILE),jnp.bfloat16),
            pltpu.SemaphoreType.DMA((2,parts)),pltpu.SemaphoreType.DMA((2,2))],
        compiler_params=pltpu.CompilerParams(vmem_limit_bytes=48*2**20),
        cost_estimate=pl.CostEstimate(flops=6*R*width*parts*block,bytes_accessed=20*2**20,transcendentals=R*parts*block))(*rows,*cots,*w_ins,*w_outs)
    return outs[:count],outs[count],outs[count+1],outs[count+2][0]

MESH = pl.DeviceIdType.MESH


def shard_peer(bit):
    return (lax.axis_index("expert"), lax.axis_index("shard") ^ bit)


def expert_peer(bit):
    return (lax.axis_index("expert") ^ bit, lax.axis_index("shard"))


def greet(peers):
    barrier = pltpu.get_barrier_semaphore()
    for peer in peers:
        pl.semaphore_signal(barrier, inc=1, device_id=peer, device_id_type=MESH)
    pl.semaphore_wait(barrier, len(peers))


def send(src, dst, send_sem, recv_sem, peer):
    copy = pltpu.make_async_remote_copy(
        src_ref=src, dst_ref=dst, send_sem=send_sem, recv_sem=recv_sem, device_id=peer, device_id_type=MESH
    )
    copy.start()
    return copy


def columns(line, block):
    return jnp.broadcast_to(line[:, block * 128 : (block + 1) * 128], (128, 128)).T


def project_kernel(
    heads, x_in, small_in, q_in, k_in, v_in, o_in, segments,
    q_ref, k_ref, v_ref, normed_ref, small_ref, segq_ref, segk_ref, bias_ref, all_ref,
    x_ref, small_buf, w_buf, unit_ref,
    sem_send, sem_recv, sem_own, sem_out, sem_load,
):
    shard = lax.axis_index("shard")
    own = q_in.shape[0]
    load = pltpu.make_async_copy(x_in, x_ref, sem_load.at[0])
    load.start()

    def rows(bit):
        return pl.ds(pl.multiple_of((shard ^ bit) * own, 64), own)

    ins = [small_in, q_in, k_in, v_in, o_in]
    bufs = [small_buf] + [w_buf.at[i] for i in range(4)]
    count = len(ins)
    kept = []
    for i in range(count):
        copy = pltpu.make_async_copy(ins[i], bufs[i].at[rows(0)], sem_own.at[i])
        copy.start()
        kept.append(copy)
    greet([shard_peer(1), shard_peer(2)])
    far, near, passed = [], [], [None] * count
    for i in range(count):
        far.append(send(ins[i], bufs[i].at[rows(0)], sem_send.at[0, i], sem_recv.at[0, i], shard_peer(2)))
    for i in range(count):
        near.append(send(ins[i], bufs[i].at[rows(0)], sem_send.at[1, i], sem_recv.at[1, i], shard_peer(1)))
    length, width = x_ref.shape
    tile = 512

    def unit(t, _):
        r = pl.ds(pl.multiple_of(t * tile, tile), tile)
        x = x_ref[r, :].astype(jnp.float32)
        unit_ref[r, :] = x * lax.rsqrt(jnp.mean(x * x, axis=-1, keepdims=True) + 1e-6)
        return 0

    def hop(i):
        far[i].wait_recv()
        here = bufs[i].at[rows(2)]
        passed[i] = send(here, here, sem_send.at[2, i], sem_recv.at[2, i], shard_peer(1))

    def finish(i):
        kept[i].wait()
        near[i].wait_recv()
        passed[i].wait_recv()

    load.wait()
    lax.fori_loop(0, length // tile, unit, 0)
    documents = segments[...].astype(jnp.float32)
    ids = lax.broadcasted_iota(jnp.int32, (128, 128), 1).astype(jnp.float32)
    for b in range(length // 128):
        r = slice(b * 128, (b + 1) * 128)
        same = (columns(documents, b) == ids).astype(jnp.float32)
        segq_ref[r, :] = same.astype(jnp.bfloat16)
        segk_ref[r, :] = jnp.where(ids < 16.0, (same - 1.0) * BIG, 0.0).astype(jnp.bfloat16)
    hop(0)
    hop(1)
    finish(0)
    small = small_buf[...]
    small_ref[...] = small
    gain = jnp.concatenate(
        [small[c * 128 : (c + 1) * 128, :].astype(jnp.float32).T[0:1] for c in range(width // 128)], axis=1
    )

    buckets = 32
    part = buckets // 4
    table = jnp.concatenate([small[j * own : j * own + part, :].astype(jnp.float32) for j in range(4)], axis=0)
    table = jnp.concatenate([table, jnp.zeros((128 - buckets, 128), jnp.float32)], axis=0).T
    wide = bias_ref.shape[2]
    offset = wide // 2 - lax.broadcasted_iota(jnp.int32, (128, wide), 1)
    onehot = (bucket_index(offset) == lax.broadcasted_iota(jnp.int32, (128, wide), 0)).astype(jnp.float32)
    lines = dot_nn(table.astype(jnp.bfloat16), onehot.astype(jnp.bfloat16))
    for p in range(heads // 2):
        bias_ref[p] = lines[128 - heads + 2 * p : 130 - heads + 2 * p]

    def norm(t, _):
        r = pl.ds(pl.multiple_of(t * tile, tile), tile)
        normed_ref[r, :] = (unit_ref[r, :] * gain).astype(jnp.bfloat16)
        return 0

    lax.fori_loop(0, length // tile, norm, 0)
    outs = []

    def project_one(i, out):
        finish(i)
        copy = pltpu.make_async_copy(w_buf.at[i - 1], all_ref.at[i - 1], sem_out.at[i - 1])
        copy.start()
        outs.append(copy)

        def run(t, _):
            r = pl.ds(pl.multiple_of(t * tile, tile), tile)
            y = dot_nn(normed_ref[r, :], w_buf[i - 1]).astype(jnp.bfloat16)
            if i == 1:
                y = (y.astype(jnp.float32) * HEAD_DIM**-0.5).astype(jnp.bfloat16)
            out[r, :] = y
            return 0

        lax.fori_loop(0, length // tile, run, 0)

    project_one(1, q_ref)
    hop(2)
    project_one(2, k_ref)
    hop(3)
    project_one(3, v_ref)
    hop(4)
    finish(4)
    copy = pltpu.make_async_copy(w_buf.at[3], all_ref.at[3], sem_out.at[3])
    copy.start()
    outs.append(copy)
    for c in outs:
        c.wait()
    for c in far + near + passed:
        c.wait_send()


def project(x, small, weights, segments, heads):
    length, width = x.shape
    vm = pl.BlockSpec(memory_space=pltpu.VMEM)
    hb = pl.BlockSpec(memory_space=pl.ANY)
    bf = jnp.bfloat16
    shape = jax.ShapeDtypeStruct
    return pl.pallas_call(
        functools.partial(project_kernel, heads),
        in_specs=[hb] * 6 + [vm],
        out_specs=[vm] * 8 + [hb],
        out_shape=[shape((length, width), bf)] * 4 + [shape((width, 128), bf), shape((length, 128), bf), shape((length, 128), bf), shape((heads // 2, 2, 512), jnp.float32)]
        + [shape((4, width, width), bf)],
        scratch_shapes=[
            pltpu.VMEM((length, width), bf),
            pltpu.VMEM((width, 128), bf),
            pltpu.VMEM((4, width, width), bf),
            pltpu.VMEM((length, width), jnp.float32),
            pltpu.SemaphoreType.DMA((3, 5)),
            pltpu.SemaphoreType.DMA((3, 5)),
            pltpu.SemaphoreType.DMA((5,)),
            pltpu.SemaphoreType.DMA((4,)),
            pltpu.SemaphoreType.DMA((1,)),
        ],
        compiler_params=pltpu.CompilerParams(collective_id=0, has_side_effects=True, vmem_limit_bytes=63 * 2**20),
        cost_estimate=pl.CostEstimate(flops=6 * 10**9, bytes_accessed=20 * 2**20, transcendentals=0),
    )(x, small, *weights, segments)


def slot_kernel(cap, route, order, cot, place_ref, cells_ref):
    length = cot.shape[0]
    keys = (route[...] * length + order[...]).astype(jnp.float32)
    starts = (route[...] * length).astype(jnp.float32)
    blocks = length // 128
    sides = [columns(keys, b) for b in range(blocks)]
    slots = []
    for t in range(blocks):
        s = slice(t * 128, (t + 1) * 128)
        sums = sum((c < keys[:, s]).astype(jnp.float32) - (c < starts[:, s]).astype(jnp.float32) for c in sides)
        slots.append(jnp.sum(sums, axis=0, keepdims=True))
    slot = jnp.concatenate(slots, axis=1).astype(jnp.int32)
    place = jnp.where(slot < cap, route[...] * cap + slot, -1)
    place_ref[...] = place
    step = 640
    for t in range(cells_ref.shape[0] // step):
        ids = lax.broadcasted_iota(jnp.int32, (step, length), 0) + t * step
        pick = (ids == place).astype(jnp.float32).astype(jnp.bfloat16)
        cells_ref[t * step : (t + 1) * step, :] = dot_nn(pick, cot[...]).astype(jnp.bfloat16)


def find_slots(route, order, cot, cells, cap):
    length, width = cot.shape
    vm = pl.BlockSpec(memory_space=pltpu.VMEM)
    return pl.pallas_call(
        functools.partial(slot_kernel, cap),
        in_specs=[vm] * 3,
        out_specs=[vm] * 2,
        out_shape=[jax.ShapeDtypeStruct((1, length), jnp.int32), jax.ShapeDtypeStruct((cells, width), jnp.bfloat16)],
        compiler_params=pltpu.CompilerParams(vmem_limit_bytes=63 * 2**20),
        cost_estimate=pl.CostEstimate(flops=2 * 10**9, bytes_accessed=4 * 2**20, transcendentals=0),
    )(route, order, cot)


def gate_columns(line, count, width):
    column = jnp.broadcast_to(line, (128, 256)).T[:count]
    return jnp.concatenate([column] * (width // 128), axis=1)


def experts_kernel(
    size, cap, tile,
    rows_in, gate_in, cot_in, inner_own, outer_own, inner_far,
    back_out, dgate_out, mine_out, other_out, result_out,
    rows, gates, cots, weights, active, d_before, total, d_gate, back, d_gates, back_in, d_gates_in,
    gated_t, g_send, g_recv, stage, result,
    w_sem, wr_sem, row_send, row_recv, gate_send, gate_recv, back_send, back_recv, dg_send, dg_recv,
    g_sem_send, g_sem_recv, cot_sem, out_sem, res_sem, back_sem, dgb_sem,
):
    width = weights.shape[2]
    block = weights.shape[3]
    per = block // tile
    group = 2
    count = group * cap
    me = lax.axis_index("expert")

    def part(k):
        return pl.ds(k * cap, cap)

    local = [
        pltpu.make_async_copy(inner_own, weights.at[0, 0], w_sem.at[0]),
        pltpu.make_async_copy(outer_own, weights.at[0, 1], w_sem.at[1]),
        pltpu.make_async_copy(inner_far, weights.at[2, 0], w_sem.at[2]),
        pltpu.make_async_copy(rows_in.at[me], rows.at[part(0)], w_sem.at[3]),
        pltpu.make_async_copy(gate_in.at[me], gates.at[0], w_sem.at[4]),
    ]
    local += [pltpu.make_async_copy(cot_in.at[me ^ k], cots.at[part(k)], cot_sem.at[k]) for k in range(size)]
    for c in local:
        c.start()
    greet([expert_peer(k) for k in range(1, size)] + [shard_peer(1), shard_peer(2)])
    sent = []
    arrive = {}
    outer_far = send(outer_own, weights.at[2, 1], wr_sem.at[0, 0], wr_sem.at[1, 0], shard_peer(2))

    def dispatch(k):
        arrive[k] = [
            send(gate_in.at[me ^ k], gates.at[k], gate_send.at[k], gate_recv.at[k], expert_peer(k)),
            send(rows_in.at[me ^ k], rows.at[part(k)], row_send.at[k], row_recv.at[k], expert_peer(k)),
        ]
        sent.append(arrive[k][0])

    for k in (4, 5, 2, 3, 6, 7, 1):
        dispatch(k)
    moved = [
        send(inner_own, weights.at[1, 0], wr_sem.at[0, 1], wr_sem.at[1, 1], shard_peer(1)),
        send(outer_own, weights.at[1, 1], wr_sem.at[0, 2], wr_sem.at[1, 2], shard_peer(1)),
        send(inner_far, weights.at[3, 0], wr_sem.at[0, 3], wr_sem.at[1, 3], shard_peer(1)),
    ]
    sent += moved + [outer_far]
    d_gates[...] = jnp.zeros_like(d_gates)
    for c in local:
        c.wait()
    for c in moved:
        c.wait_recv()
    ones = jnp.ones((8, 128), jnp.bfloat16)
    returned = {}

    def arrived(blocks):
        for k in blocks:
            if k:
                for c in arrive[k]:
                    c.wait_recv()

    def forward_back(blocks, spot, first, last):
        span = len(blocks) * cap
        mine = slice(blocks[0] * cap, blocks[0] * cap + span)
        here = slice(spot * count, spot * count + span)
        if first == 0:
            total[here, :] = jnp.zeros((span, width), jnp.float32)
            d_gate[here, :] = jnp.zeros((span, 128), jnp.float32)

        def step(t, _):
            kk = t // per
            cols = pl.ds(pl.multiple_of(lax.rem(t, per) * tile, tile), tile)
            where = pl.ds(pl.multiple_of(t * tile, tile), tile)
            wi = weights[kk, 0, :, cols]
            wo = weights[kk, 1, cols, :]
            before = dot_nn(rows[mine, :], wi)
            up = dot_nt(cots[mine, :], wo)
            value, slope = gelu_parts(before)
            prod = value * up
            d_gate[here, :] += sum(prod[:, c * 128 : (c + 1) * 128] for c in range(tile // 128))
            active[mine, where] = value.astype(jnp.bfloat16)
            db = (up * slope).astype(jnp.bfloat16)
            d_before[mine, where] = db
            total[here, :] += dot_nt(db, wi)
            return 0

        lax.fori_loop(first * per, last * per, step, 0)

    def give_back(blocks, spot):
        span = len(blocks) * cap
        here = slice(spot * count, spot * count + span)
        back[blocks[0] * cap : blocks[0] * cap + span, :] = total[here, :].astype(jnp.bfloat16)
        for k in blocks:
            start = spot * count + (k - blocks[0]) * cap
            sums = d_gate[start : start + cap, :]
            hi = sums.astype(jnp.bfloat16)
            rest = sums - hi.astype(jnp.float32)
            mid = rest.astype(jnp.bfloat16)
            low = (rest - mid.astype(jnp.float32)).astype(jnp.bfloat16)
            d_gates[k, :, 0:cap] = dot_nt(ones, hi) + dot_nt(ones, mid) + dot_nt(ones, low)
            if k:
                returned[k] = [
                    send(d_gates.at[k], d_gates_in.at[k], dg_send.at[k], dg_recv.at[k], expert_peer(k)),
                    send(back.at[part(k)], back_in.at[part(k)], back_send.at[k], back_recv.at[k], expert_peer(k)),
                ]
                sent.extend(returned[k])

    near = ((0, 1), (2, 3))
    for i, blocks in enumerate(near):
        arrived(blocks)
        forward_back(blocks, i, 0, 2)
    outer_far.wait_recv()
    passed = send(weights.at[2, 1], weights.at[3, 1], wr_sem.at[0, 4], wr_sem.at[1, 4], shard_peer(1))
    sent.append(passed)
    passed.wait_recv()
    for i, blocks in enumerate(near):
        forward_back(blocks, i, 2, 4)
        give_back(blocks, i)
    for blocks in ((4,), (5,), (6, 7)):
        arrived(blocks)
        forward_back(blocks, 2, 0, 4)
        give_back(blocks, 2)
    for k in range(size):
        span = slice(k * cap, (k + 1) * cap)
        column = gate_columns(gates[k, 0:1, :], cap, width)
        cots[span, :] = (cots[span, :].astype(jnp.float32) * column).astype(jnp.bfloat16)
        result[span, :] = (rows[span, :].astype(jnp.float32) * column).astype(jnp.bfloat16)
    every = size * cap
    for c in range(width // 128):
        for r in range(every // 128):
            gated_t[c * 128 : (c + 1) * 128, r * 128 : (r + 1) * 128] = (
                result[r * 128 : (r + 1) * 128, c * 128 : (c + 1) * 128].astype(jnp.float32).T.astype(jnp.bfloat16)
            )
    strip = block

    def inner(kk, out):
        return dot_nn(gated_t[out, :], d_before[:, kk * block : (kk + 1) * block])

    def outer(kk, out, t):
        return dot_tn(active[:, pl.ds(pl.multiple_of(kk * block + t * strip, strip), strip)], cots[...])

    def strips(body):
        def run(t, _):
            body(pl.ds(pl.multiple_of(t * strip, strip), strip), t)
            return 0

        lax.fori_loop(0, block // strip, run, 0)

    def chunk(h, kk, out, t):
        return inner(kk, out) if h == 0 else outer(kk, out, t)

    finals = []
    for h in range(2):
        shared = []
        for n, kk in enumerate((3, 1)):

            def give(out, t):
                g_send[h, n, out, :] = chunk(h, kk, out, t).astype(jnp.bfloat16)

            strips(give)
            c = send(g_send.at[h, n], g_recv.at[h, n], g_sem_send.at[h, n], g_sem_recv.at[h, n], shard_peer(1))
            shared.append(c)
        shared[0].wait_recv()
        shared[0].wait_send()

        def other(out, t):
            g_send[h, 0, out, :] = (chunk(h, 2, out, t) + g_recv[h, 0, out, :].astype(jnp.float32)).astype(jnp.bfloat16)

        strips(other)
        c = pltpu.make_async_copy(g_send.at[h, 0], other_out.at[h], out_sem.at[0, h])
        c.start()
        finals.append(c)
        shared[1].wait_recv()
        sent.append(shared[1])

        def keep(out, t):
            stage[h, out, :] = chunk(h, 0, out, t) + g_recv[h, 1, out, :].astype(jnp.float32)

        strips(keep)
        c = pltpu.make_async_copy(stage.at[h], mine_out.at[h], out_sem.at[1, h])
        c.start()
        finals.append(c)

    def produce(r, _):
        span = pl.ds(pl.multiple_of(r * 4 * cap, 16), 4 * cap)
        y = sum(dot_nn(active[span, kk * block : (kk + 1) * block], weights[kk, 1]) for kk in range(4))
        result[span, :] = y.astype(jnp.bfloat16)
        return 0

    lax.fori_loop(0, size // 4, produce, 0)
    for k in range(size):
        c = pltpu.make_async_copy(result.at[part(k)], result_out.at[me ^ k], res_sem.at[k])
        c.start()
        finals.append(c)
    back_in[part(0), :] = back[part(0), :]
    d_gates_in[0] = d_gates[0]
    for k in range(size):
        if k:
            for c in returned[k]:
                c.wait_recv()
        for c in (
            pltpu.make_async_copy(back_in.at[part(k)], back_out.at[me ^ k], back_sem.at[k]),
            pltpu.make_async_copy(d_gates_in.at[k], dgate_out.at[me ^ k], dgb_sem.at[k]),
        ):
            c.start()
            finals.append(c)
    for c in finals:
        c.wait()
    for k in range(1, size):
        arrive[k][1].wait_send()
    for c in sent:
        c.wait_send()


def run_experts(rows, gates, cots, inner_own, outer_own, inner_far):
    size, cap, width = rows.shape
    block = inner_own.shape[1]
    bf = jnp.bfloat16
    f32 = jnp.float32
    every = size * cap
    hb = pl.BlockSpec(memory_space=pl.ANY)
    vm = pltpu.VMEM
    dma = pltpu.SemaphoreType.DMA
    shape = jax.ShapeDtypeStruct
    return pl.pallas_call(
        functools.partial(experts_kernel, size, cap, block),
        in_specs=[hb] * 6,
        out_specs=[hb] * 5,
        out_shape=[
            shape((size, cap, width), bf),
            shape((size, 8, 256), f32),
            shape((2, width, block), f32),
            shape((2, width, block), bf),
            shape((size, cap, width), bf),
        ],
        scratch_shapes=[
            vm((every, width), bf),
            vm((size, 8, 256), f32),
            vm((every, width), bf),
            vm((4, 2, width, block), bf),
            vm((every, 4 * block), bf),
            vm((every, 4 * block), bf),
            vm((6 * cap, width), f32),
            vm((6 * cap, 128), f32),
            vm((every, width), bf),
            vm((size, 8, 256), f32),
            vm((every, width), bf),
            vm((size, 8, 256), f32),
            vm((width, every), bf),
            vm((2, 2, width, block), bf),
            vm((2, 2, width, block), bf),
            vm((2, width, block), f32),
            vm((every, width), bf),
            dma((5,)),
            dma((2, 5)),
        ]
        + [dma((size,))] * 8
        + [dma((2, 2)), dma((2, 2)), dma((size,)), dma((2, 2)), dma((size,)), dma((size,)), dma((size,))],
        compiler_params=pltpu.CompilerParams(collective_id=1, has_side_effects=True, vmem_limit_bytes=63 * 2**20),
        cost_estimate=pl.CostEstimate(flops=36 * 10**9, bytes_accessed=30 * 2**20, transcendentals=4 * 10**6),
    )(rows, gates, cots, inner_own, outer_own, inner_far)


def turned(small, width):
    return jnp.concatenate(
        [small[c * 128 : (c + 1) * 128, :].astype(jnp.float32).T for c in range(width // 128)], axis=1
    )


def three_parts(line):
    hi = line.astype(jnp.bfloat16)
    rest = line - hi.astype(jnp.float32)
    mid = rest.astype(jnp.bfloat16)
    low = rest - mid.astype(jnp.float32)
    none = jnp.zeros((5, line.shape[1]), jnp.float32)
    parts = jnp.concatenate([hi.astype(jnp.float32), mid.astype(jnp.float32), low, none], axis=0)
    return parts.astype(jnp.bfloat16)


def pick_cells(place, first, tile, cells):
    out = []
    for b in range(first // 128, (first + tile) // 128):
        column = columns(place, b)
        lane = lax.broadcasted_iota(jnp.int32, (128, 128), 1).astype(jnp.float32)
        out.append(
            jnp.concatenate([(column == lane + 128.0 * j).astype(jnp.float32) for j in range(cells // 128)], axis=1)
        )
    return jnp.concatenate(out, axis=0).astype(jnp.bfloat16)


def spread_column(line, first, tile, width):
    return jnp.concatenate(
        [
            jnp.concatenate([columns(line, b)] * (width // 128), axis=1)
            for b in range(first // 128, (first + tile) // 128)
        ],
        axis=0,
    )


def route_kernel(
    cap, context_in, tokens_in, weights_in, small, route, place,
    resid_out, cells_out, gate_out, probs_out,
    context, tokens, w_out, normed, sems,
):
    length, width = normed.shape
    experts = probs_out.shape[0]
    loads = [
        pltpu.make_async_copy(weights_in.at[3], w_out, sems.at[0]),
        pltpu.make_async_copy(context_in, context, sems.at[1]),
        pltpu.make_async_copy(tokens_in, tokens, sems.at[2]),
    ]
    for c in loads:
        c.start()
    lines = turned(small, width)
    gain = lines[1:2]
    for c in loads:
        c.wait()
    tile = 512
    for t in range(length // tile):
        r = slice(t * tile, (t + 1) * tile)
        resid = tokens[r, :].astype(jnp.float32) + dot_nn(context[r, :], w_out[...])
        resid_out[r, :] = resid
        scale = lax.rsqrt(jnp.mean(resid * resid, axis=-1, keepdims=True) + 1e-6)
        normed[r, :] = (resid * scale * gain).astype(jnp.bfloat16)
    logits = dot_nt(lines.astype(jnp.bfloat16), normed[...])[2 : 2 + experts]
    top = jnp.exp(logits - jnp.max(logits, axis=0, keepdims=True))
    probs = top / jnp.sum(top, axis=0, keepdims=True)
    probs_out[...] = probs
    which = lax.broadcasted_iota(jnp.int32, probs.shape, 0)
    gate = jnp.sum(jnp.where(which == route[...], probs, 0.0), axis=0, keepdims=True)
    parts = three_parts(gate)
    gate_out[...] = jnp.zeros_like(gate_out)
    for k in range(experts):
        ids = lax.broadcasted_iota(jnp.int32, (cap, length), 0) + k * cap
        pick = (ids == place[...]).astype(jnp.float32).astype(jnp.bfloat16)
        cells_out[k] = dot_nn(pick, normed[...]).astype(jnp.bfloat16)
        found = dot_nt(parts, pick)
        gate_out[k, :, 0:cap] = jnp.broadcast_to(jnp.sum(found, axis=0, keepdims=True), (8, cap))


def run_route(context, tokens, weights, small, route, place, experts, cap):
    length, width = tokens.shape
    bf, f32 = jnp.bfloat16, jnp.float32
    vm = pl.BlockSpec(memory_space=pltpu.VMEM)
    hb = pl.BlockSpec(memory_space=pl.ANY)
    shape = jax.ShapeDtypeStruct
    return pl.pallas_call(
        functools.partial(route_kernel, cap),
        in_specs=[hb] * 3 + [vm] * 3,
        out_specs=[vm] * 4,
        out_shape=[
            shape((length, width), f32),
            shape((experts, cap, width), bf),
            shape((experts, 8, 256), f32),
            shape((experts, length), f32),
        ],
        scratch_shapes=[
            pltpu.VMEM((length, width), bf),
            pltpu.VMEM((length, width), bf),
            pltpu.VMEM((width, width), bf),
            pltpu.VMEM((length, width), bf),
            pltpu.SemaphoreType.DMA((3,)),
        ],
        compiler_params=pltpu.CompilerParams(vmem_limit_bytes=63 * 2**20),
        cost_estimate=pl.CostEstimate(flops=4 * 10**9, bytes_accessed=16 * 2**20, transcendentals=0),
    )(context, tokens, weights, small, route, place)


def unroute_kernel(
    cap, back_in, d_gate_in, resid_in, cot_in, weights_in, context_in, small, route, place, probs,
    d_context_out, d_resid_out, extra, keep_out, grad_out,
    back, resid, cot, w_out, context, d_branch, d_context, d_resid, sems, tile_sems, out_sems,
):
    length, width = resid.shape
    experts = probs.shape[0]
    cells = experts * cap
    loads = [pltpu.make_async_copy(back_in.at[k], back.at[pl.ds(k * cap, cap)], sems.at[4 + k]) for k in range(experts)]
    tile = 512
    spans = [pl.ds(t * tile, tile) for t in range(length // tile)]
    loads.append(pltpu.make_async_copy(weights_in.at[3], w_out, sems.at[2]))
    last = pltpu.make_async_copy(context_in, context, sems.at[3])
    tiles = [
        [
            pltpu.make_async_copy(resid_in.at[r], resid.at[r], tile_sems.at[0, t]),
            pltpu.make_async_copy(cot_in.at[r], cot.at[r], tile_sems.at[1, t]),
        ]
        for t, r in enumerate(spans)
    ]
    for c in loads + [c for pair in tiles for c in pair] + [last]:
        c.start()
    lines = turned(small, width)
    gain = lines[1:2]
    low_lines = lines.astype(jnp.bfloat16)
    which = lax.broadcasted_iota(jnp.int32, probs.shape, 0)
    chosen = (which == route[...]).astype(jnp.float32)
    gate = jnp.sum(probs[...] * chosen, axis=0, keepdims=True)
    keep = jnp.where(place[...] >= 0, gate, 0.0)
    keep_out[...] = keep
    places = place[...].astype(jnp.float32)
    parts = three_parts(jnp.concatenate([d_gate_in[k, 0:1, 0:cap] for k in range(experts)], axis=1))
    for c in loads:
        c.wait()
    stores = []
    grads = jnp.zeros((128, width), jnp.float32)
    gains = jnp.zeros((1, width), jnp.float32)
    for t in range(length // tile):
        r = slice(t * tile, (t + 1) * tile)
        for c in tiles[t]:
            c.wait()
        pick = pick_cells(places, t * tile, tile, cells)
        d_rows = dot_nn(pick, back[...])
        d_gate = jnp.sum(dot_nt(parts, pick), axis=0, keepdims=True)
        d_logits = probs[:, r] * (chosen[:, r] - gate[:, r]) * d_gate
        padded = jnp.concatenate(
            [
                jnp.zeros((2, tile), jnp.float32),
                d_logits.astype(jnp.bfloat16).astype(jnp.float32),
                jnp.zeros((126 - experts, tile), jnp.float32),
            ],
            axis=0,
        )
        d_normed = dot_nn(padded.T.astype(jnp.bfloat16), low_lines) + spread_column(keep, t * tile, tile, width) * d_rows
        x = resid[r, :]
        scale = lax.rsqrt(jnp.mean(x * x, axis=-1, keepdims=True) + 1e-6)
        unit = x * scale
        grads = grads + dot_nn(padded.astype(jnp.bfloat16), (unit * gain).astype(jnp.bfloat16))
        gains = gains + jnp.sum(d_normed * unit, axis=0, keepdims=True)
        pulled = gain * d_normed
        out = cot[r, :].astype(jnp.float32) + scale * (
            pulled - unit * jnp.mean(unit * pulled, axis=-1, keepdims=True)
        )
        d_resid[r, :] = out
        low = out.astype(jnp.bfloat16)
        d_branch[r, :] = low
        d_context[r, :] = dot_nt(low, w_out[...]).astype(jnp.bfloat16)
        for h, (src, dst) in enumerate(((d_context, d_context_out), (d_resid, d_resid_out))):
            c = pltpu.make_async_copy(src.at[spans[t]], dst.at[spans[t]], out_sems.at[h, t])
            c.start()
            stores.append(c)
    last.wait()
    grad_out[...] = dot_tn(context[...], d_branch[...]).astype(jnp.bfloat16)
    row = lax.broadcasted_iota(jnp.int32, (128, width), 0)
    extra[...] = jnp.where(row == 1, gains, grads)
    for c in stores:
        c.wait()


def run_unroute(back, d_gate, resid, cot, weights, context, small, route, place, probs):
    experts, cap, width = back.shape
    length = resid.shape[0]
    bf, f32 = jnp.bfloat16, jnp.float32
    vm = pl.BlockSpec(memory_space=pltpu.VMEM)
    hb = pl.BlockSpec(memory_space=pl.ANY)
    shape = jax.ShapeDtypeStruct
    return pl.pallas_call(
        functools.partial(unroute_kernel, cap),
        in_specs=[hb, vm, hb, hb, hb, hb] + [vm] * 4,
        out_specs=[hb, hb] + [vm] * 3,
        out_shape=[
            shape((length, width), bf),
            shape((length, width), f32),
            shape((128, width), f32),
            shape((1, length), f32),
            shape((width, width), bf),
        ],
        scratch_shapes=[
            pltpu.VMEM((experts * cap, width), bf),
            pltpu.VMEM((length, width), f32),
            pltpu.VMEM((length, width), bf),
            pltpu.VMEM((width, width), bf),
            pltpu.VMEM((length, width), bf),
            pltpu.VMEM((length, width), bf),
            pltpu.VMEM((length, width), bf),
            pltpu.VMEM((length, width), f32),
            pltpu.SemaphoreType.DMA((4 + experts,)),
            pltpu.SemaphoreType.DMA((2, length // 256)),
            pltpu.SemaphoreType.DMA((2, length // 256)),
        ],
        compiler_params=pltpu.CompilerParams(vmem_limit_bytes=63 * 2**20),
        cost_estimate=pl.CostEstimate(flops=4 * 10**9, bytes_accessed=18 * 2**20, transcendentals=0),
    )(back, d_gate, resid, cot, weights, context, small, route, place, probs)


class Reduction:
    def __init__(self, index, partial, near, far_send, far_recv, full, x_send, x_recv, half, z_send, z_recv, piece, result, send_sems, recv_sems):
        self.partial, self.near, self.far_send, self.far_recv = partial, near, far_send, far_recv
        self.full, self.x_send, self.x_recv, self.half = full, x_send, x_recv, half
        self.z_send, self.z_recv, self.piece, self.result = z_send, z_recv, piece, result
        self.index, self.send_sems, self.recv_sems = index, send_sems, recv_sems
        self.own = full.shape[0]
        self.width = full.shape[1]
        self.type = partial.dtype
        self.copies = {}

    def block(self, bit):
        return pl.ds(pl.multiple_of((lax.axis_index("shard") ^ bit) * self.own, self.own & -self.own), self.own)

    def half_rows(self, bit):
        rows = self.own // 2
        return pl.ds(pl.multiple_of(((lax.axis_index("expert") & 1) ^ bit) * rows, rows & -rows), rows)

    def quarter(self, step):
        j = (lax.axis_index("expert") >> 1) ^ step
        rows = self.own // 2
        if self.type == jnp.float32:
            return (pl.ds(pl.multiple_of(j * (rows // 4), 8), rows // 4), slice(None))
        return (
            pl.ds(pl.multiple_of((j >> 1) * (rows // 2), 16), rows // 2),
            pl.ds(pl.multiple_of((j & 1) * (self.width // 2), 128), self.width // 2),
        )

    def go(self, slot, src, dst, peer):
        self.copies[slot] = send(src, dst, self.send_sems.at[self.index, slot], self.recv_sems.at[self.index, slot], peer)

    def core(self):
        self.go(0, self.partial.at[self.block(3)], self.near.at[1], shard_peer(1))
        self.go(1, self.partial.at[self.block(1)], self.near.at[0], shard_peer(1))

    def y(self):
        self.copies[0].wait_recv()
        other = self.partial[self.block(2), :].astype(jnp.float32) + self.near[1].astype(jnp.float32)
        self.far_send[...] = other.astype(self.type)
        self.go(2, self.far_send, self.far_recv, shard_peer(2))
        self.copies[1].wait_recv()
        self.full[...] = self.partial[self.block(0), :].astype(jnp.float32) + self.near[0].astype(jnp.float32)

    def x(self):
        self.copies[2].wait_recv()
        self.full[...] += self.far_recv[...].astype(jnp.float32)
        self.x_send[...] = self.full[self.half_rows(1), :].astype(self.type)
        self.go(3, self.x_send, self.x_recv, expert_peer(1))

    def z(self):
        self.copies[3].wait_recv()
        self.half[...] = self.own_half() + self.x_recv[...].astype(jnp.float32)
        self.z_send[...] = self.half[...].astype(self.type)
        for step in (2, 3, 1):
            self.go(3 + step, self.z_send.at[self.quarter(step)], self.z_recv.at[step - 1], expert_peer(2 * step))

    def own_half(self):
        return self.full[self.half_rows(0), :]

    def spread(self):
        for step in (1, 2, 3):
            self.copies[3 + step].wait_recv()
        rows, cols = self.quarter(0)
        total = self.half[rows, cols]
        for step in (1, 2, 3):
            total = total + self.z_recv[step - 1].astype(jnp.float32)
        self.piece[...] = total.astype(self.type)
        target = self.place()
        for step in (2, 3, 1):
            self.go(6 + step, self.piece, self.result.at[target], expert_peer(2 * step))
        self.result[target] = self.piece[...]

    def place(self):
        j = lax.axis_index("expert") >> 1
        first = (lax.axis_index("expert") & 1) * (self.own // 2)
        rows = self.own // 2
        if self.type == jnp.float32:
            return (pl.ds(pl.multiple_of(first + j * (rows // 4), 8), rows // 4), slice(None))
        return (
            pl.ds(pl.multiple_of(first + (j >> 1) * (rows // 2), 16), rows // 2),
            pl.ds(pl.multiple_of((j & 1) * (self.width // 2), 128), self.width // 2),
        )

    def cross(self):
        for step in (1, 2, 3):
            self.copies[6 + step].wait_recv()
        self.go(10, self.result.at[self.half_rows(0)], self.result.at[self.half_rows(0)], expert_peer(1))

    def finish(self, out):
        self.copies[10].wait_recv()
        out[...] = self.result[...].astype(jnp.float32)

    def drain(self):
        for c in self.copies.values():
            c.wait_send()


class Crossed(Reduction):
    other = None

    def y(self):
        rows = self.own // 2
        self.copies[0].wait_recv()
        self.other[...] = self.partial[self.block(2), :].astype(jnp.float32) + self.near[1].astype(jnp.float32)
        self.far_send[rows:, :] = self.other[self.half_rows(1), :].astype(self.type)
        self.copies[1].wait_recv()
        self.full[...] = self.partial[self.block(0), :].astype(jnp.float32) + self.near[0].astype(jnp.float32)
        self.far_send[:rows, :] = self.full[self.half_rows(1), :].astype(self.type)
        self.go(2, self.far_send, self.far_recv, expert_peer(1))

    def x(self):
        rows = self.own // 2
        self.copies[2].wait_recv()
        other = self.other[self.half_rows(0), :] + self.far_recv[rows:, :].astype(jnp.float32)
        self.x_send[...] = other.astype(self.type)
        self.go(3, self.x_send, self.x_recv, shard_peer(2))

    def own_half(self):
        return self.full[self.half_rows(0), :] + self.far_recv[: self.own // 2, :].astype(jnp.float32)


def place_table(near, far, ps, own, heads):
    buckets = 32
    wide = near.shape[2]
    offset = wide // 2 - lax.broadcasted_iota(jnp.int32, (wide, buckets), 0)
    onehot = (bucket_index(offset) == lax.broadcasted_iota(jnp.int32, (wide, buckets), 1)).astype(jnp.float32)
    sums = jnp.concatenate([near[j] for j in range(near.shape[0])], axis=0)
    table = lax.dot_general(
        sums, onehot, (((1,), (0,)), ((), ())), preferred_element_type=jnp.float32, precision=lax.Precision.HIGHEST
    )
    ends = jnp.concatenate([far[j] for j in range(far.shape[0])], axis=0)
    low = jnp.sum(ends[:, :128], axis=1, keepdims=True)
    high = jnp.sum(ends[:, 128:], axis=1, keepdims=True)
    which = lax.broadcasted_iota(jnp.int32, (heads, buckets), 1)
    table = table + jnp.where(which == 15, low, 0.0) + jnp.where(which == 31, high, 0.0)
    part = buckets // 4
    square = jnp.concatenate([table, jnp.zeros((heads, 128 - buckets), jnp.float32)], axis=1)
    square = jnp.concatenate([jnp.zeros((128 - heads, 128), jnp.float32), square], axis=0).T
    lane = lax.broadcasted_iota(jnp.int32, (part, 128), 1)
    for j in range(4):
        r = slice(j * own, j * own + part)
        ps[r, :] = jnp.where(lane >= 128 - heads, square[j * part : (j + 1) * part, :], ps[r, :])


def tail_kernel(
    heads, experts,
    normed_in, dq_in, dk_in, dv_in, p_in, weights_in, tokens_in, d_resid_in,
    cells_in, resid_in, small, extra, near_sums, far_sums, place, keep_gate,
    o_out, q_out, k_out, v_out, gain_out, gain_two_out, router_out, table_out, tokens_out, mixed_out,
    normed, dq, dk, dv, weights, tokens, d_resid, cells, resid,
    normed_t, p_ref, near, far_send, far_recv, full, x_send, x_recv, half, z_send, z_recv, piece, result, other,
    ps, s_near, s_far_send, s_far_recv, s_full, s_x_send, s_x_recv, s_half, s_z_send, s_z_recv, s_piece, s_result,
    send_sems, recv_sems, load_sems,
):
    length, width = normed.shape
    tile = 256
    loads = [
        pltpu.make_async_copy(src, dst, load_sems.at[i])
        for i, (src, dst) in enumerate(
            (
                (p_in, p_ref.at[0]),
                (weights_in.at[0:3], weights),
                (normed_in, normed),
                (dq_in, dq),
                (dk_in, dk),
                (dv_in, dv),
                (tokens_in, tokens),
                (d_resid_in, d_resid),
                (resid_in, resid),
            )
        )
    ]
    cap = cells_in.shape[1]
    loads += [
        pltpu.make_async_copy(cells_in.at[k], cells.at[pl.ds(k * cap, cap)], load_sems.at[11 + k])
        for k in range(cells_in.shape[0])
    ]
    for c in loads:
        c.start()
    greet([shard_peer(1), shard_peer(2)] + [expert_peer(k) for k in (1, 2, 4, 6)])
    work = []
    for m in range(4):
        w = (Crossed if m >= 2 else Reduction)(
            m, p_ref.at[m], near.at[m], far_send.at[m], far_recv.at[m], full.at[m], x_send.at[m], x_recv.at[m],
            half.at[m], z_send.at[m], z_recv.at[m], piece.at[m], result.at[m], send_sems, recv_sems,
        )
        w.other = other.at[m % 2]
        work.append(w)
    o, q, k, v = work
    s = Reduction(
        4, ps, s_near, s_far_send, s_far_recv, s_full, s_x_send, s_x_recv, s_half, s_z_send, s_z_recv, s_piece,
        s_result, send_sems, recv_sems,
    )

    def strips(m, make):
        p_ref[m] = make(slice(None)).astype(jnp.bfloat16)

    loads[0].wait()
    o.core()
    loads[2].wait()
    for c in range(width // 128):
        for t in range(length // 128):
            normed_t[c * 128 : (c + 1) * 128, t * 128 : (t + 1) * 128] = (
                normed[t * 128 : (t + 1) * 128, c * 128 : (c + 1) * 128].astype(jnp.float32).T.astype(jnp.bfloat16)
            )
    o.y()
    loads[3].wait()
    strips(1, lambda r: dot_nn(normed_t[r, :], dq[...]))
    q.core()
    loads[4].wait()
    strips(2, lambda r: dot_nn(normed_t[r, :], dk[...]))
    q.y()
    k.core()
    loads[5].wait()
    strips(3, lambda r: dot_nn(normed_t[r, :], dv[...]))
    v.core()
    k.y()
    head = small[...].astype(jnp.float32)
    gain = jnp.concatenate([head[c * 128 : (c + 1) * 128, :].T[0:1] for c in range(width // 128)], axis=1)
    for c in [loads[1]] + loads[6:8]:
        c.wait()

    def back(t, total):
        r = pl.ds(pl.multiple_of(t * tile, tile), tile)
        grad = dot_nt(dq[r, :], weights[0]) + dot_nt(dk[r, :], weights[1]) + dot_nt(dv[r, :], weights[2])
        x = tokens[r, :].astype(jnp.float32)
        scale = lax.rsqrt(jnp.mean(x * x, axis=-1, keepdims=True) + 1e-6)
        unit = x * scale
        pulled = grad * gain
        shift = jnp.mean(unit * pulled, axis=-1, keepdims=True)
        tokens_out[r, :] = (d_resid[r, :] + scale * (pulled - unit * shift)).astype(jnp.bfloat16)
        return total + jnp.sum(grad * unit, axis=0, keepdims=True)

    def some(first, last, total):
        return lax.fori_loop(first, last, back, total)

    def mix(t):
        r = slice(t * tile, (t + 1) * tile)
        arrived = dot_nn(pick_cells(places, t * tile, tile, cells.shape[0]), cells[...])
        mixed_out[r, :] = (resid[r, :] + spread_column(keep_gate, t * tile, tile, width) * arrived).astype(jnp.bfloat16)

    places = place[...].astype(jnp.float32)
    total = some(0, 1, jnp.zeros((1, width), jnp.float32))
    o.x()
    v.y()
    total = some(1, 3, total)
    k.x()
    total = some(3, length // tile, total)
    q.x()
    lane = lax.broadcasted_iota(jnp.int32, (128, 128), 1)
    for c in range(width // 128):
        column = jnp.broadcast_to(total[:, c * 128 : (c + 1) * 128], (128, 128)).T
        ps[c * 128 : (c + 1) * 128, :] = jnp.where(lane == 0, column, extra[:, c * 128 : (c + 1) * 128].T)
    place_table(near_sums, far_sums, ps, s.own, heads)
    s.core()
    o.z()
    k.z()
    s.y()
    for c in loads[8:]:
        c.wait()
    mix(0)
    o.spread()
    v.x()
    q.z()
    s.x()
    mix(1)
    k.spread()
    o.cross()
    v.z()
    s.z()
    mix(2)
    k.cross()
    q.spread()
    v.spread()
    s.spread()
    mix(3)
    o.finish(o_out)
    q.cross()
    v.cross()
    s.cross()
    k.finish(k_out)
    q.finish(q_out)
    v.finish(v_out)
    s.copies[10].wait_recv()
    final = s_result[...]
    pad = jnp.concatenate([final, jnp.zeros((256 - s.own, 128), jnp.float32)], axis=0)
    lines = jnp.concatenate([pad[:128, :].T, pad[128:, :].T], axis=1)
    gain_out[...] = lines[0:1, : s.own]
    gain_two_out[...] = lines[1:2, : s.own]
    router_out[...] = lines[2 : 2 + experts, : s.own]
    table_out[...] = final[: table_out.shape[0], 128 - heads :]
    for w in work + [s]:
        w.drain()


def run_tail(
    normed, dq, dk, dv, partial, weights, tokens, d_resid, cells, resid, small, extra, near, far,
    place, keep_gate, experts, own_buckets,
):
    length, width = normed.shape
    own = width // 4
    heads = near.shape[0] * near.shape[1]
    bf = jnp.bfloat16
    f32 = jnp.float32
    vm = pltpu.VMEM
    hb = pl.BlockSpec(memory_space=pl.ANY)
    mem = pl.BlockSpec(memory_space=pltpu.VMEM)
    h = own // 2
    shape = jax.ShapeDtypeStruct
    return pl.pallas_call(
        functools.partial(tail_kernel, heads, experts),
        in_specs=[hb] * 10 + [mem] * 6,
        out_specs=[mem] * 10,
        out_shape=[shape((own, width), f32)] * 4
        + [
            shape((1, own), f32),
            shape((1, own), f32),
            shape((experts, own), f32),
            shape((own_buckets, heads), f32),
            shape((length, width), bf),
            shape((length, width), bf),
        ],
        scratch_shapes=[vm((length, width), bf)] * 4
        + [
            vm((3, width, width), bf),
            vm((length, width), bf),
            vm((length, width), f32),
            vm((cells.shape[0] * cells.shape[1], width), bf),
            vm((length, width), f32),
            vm((width, length), bf),
            vm((4, width, width), bf),
            vm((4, 2, own, width), bf),
            vm((4, own, width), bf),
            vm((4, own, width), bf),
            vm((4, own, width), f32),
            vm((4, h, width), bf),
            vm((4, h, width), bf),
            vm((4, h, width), f32),
            vm((4, h, width), bf),
            vm((4, 3, h // 2, width // 2), bf),
            vm((4, h // 2, width // 2), bf),
            vm((4, own, width), bf),
            vm((2, own, width), f32),
            vm((width, 128), f32),
            vm((2, own, 128), f32),
            vm((own, 128), f32),
            vm((own, 128), f32),
            vm((own, 128), f32),
            vm((h, 128), f32),
            vm((h, 128), f32),
            vm((h, 128), f32),
            vm((h, 128), f32),
            vm((3, h // 4, 128), f32),
            vm((h // 4, 128), f32),
            vm((own, 128), f32),
            pltpu.SemaphoreType.DMA((5, 11)),
            pltpu.SemaphoreType.DMA((5, 11)),
            pltpu.SemaphoreType.DMA((20,)),
        ],
        compiler_params=pltpu.CompilerParams(collective_id=2, has_side_effects=True, vmem_limit_bytes=63 * 2**20),
        cost_estimate=pl.CostEstimate(flops=11 * 10**9, bytes_accessed=40 * 2**20, transcendentals=0),
    )(
        normed, dq, dk, dv, partial, weights, tokens, d_resid, cells, resid, small, extra, near,
        far, place, keep_gate,
    )


def finish_kernel(count, *refs):
    ins, (mine, other), outs = refs[:count], refs[count : count + 2], refs[count + 2 : 2 * count + 2]
    totals = refs[2 * count + 2 : 2 * count + 4]
    add_a, add_b = refs[2 * count + 4 : 2 * count + 6]
    bufs = refs[2 * count + 6 : 3 * count + 6]
    in_sems, out_sems = refs[3 * count + 6 :]
    first = [pltpu.make_async_copy(mine, add_a, in_sems.at[count]), pltpu.make_async_copy(other, add_b, in_sems.at[count + 1])]
    loads = [pltpu.make_async_copy(ins[i], bufs[i], in_sems.at[i]) for i in range(count)]
    for c in first + loads:
        c.start()
    for c in first:
        c.wait()
    add_a[...] = add_a[...] + add_b[...].astype(jnp.float32)
    stores = [pltpu.make_async_copy(add_a.at[h], totals[h], out_sems.at[count + h]) for h in range(2)]
    for c in stores:
        c.start()
    for i in range(count):
        loads[i].wait()
        c = pltpu.make_async_copy(bufs[i], outs[i], out_sems.at[i])
        c.start()
        stores.append(c)
    for c in stores:
        c.wait()


def run_finish(results, mine, other):
    count = len(results)
    hb = pl.BlockSpec(memory_space=pl.ANY)
    return pl.pallas_call(
        functools.partial(finish_kernel, count),
        in_specs=[hb] * (count + 2),
        out_specs=[hb] * (count + 2),
        out_shape=[jax.ShapeDtypeStruct(r.shape, r.dtype) for r in results]
        + [jax.ShapeDtypeStruct(mine.shape[1:], jnp.float32)] * 2,
        scratch_shapes=[pltpu.VMEM(mine.shape, jnp.float32), pltpu.VMEM(other.shape, jnp.bfloat16)]
        + [pltpu.VMEM(r.shape, r.dtype) for r in results]
        + [pltpu.SemaphoreType.DMA((count + 2,)), pltpu.SemaphoreType.DMA((count + 2,))],
        compiler_params=pltpu.CompilerParams(vmem_limit_bytes=63 * 2**20),
        cost_estimate=pl.CostEstimate(flops=10**6, bytes_accessed=24 * 2**20, transcendentals=0),
    )(*results, mine, other)

EPS = 1e-06
BF = jnp.bfloat16
F32 = jnp.float32


def dot_tn(a, b):
    return lax.dot_general(a, b, (((0,), (0,)), ((), ())), preferred_element_type=F32)


def swap(value, axis, size, bit):
    return lax.ppermute(value, axis, [(i, i ^ bit) for i in range(size)])


def direct(size):
    return size == 8


def exchange(blocks):
    return lax.all_to_all(blocks, "expert", split_axis=0, concat_axis=0, tiled=True)


def gather_shards(value, size):
    if size == 4:
        far = swap(value, "shard", size, 2)
        near = swap(value, "shard", size, 1)
        return [value, near, far, swap(far, "shard", size, 1)]
    return [value] + [swap(value, "shard", size, k) for k in range(1, size)]


def reduce_shards(blocks, size):
    if size == 4:
        near1 = swap(blocks[3].astype(BF), "shard", size, 1)
        near0 = swap(blocks[1].astype(BF), "shard", size, 1)
        other = swap((blocks[2].astype(F32) + near1.astype(F32)).astype(BF), "shard", size, 2)
        return blocks[0].astype(F32) + near0.astype(F32) + other.astype(F32)
    total = blocks[0].astype(F32)
    for k in range(1, size):
        total = total + swap(blocks[k].astype(BF), "shard", size, k).astype(F32)
    return total


def experts_by_collectives(row_blocks, gate_slots, cot_blocks, inner, outer, size, shards, cap):
    inners = gather_shards(inner, shards)
    outers = gather_shards(outer, shards)
    cells, width = size * cap, row_blocks.shape[2]
    rows = exchange(row_blocks).reshape(cells, width)
    cots = cot_blocks.reshape(cells, width)
    gates = exchange(gate_slots.reshape(size, cap)).reshape(cells, 1)
    half = cells // 2
    parts = [expert_half([rows[i : i + half]], [cots[i : i + half]], inners, outers) for i in (0, half)]
    back, active, d_before, d_gate = (
        jnp.concatenate([p[0][0] if i == 0 else p[i] for p in parts], axis=0) for i in range(4)
    )
    back = exchange(back.reshape(size, cap, width)).reshape(cells, width)
    d_gate = exchange(d_gate.reshape(size, cap)).reshape(cells)
    d_out = (cots.astype(F32) * gates).astype(BF)
    gated = (rows.astype(F32) * gates).astype(BF)
    block = inner.shape[1]
    spans = [slice(k * block, (k + 1) * block) for k in range(shards)]
    grad_outer = reduce_shards([dot_tn(active[:, p], d_out) for p in spans], shards)
    grad_inner = reduce_shards([dot_tn(gated, d_before[:, p]) for p in spans], shards)
    result = dot_nn(active, jnp.concatenate(outers, axis=0)).astype(BF).reshape(size, cap, width)
    result = exchange(result).reshape(cells, width)
    return back, d_gate, grad_inner, grad_outer, result


def finish_direct(
    tokens, routes, cotangent, context, weights, small, place, cot_blocks, inner_own, outer_own, inner_far,
    capacity, query, key, value, normed, forward, seg, bias, own_buckets,
):
    experts = lax.axis_size("expert")
    shards = lax.axis_size("shard")
    total, width = normed.shape
    route = routes.reshape(1, total)
    flat = tokens.reshape(total, width)
    resid, row_blocks, gate_lines, probs = run_route(context, flat, weights, small, route, place, experts, capacity)
    back, gate_back, mine, other, expert_out = run_experts(
        row_blocks, gate_lines, cot_blocks, inner_own, outer_own, inner_far
    )
    other = swap(other, "shard", shards, 2)
    out_cells = exchange(expert_out)
    d_context, d_resid, extra, keep, partial = run_unroute(
        back, gate_back, resid, cotangent.reshape(total, width), weights, context, small, route, place, probs
    )
    d_query, d_key, d_value, near_sums, far_sums = attn_bwd(
        seg[0][2], seg[0][3], query, key, value, d_context, context, forward[0][1], seg[0][0], seg[0][1], bias
    )
    (
        sum_output, sum_query, sum_key, sum_value, sum_gain, sum_gain_two, sum_router, sum_table, d_tokens, mixed,
    ) = run_tail(
        normed, d_query, d_key, d_value, partial, weights, flat, d_resid, out_cells, resid,
        small, extra, near_sums, far_sums, place, keep, experts, own_buckets,
    )
    (
        sum_output, sum_query, sum_key, sum_value, d_tokens, mixed, sum_gain, sum_gain_two, sum_router, sum_table,
        grad_inner, grad_outer,
    ) = run_finish(
        [sum_output, sum_query, sum_key, sum_value, d_tokens, mixed, sum_gain, sum_gain_two, sum_router, sum_table],
        mine, other,
    )
    return (
        mixed.reshape(tokens.shape),
        d_tokens.reshape(tokens.shape),
        sum_gain[0],
        sum_query,
        sum_key,
        sum_value,
        sum_output,
        sum_table,
        sum_gain_two[0],
        sum_router.T,
        grad_inner[None],
        grad_outer[None],
    )


def per_device(
    tokens,
    segments,
    routes,
    order,
    gain_attn,
    w_query,
    w_key,
    w_value,
    w_output,
    rel_bias,
    gain_ffn,
    w_router,
    w_in,
    w_out,
    cotangent,
):
    seq_count, length, width = tokens.shape
    total = seq_count * length
    experts = lax.axis_size("expert")
    shards = lax.axis_size("shard")
    me = lax.axis_index("expert")
    my_shard = lax.axis_index("shard")
    capacity = (5 * total + 4 * experts - 1) // (4 * experts)
    cells = experts * capacity
    heads = rel_bias.shape[1]
    own = w_query.shape[0]
    own_buckets = rel_bias.shape[0]
    buckets = own_buckets * shards
    small = jnp.concatenate([gain_attn[:, None], gain_ffn[:, None], w_router], axis=1)
    small = jnp.pad(small, ((0, 0), (0, 128 - small.shape[1])))
    small = lax.dynamic_update_slice(small, rel_bias, (0, 128 - heads))
    route = routes.reshape(total)
    chosen = (route[:, None] == jnp.arange(experts, dtype=jnp.int32)[None, :]).astype(F32)
    cot = cotangent.reshape(total, width)
    ranks = (jnp.arange(seq_count, dtype=jnp.int32)[:, None] * length + order).reshape(1, total)
    place_line, cot_cells = find_slots(routes.reshape(1, total), ranks, cot, cells, capacity)
    cot_blocks = exchange(cot_cells.reshape(experts, capacity, width))
    query, key, value, normed_low, small_all, seg_query, seg_key, bias, weights_all = project(
        tokens.reshape(total, width), small, (w_query, w_key, w_value, w_output), segments.reshape(1, total), heads
    )
    place = place_line[0]
    kept = place >= 0
    spread = (jnp.arange(cells, dtype=jnp.int32)[:, None] == place[None, :]).astype(BF)

    def to_blocks(values):
        return dot_nn(spread, values).astype(BF).reshape(experts, capacity, width)

    query_all, key_all, value_all, output_all = (weights_all[i] for i in range(4))
    inner_own, outer_own = w_in[0], w_out[0]
    if direct(experts):
        inner_own, query = lax.optimization_barrier((inner_own, query))
        inner_far = swap(inner_own, "shard", shards, 2)
    inputs = tokens.reshape(total, width).astype(F32)
    gain_two = small_all[:, 1].astype(F32)
    router_all = small_all[:, 2 : 2 + experts]
    rows_of = [slice(i * length, (i + 1) * length) for i in range(seq_count)]
    seg = [(seg_query[r], seg_key[r]) + seg_ranges(segments[i]) for i, r in enumerate(rows_of)]
    forward = [
        attn_fwd(s[2], s[3], query[r], key[r], value[r], s[0], s[1], bias)
        for s, r in zip(seg, rows_of)
    ]
    context = jnp.concatenate([f[0] for f in forward], axis=0) if seq_count > 1 else forward[0][0]
    if direct(experts):
        return finish_direct(
            tokens, routes, cotangent, context, weights_all, small_all, place_line, cot_blocks, inner_own, outer_own,
            inner_far, capacity, query, key, value, normed_low, forward, seg, bias, own_buckets,
        )
    resid = inputs + dot_nn(context, output_all)
    scale_two = lax.rsqrt(jnp.mean(resid * resid, axis=-1, keepdims=True) + EPS)
    unit_two = resid * scale_two
    normed_two_low = (unit_two * gain_two).astype(BF)
    logits = dot_nn(normed_two_low, router_all)
    probs = jax.nn.softmax(logits, axis=-1)
    gate = jnp.sum(probs * chosen, axis=-1)
    keep_weight = kept.astype(F32)
    keep_gate = gate * keep_weight
    gate_slots = jnp.sum(jnp.where(place[None, :] == jnp.arange(cells)[:, None], gate[None, :], 0), axis=1)
    row_blocks = to_blocks(normed_two_low)
    back, gate_cells, grad_inner, grad_outer, out_cells = experts_by_collectives(
        row_blocks, gate_slots, cot_blocks, w_in[0], w_out[0], experts, shards, capacity
    )
    upstream = cot.astype(F32)
    d_rows = dot_tn(spread, back)
    d_gate = jnp.sum(
        jnp.where(place[:, None] == jnp.arange(cells)[None, :], gate_cells[None, :], 0), axis=1
    )
    d_logits = (probs * (d_gate[:, None] * chosen - (d_gate * gate)[:, None])).astype(BF)
    d_router = dot_tn(normed_two_low, d_logits)
    d_normed_two = dot_nt(d_logits, router_all) + keep_gate[:, None] * d_rows
    d_gain_two = jnp.sum(d_normed_two * unit_two, axis=0)
    pulled = gain_two * d_normed_two
    d_resid = upstream + scale_two * (
        pulled - unit_two * jnp.mean(unit_two * pulled, axis=-1, keepdims=True)
    )
    d_branch = d_resid.astype(BF)
    d_context = dot_nt(d_branch, output_all).astype(BF)
    backward = [
        attn_bwd(s[2], s[3], query[r], key[r], value[r], d_context[r], f[0], f[1], s[0], s[1], bias)
        for s, r, f in zip(seg, rows_of, forward)
    ]
    d_query, d_key, d_value = (
        jnp.concatenate([b[i] for b in backward], axis=0) if seq_count > 1 else backward[0][i]
        for i in range(3)
    )
    tail = jnp.concatenate([jnp.zeros_like(d_gain_two)[:, None], d_gain_two[:, None], d_router], axis=1)
    tail = jnp.pad(tail, ((0, 0), (0, 128 - tail.shape[1])))
    flat_tokens = tokens.reshape(total, width)
    d_table = sum(table_grad(b[3], b[4], buckets) for b in backward)
    tail = lax.dynamic_update_slice(
        tail.reshape(shards, own, 128), d_table.reshape(shards, own_buckets, heads), (0, 0, 128 - heads)
    ).reshape(width, 128)
    if True:
        d_normed = (
            dot_nt(d_query, query_all) + dot_nt(d_key, key_all) + dot_nt(d_value, value_all)
        )
        inputs_again = flat_tokens.astype(F32)
        scale_one = lax.rsqrt(jnp.mean(inputs_again * inputs_again, axis=-1, keepdims=True) + EPS)
        unit_one = inputs_again * scale_one
        tail = tail.at[:, 0].set(jnp.sum(d_normed * unit_one, axis=0))
        pulled_one = small_all[:, 0].astype(F32) * d_normed
        d_tokens = d_resid + scale_one * (
            pulled_one - unit_one * jnp.mean(unit_one * pulled_one, axis=-1, keepdims=True)
        )
        pairs = ((context, d_branch), (normed_low, d_query), (normed_low, d_key), (normed_low, d_value))
        parts = [dot_tn(left, right) for left, right in pairs] + [tail]
        sum_output, sum_query, sum_key, sum_value, sums = (
            lax.psum(
                reduce_shards(
                    [lax.dynamic_slice_in_dim(p, (my_shard ^ k) * own, own, 0) for k in range(shards)], shards
                ),
                "expert",
            )
            for p in parts
        )
    arrived = dot_tn(spread, out_cells)
    mixed = resid + keep_gate[:, None] * arrived
    return (
        mixed.astype(BF).reshape(tokens.shape),
        d_tokens.astype(BF).reshape(tokens.shape),
        sums[:, 0],
        sum_query,
        sum_key,
        sum_value,
        sum_output,
        sums[:own_buckets, 128 - heads :],
        sums[:, 1],
        sums[:, 2 : 2 + experts],
        grad_inner[None],
        grad_outer[None],
    )


def solution(mesh):
    in_specs = (
        P(("expert", "shard"), None, None),
        P(("expert", "shard"), None),
        P(("expert", "shard"), None, None),
        P(("expert", "shard"), None),
        P("shard"),
        P("shard", None),
        P("shard", None),
        P("shard", None),
        P("shard", None),
        P("shard", None),
        P("shard"),
        P("shard", None),
        P("expert", None, "shard"),
        P("expert", "shard", None),
        P(("expert", "shard"), None, None),
    )
    out_specs = (
        P(("expert", "shard"), None, None),
        P(("expert", "shard"), None, None),
        P("shard"),
        P("shard", None),
        P("shard", None),
        P("shard", None),
        P("shard", None),
        P("shard", None),
        P("shard"),
        P("shard", None),
        P("expert", None, "shard"),
        P("expert", "shard", None),
    )
    return jax.shard_map(
        per_device, mesh=mesh, in_specs=in_specs, out_specs=out_specs, check_vma=False
    )
```

```python
import functools

import jax
import jax.numpy as jnp
from jax import lax
from jax.experimental import pallas as pl
from jax.experimental.pallas import tpu as pltpu
from jax.sharding import PartitionSpec as P
HEAD_DIM=64
BLK=128
EDGES = (12, 16, 23, 32, 46, 64, 91)
BIG=1e9
def bucket_index(offset):
    magnitude = jnp.abs(offset)
    far = 8 + sum(((magnitude >= edge).astype(jnp.int32) for edge in EDGES))
    near = jnp.where(magnitude < 8, magnitude, far)
    return near + 16 * (offset > 0).astype(jnp.int32)

def dot_nt(a,b): return lax.dot_general(a,b,(((1,),(1,)),((),())),preferred_element_type=jnp.float32)
def dot_nn(a,b): return lax.dot_general(a,b,(((1,),(0,)),((),())),preferred_element_type=jnp.float32)

def head_mask():
    lane=lax.broadcasted_iota(jnp.int32,(BLK,2*HEAD_DIM),1)
    return (lane<HEAD_DIM).astype(jnp.float32).astype(jnp.bfloat16)

def build_bias(w_ref, bias_ref, nblk, pairs):
    rows = (2 * nblk - 1) * BLK
    near = (nblk - 2) * BLK
    for j in range(pairs):
        for h in range(2):
            c = slice((2 * j + h) * BLK, (2 * j + h + 1) * BLK)
            w = w_ref[j, h : h + 1, :]
            bias_ref[0:near, c] = jnp.broadcast_to(w[:, 511:512], (near, BLK))
            bias_ref[near + 3 * BLK : rows, c] = jnp.broadcast_to(w[:, 0:1], (near, BLK))
            r = pltpu.roll(jnp.broadcast_to(w, (BLK, 512)), 0, 1, stride=1, stride_axis=0)
            bias_ref[near : near + BLK, c] = r[:, 384:512]
            bias_ref[near + BLK : near + 2 * BLK, c] = r[:, 256:384]
            bias_ref[near + 2 * BLK : near + 3 * BLK, c] = r[:, 128:256]


def by_width(nblk, count, run):
    for n in range(1, nblk + 1):

        @pl.when(count == n)
        def _():
            run(n * BLK)


def pair_of(block, mask):
    return jnp.concatenate([block * mask, block * (1 - mask)], axis=0)


def flip(src_ref, dst_ref, nblk, pairs):
    for j in range(pairs):
        c = slice(j * BLK, (j + 1) * BLK)
        for b in range(nblk):
            s = slice(b * BLK, (b + 1) * BLK)
            dst_ref[c, s] = src_ref[s, c].astype(jnp.float32).T.astype(jnp.bfloat16)


def join_heads(wide):
    return jnp.concatenate([wide[:HEAD_DIM, :BLK], wide[HEAD_DIM:, BLK:]], axis=0)


def fwd_kernel(nblk, pairs, lo_ref, nb_ref, q_ref, k_ref, v_ref, segq_ref, segk_ref, w_ref, ctx_ref, lse_ref, vt_ref, bias_ref):
    build_bias(w_ref, bias_ref, nblk, pairs)
    flip(v_ref, vt_ref, nblk, pairs)
    mask = head_mask()
    lanes = [slice(j * BLK, (j + 1) * BLK) for j in range(pairs)]
    both = [slice(2 * j * BLK, 2 * (j + 1) * BLK) for j in range(pairs)]

    def body(qb, _):
        rows = pl.ds(pl.multiple_of(qb * BLK, BLK), BLK)
        lob = lo_ref[qb]
        sq = segq_ref[rows, :]
        sq = jnp.concatenate([sq, sq], axis=0)
        q_cat = [jnp.concatenate([pair_of(q_ref[rows, c], mask), sq], axis=1) for c in lanes]

        def run(W):
            ks = pl.ds(pl.multiple_of(lob * BLK, BLK), W)
            bs = pl.ds(pl.multiple_of((lob - qb + nblk - 1) * BLK, BLK), W)
            sk = segk_ref[ks, :]
            st = [
                dot_nt(jnp.concatenate([k_ref[ks, c], sk], axis=1), q) + bias_ref[bs, d]
                for c, d, q in zip(lanes, both, q_cat)
            ]
            m = [jnp.max(x, axis=0, keepdims=True) for x in st]
            e = [jnp.exp(x - y) for x, y in zip(st, m)]
            l = [jnp.sum(x, axis=0, keepdims=True) for x in e]
            ot = [dot_nn(vt_ref[c, ks], x.astype(jnp.bfloat16)) / y for c, x, y in zip(lanes, e, l)]
            for j, c in enumerate(lanes):
                ctx_ref[rows, c] = join_heads(ot[j]).T.astype(jnp.bfloat16)
                lse_ref[j, pl.ds(qb, 1), :] = m[j] + jnp.log(l[j])

        by_width(nblk, nb_ref[qb], run)
        return 0

    lax.fori_loop(0, nblk, body, 0)


def bwd_kernel(
    nblk, pairs, lo_ref, nb_ref, q_ref, k_ref, v_ref, do_ref, ctx_ref, lse_ref, segq_ref, segk_ref, w_ref,
    dq_ref, dk_ref, dv_ref, near_ref, far_ref, kt_ref, bias_ref, acc_ref, dka_ref, dva_ref,
):
    build_bias(w_ref, bias_ref, nblk, pairs)
    flip(k_ref, kt_ref, nblk, pairs)
    acc_ref[...] = jnp.zeros_like(acc_ref)
    dka_ref[...] = jnp.zeros_like(dka_ref)
    dva_ref[...] = jnp.zeros_like(dva_ref)
    mask = head_mask()
    lanes = [slice(j * BLK, (j + 1) * BLK) for j in range(pairs)]
    both = [slice(2 * j * BLK, 2 * (j + 1) * BLK) for j in range(pairs)]
    row = lax.broadcasted_iota(jnp.int32, (16, 2 * HEAD_DIM), 0)
    lane = lax.broadcasted_iota(jnp.int32, (16, 2 * HEAD_DIM), 1)
    pick = ((lane // HEAD_DIM) == row).astype(jnp.float32).astype(jnp.bfloat16)

    def body(qb, _):
        rows = pl.ds(pl.multiple_of(qb * BLK, BLK), BLK)
        lob = lo_ref[qb]
        sq = segq_ref[rows, :]
        sq = jnp.concatenate([sq, sq], axis=0)
        q2 = [pair_of(q_ref[rows, c], mask) for c in lanes]
        q_cat = [jnp.concatenate([q, sq], axis=1) for q in q2]
        do2 = [pair_of(do_ref[rows, c], mask) for c in lanes]
        delta = []
        for c in lanes:
            prod = do_ref[rows, c].astype(jnp.float32) * ctx_ref[rows, c].astype(jnp.float32)
            hi = prod.astype(jnp.bfloat16)
            low = (prod - hi.astype(jnp.float32)).astype(jnp.bfloat16)
            dl = dot_nt(pick, hi) + dot_nt(pick, low)
            delta.append(jnp.concatenate([dl[0:1], dl[1:2]], axis=1))
        lse = [lse_ref[j, pl.ds(qb, 1), :] for j in range(pairs)]

        def run(W):
            ks = pl.ds(pl.multiple_of(lob * BLK, BLK), W)
            bs = pl.ds(pl.multiple_of((lob - qb + nblk - 1) * BLK, BLK), W)
            sk = segk_ref[ks, :]
            st = [dot_nt(jnp.concatenate([k_ref[ks, c], sk], axis=1), q) for c, q in zip(lanes, q_cat)]
            dp = [dot_nt(v_ref[ks, c], d) for c, d in zip(lanes, do2)]
            p = [jnp.exp(x + bias_ref[bs, d] - y) for x, d, y in zip(st, both, lse)]
            ds = [x * (y - z) for x, y, z in zip(p, dp, delta)]
            dsb = [x.astype(jnp.bfloat16) for x in ds]
            for j, (c, d) in enumerate(zip(lanes, both)):
                acc_ref[bs, d] += ds[j]
                dva_ref[ks, c] += dot_nn(p[j].astype(jnp.bfloat16), do2[j])
                dka_ref[ks, c] += dot_nn(dsb[j], q2[j])
                dqt = join_heads(dot_nn(kt_ref[c, ks], dsb[j])) * (HEAD_DIM**-0.5)
                dq_ref[rows, c] = dqt.T.astype(jnp.bfloat16)

        by_width(nblk, nb_ref[qb], run)
        return 0

    lax.fori_loop(0, nblk, body, 0)
    dk_ref[...] = dka_ref[...].astype(jnp.bfloat16)
    dv_ref[...] = dva_ref[...].astype(jnp.bfloat16)
    near = (nblk - 2) * BLK
    total = (2 * nblk - 1) * BLK
    for j in range(pairs):
        for h in range(2):
            c = slice((2 * j + h) * BLK, (2 * j + h + 1) * BLK)
            wide = jnp.concatenate(
                [
                    jnp.zeros((BLK, BLK), jnp.float32),
                    acc_ref[near + 2 * BLK : near + 3 * BLK, c],
                    acc_ref[near + BLK : near + 2 * BLK, c],
                    acc_ref[near : near + BLK, c],
                ],
                axis=1,
            )
            near_ref[j, h : h + 1, :] = jnp.sum(unroll_rows(wide), axis=0, keepdims=True)
            low = jnp.sum(acc_ref[0:near, c], axis=0, keepdims=True)
            high = jnp.sum(acc_ref[near + 3 * BLK : total, c], axis=0, keepdims=True)
            far_ref[j, h : h + 1, :] = jnp.concatenate([low, high], axis=1)


def unroll_rows(wide):
    n=wide.shape[1]
    out=wide
    row=lax.broadcasted_iota(jnp.int32,wide.shape,0)
    bit=1
    while bit<wide.shape[0]:
        out=jnp.where((row & bit)!=0,pltpu.roll(out,n-bit,1),out)
        bit*=2
    return out

FWD_PAIRS = 6
BWD_PAIRS = 3


def pair_spec(nrow, pairs):
    return pl.BlockSpec((nrow, 2 * HEAD_DIM * pairs), lambda p, *_: (0, p))


def full_spec(shape):
    return pl.BlockSpec(shape, lambda p, *_: (0,) * len(shape))


def lead_spec(pairs, shape):
    return pl.BlockSpec((pairs,) + shape, lambda p, *_: (p, 0, 0))


def attn_fwd(lo, nb, q, k, v, segq, segk, w):
    L, D = q.shape
    nblk = L // BLK
    every = D // (2 * HEAD_DIM)
    pairs = FWD_PAIRS
    return pl.pallas_call(
        functools.partial(fwd_kernel, nblk, pairs),
        grid_spec=pltpu.PrefetchScalarGridSpec(
            num_scalar_prefetch=2,
            grid=(every // pairs,),
            in_specs=[pair_spec(L, pairs)] * 3 + [full_spec((L, 128))] * 2 + [lead_spec(pairs, (2, 512))],
            out_specs=[pair_spec(L, pairs), lead_spec(pairs, (nblk, 2 * BLK))],
            scratch_shapes=[
                pltpu.VMEM((2 * HEAD_DIM * pairs, L), jnp.bfloat16),
                pltpu.VMEM(((2 * nblk - 1) * BLK, 2 * BLK * pairs), jnp.float32),
            ],
        ),
        out_shape=[
            jax.ShapeDtypeStruct((L, D), jnp.bfloat16),
            jax.ShapeDtypeStruct((every, nblk, 2 * BLK), jnp.float32),
        ],
        compiler_params=pltpu.CompilerParams(vmem_limit_bytes=63 * 2**20),
        cost_estimate=pl.CostEstimate(flops=2 * 10**9, bytes_accessed=8 * 2**20, transcendentals=6 * 10**6),
    )(lo, nb, q, k, v, segq, segk, w)


def attn_bwd(lo, nb, q, k, v, do, ctx, lse, segq, segk, w):
    L, D = q.shape
    nblk = L // BLK
    every = D // (2 * HEAD_DIM)
    pairs = BWD_PAIRS
    rows = (2 * nblk - 1) * BLK
    return pl.pallas_call(
        functools.partial(bwd_kernel, nblk, pairs),
        grid_spec=pltpu.PrefetchScalarGridSpec(
            num_scalar_prefetch=2,
            grid=(every // pairs,),
            in_specs=[pair_spec(L, pairs)] * 5
            + [lead_spec(pairs, (nblk, 2 * BLK))]
            + [full_spec((L, 128))] * 2
            + [lead_spec(pairs, (2, 512))],
            out_specs=[pair_spec(L, pairs)] * 3 + [lead_spec(pairs, (2, 512)), lead_spec(pairs, (2, 256))],
            scratch_shapes=[
                pltpu.VMEM((2 * HEAD_DIM * pairs, L), jnp.bfloat16),
                pltpu.VMEM((rows, 2 * BLK * pairs), jnp.float32),
                pltpu.VMEM((rows, 2 * BLK * pairs), jnp.float32),
                pltpu.VMEM((L, 2 * HEAD_DIM * pairs), jnp.float32),
                pltpu.VMEM((L, 2 * HEAD_DIM * pairs), jnp.float32),
            ],
        ),
        out_shape=[jax.ShapeDtypeStruct((L, D), jnp.bfloat16)] * 3
        + [jax.ShapeDtypeStruct((every, 2, 512), jnp.float32), jax.ShapeDtypeStruct((every, 2, 256), jnp.float32)],
        compiler_params=pltpu.CompilerParams(vmem_limit_bytes=63 * 2**20),
        cost_estimate=pl.CostEstimate(flops=4 * 10**9, bytes_accessed=16 * 2**20, transcendentals=6 * 10**6),
    )(lo, nb, q, k, v, do, ctx, lse, segq, segk, w)


def seg_ranges(seg):
    L = seg.shape[0]
    nblk = L // BLK
    sb = seg.reshape(nblk, BLK)
    first = jnp.sum((seg[None, :] < sb[:, :1]).astype(jnp.int32), axis=1)
    last = jnp.sum((seg[None, :] <= sb[:, -1:]).astype(jnp.int32), axis=1)
    lo = first // BLK
    nb = (last + BLK - 1) // BLK - lo
    return lo.astype(jnp.int32), nb.astype(jnp.int32)


def table_grad(near,far,buckets):
    off=-(jnp.arange(512,dtype=jnp.int32)-256)
    oh=(bucket_index(off)[:,None]==jnp.arange(buckets,dtype=jnp.int32)[None,:]).astype(jnp.float32)
    n=jnp.einsum("hx,xb->bh",near.reshape(-1,512),oh,precision=lax.Precision.HIGHEST)
    f=far.reshape(-1,2,128).sum(-1)
    ids=jnp.arange(buckets,dtype=jnp.int32)[:,None]
    return n+jnp.where(ids==15,f[None,:,0],0)+jnp.where(ids==31,f[None,:,1],0)

TILE=256
def gelu_parts(x):
    c=0.7978845608028654
    x2=x*x
    t=jnp.tanh(x*(c+(c*0.044715)*x2))
    half=0.5*(1.0+t)
    slope=half+0.5*x*(1.0-t*t)*(c+(3*c*0.044715)*x2)
    return x*half,slope

def expert_kernel(count, parts, *refs):
    rows=refs[:count]; cots=refs[count:2*count]
    wi_refs=refs[2*count:2*count+parts]; wo_refs=refs[2*count+parts:2*count+2*parts]
    refs=refs[2*count+2*parts:]
    outs=refs[:count]; act_ref,db_ref,dg_ref=refs[count:count+3]
    x_ref,c_ref,wi_buf,wo_buf,acc_ref,dga_ref,act_buf,db_buf,w_sem,o_sem=refs[count+3:]
    block=wi_refs[0].shape[1]
    per=block//TILE
    total=parts*per
    for k in range(parts):
        pltpu.make_async_copy(wi_refs[k],wi_buf.at[k],w_sem.at[0,k]).start()
        pltpu.make_async_copy(wo_refs[k],wo_buf.at[k],w_sem.at[1,k]).start()
    first=0
    for i in range(count):
        n=rows[i].shape[0]
        x_ref[first:first+n,:]=rows[i][...]
        c_ref[first:first+n,:]=cots[i][...]
        first+=n
    acc_ref[...]=jnp.zeros_like(acc_ref)
    dga_ref[...]=jnp.zeros_like(dga_ref)
    def out_copies(step,slot):
        cols=pl.ds(pl.multiple_of(step*TILE,TILE),TILE)
        return (pltpu.make_async_copy(act_buf.at[slot],act_ref.at[:,cols],o_sem.at[0,slot]),
                pltpu.make_async_copy(db_buf.at[slot],db_ref.at[:,cols],o_sem.at[1,slot]))
    for k in range(parts):
        pltpu.make_async_copy(wi_refs[k],wi_buf.at[k],w_sem.at[0,k]).wait()
        pltpu.make_async_copy(wo_refs[k],wo_buf.at[k],w_sem.at[1,k]).wait()
        def body(c,_):
            step=k*per+c
            slot=lax.rem(step,2)
            @pl.when(step>=2)
            def _():
                for cp in out_copies(step-2,slot): cp.wait()
            cols=pl.ds(pl.multiple_of(c*TILE,TILE),TILE)
            wi=wi_buf[k,:,cols]
            wo=wo_buf[k,cols,:]
            before=dot_nn(x_ref[...],wi)
            up=dot_nt(c_ref[...],wo)
            active,slope=gelu_parts(before)
            prod=active*up
            dga_ref[...]+=prod[:,:128]+prod[:,128:]
            act_buf[slot]=active.astype(jnp.bfloat16)
            db=(up*slope).astype(jnp.bfloat16)
            db_buf[slot]=db
            acc_ref[...]+=dot_nt(db,wi)
            for cp in out_copies(step,slot): cp.start()
            return 0
        lax.fori_loop(0,per,body,0)
    first=0
    for i in range(count):
        n=rows[i].shape[0]
        outs[i][...]=acc_ref[first:first+n,:].astype(jnp.bfloat16)
        first+=n
    ones=jnp.ones((8,128),jnp.bfloat16)
    sums=dga_ref[...]
    hi=sums.astype(jnp.bfloat16)
    rest=sums-hi.astype(jnp.float32)
    mid=rest.astype(jnp.bfloat16)
    low=(rest-mid.astype(jnp.float32)).astype(jnp.bfloat16)
    dg_ref[...]=dot_nt(ones,hi)+dot_nt(ones,mid)+dot_nt(ones,low)
    for step in (total-2,total-1):
        for cp in out_copies(step,step%2): cp.wait()

def expert_half(rows,cots,w_ins,w_outs):
    count=len(rows); parts=len(w_ins)
    width,block=w_ins[0].shape
    R=sum(r.shape[0] for r in rows)
    vm=pl.BlockSpec(memory_space=pltpu.VMEM); hb=pl.BlockSpec(memory_space=pl.ANY)
    outs=pl.pallas_call(functools.partial(expert_kernel,count,parts),
        in_specs=[vm]*(2*count)+[hb]*(2*parts),
        out_specs=[vm]*count+[hb,hb,vm],
        out_shape=[jax.ShapeDtypeStruct(r.shape,jnp.bfloat16) for r in rows]+[jax.ShapeDtypeStruct((R,parts*block),jnp.bfloat16)]*2+[jax.ShapeDtypeStruct((8,R),jnp.float32)],
        scratch_shapes=[pltpu.VMEM((R,width),jnp.bfloat16)]*2+[pltpu.VMEM((parts,width,block),jnp.bfloat16),pltpu.VMEM((parts,block,width),jnp.bfloat16),
            pltpu.VMEM((R,width),jnp.float32),pltpu.VMEM((R,128),jnp.float32),pltpu.VMEM((2,R,TILE),jnp.bfloat16),pltpu.VMEM((2,R,TILE),jnp.bfloat16),
            pltpu.SemaphoreType.DMA((2,parts)),pltpu.SemaphoreType.DMA((2,2))],
        compiler_params=pltpu.CompilerParams(vmem_limit_bytes=48*2**20),
        cost_estimate=pl.CostEstimate(flops=6*R*width*parts*block,bytes_accessed=20*2**20,transcendentals=R*parts*block))(*rows,*cots,*w_ins,*w_outs)
    return outs[:count],outs[count],outs[count+1],outs[count+2][0]

MESH = pl.DeviceIdType.MESH


def shard_peer(bit):
    return (lax.axis_index("expert"), lax.axis_index("shard") ^ bit)


def expert_peer(bit):
    return (lax.axis_index("expert") ^ bit, lax.axis_index("shard"))


def greet(peers):
    barrier = pltpu.get_barrier_semaphore()
    for peer in peers:
        pl.semaphore_signal(barrier, inc=1, device_id=peer, device_id_type=MESH)
    pl.semaphore_wait(barrier, len(peers))


def send(src, dst, send_sem, recv_sem, peer):
    copy = pltpu.make_async_remote_copy(
        src_ref=src, dst_ref=dst, send_sem=send_sem, recv_sem=recv_sem, device_id=peer, device_id_type=MESH
    )
    copy.start()
    return copy


def columns(line, block):
    return jnp.broadcast_to(line[:, block * 128 : (block + 1) * 128], (128, 128)).T


def project_kernel(
    heads, x_in, small_in, q_in, k_in, v_in, o_in, segments,
    q_ref, k_ref, v_ref, normed_ref, small_ref, segq_ref, segk_ref, bias_ref, all_ref,
    x_ref, small_buf, w_buf, unit_ref,
    sem_send, sem_recv, sem_own, sem_out, sem_load,
):
    shard = lax.axis_index("shard")
    own = q_in.shape[0]
    load = pltpu.make_async_copy(x_in, x_ref, sem_load.at[0])
    load.start()

    def rows(bit):
        return pl.ds(pl.multiple_of((shard ^ bit) * own, 64), own)

    ins = [small_in, q_in, k_in, v_in, o_in]
    bufs = [small_buf] + [w_buf.at[i] for i in range(4)]
    count = len(ins)
    kept = []
    for i in range(count):
        copy = pltpu.make_async_copy(ins[i], bufs[i].at[rows(0)], sem_own.at[i])
        copy.start()
        kept.append(copy)
    greet([shard_peer(1), shard_peer(2)])
    far, near, passed = [], [], [None] * count
    for i in range(count):
        far.append(send(ins[i], bufs[i].at[rows(0)], sem_send.at[0, i], sem_recv.at[0, i], shard_peer(2)))
    for i in range(count):
        near.append(send(ins[i], bufs[i].at[rows(0)], sem_send.at[1, i], sem_recv.at[1, i], shard_peer(1)))
    length, width = x_ref.shape
    tile = 512

    def unit(t, _):
        r = pl.ds(pl.multiple_of(t * tile, tile), tile)
        x = x_ref[r, :].astype(jnp.float32)
        unit_ref[r, :] = x * lax.rsqrt(jnp.mean(x * x, axis=-1, keepdims=True) + 1e-6)
        return 0

    def hop(i):
        far[i].wait_recv()
        here = bufs[i].at[rows(2)]
        passed[i] = send(here, here, sem_send.at[2, i], sem_recv.at[2, i], shard_peer(1))

    def finish(i):
        kept[i].wait()
        near[i].wait_recv()
        passed[i].wait_recv()

    load.wait()
    lax.fori_loop(0, length // tile, unit, 0)
    documents = segments[...].astype(jnp.float32)
    ids = lax.broadcasted_iota(jnp.int32, (128, 128), 1).astype(jnp.float32)
    for b in range(length // 128):
        r = slice(b * 128, (b + 1) * 128)
        same = (columns(documents, b) == ids).astype(jnp.float32)
        segq_ref[r, :] = same.astype(jnp.bfloat16)
        segk_ref[r, :] = jnp.where(ids < 16.0, (same - 1.0) * BIG, 0.0).astype(jnp.bfloat16)
    hop(0)
    hop(1)
    finish(0)
    small = small_buf[...]
    small_ref[...] = small
    gain = jnp.concatenate(
        [small[c * 128 : (c + 1) * 128, :].astype(jnp.float32).T[0:1] for c in range(width // 128)], axis=1
    )

    buckets = 32
    part = buckets // 4
    table = jnp.concatenate([small[j * own : j * own + part, :].astype(jnp.float32) for j in range(4)], axis=0)
    table = jnp.concatenate([table, jnp.zeros((128 - buckets, 128), jnp.float32)], axis=0).T
    wide = bias_ref.shape[2]
    offset = wide // 2 - lax.broadcasted_iota(jnp.int32, (128, wide), 1)
    onehot = (bucket_index(offset) == lax.broadcasted_iota(jnp.int32, (128, wide), 0)).astype(jnp.float32)
    lines = dot_nn(table.astype(jnp.bfloat16), onehot.astype(jnp.bfloat16))
    for p in range(heads // 2):
        bias_ref[p] = lines[128 - heads + 2 * p : 130 - heads + 2 * p]

    def norm(t, _):
        r = pl.ds(pl.multiple_of(t * tile, tile), tile)
        normed_ref[r, :] = (unit_ref[r, :] * gain).astype(jnp.bfloat16)
        return 0

    lax.fori_loop(0, length // tile, norm, 0)
    outs = []

    def project_one(i, out):
        finish(i)
        copy = pltpu.make_async_copy(w_buf.at[i - 1], all_ref.at[i - 1], sem_out.at[i - 1])
        copy.start()
        outs.append(copy)

        def run(t, _):
            r = pl.ds(pl.multiple_of(t * tile, tile), tile)
            y = dot_nn(normed_ref[r, :], w_buf[i - 1]).astype(jnp.bfloat16)
            if i == 1:
                y = (y.astype(jnp.float32) * HEAD_DIM**-0.5).astype(jnp.bfloat16)
            out[r, :] = y
            return 0

        lax.fori_loop(0, length // tile, run, 0)

    project_one(1, q_ref)
    hop(2)
    project_one(2, k_ref)
    hop(3)
    project_one(3, v_ref)
    hop(4)
    finish(4)
    copy = pltpu.make_async_copy(w_buf.at[3], all_ref.at[3], sem_out.at[3])
    copy.start()
    outs.append(copy)
    for c in outs:
        c.wait()
    for c in far + near + passed:
        c.wait_send()


def project(x, small, weights, segments, heads):
    length, width = x.shape
    vm = pl.BlockSpec(memory_space=pltpu.VMEM)
    hb = pl.BlockSpec(memory_space=pl.ANY)
    bf = jnp.bfloat16
    shape = jax.ShapeDtypeStruct
    return pl.pallas_call(
        functools.partial(project_kernel, heads),
        in_specs=[hb] * 6 + [vm],
        out_specs=[vm] * 8 + [hb],
        out_shape=[shape((length, width), bf)] * 4 + [shape((width, 128), bf), shape((length, 128), bf), shape((length, 128), bf), shape((heads // 2, 2, 512), jnp.float32)]
        + [shape((4, width, width), bf)],
        scratch_shapes=[
            pltpu.VMEM((length, width), bf),
            pltpu.VMEM((width, 128), bf),
            pltpu.VMEM((4, width, width), bf),
            pltpu.VMEM((length, width), jnp.float32),
            pltpu.SemaphoreType.DMA((3, 5)),
            pltpu.SemaphoreType.DMA((3, 5)),
            pltpu.SemaphoreType.DMA((5,)),
            pltpu.SemaphoreType.DMA((4,)),
            pltpu.SemaphoreType.DMA((1,)),
        ],
        compiler_params=pltpu.CompilerParams(collective_id=0, has_side_effects=True, vmem_limit_bytes=63 * 2**20),
        cost_estimate=pl.CostEstimate(flops=6 * 10**9, bytes_accessed=20 * 2**20, transcendentals=0),
    )(x, small, *weights, segments)


def slot_kernel(cap, route, order, cot, place_ref, cells_ref):
    length = cot.shape[0]
    keys = (route[...] * length + order[...]).astype(jnp.float32)
    starts = (route[...] * length).astype(jnp.float32)
    blocks = length // 128
    sides = [columns(keys, b) for b in range(blocks)]
    slots = []
    for t in range(blocks):
        s = slice(t * 128, (t + 1) * 128)
        sums = sum((c < keys[:, s]).astype(jnp.float32) - (c < starts[:, s]).astype(jnp.float32) for c in sides)
        slots.append(jnp.sum(sums, axis=0, keepdims=True))
    slot = jnp.concatenate(slots, axis=1).astype(jnp.int32)
    place = jnp.where(slot < cap, route[...] * cap + slot, -1)
    place_ref[...] = place
    step = 640
    for t in range(cells_ref.shape[0] // step):
        ids = lax.broadcasted_iota(jnp.int32, (step, length), 0) + t * step
        pick = (ids == place).astype(jnp.float32).astype(jnp.bfloat16)
        cells_ref[t * step : (t + 1) * step, :] = dot_nn(pick, cot[...]).astype(jnp.bfloat16)


def find_slots(route, order, cot, cells, cap):
    length, width = cot.shape
    vm = pl.BlockSpec(memory_space=pltpu.VMEM)
    return pl.pallas_call(
        functools.partial(slot_kernel, cap),
        in_specs=[vm] * 3,
        out_specs=[vm] * 2,
        out_shape=[jax.ShapeDtypeStruct((1, length), jnp.int32), jax.ShapeDtypeStruct((cells, width), jnp.bfloat16)],
        compiler_params=pltpu.CompilerParams(vmem_limit_bytes=63 * 2**20),
        cost_estimate=pl.CostEstimate(flops=2 * 10**9, bytes_accessed=4 * 2**20, transcendentals=0),
    )(route, order, cot)


def gate_columns(line, count, width):
    column = jnp.broadcast_to(line, (128, 256)).T[:count]
    return jnp.concatenate([column] * (width // 128), axis=1)


def experts_kernel(
    size, cap, tile,
    rows_in, gate_in, cot_in, inner_own, outer_own, inner_far,
    back_out, dgate_out, mine_out, other_out, result_out,
    rows, gates, cots, weights, active, d_before, total, d_gate, back, d_gates, back_in, d_gates_in,
    gated_t, g_send, g_recv, stage, result,
    w_sem, wr_sem, row_send, row_recv, gate_send, gate_recv, back_send, back_recv, dg_send, dg_recv,
    g_sem_send, g_sem_recv, cot_sem, out_sem, res_sem, back_sem, dgb_sem,
):
    width = weights.shape[2]
    block = weights.shape[3]
    per = block // tile
    group = 2
    count = group * cap
    me = lax.axis_index("expert")

    def part(k):
        return pl.ds(k * cap, cap)

    local = [
        pltpu.make_async_copy(inner_own, weights.at[0, 0], w_sem.at[0]),
        pltpu.make_async_copy(outer_own, weights.at[0, 1], w_sem.at[1]),
        pltpu.make_async_copy(inner_far, weights.at[2, 0], w_sem.at[2]),
        pltpu.make_async_copy(rows_in.at[me], rows.at[part(0)], w_sem.at[3]),
        pltpu.make_async_copy(gate_in.at[me], gates.at[0], w_sem.at[4]),
    ]
    local += [pltpu.make_async_copy(cot_in.at[me ^ k], cots.at[part(k)], cot_sem.at[k]) for k in range(size)]
    for c in local:
        c.start()
    greet([expert_peer(k) for k in range(1, size)] + [shard_peer(1), shard_peer(2)])
    sent = []
    arrive = {}
    outer_far = send(outer_own, weights.at[2, 1], wr_sem.at[0, 0], wr_sem.at[1, 0], shard_peer(2))

    def dispatch(k):
        arrive[k] = [
            send(gate_in.at[me ^ k], gates.at[k], gate_send.at[k], gate_recv.at[k], expert_peer(k)),
            send(rows_in.at[me ^ k], rows.at[part(k)], row_send.at[k], row_recv.at[k], expert_peer(k)),
        ]
        sent.append(arrive[k][0])

    for k in (4, 5, 2, 3, 6, 7, 1):
        dispatch(k)
    moved = [
        send(inner_own, weights.at[1, 0], wr_sem.at[0, 1], wr_sem.at[1, 1], shard_peer(1)),
        send(outer_own, weights.at[1, 1], wr_sem.at[0, 2], wr_sem.at[1, 2], shard_peer(1)),
        send(inner_far, weights.at[3, 0], wr_sem.at[0, 3], wr_sem.at[1, 3], shard_peer(1)),
    ]
    sent += moved + [outer_far]
    d_gates[...] = jnp.zeros_like(d_gates)
    for c in local:
        c.wait()
    for c in moved:
        c.wait_recv()
    ones = jnp.ones((8, 128), jnp.bfloat16)
    returned = {}

    def arrived(blocks):
        for k in blocks:
            if k:
                for c in arrive[k]:
                    c.wait_recv()

    def forward_back(blocks, spot, first, last):
        span = len(blocks) * cap
        mine = slice(blocks[0] * cap, blocks[0] * cap + span)
        here = slice(spot * count, spot * count + span)
        if first == 0:
            total[here, :] = jnp.zeros((span, width), jnp.float32)
            d_gate[here, :] = jnp.zeros((span, 128), jnp.float32)

        def step(t, _):
            kk = t // per
            cols = pl.ds(pl.multiple_of(lax.rem(t, per) * tile, tile), tile)
            where = pl.ds(pl.multiple_of(t * tile, tile), tile)
            wi = weights[kk, 0, :, cols]
            wo = weights[kk, 1, cols, :]
            before = dot_nn(rows[mine, :], wi)
            up = dot_nt(cots[mine, :], wo)
            value, slope = gelu_parts(before)
            prod = value * up
            d_gate[here, :] += sum(prod[:, c * 128 : (c + 1) * 128] for c in range(tile // 128))
            active[mine, where] = value.astype(jnp.bfloat16)
            db = (up * slope).astype(jnp.bfloat16)
            d_before[mine, where] = db
            total[here, :] += dot_nt(db, wi)
            return 0

        lax.fori_loop(first * per, last * per, step, 0)

    def give_back(blocks, spot):
        span = len(blocks) * cap
        here = slice(spot * count, spot * count + span)
        back[blocks[0] * cap : blocks[0] * cap + span, :] = total[here, :].astype(jnp.bfloat16)
        for k in blocks:
            start = spot * count + (k - blocks[0]) * cap
            sums = d_gate[start : start + cap, :]
            hi = sums.astype(jnp.bfloat16)
            rest = sums - hi.astype(jnp.float32)
            mid = rest.astype(jnp.bfloat16)
            low = (rest - mid.astype(jnp.float32)).astype(jnp.bfloat16)
            d_gates[k, :, 0:cap] = dot_nt(ones, hi) + dot_nt(ones, mid) + dot_nt(ones, low)
            if k:
                returned[k] = [
                    send(d_gates.at[k], d_gates_in.at[k], dg_send.at[k], dg_recv.at[k], expert_peer(k)),
                    send(back.at[part(k)], back_in.at[part(k)], back_send.at[k], back_recv.at[k], expert_peer(k)),
                ]
                sent.extend(returned[k])

    near = ((0, 1), (2, 3))
    for i, blocks in enumerate(near):
        arrived(blocks)
        forward_back(blocks, i, 0, 2)
    outer_far.wait_recv()
    passed = send(weights.at[2, 1], weights.at[3, 1], wr_sem.at[0, 4], wr_sem.at[1, 4], shard_peer(1))
    sent.append(passed)
    passed.wait_recv()
    for i, blocks in enumerate(near):
        forward_back(blocks, i, 2, 4)
        give_back(blocks, i)
    for blocks in ((4,), (5,), (6, 7)):
        arrived(blocks)
        forward_back(blocks, 2, 0, 4)
        give_back(blocks, 2)
    for k in range(size):
        span = slice(k * cap, (k + 1) * cap)
        column = gate_columns(gates[k, 0:1, :], cap, width)
        cots[span, :] = (cots[span, :].astype(jnp.float32) * column).astype(jnp.bfloat16)
        result[span, :] = (rows[span, :].astype(jnp.float32) * column).astype(jnp.bfloat16)
    every = size * cap
    for c in range(width // 128):
        for r in range(every // 128):
            gated_t[c * 128 : (c + 1) * 128, r * 128 : (r + 1) * 128] = (
                result[r * 128 : (r + 1) * 128, c * 128 : (c + 1) * 128].astype(jnp.float32).T.astype(jnp.bfloat16)
            )
    strip = block

    def inner(kk, out):
        return dot_nn(gated_t[out, :], d_before[:, kk * block : (kk + 1) * block])

    def outer(kk, out, t):
        return dot_tn(active[:, pl.ds(pl.multiple_of(kk * block + t * strip, strip), strip)], cots[...])

    def strips(body):
        def run(t, _):
            body(pl.ds(pl.multiple_of(t * strip, strip), strip), t)
            return 0

        lax.fori_loop(0, block // strip, run, 0)

    def chunk(h, kk, out, t):
        return inner(kk, out) if h == 0 else outer(kk, out, t)

    finals = []
    for h in range(2):
        shared = []
        for n, kk in enumerate((3, 1)):

            def give(out, t):
                g_send[h, n, out, :] = chunk(h, kk, out, t).astype(jnp.bfloat16)

            strips(give)
            c = send(g_send.at[h, n], g_recv.at[h, n], g_sem_send.at[h, n], g_sem_recv.at[h, n], shard_peer(1))
            shared.append(c)
        shared[0].wait_recv()
        shared[0].wait_send()

        def other(out, t):
            g_send[h, 0, out, :] = (chunk(h, 2, out, t) + g_recv[h, 0, out, :].astype(jnp.float32)).astype(jnp.bfloat16)

        strips(other)
        c = pltpu.make_async_copy(g_send.at[h, 0], other_out.at[h], out_sem.at[0, h])
        c.start()
        finals.append(c)
        shared[1].wait_recv()
        sent.append(shared[1])

        def keep(out, t):
            stage[h, out, :] = chunk(h, 0, out, t) + g_recv[h, 1, out, :].astype(jnp.float32)

        strips(keep)
        c = pltpu.make_async_copy(stage.at[h], mine_out.at[h], out_sem.at[1, h])
        c.start()
        finals.append(c)

    def produce(r, _):
        span = pl.ds(pl.multiple_of(r * 4 * cap, 16), 4 * cap)
        y = sum(dot_nn(active[span, kk * block : (kk + 1) * block], weights[kk, 1]) for kk in range(4))
        result[span, :] = y.astype(jnp.bfloat16)
        return 0

    lax.fori_loop(0, size // 4, produce, 0)
    for k in range(size):
        c = pltpu.make_async_copy(result.at[part(k)], result_out.at[me ^ k], res_sem.at[k])
        c.start()
        finals.append(c)
    back_in[part(0), :] = back[part(0), :]
    d_gates_in[0] = d_gates[0]
    for k in range(size):
        if k:
            for c in returned[k]:
                c.wait_recv()
        for c in (
            pltpu.make_async_copy(back_in.at[part(k)], back_out.at[me ^ k], back_sem.at[k]),
            pltpu.make_async_copy(d_gates_in.at[k], dgate_out.at[me ^ k], dgb_sem.at[k]),
        ):
            c.start()
            finals.append(c)
    for c in finals:
        c.wait()
    for k in range(1, size):
        arrive[k][1].wait_send()
    for c in sent:
        c.wait_send()


def run_experts(rows, gates, cots, inner_own, outer_own, inner_far):
    size, cap, width = rows.shape
    block = inner_own.shape[1]
    bf = jnp.bfloat16
    f32 = jnp.float32
    every = size * cap
    hb = pl.BlockSpec(memory_space=pl.ANY)
    vm = pltpu.VMEM
    dma = pltpu.SemaphoreType.DMA
    shape = jax.ShapeDtypeStruct
    return pl.pallas_call(
        functools.partial(experts_kernel, size, cap, block),
        in_specs=[hb] * 6,
        out_specs=[hb] * 5,
        out_shape=[
            shape((size, cap, width), bf),
            shape((size, 8, 256), f32),
            shape((2, width, block), f32),
            shape((2, width, block), bf),
            shape((size, cap, width), bf),
        ],
        scratch_shapes=[
            vm((every, width), bf),
            vm((size, 8, 256), f32),
            vm((every, width), bf),
            vm((4, 2, width, block), bf),
            vm((every, 4 * block), bf),
            vm((every, 4 * block), bf),
            vm((6 * cap, width), f32),
            vm((6 * cap, 128), f32),
            vm((every, width), bf),
            vm((size, 8, 256), f32),
            vm((every, width), bf),
            vm((size, 8, 256), f32),
            vm((width, every), bf),
            vm((2, 2, width, block), bf),
            vm((2, 2, width, block), bf),
            vm((2, width, block), f32),
            vm((every, width), bf),
            dma((5,)),
            dma((2, 5)),
        ]
        + [dma((size,))] * 8
        + [dma((2, 2)), dma((2, 2)), dma((size,)), dma((2, 2)), dma((size,)), dma((size,)), dma((size,))],
        compiler_params=pltpu.CompilerParams(collective_id=1, has_side_effects=True, vmem_limit_bytes=63 * 2**20),
        cost_estimate=pl.CostEstimate(flops=36 * 10**9, bytes_accessed=30 * 2**20, transcendentals=4 * 10**6),
    )(rows, gates, cots, inner_own, outer_own, inner_far)


def turned(small, width):
    return jnp.concatenate(
        [small[c * 128 : (c + 1) * 128, :].astype(jnp.float32).T for c in range(width // 128)], axis=1
    )


def three_parts(line):
    hi = line.astype(jnp.bfloat16)
    rest = line - hi.astype(jnp.float32)
    mid = rest.astype(jnp.bfloat16)
    low = rest - mid.astype(jnp.float32)
    none = jnp.zeros((5, line.shape[1]), jnp.float32)
    parts = jnp.concatenate([hi.astype(jnp.float32), mid.astype(jnp.float32), low, none], axis=0)
    return parts.astype(jnp.bfloat16)


def pick_cells(place, first, tile, cells):
    out = []
    for b in range(first // 128, (first + tile) // 128):
        column = columns(place, b)
        lane = lax.broadcasted_iota(jnp.int32, (128, 128), 1).astype(jnp.float32)
        out.append(
            jnp.concatenate([(column == lane + 128.0 * j).astype(jnp.float32) for j in range(cells // 128)], axis=1)
        )
    return jnp.concatenate(out, axis=0).astype(jnp.bfloat16)


def spread_column(line, first, tile, width):
    return jnp.concatenate(
        [
            jnp.concatenate([columns(line, b)] * (width // 128), axis=1)
            for b in range(first // 128, (first + tile) // 128)
        ],
        axis=0,
    )


def route_kernel(
    cap, context_in, tokens_in, weights_in, small, route, place,
    resid_out, cells_out, gate_out, probs_out,
    context, tokens, w_out, normed, sems,
):
    length, width = normed.shape
    experts = probs_out.shape[0]
    loads = [
        pltpu.make_async_copy(weights_in.at[3], w_out, sems.at[0]),
        pltpu.make_async_copy(context_in, context, sems.at[1]),
        pltpu.make_async_copy(tokens_in, tokens, sems.at[2]),
    ]
    for c in loads:
        c.start()
    lines = turned(small, width)
    gain = lines[1:2]
    for c in loads:
        c.wait()
    tile = 512
    for t in range(length // tile):
        r = slice(t * tile, (t + 1) * tile)
        resid = tokens[r, :].astype(jnp.float32) + dot_nn(context[r, :], w_out[...])
        resid_out[r, :] = resid
        scale = lax.rsqrt(jnp.mean(resid * resid, axis=-1, keepdims=True) + 1e-6)
        normed[r, :] = (resid * scale * gain).astype(jnp.bfloat16)
    logits = dot_nt(lines.astype(jnp.bfloat16), normed[...])[2 : 2 + experts]
    top = jnp.exp(logits - jnp.max(logits, axis=0, keepdims=True))
    probs = top / jnp.sum(top, axis=0, keepdims=True)
    probs_out[...] = probs
    which = lax.broadcasted_iota(jnp.int32, probs.shape, 0)
    gate = jnp.sum(jnp.where(which == route[...], probs, 0.0), axis=0, keepdims=True)
    parts = three_parts(gate)
    gate_out[...] = jnp.zeros_like(gate_out)
    for k in range(experts):
        ids = lax.broadcasted_iota(jnp.int32, (cap, length), 0) + k * cap
        pick = (ids == place[...]).astype(jnp.float32).astype(jnp.bfloat16)
        cells_out[k] = dot_nn(pick, normed[...]).astype(jnp.bfloat16)
        found = dot_nt(parts, pick)
        gate_out[k, :, 0:cap] = jnp.broadcast_to(jnp.sum(found, axis=0, keepdims=True), (8, cap))


def run_route(context, tokens, weights, small, route, place, experts, cap):
    length, width = tokens.shape
    bf, f32 = jnp.bfloat16, jnp.float32
    vm = pl.BlockSpec(memory_space=pltpu.VMEM)
    hb = pl.BlockSpec(memory_space=pl.ANY)
    shape = jax.ShapeDtypeStruct
    return pl.pallas_call(
        functools.partial(route_kernel, cap),
        in_specs=[hb] * 3 + [vm] * 3,
        out_specs=[vm] * 4,
        out_shape=[
            shape((length, width), f32),
            shape((experts, cap, width), bf),
            shape((experts, 8, 256), f32),
            shape((experts, length), f32),
        ],
        scratch_shapes=[
            pltpu.VMEM((length, width), bf),
            pltpu.VMEM((length, width), bf),
            pltpu.VMEM((width, width), bf),
            pltpu.VMEM((length, width), bf),
            pltpu.SemaphoreType.DMA((3,)),
        ],
        compiler_params=pltpu.CompilerParams(vmem_limit_bytes=63 * 2**20),
        cost_estimate=pl.CostEstimate(flops=4 * 10**9, bytes_accessed=16 * 2**20, transcendentals=0),
    )(context, tokens, weights, small, route, place)


def unroute_kernel(
    cap, back_in, d_gate_in, resid_in, cot_in, weights_in, context_in, small, route, place, probs,
    d_context_out, d_resid_out, extra, keep_out, grad_out,
    back, resid, cot, w_out, context, d_branch, d_context, d_resid, sems, tile_sems, out_sems,
):
    length, width = resid.shape
    experts = probs.shape[0]
    cells = experts * cap
    loads = [pltpu.make_async_copy(back_in.at[k], back.at[pl.ds(k * cap, cap)], sems.at[4 + k]) for k in range(experts)]
    tile = 1024
    spans = [pl.ds(t * tile, tile) for t in range(length // tile)]
    loads.append(pltpu.make_async_copy(weights_in.at[3], w_out, sems.at[2]))
    last = pltpu.make_async_copy(context_in, context, sems.at[3])
    tiles = [
        [
            pltpu.make_async_copy(resid_in.at[r], resid.at[r], tile_sems.at[0, t]),
            pltpu.make_async_copy(cot_in.at[r], cot.at[r], tile_sems.at[1, t]),
        ]
        for t, r in enumerate(spans)
    ]
    for c in loads + [c for pair in tiles for c in pair] + [last]:
        c.start()
    lines = turned(small, width)
    gain = lines[1:2]
    low_lines = lines.astype(jnp.bfloat16)
    which = lax.broadcasted_iota(jnp.int32, probs.shape, 0)
    chosen = (which == route[...]).astype(jnp.float32)
    gate = jnp.sum(probs[...] * chosen, axis=0, keepdims=True)
    keep = jnp.where(place[...] >= 0, gate, 0.0)
    keep_out[...] = keep
    places = place[...].astype(jnp.float32)
    parts = three_parts(jnp.concatenate([d_gate_in[k, 0:1, 0:cap] for k in range(experts)], axis=1))
    for c in loads:
        c.wait()
    stores = []
    grads = jnp.zeros((128, width), jnp.float32)
    gains = jnp.zeros((1, width), jnp.float32)
    for t in range(length // tile):
        r = slice(t * tile, (t + 1) * tile)
        for c in tiles[t]:
            c.wait()
        pick = pick_cells(places, t * tile, tile, cells)
        d_rows = dot_nn(pick, back[...])
        d_gate = jnp.sum(dot_nt(parts, pick), axis=0, keepdims=True)
        d_logits = probs[:, r] * (chosen[:, r] - gate[:, r]) * d_gate
        padded = jnp.concatenate(
            [
                jnp.zeros((2, tile), jnp.float32),
                d_logits.astype(jnp.bfloat16).astype(jnp.float32),
                jnp.zeros((126 - experts, tile), jnp.float32),
            ],
            axis=0,
        )
        d_normed = dot_nn(padded.T.astype(jnp.bfloat16), low_lines) + spread_column(keep, t * tile, tile, width) * d_rows
        x = resid[r, :]
        scale = lax.rsqrt(jnp.mean(x * x, axis=-1, keepdims=True) + 1e-6)
        unit = x * scale
        grads = grads + dot_nn(padded.astype(jnp.bfloat16), (unit * gain).astype(jnp.bfloat16))
        gains = gains + jnp.sum(d_normed * unit, axis=0, keepdims=True)
        pulled = gain * d_normed
        out = cot[r, :].astype(jnp.float32) + scale * (
            pulled - unit * jnp.mean(unit * pulled, axis=-1, keepdims=True)
        )
        d_resid[r, :] = out
        low = out.astype(jnp.bfloat16)
        d_branch[r, :] = low
        d_context[r, :] = dot_nt(low, w_out[...]).astype(jnp.bfloat16)
        for h, (src, dst) in enumerate(((d_context, d_context_out), (d_resid, d_resid_out))):
            c = pltpu.make_async_copy(src.at[spans[t]], dst.at[spans[t]], out_sems.at[h, t])
            c.start()
            stores.append(c)
    last.wait()
    grad_out[...] = dot_tn(context[...], d_branch[...]).astype(jnp.bfloat16)
    row = lax.broadcasted_iota(jnp.int32, (128, width), 0)
    extra[...] = jnp.where(row == 1, gains, grads)
    for c in stores:
        c.wait()


def run_unroute(back, d_gate, resid, cot, weights, context, small, route, place, probs):
    experts, cap, width = back.shape
    length = resid.shape[0]
    bf, f32 = jnp.bfloat16, jnp.float32
    vm = pl.BlockSpec(memory_space=pltpu.VMEM)
    hb = pl.BlockSpec(memory_space=pl.ANY)
    shape = jax.ShapeDtypeStruct
    return pl.pallas_call(
        functools.partial(unroute_kernel, cap),
        in_specs=[hb, vm, hb, hb, hb, hb] + [vm] * 4,
        out_specs=[hb, hb] + [vm] * 3,
        out_shape=[
            shape((length, width), bf),
            shape((length, width), f32),
            shape((128, width), f32),
            shape((1, length), f32),
            shape((width, width), bf),
        ],
        scratch_shapes=[
            pltpu.VMEM((experts * cap, width), bf),
            pltpu.VMEM((length, width), f32),
            pltpu.VMEM((length, width), bf),
            pltpu.VMEM((width, width), bf),
            pltpu.VMEM((length, width), bf),
            pltpu.VMEM((length, width), bf),
            pltpu.VMEM((length, width), bf),
            pltpu.VMEM((length, width), f32),
            pltpu.SemaphoreType.DMA((4 + experts,)),
            pltpu.SemaphoreType.DMA((2, length // 256)),
            pltpu.SemaphoreType.DMA((2, length // 256)),
        ],
        compiler_params=pltpu.CompilerParams(vmem_limit_bytes=63 * 2**20),
        cost_estimate=pl.CostEstimate(flops=4 * 10**9, bytes_accessed=18 * 2**20, transcendentals=0),
    )(back, d_gate, resid, cot, weights, context, small, route, place, probs)


class Reduction:
    def __init__(self, index, partial, near, far_send, far_recv, full, x_send, x_recv, half, z_send, z_recv, piece, result, send_sems, recv_sems):
        self.partial, self.near, self.far_send, self.far_recv = partial, near, far_send, far_recv
        self.full, self.x_send, self.x_recv, self.half = full, x_send, x_recv, half
        self.z_send, self.z_recv, self.piece, self.result = z_send, z_recv, piece, result
        self.index, self.send_sems, self.recv_sems = index, send_sems, recv_sems
        self.own = full.shape[0]
        self.width = full.shape[1]
        self.type = partial.dtype
        self.copies = {}

    def block(self, bit):
        return pl.ds(pl.multiple_of((lax.axis_index("shard") ^ bit) * self.own, self.own & -self.own), self.own)

    def half_rows(self, bit):
        rows = self.own // 2
        return pl.ds(pl.multiple_of(((lax.axis_index("expert") & 1) ^ bit) * rows, rows & -rows), rows)

    def quarter(self, step):
        j = (lax.axis_index("expert") >> 1) ^ step
        rows = self.own // 2
        if self.type == jnp.float32:
            return (pl.ds(pl.multiple_of(j * (rows // 4), 8), rows // 4), slice(None))
        return (
            pl.ds(pl.multiple_of((j >> 1) * (rows // 2), 16), rows // 2),
            pl.ds(pl.multiple_of((j & 1) * (self.width // 2), 128), self.width // 2),
        )

    def go(self, slot, src, dst, peer):
        self.copies[slot] = send(src, dst, self.send_sems.at[self.index, slot], self.recv_sems.at[self.index, slot], peer)

    def core(self):
        self.go(0, self.partial.at[self.block(3)], self.near.at[1], shard_peer(1))
        self.go(1, self.partial.at[self.block(1)], self.near.at[0], shard_peer(1))

    def y(self):
        self.copies[0].wait_recv()
        other = self.partial[self.block(2), :].astype(jnp.float32) + self.near[1].astype(jnp.float32)
        self.far_send[...] = other.astype(self.type)
        self.go(2, self.far_send, self.far_recv, shard_peer(2))
        self.copies[1].wait_recv()
        self.full[...] = self.partial[self.block(0), :].astype(jnp.float32) + self.near[0].astype(jnp.float32)

    def x(self):
        self.copies[2].wait_recv()
        self.full[...] += self.far_recv[...].astype(jnp.float32)
        self.x_send[...] = self.full[self.half_rows(1), :].astype(self.type)
        self.go(3, self.x_send, self.x_recv, expert_peer(1))

    def z(self):
        self.copies[3].wait_recv()
        self.half[...] = self.own_half() + self.x_recv[...].astype(jnp.float32)
        self.z_send[...] = self.half[...].astype(self.type)
        for step in (2, 3, 1):
            self.go(3 + step, self.z_send.at[self.quarter(step)], self.z_recv.at[step - 1], expert_peer(2 * step))

    def own_half(self):
        return self.full[self.half_rows(0), :]

    def spread(self):
        for step in (1, 2, 3):
            self.copies[3 + step].wait_recv()
        rows, cols = self.quarter(0)
        total = self.half[rows, cols]
        for step in (1, 2, 3):
            total = total + self.z_recv[step - 1].astype(jnp.float32)
        self.piece[...] = total.astype(self.type)
        target = self.place()
        for step in (2, 3, 1):
            self.go(6 + step, self.piece, self.result.at[target], expert_peer(2 * step))
        self.result[target] = self.piece[...]

    def place(self):
        j = lax.axis_index("expert") >> 1
        first = (lax.axis_index("expert") & 1) * (self.own // 2)
        rows = self.own // 2
        if self.type == jnp.float32:
            return (pl.ds(pl.multiple_of(first + j * (rows // 4), 8), rows // 4), slice(None))
        return (
            pl.ds(pl.multiple_of(first + (j >> 1) * (rows // 2), 16), rows // 2),
            pl.ds(pl.multiple_of((j & 1) * (self.width // 2), 128), self.width // 2),
        )

    def cross(self):
        for step in (1, 2, 3):
            self.copies[6 + step].wait_recv()
        self.go(10, self.result.at[self.half_rows(0)], self.result.at[self.half_rows(0)], expert_peer(1))

    def finish(self, out):
        self.copies[10].wait_recv()
        out[...] = self.result[...].astype(jnp.float32)

    def drain(self):
        for c in self.copies.values():
            c.wait_send()


class Crossed(Reduction):
    other = None

    def y(self):
        rows = self.own // 2
        self.copies[0].wait_recv()
        self.other[...] = self.partial[self.block(2), :].astype(jnp.float32) + self.near[1].astype(jnp.float32)
        self.far_send[rows:, :] = self.other[self.half_rows(1), :].astype(self.type)
        self.copies[1].wait_recv()
        self.full[...] = self.partial[self.block(0), :].astype(jnp.float32) + self.near[0].astype(jnp.float32)
        self.far_send[:rows, :] = self.full[self.half_rows(1), :].astype(self.type)
        self.go(2, self.far_send, self.far_recv, expert_peer(1))

    def x(self):
        rows = self.own // 2
        self.copies[2].wait_recv()
        other = self.other[self.half_rows(0), :] + self.far_recv[rows:, :].astype(jnp.float32)
        self.x_send[...] = other.astype(self.type)
        self.go(3, self.x_send, self.x_recv, shard_peer(2))

    def own_half(self):
        return self.full[self.half_rows(0), :] + self.far_recv[: self.own // 2, :].astype(jnp.float32)


def place_table(near, far, ps, own, heads):
    buckets = 32
    wide = near.shape[2]
    offset = wide // 2 - lax.broadcasted_iota(jnp.int32, (wide, buckets), 0)
    onehot = (bucket_index(offset) == lax.broadcasted_iota(jnp.int32, (wide, buckets), 1)).astype(jnp.float32)
    sums = jnp.concatenate([near[j] for j in range(near.shape[0])], axis=0)
    table = lax.dot_general(
        sums, onehot, (((1,), (0,)), ((), ())), preferred_element_type=jnp.float32, precision=lax.Precision.HIGHEST
    )
    ends = jnp.concatenate([far[j] for j in range(far.shape[0])], axis=0)
    low = jnp.sum(ends[:, :128], axis=1, keepdims=True)
    high = jnp.sum(ends[:, 128:], axis=1, keepdims=True)
    which = lax.broadcasted_iota(jnp.int32, (heads, buckets), 1)
    table = table + jnp.where(which == 15, low, 0.0) + jnp.where(which == 31, high, 0.0)
    part = buckets // 4
    square = jnp.concatenate([table, jnp.zeros((heads, 128 - buckets), jnp.float32)], axis=1)
    square = jnp.concatenate([jnp.zeros((128 - heads, 128), jnp.float32), square], axis=0).T
    lane = lax.broadcasted_iota(jnp.int32, (part, 128), 1)
    for j in range(4):
        r = slice(j * own, j * own + part)
        ps[r, :] = jnp.where(lane >= 128 - heads, square[j * part : (j + 1) * part, :], ps[r, :])


def tail_kernel(
    heads, experts,
    normed_in, dq_in, dk_in, dv_in, p_in, weights_in, tokens_in, d_resid_in,
    cells_in, resid_in, small, extra, near_sums, far_sums, place, keep_gate,
    o_out, q_out, k_out, v_out, gain_out, gain_two_out, router_out, table_out, tokens_out, mixed_out,
    normed, dq, dk, dv, weights, tokens, d_resid, cells, resid,
    normed_t, p_ref, near, far_send, far_recv, full, x_send, x_recv, half, z_send, z_recv, piece, result, other,
    ps, s_near, s_far_send, s_far_recv, s_full, s_x_send, s_x_recv, s_half, s_z_send, s_z_recv, s_piece, s_result,
    send_sems, recv_sems, load_sems,
):
    length, width = normed.shape
    tile = 256
    loads = [
        pltpu.make_async_copy(src, dst, load_sems.at[i])
        for i, (src, dst) in enumerate(
            (
                (p_in, p_ref.at[0]),
                (weights_in.at[0:3], weights),
                (normed_in, normed),
                (dq_in, dq),
                (dk_in, dk),
                (dv_in, dv),
                (tokens_in, tokens),
                (d_resid_in, d_resid),
                (resid_in, resid),
            )
        )
    ]
    cap = cells_in.shape[1]
    loads += [
        pltpu.make_async_copy(cells_in.at[k], cells.at[pl.ds(k * cap, cap)], load_sems.at[11 + k])
        for k in range(cells_in.shape[0])
    ]
    for c in loads:
        c.start()
    greet([shard_peer(1), shard_peer(2)] + [expert_peer(k) for k in (1, 2, 4, 6)])
    work = []
    for m in range(4):
        w = (Crossed if m >= 2 else Reduction)(
            m, p_ref.at[m], near.at[m], far_send.at[m], far_recv.at[m], full.at[m], x_send.at[m], x_recv.at[m],
            half.at[m], z_send.at[m], z_recv.at[m], piece.at[m], result.at[m], send_sems, recv_sems,
        )
        w.other = other.at[m % 2]
        work.append(w)
    o, q, k, v = work
    s = Reduction(
        4, ps, s_near, s_far_send, s_far_recv, s_full, s_x_send, s_x_recv, s_half, s_z_send, s_z_recv, s_piece,
        s_result, send_sems, recv_sems,
    )

    def strips(m, make):
        p_ref[m] = make(slice(None)).astype(jnp.bfloat16)

    loads[0].wait()
    o.core()
    loads[2].wait()
    for c in range(width // 128):
        for t in range(length // 128):
            normed_t[c * 128 : (c + 1) * 128, t * 128 : (t + 1) * 128] = (
                normed[t * 128 : (t + 1) * 128, c * 128 : (c + 1) * 128].astype(jnp.float32).T.astype(jnp.bfloat16)
            )
    o.y()
    loads[3].wait()
    strips(1, lambda r: dot_nn(normed_t[r, :], dq[...]))
    q.core()
    loads[4].wait()
    strips(2, lambda r: dot_nn(normed_t[r, :], dk[...]))
    q.y()
    k.core()
    loads[5].wait()
    strips(3, lambda r: dot_nn(normed_t[r, :], dv[...]))
    v.core()
    k.y()
    head = small[...].astype(jnp.float32)
    gain = jnp.concatenate([head[c * 128 : (c + 1) * 128, :].T[0:1] for c in range(width // 128)], axis=1)
    for c in [loads[1]] + loads[6:8]:
        c.wait()

    def back(t, total):
        r = pl.ds(pl.multiple_of(t * tile, tile), tile)
        grad = dot_nt(dq[r, :], weights[0]) + dot_nt(dk[r, :], weights[1]) + dot_nt(dv[r, :], weights[2])
        x = tokens[r, :].astype(jnp.float32)
        scale = lax.rsqrt(jnp.mean(x * x, axis=-1, keepdims=True) + 1e-6)
        unit = x * scale
        pulled = grad * gain
        shift = jnp.mean(unit * pulled, axis=-1, keepdims=True)
        tokens_out[r, :] = (d_resid[r, :] + scale * (pulled - unit * shift)).astype(jnp.bfloat16)
        return total + jnp.sum(grad * unit, axis=0, keepdims=True)

    def some(first, last, total):
        return lax.fori_loop(first, last, back, total)

    def mix(t):
        r = slice(t * tile, (t + 1) * tile)
        arrived = dot_nn(pick_cells(places, t * tile, tile, cells.shape[0]), cells[...])
        mixed_out[r, :] = (resid[r, :] + spread_column(keep_gate, t * tile, tile, width) * arrived).astype(jnp.bfloat16)

    places = place[...].astype(jnp.float32)
    total = some(0, 1, jnp.zeros((1, width), jnp.float32))
    o.x()
    v.y()
    total = some(1, 3, total)
    k.x()
    total = some(3, length // tile, total)
    q.x()
    lane = lax.broadcasted_iota(jnp.int32, (128, 128), 1)
    for c in range(width // 128):
        column = jnp.broadcast_to(total[:, c * 128 : (c + 1) * 128], (128, 128)).T
        ps[c * 128 : (c + 1) * 128, :] = jnp.where(lane == 0, column, extra[:, c * 128 : (c + 1) * 128].T)
    place_table(near_sums, far_sums, ps, s.own, heads)
    s.core()
    o.z()
    k.z()
    s.y()
    for c in loads[8:]:
        c.wait()
    mix(0)
    o.spread()
    v.x()
    q.z()
    s.x()
    mix(1)
    k.spread()
    o.cross()
    v.z()
    s.z()
    mix(2)
    k.cross()
    q.spread()
    v.spread()
    s.spread()
    mix(3)
    o.finish(o_out)
    q.cross()
    v.cross()
    s.cross()
    k.finish(k_out)
    q.finish(q_out)
    v.finish(v_out)
    s.copies[10].wait_recv()
    final = s_result[...]
    pad = jnp.concatenate([final, jnp.zeros((256 - s.own, 128), jnp.float32)], axis=0)
    lines = jnp.concatenate([pad[:128, :].T, pad[128:, :].T], axis=1)
    gain_out[...] = lines[0:1, : s.own]
    gain_two_out[...] = lines[1:2, : s.own]
    router_out[...] = lines[2 : 2 + experts, : s.own]
    table_out[...] = final[: table_out.shape[0], 128 - heads :]
    for w in work + [s]:
        w.drain()


def run_tail(
    normed, dq, dk, dv, partial, weights, tokens, d_resid, cells, resid, small, extra, near, far,
    place, keep_gate, experts, own_buckets,
):
    length, width = normed.shape
    own = width // 4
    heads = near.shape[0] * near.shape[1]
    bf = jnp.bfloat16
    f32 = jnp.float32
    vm = pltpu.VMEM
    hb = pl.BlockSpec(memory_space=pl.ANY)
    mem = pl.BlockSpec(memory_space=pltpu.VMEM)
    h = own // 2
    shape = jax.ShapeDtypeStruct
    return pl.pallas_call(
        functools.partial(tail_kernel, heads, experts),
        in_specs=[hb] * 10 + [mem] * 6,
        out_specs=[mem] * 10,
        out_shape=[shape((own, width), f32)] * 4
        + [
            shape((1, own), f32),
            shape((1, own), f32),
            shape((experts, own), f32),
            shape((own_buckets, heads), f32),
            shape((length, width), bf),
            shape((length, width), bf),
        ],
        scratch_shapes=[vm((length, width), bf)] * 4
        + [
            vm((3, width, width), bf),
            vm((length, width), bf),
            vm((length, width), f32),
            vm((cells.shape[0] * cells.shape[1], width), bf),
            vm((length, width), f32),
            vm((width, length), bf),
            vm((4, width, width), bf),
            vm((4, 2, own, width), bf),
            vm((4, own, width), bf),
            vm((4, own, width), bf),
            vm((4, own, width), f32),
            vm((4, h, width), bf),
            vm((4, h, width), bf),
            vm((4, h, width), f32),
            vm((4, h, width), bf),
            vm((4, 3, h // 2, width // 2), bf),
            vm((4, h // 2, width // 2), bf),
            vm((4, own, width), bf),
            vm((2, own, width), f32),
            vm((width, 128), f32),
            vm((2, own, 128), f32),
            vm((own, 128), f32),
            vm((own, 128), f32),
            vm((own, 128), f32),
            vm((h, 128), f32),
            vm((h, 128), f32),
            vm((h, 128), f32),
            vm((h, 128), f32),
            vm((3, h // 4, 128), f32),
            vm((h // 4, 128), f32),
            vm((own, 128), f32),
            pltpu.SemaphoreType.DMA((5, 11)),
            pltpu.SemaphoreType.DMA((5, 11)),
            pltpu.SemaphoreType.DMA((20,)),
        ],
        compiler_params=pltpu.CompilerParams(collective_id=2, has_side_effects=True, vmem_limit_bytes=63 * 2**20),
        cost_estimate=pl.CostEstimate(flops=11 * 10**9, bytes_accessed=40 * 2**20, transcendentals=0),
    )(
        normed, dq, dk, dv, partial, weights, tokens, d_resid, cells, resid, small, extra, near,
        far, place, keep_gate,
    )


def finish_kernel(count, *refs):
    ins, (mine, other), outs = refs[:count], refs[count : count + 2], refs[count + 2 : 2 * count + 2]
    totals = refs[2 * count + 2 : 2 * count + 4]
    add_a, add_b = refs[2 * count + 4 : 2 * count + 6]
    bufs = refs[2 * count + 6 : 3 * count + 6]
    in_sems, out_sems = refs[3 * count + 6 :]
    first = [pltpu.make_async_copy(mine, add_a, in_sems.at[count]), pltpu.make_async_copy(other, add_b, in_sems.at[count + 1])]
    loads = [pltpu.make_async_copy(ins[i], bufs[i], in_sems.at[i]) for i in range(count)]
    for c in first + loads:
        c.start()
    for c in first:
        c.wait()
    add_a[...] = add_a[...] + add_b[...].astype(jnp.float32)
    stores = [pltpu.make_async_copy(add_a.at[h], totals[h], out_sems.at[count + h]) for h in range(2)]
    for c in stores:
        c.start()
    for i in range(count):
        loads[i].wait()
        c = pltpu.make_async_copy(bufs[i], outs[i], out_sems.at[i])
        c.start()
        stores.append(c)
    for c in stores:
        c.wait()


def run_finish(results, mine, other):
    count = len(results)
    hb = pl.BlockSpec(memory_space=pl.ANY)
    return pl.pallas_call(
        functools.partial(finish_kernel, count),
        in_specs=[hb] * (count + 2),
        out_specs=[hb] * (count + 2),
        out_shape=[jax.ShapeDtypeStruct(r.shape, r.dtype) for r in results]
        + [jax.ShapeDtypeStruct(mine.shape[1:], jnp.float32)] * 2,
        scratch_shapes=[pltpu.VMEM(mine.shape, jnp.float32), pltpu.VMEM(other.shape, jnp.bfloat16)]
        + [pltpu.VMEM(r.shape, r.dtype) for r in results]
        + [pltpu.SemaphoreType.DMA((count + 2,)), pltpu.SemaphoreType.DMA((count + 2,))],
        compiler_params=pltpu.CompilerParams(vmem_limit_bytes=63 * 2**20),
        cost_estimate=pl.CostEstimate(flops=10**6, bytes_accessed=24 * 2**20, transcendentals=0),
    )(*results, mine, other)

EPS = 1e-06
BF = jnp.bfloat16
F32 = jnp.float32


def dot_tn(a, b):
    return lax.dot_general(a, b, (((0,), (0,)), ((), ())), preferred_element_type=F32)


def swap(value, axis, size, bit):
    return lax.ppermute(value, axis, [(i, i ^ bit) for i in range(size)])


def direct(size):
    return size == 8


def exchange(blocks):
    return lax.all_to_all(blocks, "expert", split_axis=0, concat_axis=0, tiled=True)


def gather_shards(value, size):
    if size == 4:
        far = swap(value, "shard", size, 2)
        near = swap(value, "shard", size, 1)
        return [value, near, far, swap(far, "shard", size, 1)]
    return [value] + [swap(value, "shard", size, k) for k in range(1, size)]


def reduce_shards(blocks, size):
    if size == 4:
        near1 = swap(blocks[3].astype(BF), "shard", size, 1)
        near0 = swap(blocks[1].astype(BF), "shard", size, 1)
        other = swap((blocks[2].astype(F32) + near1.astype(F32)).astype(BF), "shard", size, 2)
        return blocks[0].astype(F32) + near0.astype(F32) + other.astype(F32)
    total = blocks[0].astype(F32)
    for k in range(1, size):
        total = total + swap(blocks[k].astype(BF), "shard", size, k).astype(F32)
    return total


def experts_by_collectives(row_blocks, gate_slots, cot_blocks, inner, outer, size, shards, cap):
    inners = gather_shards(inner, shards)
    outers = gather_shards(outer, shards)
    cells, width = size * cap, row_blocks.shape[2]
    rows = exchange(row_blocks).reshape(cells, width)
    cots = cot_blocks.reshape(cells, width)
    gates = exchange(gate_slots.reshape(size, cap)).reshape(cells, 1)
    half = cells // 2
    parts = [expert_half([rows[i : i + half]], [cots[i : i + half]], inners, outers) for i in (0, half)]
    back, active, d_before, d_gate = (
        jnp.concatenate([p[0][0] if i == 0 else p[i] for p in parts], axis=0) for i in range(4)
    )
    back = exchange(back.reshape(size, cap, width)).reshape(cells, width)
    d_gate = exchange(d_gate.reshape(size, cap)).reshape(cells)
    d_out = (cots.astype(F32) * gates).astype(BF)
    gated = (rows.astype(F32) * gates).astype(BF)
    block = inner.shape[1]
    spans = [slice(k * block, (k + 1) * block) for k in range(shards)]
    grad_outer = reduce_shards([dot_tn(active[:, p], d_out) for p in spans], shards)
    grad_inner = reduce_shards([dot_tn(gated, d_before[:, p]) for p in spans], shards)
    result = dot_nn(active, jnp.concatenate(outers, axis=0)).astype(BF).reshape(size, cap, width)
    result = exchange(result).reshape(cells, width)
    return back, d_gate, grad_inner, grad_outer, result


def finish_direct(
    tokens, routes, cotangent, context, weights, small, place, cot_blocks, inner_own, outer_own, inner_far,
    capacity, query, key, value, normed, forward, seg, bias, own_buckets,
):
    experts = lax.axis_size("expert")
    shards = lax.axis_size("shard")
    total, width = normed.shape
    route = routes.reshape(1, total)
    flat = tokens.reshape(total, width)
    resid, row_blocks, gate_lines, probs = run_route(context, flat, weights, small, route, place, experts, capacity)
    back, gate_back, mine, other, expert_out = run_experts(
        row_blocks, gate_lines, cot_blocks, inner_own, outer_own, inner_far
    )
    other = swap(other, "shard", shards, 2)
    out_cells = exchange(expert_out)
    d_context, d_resid, extra, keep, partial = run_unroute(
        back, gate_back, resid, cotangent.reshape(total, width), weights, context, small, route, place, probs
    )
    d_query, d_key, d_value, near_sums, far_sums = attn_bwd(
        seg[0][2], seg[0][3], query, key, value, d_context, context, forward[0][1], seg[0][0], seg[0][1], bias
    )
    (
        sum_output, sum_query, sum_key, sum_value, sum_gain, sum_gain_two, sum_router, sum_table, d_tokens, mixed,
    ) = run_tail(
        normed, d_query, d_key, d_value, partial, weights, flat, d_resid, out_cells, resid,
        small, extra, near_sums, far_sums, place, keep, experts, own_buckets,
    )
    (
        sum_output, sum_query, sum_key, sum_value, d_tokens, mixed, sum_gain, sum_gain_two, sum_router, sum_table,
        grad_inner, grad_outer,
    ) = run_finish(
        [sum_output, sum_query, sum_key, sum_value, d_tokens, mixed, sum_gain, sum_gain_two, sum_router, sum_table],
        mine, other,
    )
    return (
        mixed.reshape(tokens.shape),
        d_tokens.reshape(tokens.shape),
        sum_gain[0],
        sum_query,
        sum_key,
        sum_value,
        sum_output,
        sum_table,
        sum_gain_two[0],
        sum_router.T,
        grad_inner[None],
        grad_outer[None],
    )


def per_device(
    tokens,
    segments,
    routes,
    order,
    gain_attn,
    w_query,
    w_key,
    w_value,
    w_output,
    rel_bias,
    gain_ffn,
    w_router,
    w_in,
    w_out,
    cotangent,
):
    seq_count, length, width = tokens.shape
    total = seq_count * length
    experts = lax.axis_size("expert")
    shards = lax.axis_size("shard")
    me = lax.axis_index("expert")
    my_shard = lax.axis_index("shard")
    capacity = (5 * total + 4 * experts - 1) // (4 * experts)
    cells = experts * capacity
    heads = rel_bias.shape[1]
    own = w_query.shape[0]
    own_buckets = rel_bias.shape[0]
    buckets = own_buckets * shards
    small = jnp.concatenate([gain_attn[:, None], gain_ffn[:, None], w_router], axis=1)
    small = jnp.pad(small, ((0, 0), (0, 128 - small.shape[1])))
    small = lax.dynamic_update_slice(small, rel_bias, (0, 128 - heads))
    route = routes.reshape(total)
    chosen = (route[:, None] == jnp.arange(experts, dtype=jnp.int32)[None, :]).astype(F32)
    cot = cotangent.reshape(total, width)
    ranks = (jnp.arange(seq_count, dtype=jnp.int32)[:, None] * length + order).reshape(1, total)
    place_line, cot_cells = find_slots(routes.reshape(1, total), ranks, cot, cells, capacity)
    cot_blocks = exchange(cot_cells.reshape(experts, capacity, width))
    query, key, value, normed_low, small_all, seg_query, seg_key, bias, weights_all = project(
        tokens.reshape(total, width), small, (w_query, w_key, w_value, w_output), segments.reshape(1, total), heads
    )
    place = place_line[0]
    kept = place >= 0
    spread = (jnp.arange(cells, dtype=jnp.int32)[:, None] == place[None, :]).astype(BF)

    def to_blocks(values):
        return dot_nn(spread, values).astype(BF).reshape(experts, capacity, width)

    query_all, key_all, value_all, output_all = (weights_all[i] for i in range(4))
    inner_own, outer_own = w_in[0], w_out[0]
    if direct(experts):
        inner_own, query = lax.optimization_barrier((inner_own, query))
        inner_far = swap(inner_own, "shard", shards, 2)
    inputs = tokens.reshape(total, width).astype(F32)
    gain_two = small_all[:, 1].astype(F32)
    router_all = small_all[:, 2 : 2 + experts]
    rows_of = [slice(i * length, (i + 1) * length) for i in range(seq_count)]
    seg = [(seg_query[r], seg_key[r]) + seg_ranges(segments[i]) for i, r in enumerate(rows_of)]
    forward = [
        attn_fwd(s[2], s[3], query[r], key[r], value[r], s[0], s[1], bias)
        for s, r in zip(seg, rows_of)
    ]
    context = jnp.concatenate([f[0] for f in forward], axis=0) if seq_count > 1 else forward[0][0]
    if direct(experts):
        return finish_direct(
            tokens, routes, cotangent, context, weights_all, small_all, place_line, cot_blocks, inner_own, outer_own,
            inner_far, capacity, query, key, value, normed_low, forward, seg, bias, own_buckets,
        )
    resid = inputs + dot_nn(context, output_all)
    scale_two = lax.rsqrt(jnp.mean(resid * resid, axis=-1, keepdims=True) + EPS)
    unit_two = resid * scale_two
    normed_two_low = (unit_two * gain_two).astype(BF)
    logits = dot_nn(normed_two_low, router_all)
    probs = jax.nn.softmax(logits, axis=-1)
    gate = jnp.sum(probs * chosen, axis=-1)
    keep_weight = kept.astype(F32)
    keep_gate = gate * keep_weight
    gate_slots = jnp.sum(jnp.where(place[None, :] == jnp.arange(cells)[:, None], gate[None, :], 0), axis=1)
    row_blocks = to_blocks(normed_two_low)
    back, gate_cells, grad_inner, grad_outer, out_cells = experts_by_collectives(
        row_blocks, gate_slots, cot_blocks, w_in[0], w_out[0], experts, shards, capacity
    )
    upstream = cot.astype(F32)
    d_rows = dot_tn(spread, back)
    d_gate = jnp.sum(
        jnp.where(place[:, None] == jnp.arange(cells)[None, :], gate_cells[None, :], 0), axis=1
    )
    d_logits = (probs * (d_gate[:, None] * chosen - (d_gate * gate)[:, None])).astype(BF)
    d_router = dot_tn(normed_two_low, d_logits)
    d_normed_two = dot_nt(d_logits, router_all) + keep_gate[:, None] * d_rows
    d_gain_two = jnp.sum(d_normed_two * unit_two, axis=0)
    pulled = gain_two * d_normed_two
    d_resid = upstream + scale_two * (
        pulled - unit_two * jnp.mean(unit_two * pulled, axis=-1, keepdims=True)
    )
    d_branch = d_resid.astype(BF)
    d_context = dot_nt(d_branch, output_all).astype(BF)
    backward = [
        attn_bwd(s[2], s[3], query[r], key[r], value[r], d_context[r], f[0], f[1], s[0], s[1], bias)
        for s, r, f in zip(seg, rows_of, forward)
    ]
    d_query, d_key, d_value = (
        jnp.concatenate([b[i] for b in backward], axis=0) if seq_count > 1 else backward[0][i]
        for i in range(3)
    )
    tail = jnp.concatenate([jnp.zeros_like(d_gain_two)[:, None], d_gain_two[:, None], d_router], axis=1)
    tail = jnp.pad(tail, ((0, 0), (0, 128 - tail.shape[1])))
    flat_tokens = tokens.reshape(total, width)
    d_table = sum(table_grad(b[3], b[4], buckets) for b in backward)
    tail = lax.dynamic_update_slice(
        tail.reshape(shards, own, 128), d_table.reshape(shards, own_buckets, heads), (0, 0, 128 - heads)
    ).reshape(width, 128)
    if True:
        d_normed = (
            dot_nt(d_query, query_all) + dot_nt(d_key, key_all) + dot_nt(d_value, value_all)
        )
        inputs_again = flat_tokens.astype(F32)
        scale_one = lax.rsqrt(jnp.mean(inputs_again * inputs_again, axis=-1, keepdims=True) + EPS)
        unit_one = inputs_again * scale_one
        tail = tail.at[:, 0].set(jnp.sum(d_normed * unit_one, axis=0))
        pulled_one = small_all[:, 0].astype(F32) * d_normed
        d_tokens = d_resid + scale_one * (
            pulled_one - unit_one * jnp.mean(unit_one * pulled_one, axis=-1, keepdims=True)
        )
        pairs = ((context, d_branch), (normed_low, d_query), (normed_low, d_key), (normed_low, d_value))
        parts = [dot_tn(left, right) for left, right in pairs] + [tail]
        sum_output, sum_query, sum_key, sum_value, sums = (
            lax.psum(
                reduce_shards(
                    [lax.dynamic_slice_in_dim(p, (my_shard ^ k) * own, own, 0) for k in range(shards)], shards
                ),
                "expert",
            )
            for p in parts
        )
    arrived = dot_tn(spread, out_cells)
    mixed = resid + keep_gate[:, None] * arrived
    return (
        mixed.astype(BF).reshape(tokens.shape),
        d_tokens.astype(BF).reshape(tokens.shape),
        sums[:, 0],
        sum_query,
        sum_key,
        sum_value,
        sum_output,
        sums[:own_buckets, 128 - heads :],
        sums[:, 1],
        sums[:, 2 : 2 + experts],
        grad_inner[None],
        grad_outer[None],
    )


def solution(mesh):
    in_specs = (
        P(("expert", "shard"), None, None),
        P(("expert", "shard"), None),
        P(("expert", "shard"), None, None),
        P(("expert", "shard"), None),
        P("shard"),
        P("shard", None),
        P("shard", None),
        P("shard", None),
        P("shard", None),
        P("shard", None),
        P("shard"),
        P("shard", None),
        P("expert", None, "shard"),
        P("expert", "shard", None),
        P(("expert", "shard"), None, None),
    )
    out_specs = (
        P(("expert", "shard"), None, None),
        P(("expert", "shard"), None, None),
        P("shard"),
        P("shard", None),
        P("shard", None),
        P("shard", None),
        P("shard", None),
        P("shard", None),
        P("shard"),
        P("shard", None),
        P("expert", None, "shard"),
        P("expert", "shard", None),
    )
    return jax.shard_map(
        per_device, mesh=mesh, in_specs=in_specs, out_specs=out_specs, check_vma=False
    )
```
